32 devices in a mesh: rep: 8 (over z, core), shard: 4 (over y, x).
Axes of the slice: x: 2, y: 2, z: 4, core: 2. Of those that a mesh axis runs over, the one named last changes fastest.
Arguments:
- hidden: bfloat16 [16384, 1536], P(('rep', 'shard')), may hold values from -6 to 6
- out_grad: bfloat16 [16384, 1536], P(('rep', 'shard')), may hold values from -6 to 6
- norm_gain: bfloat16 [1536], P('shard'), may hold values from 0.5 to 1.5
- in_w: bfloat16 [1536, 6448], P('shard'), may hold values from -0.15625 to 0.15625
- conv_w: bfloat16 [3328, 4], P('shard'), may hold values from -3 to 3
- conv_b: bfloat16 [3328], P('shard'), may hold values from -0.5 to 0.5
- dt_bias: bfloat16 [48], P('shard'), may hold values from -7 to -2.5
- a_log: bfloat16 [48], P('shard'), may hold values from 0 to 2.5
- skip: bfloat16 [48], P('shard'), may hold values from 0.5 to 1.5
- out_gain: bfloat16 [3072], P('shard'), may hold values from 0.5 to 1.5
- out_w: bfloat16 [3072, 1536], P('shard'), may hold values from -0.109375 to 0.109375
- lengths: int32 [32], P(('rep', 'shard')), may hold values from 256 to 512, as said below
- offsets: int32 [32], P(('rep', 'shard')), may hold values from 0 to 256, as said below
Outputs:
- block_out: bfloat16 [16384, 1536], P(('rep', 'shard'))
- hidden_grad: float32 [16384, 1536], P(('rep', 'shard'))
- norm_gain_grad: float32 [1536], P('shard')
- in_w_grad: float32 [1536, 6448], P('shard')
- conv_w_grad: float32 [3328, 4], P('shard')
- conv_b_grad: float32 [3328], P('shard')
- dt_bias_grad: float32 [48], P('shard')
- a_log_grad: float32 [48], P('shard')
- skip_grad: float32 [48], P('shard')
- out_gain_grad: float32 [3072], P('shard')
- out_w_grad: float32 [3072, 1536], P('shard')
The draws below stay inside these ranges and needn't reach their ends.
Inputs may be any that keep to these rules, and one draw needn't show every extreme that they name: `lengths`: in every draw some device's sequence fills all 512 slots, and another device's sequence holds exactly 256 tokens. offsets + lengths <= 512 for every device; in every draw the device with 256 live tokens has its sequence end at its last slot.
All inputs are finite; a program needn't handle non-finite values.
Results may differ from the reference program's by a relative error of at most 0.012.
The reference program's roundings to bfloat16 on the way count: a program that leaves them out, or rounds other values in their place, can miss the bound.
Values may be sent and summed in bfloat16 or wider, within the bound.
No kernel may reach another device: no remote copies, remote signals or barrier semaphores. Data moves between devices by JAX's collectives and lax.ppermute only.
A program may use at most 256 MiB of HBM per device.

```python
import jax
import jax.numpy as jnp
from jax import lax

D = 1536
HEADS = 48
HEADDIM = 64
DSTATE = 128
CONV = 4
SPAN = 256
TOK_DEV = 512
SEQ_MIN = 256
DI = 3072
CC = 3328
PROJ = 6448
TOKENS = 16384
DEVICES = 32


def deal_sequences(key):
    first = jax.random.fold_in(key, 11)
    second = jax.random.fold_in(key, 12)
    third = jax.random.fold_in(key, 13)
    fourth = jax.random.fold_in(key, 14)
    sizes = jax.random.randint(first, (DEVICES,), SEQ_MIN, TOK_DEV + 1)
    fullest = jax.random.randint(second, (), 0, DEVICES)
    shortest = (fullest + 1 + jax.random.randint(fourth, (), 0, DEVICES - 1)) % DEVICES
    device_ids = jnp.arange(DEVICES)
    sizes = jnp.where(device_ids == fullest, TOK_DEV, sizes)
    sizes = jnp.where(device_ids == shortest, SEQ_MIN, sizes)
    starts = jax.random.randint(third, (DEVICES,), 0, 1048576) % (TOK_DEV - sizes + 1)
    starts = jnp.where(device_ids == shortest, TOK_DEV - SEQ_MIN, starts)
    return (sizes.astype(jnp.int32), starts.astype(jnp.int32))


def draw_lengths(key, part):
    return deal_sequences(key)[0]


def draw_offsets(key, part):
    return deal_sequences(key)[1]


def block_scale(key, dims, cuts, smallest, largest):
    def one(axis_at, blocks):
        draws = jax.random.uniform(jax.random.fold_in(jax.random.fold_in(key, 6), axis_at), (blocks,), jnp.float32, smallest / len(cuts), largest / len(cuts))
        return jnp.repeat(jnp.exp(draws), dims[axis_at] // blocks).reshape((-1,) + (1,) * (len(dims) - axis_at - 1))

    level = one(*cuts[0])
    for cut in cuts[1:]:
        level = level * one(*cut)
    return level


def bell_draw(rng, extent, width, bound, cuts=(), held_as=jnp.bfloat16):
    array = width * jax.random.normal(rng, extent, jnp.float32)
    if cuts:
        array = array * block_scale(rng, extent, cuts, -0.22, 0.18)
    return jnp.clip(array, -bound, bound).astype(held_as)


def setup_inputs(seed: int = 0) -> dict:
    seeds = jax.random.split(jax.random.key(seed), 14)
    hidden = bell_draw(seeds[0], (TOKENS, D), 1.0, 6.0, ((0, 32),))
    out_grad = bell_draw(seeds[1], (TOKENS, D), 1.0, 6.0, ((0, 32),))
    norm_gain = jnp.clip(1.0 + 0.1 * jax.random.normal(seeds[2], (D,), jnp.float32), 0.5, 1.5).astype(jnp.bfloat16)
    in_w = bell_draw(seeds[3], (D, PROJ), D ** -0.5, 0.15625, ((0, 4),))
    conv_w = bell_draw(seeds[4], (CC, CONV), CONV ** -0.5, 3.0, ((0, 4),))
    conv_b = jnp.clip(jax.random.uniform(seeds[5], (CC,), jnp.float32, -0.5, 0.5) * block_scale(seeds[5], (CC,), ((0, 4),), -0.4, 0.0), -0.5, 0.5).astype(jnp.bfloat16)
    dt_bias = jnp.clip(-7.0 + 4.5 * jax.random.uniform(seeds[6], (HEADS,), jnp.float32) ** block_scale(seeds[6], (HEADS,), ((0, 4),), -0.2, 0.2), -7.0, -2.5).astype(jnp.bfloat16)
    a_log = jnp.clip(2.5 * jax.random.uniform(seeds[7], (HEADS,), jnp.float32) ** block_scale(seeds[7], (HEADS,), ((0, 4),), -0.2, 0.2), 0.0, 2.5).astype(jnp.bfloat16)
    skip = jnp.clip(0.5 + 1.0 * jax.random.uniform(seeds[8], (HEADS,), jnp.float32) ** block_scale(seeds[8], (HEADS,), ((0, 4),), -0.2, 0.2), 0.5, 1.5).astype(jnp.bfloat16)
    out_gain = jnp.clip(1.0 + 0.1 * jax.random.normal(seeds[9], (DI,), jnp.float32), 0.5, 1.5).astype(jnp.bfloat16)
    out_w = bell_draw(seeds[10], (DI, D), DI ** -0.5, 0.109375, ((0, 4),))
    lengths = draw_lengths(jax.random.fold_in(seeds[13], 71), 0)
    offsets = draw_offsets(jax.random.fold_in(seeds[13], 71), 0)
    return {"hidden": hidden, "out_grad": out_grad, "norm_gain": norm_gain, "in_w": in_w, "conv_w": conv_w, "conv_b": conv_b, "dt_bias": dt_bias, "a_log": a_log, "skip": skip, "out_gain": out_gain, "out_w": out_w, "lengths": lengths, "offsets": offsets}


@jax.custom_vjp
def low(v):
    return lax.optimization_barrier(v.astype(jnp.bfloat16)).astype(jnp.float32)

@jax.custom_vjp
def low_back(v):
    return v

def low_keep(v):
    return (low(v), None)

def low_pass(kept, grad):
    return (grad,)

def back_keep(v):
    return (v, None)

def back_low(kept, grad):
    return (low(grad),)
low.defvjp(low_keep, low_pass)
low_back.defvjp(back_keep, back_low)
epsilon = 1e-05

def decay_matrix(log_decay):
    by_head = log_decay.T
    spread_diff = by_head[:, :, None] - by_head[:, None, :]
    positions = jnp.arange(log_decay.shape[0])
    causal = (positions[:, None] >= positions[None, :])[None]
    return jnp.where(causal, jnp.exp(jnp.where(causal, spread_diff, 0.0)), 0.0)

def span_state(pieces):
    content, write_key, step_size, log_decay, span_total = pieces
    weight = write_key[:, None, :] * (jnp.exp(span_total[None, :] - log_decay) * step_size)[:, :, None]
    weight = low_back(low(weight))
    return low_back(jnp.einsum('shn,shp->hnp', weight, content, precision=lax.Precision.HIGHEST))

def advance(state_carry, pieces):
    span_states, span_total = pieces
    return (jnp.exp(span_total)[:, None, None] * state_carry + span_states, state_carry)

def span_output(pieces):
    content, write_key, read_key, step_size, log_decay, state_in = pieces
    scores = jnp.dot(read_key, write_key.T, precision=lax.Precision.HIGHEST)
    mixing = low_back(low(scores[None] * decay_matrix(log_decay) * step_size.T[:, None, :]))
    inner_out = jnp.einsum('hts,shp->thp', mixing, content, precision=lax.Precision.HIGHEST)
    reader = low_back(low(read_key[:, None, :] * jnp.exp(log_decay)[:, :, None]))
    carried = jnp.einsum('thn,hnp->thp', reader, state_in, precision=lax.Precision.HIGHEST)
    return inner_out + carried

def forward(hidden, norm_gain, in_w, conv_w, conv_b, dt_bias, a_log, skip, out_gain, out_w, live_mask):
    row_count = hidden.shape[0]
    inv_rms = lax.rsqrt(lax.optimization_barrier(jnp.mean(hidden * hidden, axis=1, keepdims=True)) + epsilon)
    normed = low(hidden * inv_rms * norm_gain)
    projected = low_back(low(jnp.dot(normed, in_w, precision=lax.Precision.HIGHEST)))
    gate_z = projected[:, :DI]
    conv_in = projected[:, DI:DI + CC] * live_mask[:, None]
    raw_dt = projected[:, DI + CC:]
    padded = jnp.pad(conv_in, ((CONV - 1, 0), (0, 0)))
    conv_out = conv_b
    for tap_index in range(CONV):
        conv_out = conv_out + padded[tap_index:tap_index + row_count] * conv_w[:, tap_index]
    signal = low_back(low(jax.nn.silu(conv_out) * live_mask[:, None]))
    span_count = row_count // SPAN
    content = signal[:, :DI].reshape(span_count, SPAN, HEADS, HEADDIM)
    write_key = signal[:, DI:DI + DSTATE].reshape(span_count, SPAN, DSTATE)
    read_key = signal[:, DI + DSTATE:].reshape(span_count, SPAN, DSTATE)
    step_size = jax.nn.softplus(raw_dt + dt_bias).reshape(span_count, SPAN, HEADS)
    decay_rate = -jnp.exp(a_log)
    log_decay = jnp.cumsum(step_size * decay_rate, axis=1)
    span_total = log_decay[:, -1]
    states = lax.map(jax.checkpoint(span_state), (content, write_key, step_size, log_decay, span_total))
    start_state = jnp.zeros((HEADS, DSTATE, HEADDIM), jnp.float32)
    _, entering = lax.scan(advance, start_state, (states, span_total))
    entering = low_back(low(entering))
    ssd_out = lax.map(jax.checkpoint(span_output), (content, write_key, read_key, step_size, log_decay, entering))
    ssd_out = low_back(ssd_out + skip[None, None, :, None] * content).reshape(row_count, DI)
    gated_out = ssd_out * jax.nn.silu(gate_z)
    out_rms = lax.rsqrt(lax.optimization_barrier(jnp.mean(gated_out * gated_out, axis=1, keepdims=True)) + epsilon)
    normed_out = low_back(low(gated_out * out_rms * out_gain))
    return hidden + jnp.dot(normed_out, out_w, precision=lax.Precision.HIGHEST) * live_mask[:, None]

def reference(hidden, out_grad, norm_gain, in_w, conv_w, conv_b, dt_bias, a_log, skip, out_gain, out_w, lengths, offsets):
    params = tuple((param.astype(jnp.float32) for param in (norm_gain, in_w, conv_w, conv_b, dt_bias, a_log, skip, out_gain, out_w)))
    blocks = hidden.astype(jnp.float32).reshape(DEVICES, TOK_DEV, D)
    pulls = out_grad.astype(jnp.float32).reshape(DEVICES, TOK_DEV, D)
    positions = jnp.arange(TOK_DEV, dtype=jnp.int32)

    def one_device(totals, pieces):
        block, pull, length, offset = pieces
        live_mask = ((positions >= offset) & (positions < offset + length)).astype(jnp.float32)
        result, backward = jax.vjp(lambda inputs, *weights: forward(inputs, *weights, live_mask), block, *params)
        grads = backward(pull)
        totals = tuple((total_now + grad for total_now, grad in zip(totals, grads[1:])))
        return (totals, (result.astype(jnp.bfloat16), grads[0]))
    start = tuple((jnp.zeros_like(param) for param in params))
    totals, (outputs, input_grads) = lax.scan(one_device, start, (blocks, pulls, lengths.astype(jnp.int32), offsets.astype(jnp.int32)))
    return (outputs.reshape(TOKENS, D), input_grads.reshape(TOKENS, D), totals[0], totals[1], totals[2], totals[3], totals[4], totals[5], totals[6], totals[7], totals[8])
```

```python
import jax
import jax.numpy as jnp
from jax import lax
from jax.sharding import PartitionSpec as P

HEADS = 48
HEADDIM = 64
DSTATE = 128
CONV = 4
SPAN = 256
DI = 3072
CC = 3328


epsilon = 1e-05


def decay_matrix(log_decay):
    by_head = log_decay.T
    spread_diff = by_head[:, :, None] - by_head[:, None, :]
    positions = jnp.arange(log_decay.shape[0])
    causal = (positions[:, None] >= positions[None, :])[None]
    return jnp.where(causal, jnp.exp(jnp.where(causal, spread_diff, 0.0)), 0.0)


def state_forward(pieces):
    content, write_key, step_size, log_decay, span_total = pieces
    spread = jnp.exp(span_total[None, :] - log_decay) * step_size
    weight = (write_key.astype(jnp.float32)[:, None, :] * spread[:, :, None]).astype(jnp.bfloat16)
    return jnp.einsum("shn,shp->hnp", weight, content, preferred_element_type=jnp.float32)


def advance(state_carry, pieces):
    span_states, span_total = pieces
    return (jnp.exp(span_total)[:, None, None] * state_carry + span_states, state_carry)


def output_forward(pieces):
    content, write_key, read_key, step_size, log_decay, state_in = pieces
    scores = jnp.einsum("tn,sn->ts", read_key, write_key, preferred_element_type=jnp.float32)
    mixing = (scores[None] * decay_matrix(log_decay) * step_size.T[:, None, :]).astype(jnp.bfloat16)
    inner_out = jnp.einsum("hts,shp->thp", mixing, content, preferred_element_type=jnp.float32)
    reader = (read_key.astype(jnp.float32)[:, None, :] * jnp.exp(log_decay)[:, :, None]).astype(
        jnp.bfloat16
    )
    carried = jnp.einsum("thn,hnp->thp", reader, state_in, preferred_element_type=jnp.float32)
    return inner_out + carried


def carried_backward(pieces):
    read_key, log_decay, state_in, grad_out = pieces
    growth = jnp.exp(log_decay)
    reader_full = read_key.astype(jnp.float32)[:, None, :] * growth[:, :, None]
    reader = reader_full.astype(jnp.bfloat16)
    grad_reader = jnp.einsum(
        "thp,hnp->thn", grad_out, state_in, preferred_element_type=jnp.float32
    ).astype(jnp.bfloat16)
    grad_reader = grad_reader.astype(jnp.float32)
    grad_read = jnp.sum(grad_reader * growth[:, :, None], axis=1)
    grad_log = jnp.sum(grad_reader * reader_full, axis=2)
    grad_state = jnp.einsum(
        "thn,thp->hnp", reader, grad_out, preferred_element_type=jnp.float32
    ).astype(jnp.bfloat16)
    return (grad_read, grad_log, grad_state)


def retreat(state_carry, pieces):
    grad_state, state_in, span_total = pieces
    growth = jnp.exp(span_total)
    grad_total = growth * jnp.sum(state_carry * state_in, axis=(1, 2))
    return (
        grad_state.astype(jnp.float32) + growth[:, None, None] * state_carry,
        (state_carry.astype(jnp.bfloat16), grad_total),
    )


def inner_backward(pieces):
    content, write_key, read_key, step_size, log_decay, span_total, grad_out, grad_state = pieces
    write_full = write_key.astype(jnp.float32)
    read_full = read_key.astype(jnp.float32)
    spread = jnp.exp(span_total[None, :] - log_decay)
    scaled = spread * step_size
    weight = (write_full[:, None, :] * scaled[:, :, None]).astype(jnp.bfloat16)
    grad_content = jnp.einsum(
        "shn,hnp->shp", weight, grad_state, preferred_element_type=jnp.float32
    )
    grad_weight = jnp.einsum(
        "shp,hnp->shn", content, grad_state, preferred_element_type=jnp.float32
    ).astype(jnp.bfloat16)
    grad_weight = grad_weight.astype(jnp.float32)
    along = jnp.sum(grad_weight * write_full[:, None, :], axis=2)
    grad_step = along * spread
    quick = along * scaled
    grad_total = jnp.sum(quick, axis=0)
    grad_log = -quick
    grad_write = jnp.sum(grad_weight * scaled[:, :, None], axis=1)
    scores = jnp.einsum("tn,sn->ts", read_key, write_key, preferred_element_type=jnp.float32)
    decay_mat = decay_matrix(log_decay)
    through = scores[None] * decay_mat
    step_row = step_size.T[:, None, :]
    mixing_full = through * step_row
    mixing = mixing_full.astype(jnp.bfloat16)
    grad_mix = jnp.einsum(
        "thp,shp->hts", grad_out, content, preferred_element_type=jnp.float32
    ).astype(jnp.bfloat16)
    grad_mix = grad_mix.astype(jnp.float32)
    grad_content = grad_content + jnp.einsum(
        "hts,thp->shp", mixing, grad_out, preferred_element_type=jnp.float32
    )
    grad_scores = jnp.sum(grad_mix * decay_mat * step_row, axis=0)
    grad_step = grad_step + jnp.sum(grad_mix * through, axis=1).T
    flow = grad_mix * mixing_full
    grad_log = grad_log + jnp.sum(flow, axis=2).T - jnp.sum(flow, axis=1).T
    grad_read = jnp.dot(grad_scores, write_full, precision=lax.Precision.HIGHEST)
    grad_write = grad_write + jnp.dot(grad_scores.T, read_full, precision=lax.Precision.HIGHEST)
    return (grad_content, grad_write, grad_read, grad_step, grad_log, grad_total)


BF = jnp.bfloat16
F32 = jnp.float32


def sibling():
    return [(r, r ^ 1) for r in range(lax.axis_size("rep"))]


def swap(x):
    return lax.ppermute(x, "rep", sibling())


def across(x, bit):
    count = lax.axis_size("shard")
    return lax.ppermute(x, "shard", [(k, k ^ bit) for k in range(count)])


def gather_rows(weight, core):
    half = weight.shape[0] // 2
    mine = lax.dynamic_slice_in_dim(weight, core * half, half, 0)
    own = lax.all_gather(mine, "shard", axis=0, tiled=True)
    return own, swap(own)


def pick_half(matrix, core, count):
    rows, width = matrix.shape
    cut = matrix.reshape(rows, count, 2, width // (2 * count))
    return lax.dynamic_index_in_dim(cut, core, 2, keepdims=False).reshape(rows, width // 2)


def bit_order(count, ascending):
    bits = []
    bit = 1
    while bit < count:
        bits.append(bit)
        bit *= 2
    if not ascending:
        bits = bits[::-1]
    order = [0]
    for bit in bits[::-1]:
        order = order + [k | bit for k in order]
    return bits, order


def relative_columns(matrix, shard, order, part):
    count = len(order)
    rows, width = matrix.shape
    group = width // (2 * count)
    return [
        lax.dynamic_slice_in_dim(matrix, (shard ^ k) * (2 * group) + part * group, group, 1)
        for k in order
    ]


def product(lhs, rhs):
    return lax.dot_general(
        lhs, rhs, (((0,), (0,)), ((), ())), preferred_element_type=jnp.float32
    )


def scatter_sum(lhs, rhs, shard):
    count = lax.axis_size("shard")
    kept = []
    for part in range(2):
        bits, order = bit_order(count, part == 1)
        columns = relative_columns(lhs, shard, order, part)
        upper = product(jnp.concatenate(columns[count // 2 :], axis=1), rhs).astype(BF)
        arrived = across(upper, bits[0])
        lower = product(jnp.concatenate(columns[: count // 2], axis=1), rhs)
        held = lower + arrived.astype(F32)
        for bit in bits[1:]:
            middle = held.shape[0] // 2
            arrived = across(held[middle:].astype(BF), bit)
            held = held[:middle] + arrived.astype(F32)
        kept.append(held)
    return jnp.concatenate(kept, axis=0)


def line_sum(held):
    chips = lax.axis_size("rep") // 2

    def move(x, pairs):
        return lax.ppermute(x, "rep", [(2 * a + k, 2 * b + k) for a, b in pairs for k in range(2)])

    if chips == 4:
        place = lax.axis_index("rep") // 2
        arrived = move(held.astype(BF), [(0, 1), (3, 2)])
        inner = (held + arrived.astype(F32)).astype(BF)
        arrived = move(inner, [(1, 2), (2, 1)])
        total = (inner.astype(F32) + arrived.astype(F32)).astype(BF)
        arrived = move(total, [(1, 0), (2, 3)])
        return jnp.where((place == 1) | (place == 2), total, arrived)
    total = held.astype(BF)
    bit = 1
    while bit < chips:
        arrived = move(total, [(k, k ^ bit) for k in range(chips)])
        total = (total.astype(F32) + arrived.astype(F32)).astype(BF)
        bit *= 2
    return total


def interleave(own, other, core, count):
    rows, width = own.shape
    first, second = in_order(own, other, core)
    cut = (rows, count, 1, width // count)
    return jnp.concatenate([first.reshape(cut), second.reshape(cut)], axis=2).reshape(rows, 2 * width)


def column_sum(normed_both, columns, core, shard):
    half = columns.shape[1] // 2
    mine = lax.dynamic_slice_in_dim(columns, core * half, half, 1)
    theirs = swap(lax.dynamic_slice_in_dim(columns, (1 - core) * half, half, 1))
    total = line_sum(scatter_sum(normed_both, jnp.concatenate([mine, theirs], axis=0), shard))
    return [part.astype(F32) for part in in_order(total, swap(total), core)]


def in_order(own, other, core):
    first = jnp.where(core == 0, own, other)
    second = jnp.where(core == 0, other, own)
    return first, second


def shards(
    hidden,
    out_grad,
    norm_gain,
    in_w,
    conv_w,
    conv_b,
    dt_bias,
    a_log,
    skip,
    out_gain,
    out_w,
    lengths,
    offsets,
):
    core = lax.axis_index("rep") % 2
    shard = lax.axis_index("shard")
    count = lax.axis_size("shard")
    small = (norm_gain, conv_w, conv_b, dt_bias, a_log, skip, out_gain)
    packed = jnp.concatenate([part.reshape(-1) for part in small])
    everyone = lax.all_gather(packed, "shard", axis=0, tiled=False)
    whole, start = [], 0
    for part in small:
        cut = everyone[:, start : start + part.size].astype(jnp.float32)
        whole.append(cut.reshape((count * part.shape[0],) + part.shape[1:]))
        start += part.size
    gain_one, kernel, bias_conv, bias_step, log_rate, skip_full, gain_two = whole
    decay_rate = -jnp.exp(log_rate)
    conv_own, conv_other = gather_rows(in_w[:, DI:], core)
    gate_own, gate_other = gather_rows(in_w[:, :DI], core)
    out_own, out_other = gather_rows(out_w, core)
    row_count = hidden.shape[0]
    positions = jnp.arange(row_count, dtype=jnp.int32)
    live_mask = ((positions >= offsets[0]) & (positions < offsets[0] + lengths[0])).astype(
        jnp.float32
    )
    hidden_full = hidden.astype(jnp.float32)
    inv_rms = lax.rsqrt(jnp.mean(hidden_full * hidden_full, axis=1, keepdims=True) + epsilon)
    normed = (hidden_full * inv_rms * gain_one).astype(jnp.bfloat16)
    normed_own = pick_half(normed, core, count)
    normed_rest = pick_half(normed, 1 - core, count)
    normed_other = swap(normed)
    projected = (
        jnp.dot(normed_own, conv_own, preferred_element_type=jnp.float32)
        + jnp.dot(normed_rest, conv_other, preferred_element_type=jnp.float32)
    ).astype(jnp.bfloat16)
    conv_in = projected[:, :CC].astype(jnp.float32) * live_mask[:, None]
    raw_dt = projected[:, CC:].astype(jnp.float32)
    padded = jnp.pad(conv_in, ((CONV - 1, 0), (0, 0)))
    conv_out = bias_conv
    for tap_index in range(CONV):
        conv_out = conv_out + padded[tap_index : tap_index + row_count] * kernel[:, tap_index]
    signal = (jax.nn.silu(conv_out) * live_mask[:, None]).astype(jnp.bfloat16)
    span_count = row_count // SPAN
    content = signal[:, :DI].reshape(span_count, SPAN, HEADS, HEADDIM)
    write_key = signal[:, DI : DI + DSTATE].reshape(span_count, SPAN, DSTATE)
    read_key = signal[:, DI + DSTATE :].reshape(span_count, SPAN, DSTATE)
    pre_step = raw_dt + bias_step
    step_size = jax.nn.softplus(pre_step).reshape(span_count, SPAN, HEADS)
    log_decay = jnp.cumsum(step_size * decay_rate, axis=1)
    span_total = log_decay[:, -1]
    states = lax.map(state_forward, (content, write_key, step_size, log_decay, span_total))
    start_state = jnp.zeros((HEADS, DSTATE, HEADDIM), jnp.float32)
    _, entering = lax.scan(advance, start_state, (states, span_total))
    entering_low = entering.astype(jnp.bfloat16)
    mixed_out = lax.map(
        output_forward, (content, write_key, read_key, step_size, log_decay, entering_low)
    )
    content_full = content.astype(jnp.float32)
    ssd_out = (mixed_out + skip_full[None, None, :, None] * content_full).reshape(row_count, DI)
    gate_z = (
        jnp.dot(normed_own, gate_own, preferred_element_type=jnp.float32)
        + jnp.dot(normed_rest, gate_other, preferred_element_type=jnp.float32)
    ).astype(jnp.bfloat16)
    gate_z = gate_z.astype(jnp.float32)
    silu_z = jax.nn.silu(gate_z)
    gated_out = ssd_out * silu_z
    out_rms = lax.rsqrt(jnp.mean(gated_out * gated_out, axis=1, keepdims=True) + epsilon)
    normed_out = (gated_out * out_rms * gain_two).astype(jnp.bfloat16)
    out_half_own = pick_half(normed_out, core, count)
    out_half_rest = pick_half(normed_out, 1 - core, count)
    branch = jnp.dot(out_half_own, out_own, preferred_element_type=jnp.float32) + jnp.dot(
        out_half_rest, out_other, preferred_element_type=jnp.float32
    )
    block_out = (hidden_full + branch * live_mask[:, None]).astype(jnp.bfloat16)
    out_grad_full = out_grad.astype(jnp.float32)
    pulled = (out_grad_full * live_mask[:, None]).astype(jnp.bfloat16)
    pulled_other = swap(pulled)
    grad_normed_out = interleave(
        jnp.einsum("te,de->td", pulled, out_own, preferred_element_type=jnp.float32).astype(BF),
        jnp.einsum("te,de->td", pulled, out_other, preferred_element_type=jnp.float32).astype(BF),
        core,
        count,
    )
    out_sum = scatter_sum(
        jnp.concatenate([out_half_own, swap(out_half_rest)], axis=0),
        jnp.concatenate([pulled, pulled_other], axis=0),
        shard,
    )
    out_total = line_sum(out_sum)
    out_w_grad = jnp.concatenate(in_order(out_total, swap(out_total), core), axis=0).astype(F32)
    grad_no = grad_normed_out.astype(jnp.float32)
    grad_gain_two = jnp.sum(grad_no * gated_out * out_rms, axis=0)
    grad_norm_two = grad_no * gain_two
    grad_gated = out_rms * grad_norm_two - gated_out * (out_rms * out_rms * out_rms) * jnp.mean(
        grad_norm_two * gated_out, axis=1, keepdims=True
    )
    grad_ssd = (grad_gated * silu_z).astype(jnp.bfloat16)
    sigma_z = jax.nn.sigmoid(gate_z)
    grad_z = grad_gated * ssd_out * sigma_z * (1.0 + gate_z * (1.0 - sigma_z))
    grad_z = grad_z.astype(BF)
    normed_both = jnp.concatenate([normed, normed_other], axis=0)
    gate_grads = column_sum(normed_both, grad_z, core, shard)
    grad_blocks = grad_ssd.reshape(span_count, SPAN, HEADS, HEADDIM)
    grad_blocks_full = grad_blocks.astype(jnp.float32)
    grad_skip = jnp.sum(grad_blocks_full * content_full, axis=(0, 1, 3))
    grad_read_two, grad_log_two, grad_enter = lax.map(
        carried_backward, (read_key, log_decay, entering_low, grad_blocks)
    )
    _, (grad_states, grad_total_rec) = lax.scan(
        retreat, start_state, (grad_enter, entering, span_total), reverse=True
    )
    grad_content, grad_write, grad_read, grad_step, grad_log, grad_total = lax.map(
        inner_backward,
        (content, write_key, read_key, step_size, log_decay, span_total, grad_blocks, grad_states),
    )
    grad_content = grad_content + skip_full[None, None, :, None] * grad_blocks_full
    grad_read = grad_read + grad_read_two
    grad_log = grad_log + grad_log_two
    grad_log = jnp.concatenate(
        [grad_log[:, :-1], grad_log[:, -1:] + (grad_total + grad_total_rec)[:, None, :]], axis=1
    )
    grad_rate = jnp.cumsum(grad_log[:, ::-1], axis=1)[:, ::-1]
    grad_step = grad_step + grad_rate * decay_rate
    grad_a_log = jnp.sum(grad_rate * step_size, axis=(0, 1)) * decay_rate
    grad_raw = grad_step.reshape(row_count, HEADS) * jax.nn.sigmoid(pre_step)
    grad_dt_bias = jnp.sum(grad_raw, axis=0)
    grad_signal = jnp.concatenate(
        [
            grad_content.reshape(row_count, DI),
            grad_write.reshape(row_count, DSTATE),
            grad_read.reshape(row_count, DSTATE),
        ],
        axis=1,
    ).astype(jnp.bfloat16)
    sigma_conv = jax.nn.sigmoid(conv_out)
    grad_conv = (
        grad_signal.astype(jnp.float32)
        * live_mask[:, None]
        * sigma_conv
        * (1.0 + conv_out * (1.0 - sigma_conv))
    )
    grad_conv_b = jnp.sum(grad_conv, axis=0)
    grad_conv_w = jnp.stack(
        [
            jnp.sum(grad_conv * padded[tap_index : tap_index + row_count], axis=0)
            for tap_index in range(CONV)
        ],
        axis=1,
    )
    grad_padded = jnp.zeros((row_count + CONV - 1, CC), jnp.float32)
    for tap_index in range(CONV):
        grad_padded = grad_padded + jnp.pad(
            grad_conv * kernel[:, tap_index], ((tap_index, CONV - 1 - tap_index), (0, 0))
        )
    grad_conv_in = grad_padded[CONV - 1 :] * live_mask[:, None]
    grad_conv_low = grad_conv_in.astype(BF)
    grad_raw_low = grad_raw.astype(BF)
    cut_conv, cut_raw = CC // 2, HEADS // 2
    later = jnp.concatenate(
        [
            grad_conv_low[:, :cut_conv],
            grad_raw_low[:, :cut_raw],
            grad_conv_low[:, cut_conv:],
            grad_raw_low[:, cut_raw:],
        ],
        axis=1,
    )
    later_grads = column_sum(normed_both, later, core, shard)
    in_w_grad = jnp.concatenate(
        gate_grads
        + [later_grads[0][:, :cut_conv], later_grads[1][:, :cut_conv]]
        + [later_grads[0][:, cut_conv:], later_grads[1][:, cut_conv:]],
        axis=1,
    )
    grad_later = jnp.concatenate([grad_conv_low, grad_raw_low], axis=1)

    def back(gate_weight, conv_weight):
        return jnp.einsum(
            "tf,df->td", grad_z, gate_weight, preferred_element_type=jnp.float32
        ) + jnp.einsum("tf,df->td", grad_later, conv_weight, preferred_element_type=jnp.float32)

    grad_normed = interleave(
        back(gate_own, conv_own), back(gate_other, conv_other), core, count
    )
    grad_gain_one = jnp.sum(grad_normed * hidden_full * inv_rms, axis=0)
    grad_norm_one = grad_normed * gain_one
    hidden_grad = (
        inv_rms * grad_norm_one
        - hidden_full
        * (inv_rms * inv_rms * inv_rms)
        * jnp.mean(grad_norm_one * hidden_full, axis=1, keepdims=True)
        + out_grad_full
    )
    local = (
        grad_gain_one,
        grad_conv_w,
        grad_conv_b,
        grad_dt_bias,
        grad_a_log,
        grad_skip,
        grad_gain_two,
    )
    summed = lax.psum(jnp.concatenate([part.reshape(-1) for part in local]), ("rep", "shard"))
    mine, start = [], 0
    for part in local:
        cut = summed[start : start + part.size].reshape(part.shape)
        length = part.shape[0] // count
        mine.append(lax.dynamic_slice_in_dim(cut, shard * length, length, 0))
        start += part.size
    return (
        block_out,
        hidden_grad,
        mine[0],
        in_w_grad,
        mine[1],
        mine[2],
        mine[3],
        mine[4],
        mine[5],
        mine[6],
        out_w_grad,
    )


def solution(mesh):
    return jax.shard_map(
        shards,
        mesh=mesh,
        in_specs=(
            P(("rep", "shard"), None),
            P(("rep", "shard"), None),
            P("shard"),
            P("shard", None),
            P("shard", None),
            P("shard"),
            P("shard"),
            P("shard"),
            P("shard"),
            P("shard"),
            P("shard", None),
            P(("rep", "shard")),
            P(("rep", "shard")),
        ),
        out_specs=(
            P(("rep", "shard"), None),
            P(("rep", "shard"), None),
            P("shard"),
            P("shard", None),
            P("shard", None),
            P("shard"),
            P("shard"),
            P("shard"),
            P("shard"),
            P("shard"),
            P("shard", None),
        ),
        check_vma=False,
    )
```

```python
import functools

import jax
import jax.numpy as jnp
from jax import lax
from jax.experimental import pallas as pl
from jax.experimental.pallas import tpu as pltpu
from jax.sharding import PartitionSpec as P

HEADS = 48
HEADDIM = 64
DSTATE = 128
CONV = 4
SPAN = 256
DI = 3072
CC = 3328
TILE = 256
GROUPS = DI // TILE
PER = TILE // HEADDIM
CHUNK = 64
LANES = 128
epsilon = 1e-05
FAR = -1e30

BF = jnp.bfloat16
F32 = jnp.float32
MIB = 1 << 20


def dot(lhs, rhs):
    return jnp.dot(lhs, rhs, preferred_element_type=F32)


def dot_nt(lhs, rhs):
    return lax.dot_general(lhs, rhs, (((1,), (1,)), ((), ())), preferred_element_type=F32)


def dot_tn(lhs, rhs):
    return lax.dot_general(lhs, rhs, (((0,), (0,)), ((), ())), preferred_element_type=F32)


def pieces(value):
    high = value.astype(BF)
    rest = value - high.astype(F32)
    middle = rest.astype(BF)
    low = (rest - middle.astype(F32)).astype(BF)
    return high, middle, low


def fine_dot(lhs, rhs, product):
    high, middle, low = pieces(lhs)
    return product(high, rhs) + (product(middle, rhs) + product(low, rhs))


def row_ids(start, shape):
    return start + lax.broadcasted_iota(jnp.int32, shape, 0)


def live_rows(meta, start, shape):
    ids = row_ids(start, shape)
    return (ids >= meta[1]) & (ids < meta[1] + meta[2])


def assemble(target, own, rest, core, count):
    half = own.shape[0] // count
    for k in range(count):
        here = pl.multiple_of(2 * k * half + core * half, 16)
        there = pl.multiple_of(2 * k * half + (1 - core) * half, 16)
        target[pl.ds(here, half), :] = own[k * half : (k + 1) * half, :]
        target[pl.ds(there, half), :] = rest[k * half : (k + 1) * half, :]


def call(body, name, meta, operands, in_specs, outs, out_specs, scratch, grid, flops, moved, limit):
    return pl.pallas_call(
        body,
        name=name,
        grid_spec=pltpu.PrefetchScalarGridSpec(
            num_scalar_prefetch=1,
            grid=(grid,),
            in_specs=in_specs,
            out_specs=out_specs,
            scratch_shapes=scratch,
        ),
        out_shape=outs,
        compiler_params=pltpu.CompilerParams(vmem_limit_bytes=limit * MIB),
        cost_estimate=pl.CostEstimate(flops=flops, bytes_accessed=moved, transcendentals=0),
    )(meta, *operands)


def whole(shape):
    rank = len(shape)
    return pl.BlockSpec(shape, lambda i, meta: (0,) * rank)


def tiles(rows, width, shift=0, last=None):
    def index(i, meta):
        at = i + shift
        if last is not None:
            at = jnp.clip(at, 0, last)
        return (0, at)

    return pl.BlockSpec((rows, width), index)


def shape_of(shape, kind=F32):
    return jax.ShapeDtypeStruct(shape, kind)


def conv_body(
    count, meta, x, own, rest, own_dt, rest_dt, taps, steps,
    masked, signal, columns, rows, trio, weight, weight_dt, shifted,
):
    tokens = x.shape[0]
    core = meta[0]
    assemble(weight, own, rest, core, count)
    low = dot(x[...], weight[...]).astype(BF)
    low = jnp.where(live_rows(meta, 0, low.shape), low, jnp.zeros_like(low))
    masked[...] = low
    shifted[0:8, :] = jnp.zeros((8, TILE), F32)
    shifted[8:, :] = low.astype(F32)
    for at in range(0, tokens, CHUNK):
        out = taps[4:5, :]
        for k in range(CONV):
            out = out + shifted[at + 5 + k : at + 5 + k + CHUNK, :] * taps[k : k + 1, :]
        out = out * jax.nn.sigmoid(out)
        out = jnp.where(live_rows(meta, at, out.shape), out, 0.0)
        signal[at : at + CHUNK, :] = out.astype(BF)

    @pl.when(pl.program_id(0) == 0)
    def _():
        assemble(weight_dt, own_dt, rest_dt, core, count)
        raw = dot(x[...], weight_dt[...]).astype(BF).astype(F32)
        pre = raw + steps[0:1, :]
        size = jnp.maximum(pre, 0.0) + jnp.log1p(jnp.exp(-jnp.abs(pre)))
        rate = size * steps[1:2, :]
        lower = row_ids(0, (SPAN, SPAN)) >= lax.broadcasted_iota(jnp.int32, (SPAN, SPAN), 1)
        lower = jnp.where(lower, 1.0, 0.0).astype(BF)
        trio[0] = pre
        trio[1] = size
        for at in range(0, tokens, SPAN):
            high, middle, small = pieces(rate[at : at + SPAN])
            trio[2, at : at + SPAN, :] = dot(lower, high) + (dot(lower, middle) + dot(lower, small))
        log = trio[2]
        size_rows = size.T
        log_rows = log.T
        for g in range(GROUPS):
            a, b = g * PER, (g + 1) * PER
            columns[g] = jnp.concatenate([log[:, a:b], size[:, a:b]], axis=1)
            rows[g] = jnp.concatenate([log_rows[a:b], size_rows[a:b]], axis=0)


def conv_forward(meta, x, own, rest, own_dt, rest_dt, taps, steps, count):
    tokens, width = x.shape
    half = own.shape[0]
    return call(
        functools.partial(conv_body, count), "conv_forward", meta,
        (x, own, rest, own_dt, rest_dt, taps, steps),
        [
            whole((tokens, width)), tiles(half, TILE), tiles(half, TILE),
            whole((half, LANES)), whole((half, LANES)), tiles(8, TILE), whole((8, LANES)),
        ],
        [
            shape_of((tokens, CC), BF), shape_of((tokens, CC), BF),
            shape_of((GROUPS, tokens, 2 * PER)), shape_of((GROUPS, 2 * PER, tokens)),
            shape_of((3, tokens, LANES)),
        ],
        [
            tiles(tokens, TILE), tiles(tokens, TILE),
            whole((GROUPS, tokens, 2 * PER)), whole((GROUPS, 2 * PER, tokens)),
            whole((3, tokens, LANES)),
        ],
        [
            pltpu.VMEM((2 * half, TILE), BF), pltpu.VMEM((2 * half, LANES), BF),
            pltpu.VMEM((tokens + 8, TILE), F32),
        ],
        CC // TILE, 2 * tokens * width * CC, 24 * MIB, 40,
    )


def lane_half(shape, half):
    ids = lax.broadcasted_iota(jnp.int32, shape, 1)
    return (ids >= HEADDIM) if half else (ids < HEADDIM)


def scan_body(meta, content, keys, columns, rows, skip, out, entering, scores, write_rows):
    half = SPAN // 2

    @pl.when(pl.program_id(0) == 0)
    def _():
        for span in range(2):
            at = span * SPAN
            scores[span] = dot_nt(keys[at : at + SPAN, DSTATE:], keys[at : at + SPAN, :DSTATE])
        write_rows[...] = keys[0:SPAN, :DSTATE].astype(F32).T

    causal = row_ids(0, (half, half)) >= lax.broadcasted_iota(jnp.int32, (half, half), 1)
    causal_low = row_ids(half, (half, SPAN)) >= lax.broadcasted_iota(jnp.int32, (half, SPAN), 1)
    read = keys[SPAN:, DSTATE:].astype(F32)
    for pair in range(PER // 2):
        lanes = slice(pair * 2 * HEADDIM, (pair + 1) * 2 * HEADDIM)
        first, second, states = [], [], []
        for h in range(2):
            n = 2 * pair + h
            for span in range(2):
                at = span * SPAN
                value = content[at : at + SPAN, lanes]
                log_row = rows[0, n : n + 1, at : at + SPAN]
                step_row = rows[0, PER + n : PER + n + 1, at : at + SPAN]
                upper = columns[0, at : at + half, n : n + 1] - log_row[:, :half]
                upper = jnp.exp(jnp.where(causal, upper, FAR))
                mix = (scores[span, :half, :half] * upper * step_row[:, :half]).astype(BF)
                top = dot(mix, value[:half])
                lower = columns[0, at + half : at + SPAN, n : n + 1] - log_row
                lower = jnp.exp(jnp.where(causal_low, lower, FAR))
                mix = (scores[span, half:, :] * lower * step_row).astype(BF)
                bottom = dot(mix, value)
                both = jnp.concatenate([top, bottom], axis=0)
                if span == 0:
                    spread = jnp.exp(log_row[:, SPAN - 1 :] - log_row) * step_row
                    weight = (write_rows[...] * spread).astype(BF)
                    states.append(dot(weight, value))
                    first.append(both)
                else:
                    second.append(both)
        chosen = lane_half((DSTATE, 2 * HEADDIM), 0)
        state = jnp.where(chosen, states[0], states[1]).astype(BF)
        entering[0, :, lanes] = state
        for h in range(2):
            n = 2 * pair + h
            growth = jnp.exp(columns[0, SPAN:, n : n + 1])
            second[h] = second[h] + dot((read * growth).astype(BF), state)
        chosen = lane_half((SPAN, 2 * HEADDIM), 0)
        for span, parts in ((0, first), (1, second)):
            at = span * SPAN
            mixed = jnp.where(chosen, parts[0], parts[1])
            value = content[at : at + SPAN, lanes].astype(F32)
            out[at : at + SPAN, lanes] = mixed + skip[:, lanes] * value


def scan_forward(meta, signal, columns, rows, skip):
    tokens = signal.shape[0]
    last = DI // TILE
    return call(
        scan_body, "scan_forward", meta, (signal, signal, columns, rows, skip),
        [
            tiles(tokens, TILE), pl.BlockSpec((tokens, TILE), lambda i, meta: (0, last)),
            pl.BlockSpec((1, tokens, 2 * PER), lambda i, meta: (i, 0, 0)),
            pl.BlockSpec((1, 2 * PER, tokens), lambda i, meta: (i, 0, 0)),
            tiles(1, TILE),
        ],
        [shape_of((tokens, DI)), shape_of((GROUPS, DSTATE, TILE), BF)],
        [tiles(tokens, TILE), pl.BlockSpec((1, DSTATE, TILE), lambda i, meta: (i, 0, 0))],
        [pltpu.VMEM((2, SPAN, SPAN), F32), pltpu.VMEM((DSTATE, SPAN), F32)],
        GROUPS, 10 * 10**9, 12 * MIB, 32,
    )


def gate_body(count, meta, x, own, rest, mixed, gain, gate, normed, scale, weight, gated, total):
    step = pl.program_id(0)
    tokens = x.shape[0]
    assemble(weight, own, rest, meta[0], count)
    low = dot(x[...], weight[...]).astype(BF)
    gate[...] = low

    @pl.when(step == 0)
    def _():
        total[...] = jnp.zeros_like(total)

    for at in range(0, tokens, CHUNK):
        part = gate[at : at + CHUNK, :].astype(F32)
        part = mixed[at : at + CHUNK, :] * (part * jax.nn.sigmoid(part))
        gated[step, at : at + CHUNK, :] = part
        square = part * part
        total[at : at + CHUNK, :] += square[:, :LANES] + square[:, LANES:]

    @pl.when(step == pl.num_programs(0) - 1)
    def _():
        mean = jnp.sum(total[...], axis=1, keepdims=True) / DI
        scale[...] = lax.rsqrt(mean + epsilon)

        def finish(g, carry):
            lanes = pl.ds(pl.multiple_of(g * TILE, TILE), TILE)
            for at in range(0, tokens, CHUNK):
                part = gated[g, at : at + CHUNK, :] * scale[at : at + CHUNK, :] * gain[:, lanes]
                normed[at : at + CHUNK, lanes] = part.astype(BF)
            return carry

        lax.fori_loop(0, GROUPS, finish, 0)


def gate_forward(meta, x, own, rest, mixed, gain, count):
    tokens, width = x.shape
    half = own.shape[0]
    return call(
        functools.partial(gate_body, count), "gate_forward", meta, (x, own, rest, mixed, gain),
        [
            whole((tokens, width)), tiles(half, TILE), tiles(half, TILE),
            tiles(tokens, TILE), whole((1, DI)),
        ],
        [shape_of((tokens, DI), BF), shape_of((tokens, DI), BF), shape_of((tokens, 1))],
        [tiles(tokens, TILE), whole((tokens, DI)), whole((tokens, 1))],
        [
            pltpu.VMEM((2 * half, TILE), BF), pltpu.VMEM((GROUPS, tokens, TILE), F32),
            pltpu.VMEM((tokens, LANES), F32),
        ],
        GROUPS, 2 * tokens * width * DI, 28 * MIB, 48,
    )


def out_body(
    count, meta, normed, own, rest, pulled, hidden, mixed, gate, scale, gain,
    block, grad_gate, grad_mixed, grad_gain, weight, branch, back, total,
):
    step = pl.program_id(0)
    tokens = pulled.shape[0]
    width = mixed.shape[1]
    lanes = [slice(at, at + TILE) for at in range(0, width, TILE)] if width % TILE == 0 else [
        slice(at, at + LANES) for at in range(0, width, LANES)
    ]

    @pl.when(step == 0)
    def _():
        branch[...] = jnp.zeros_like(branch)
        total[...] = jnp.zeros_like(total)

    @pl.when(step < count)
    def _():
        assemble(weight, own, rest, meta[0], 1)
        branch[...] += dot(normed[...], weight[...])
        back[step] = dot_nt(pulled[...], weight[...]).astype(BF)
        grad_gain[...] = jnp.zeros_like(grad_gain)

        def first(n, carry):
            rows = pl.ds(pl.multiple_of(n * CHUNK, CHUNK), CHUNK)
            r = scale[rows, :]
            for cut in lanes:
                z = gate[rows, cut].astype(F32)
                gated = mixed[rows, cut] * (z * jax.nn.sigmoid(z))
                grad = back[step, rows, cut].astype(F32)
                inner = grad * gain[:, cut] * gated
                for at in range(0, inner.shape[1], LANES):
                    total[rows, :] += inner[:, at : at + LANES]
                grad_gain[:, cut] += jnp.sum(grad * gated * r, axis=0, keepdims=True)
            return carry

        lax.fori_loop(0, tokens // CHUNK, first, 0)

    @pl.when(step == count - 1)
    def _():
        for at in range(0, tokens, CHUNK):
            part = branch[at : at + CHUNK, :]
            part = jnp.where(live_rows(meta, at, part.shape), part, 0.0)
            block[at : at + CHUNK, :] = (hidden[at : at + CHUNK, :].astype(F32) + part).astype(BF)

    @pl.when(step >= count)
    def _():
        def second(n, carry):
            rows = pl.ds(pl.multiple_of(n * CHUNK, CHUNK), CHUNK)
            r = scale[rows, :]
            mean = jnp.sum(total[rows, :], axis=1, keepdims=True) / DI
            factor = r * r * r * mean
            for cut in lanes:
                z = gate[rows, cut].astype(F32)
                sigma = jax.nn.sigmoid(z)
                silu = z * sigma
                out = mixed[rows, cut]
                gated = out * silu
                grad = back[step - count, rows, cut].astype(F32) * gain[:, cut]
                grad = r * grad - gated * factor
                grad_mixed[rows, cut] = (grad * silu).astype(BF)
                grad_gate[rows, cut] = (grad * out * sigma * (1.0 + z * (1.0 - sigma))).astype(BF)
            return carry

        lax.fori_loop(0, tokens // CHUNK, second, 0)


def out_forward(meta, normed, own, rest, pulled, hidden, mixed, gate, scale, gain, count):
    tokens, width = hidden.shape
    part = DI // count
    half = part // 2

    def early(rows, columns):
        return pl.BlockSpec((rows, columns), lambda i, meta: (0, jnp.minimum(i, count - 1)))

    def twice(rows, columns):
        return pl.BlockSpec((rows, columns), lambda i, meta: (0, lax.rem(i, count)))

    weight_spec = pl.BlockSpec((half, width), lambda i, meta: (jnp.minimum(i, count - 1), 0))
    return call(
        functools.partial(out_body, count), "out_forward", meta,
        (normed, own, rest, pulled, hidden, mixed, gate, scale, gain),
        [
            early(tokens, part), weight_spec, weight_spec, whole((tokens, width)),
            whole((tokens, width)), twice(tokens, part), twice(tokens, part), whole((tokens, 1)),
            twice(1, part),
        ],
        [
            shape_of((tokens, width), BF), shape_of((tokens, DI), BF), shape_of((tokens, DI), BF),
            shape_of((1, DI)),
        ],
        [
            whole((tokens, width)), tiles(tokens, part, -count, count - 1),
            tiles(tokens, part, -count, count - 1), early(1, part),
        ],
        [
            pltpu.VMEM((part, width), BF), pltpu.VMEM((tokens, width), F32),
            pltpu.VMEM((count, tokens, part), BF), pltpu.VMEM((tokens, LANES), F32),
        ],
        2 * count, 4 * tokens * width * DI, 40 * MIB, 56,
    )


def conv_back(meta, grad, masked, taps, result, sums, shifted, grad_conv):
    tokens = masked.shape[0]
    shifted[0:8, :] = jnp.zeros((8, TILE), F32)
    shifted[8:, :] = masked[...].astype(F32)
    grad_conv[tokens:, :] = jnp.zeros((8, TILE), F32)
    sums[...] = jnp.zeros_like(sums)
    for at in range(0, tokens, CHUNK):
        near = [shifted[at + 5 + k : at + 5 + k + CHUNK, :] for k in range(CONV)]
        out = taps[4:5, :]
        for k in range(CONV):
            out = out + near[k] * taps[k : k + 1, :]
        sigma = jax.nn.sigmoid(out)
        low = grad[at : at + CHUNK, :].astype(BF).astype(F32)
        back = low * sigma * (1.0 + out * (1.0 - sigma))
        back = jnp.where(live_rows(meta, at, back.shape), back, 0.0)
        grad_conv[at : at + CHUNK, :] = back
        for k in range(CONV):
            sums[k : k + 1, :] += jnp.sum(back * near[k], axis=0, keepdims=True)
        sums[4:5, :] += jnp.sum(back, axis=0, keepdims=True)
    for at in range(0, tokens, CHUNK):
        out = grad_conv[at + 3 : at + 3 + CHUNK, :] * taps[0:1, :]
        for k in range(1, CONV):
            out = out + grad_conv[at + 3 - k : at + 3 - k + CHUNK, :] * taps[k : k + 1, :]
        out = jnp.where(live_rows(meta, at, out.shape), out, 0.0)
        result[at : at + CHUNK, :] = out.astype(BF)


def scan_back_body(
    meta, content, keys, grad_out, entering, columns, rows, skip, masked, taps,
    scores_in, write_in, read_in,
    result, sums, grad_columns, grad_rows, grad_scores, grad_write, grad_read,
    scores, read_rows, grad, shifted, grad_conv,
):
    half = SPAN // 2

    @pl.when(pl.program_id(0) == 0)
    def _():
        for span in range(2):
            at = span * SPAN
            scores[span] = dot_nt(keys[at : at + SPAN, :DSTATE], keys[at : at + SPAN, DSTATE:])
        read_rows[...] = keys[SPAN:, DSTATE:].astype(F32).T
        grad_scores[...] = scores_in[...]
        grad_write[...] = write_in[...]
        grad_read[...] = read_in[...]

    causal = row_ids(0, (half, SPAN)) <= lax.broadcasted_iota(jnp.int32, (half, SPAN), 1)
    causal_low = row_ids(0, (half, half)) <= lax.broadcasted_iota(jnp.int32, (half, half), 1)
    final = row_ids(0, (SPAN, 1)) == SPAN - 1
    write = keys[0:SPAN, :DSTATE].astype(F32)
    read = keys[SPAN:, DSTATE:].astype(F32)
    chosen = [lane_half((SPAN, 2 * HEADDIM), h) for h in range(2)]
    for pair in range(PER // 2):
        lanes = slice(pair * 2 * HEADDIM, (pair + 1) * 2 * HEADDIM)
        found = {}
        log_parts = {}
        step_parts = {}
        for h in range(2):
            n = 2 * pair + h
            for span in range(2):
                at = span * SPAN
                value = content[at : at + SPAN, lanes]
                value = jnp.where(chosen[h], value, jnp.zeros_like(value))
                pull = grad_out[at : at + SPAN, lanes]
                log_row = rows[0, n : n + 1, at : at + SPAN]
                log_col = columns[0, at : at + SPAN, n : n + 1]
                step_col = columns[0, at : at + SPAN, PER + n : PER + n + 1]
                halves, sums_step, flows = [], [], []
                for low in range(2):
                    a = low * half
                    value_part = value[a : a + half]
                    pull_part = pull[a:] if low else pull
                    mix_grad = dot_nt(value_part, pull_part).astype(BF).astype(F32)
                    decay = log_row[:, a:] - log_col[a : a + half]
                    decay = jnp.exp(jnp.where(causal_low if low else causal, decay, FAR))
                    step_part = step_col[a : a + half]
                    through = scores[span, a : a + half, a:] * decay
                    mix = (through * step_part).astype(BF)
                    halves.append(dot(mix, pull_part))
                    grad_scores[span, a : a + half, a:] += mix_grad * (decay * step_part)
                    product = mix_grad * through
                    sums_step.append(jnp.sum(product, axis=1, keepdims=True))
                    flows.append(jnp.sum(product * step_part, axis=0, keepdims=True))
                flow = flows[0]
                flow = jnp.concatenate([flow[:, :half], flow[:, half:] + flows[1]], axis=1)
                grad_rows[0, n : n + 1, at : at + SPAN] = flow
                along = jnp.concatenate(sums_step, axis=0)
                step_parts[h, span] = along
                log_parts[h, span] = -(along * step_col)
                found[h, span] = jnp.concatenate(halves, axis=0)
        state = entering[0, :, lanes]
        grad_states = []
        for h in range(2):
            n = 2 * pair + h
            pull = grad_out[SPAN:, lanes]
            growth = jnp.exp(columns[0, SPAN:, n : n + 1])
            own = jnp.where(chosen[h], pull, jnp.zeros_like(pull))
            back = dot_nt(own, state).astype(BF).astype(F32)
            grown = back * growth
            grad_read[...] += grown
            log_parts[h, 1] = log_parts[h, 1] + jnp.sum(grown * read, axis=1, keepdims=True)
            reader = (read_rows[...] * jnp.exp(rows[0, n : n + 1, SPAN:])).astype(BF)
            grad_states.append(dot(reader, pull))
        grad_state = jnp.where(
            lane_half((DSTATE, 2 * HEADDIM), 0), grad_states[0], grad_states[1]
        ).astype(BF)
        for h in range(2):
            n = 2 * pair + h
            value = content[0:SPAN, lanes]
            value = jnp.where(chosen[h], value, jnp.zeros_like(value))
            log_col = columns[0, 0:SPAN, n : n + 1]
            spread = jnp.exp(log_col[SPAN - 1 :] - log_col)
            scaled = spread * columns[0, 0:SPAN, PER + n : PER + n + 1]
            back = dot_nt(value, grad_state).astype(BF).astype(F32)
            along = jnp.sum(back * write, axis=1, keepdims=True)
            grad_write[...] += back * scaled
            quick = along * scaled
            step_parts[h, 0] = step_parts[h, 0] + along * spread
            ended = jnp.where(final, jnp.sum(quick, axis=0, keepdims=True), 0.0)
            log_parts[h, 0] = log_parts[h, 0] - quick + ended
            weight = (write * scaled).astype(BF)
            found[h, 0] = found[h, 0] + dot(weight, grad_state)
            for span in range(2):
                at = span * SPAN
                grad_columns[0, at : at + SPAN, n : n + 1] = step_parts[h, span]
                grad_columns[0, at : at + SPAN, PER + n : PER + n + 1] = log_parts[h, span]
        for span in range(2):
            at = span * SPAN
            both = jnp.where(chosen[0], found[0, span], found[1, span])
            pull = grad_out[at : at + SPAN, lanes].astype(F32)
            grad[at : at + SPAN, lanes] = both + skip[:, lanes] * pull
    conv_back(meta, grad, masked, taps, result, sums, shifted, grad_conv)
    for at in range(0, content.shape[0], CHUNK):
        value = content[at : at + CHUNK, :].astype(F32) * grad_out[at : at + CHUNK, :].astype(F32)
        sums[5:6, :] += jnp.sum(value, axis=0, keepdims=True)


def scan_backward(
    meta, signal, grad_out, entering, columns, rows, skip, masked, taps, kept, first, count
):
    tokens = signal.shape[0]
    last = DI // TILE

    def group(*shape):
        return pl.BlockSpec((1,) + shape, lambda i, meta: (i + first, 0, 0))

    def fresh(*shape):
        return pl.BlockSpec((1,) + shape, lambda i, meta: (i, 0, 0))

    kept_specs = [whole((2, SPAN, SPAN)), whole((SPAN, DSTATE)), whole((SPAN, DSTATE))]
    return call(
        scan_back_body, "scan_backward", meta,
        (signal, signal, grad_out, entering, columns, rows, skip, masked, taps) + tuple(kept),
        [
            tiles(tokens, TILE, first), pl.BlockSpec((tokens, TILE), lambda i, meta: (0, last)),
            tiles(tokens, TILE, first), group(DSTATE, TILE), group(tokens, 2 * PER),
            group(2 * PER, tokens), tiles(1, TILE, first), tiles(tokens, TILE, first),
            tiles(8, TILE, first),
        ]
        + kept_specs,
        [
            shape_of((tokens, count * TILE), BF), shape_of((8, count * TILE)),
            shape_of((count, tokens, 2 * PER)), shape_of((count, 2 * PER, tokens)),
            shape_of((2, SPAN, SPAN)), shape_of((SPAN, DSTATE)), shape_of((SPAN, DSTATE)),
        ],
        [
            tiles(tokens, TILE), tiles(8, TILE), fresh(tokens, 2 * PER), fresh(2 * PER, tokens),
        ]
        + kept_specs,
        [
            pltpu.VMEM((2, SPAN, SPAN), F32), pltpu.VMEM((DSTATE, SPAN), F32),
            pltpu.VMEM((tokens, TILE), F32), pltpu.VMEM((tokens + 8, TILE), F32),
            pltpu.VMEM((tokens + 8, TILE), F32),
        ],
        count, 3 * 10**9 * count, count * MIB, 40,
    )


def tail_body(parts, meta, *refs):
    keys, masked, taps, trio, steps, grad_scores, grad_write, grad_read = refs[:8]
    grad_columns = refs[8 : 8 + parts]
    grad_rows = refs[8 + parts : 8 + 2 * parts]
    result, sums, raw, small, grad, shifted, grad_conv = refs[8 + 2 * parts :]
    tokens = keys.shape[0]
    for span in range(2):
        at = span * SPAN
        write = keys[at : at + SPAN, :DSTATE]
        read = keys[at : at + SPAN, DSTATE:]
        to_write = fine_dot(grad_scores[span], read, dot)
        to_read = fine_dot(grad_scores[span], write, dot_tn)
        if span == 0:
            to_write = to_write + grad_write[...]
        else:
            to_read = to_read + grad_read[...]
        grad[at : at + SPAN, :DSTATE] = to_write
        grad[at : at + SPAN, DSTATE:] = to_read
    conv_back(meta, grad, masked, taps, result, sums, shifted, grad_conv)

    blank = jnp.zeros((tokens, LANES - HEADS), F32)
    of_step, of_log, of_row = [], [], []
    for column_ref, row_ref in zip(grad_columns, grad_rows):
        for g in range(column_ref.shape[0]):
            of_step.append(column_ref[g, :, :PER])
            of_log.append(column_ref[g, :, PER:])
            of_row.append(row_ref[g, :PER, :])
    grad_step = jnp.concatenate(of_step + [blank], axis=1)
    grad_log = jnp.concatenate(of_log + [blank], axis=1)
    across = jnp.concatenate(of_row + [jnp.zeros((LANES - HEADS, tokens), F32)], axis=0)
    grad_log = grad_log + across.T
    upper = row_ids(0, (SPAN, SPAN)) <= lax.broadcasted_iota(jnp.int32, (SPAN, SPAN), 1)
    upper = jnp.where(upper, 1.0, 0.0).astype(BF)
    rates = []
    for at in range(0, tokens, SPAN):
        high, middle, low = pieces(grad_log[at : at + SPAN])
        rates.append(dot(upper, high) + (dot(upper, middle) + dot(upper, low)))
    grad_rate = jnp.concatenate(rates, axis=0)
    decay_rate = steps[1:2, :]
    grad_step = grad_step + grad_rate * decay_rate
    grad_raw = grad_step * jax.nn.sigmoid(trio[0])
    raw[...] = grad_raw.astype(BF)
    small[...] = jnp.zeros_like(small)
    small[0:1, :] = jnp.sum(grad_raw, axis=0, keepdims=True)
    small[1:2, :] = jnp.sum(grad_rate * trio[1], axis=0, keepdims=True) * decay_rate


def tail_backward(meta, signal, masked, taps, trio, steps, kept, grad_columns, grad_rows):
    tokens = signal.shape[0]
    last = DI // TILE
    key_spec = pl.BlockSpec((tokens, TILE), lambda i, meta: (0, last))
    return call(
        functools.partial(tail_body, len(grad_columns)), "tail_backward", meta,
        (signal, masked, taps, trio, steps) + tuple(kept) + tuple(grad_columns) + tuple(grad_rows),
        [
            key_spec, key_spec, pl.BlockSpec((8, TILE), lambda i, meta: (0, last)),
            whole((3, tokens, LANES)), whole((8, LANES)), whole((2, SPAN, SPAN)),
            whole((SPAN, DSTATE)), whole((SPAN, DSTATE)),
        ]
        + [whole(part.shape) for part in tuple(grad_columns) + tuple(grad_rows)],
        [
            shape_of((tokens, TILE), BF), shape_of((8, TILE)), shape_of((tokens, LANES), BF),
            shape_of((8, LANES)),
        ],
        [whole((tokens, TILE)), whole((8, TILE)), whole((tokens, LANES)), whole((8, LANES))],
        [
            pltpu.VMEM((tokens, TILE), F32), pltpu.VMEM((tokens + 8, TILE), F32),
            pltpu.VMEM((tokens + 8, TILE), F32),
        ],
        1, 2 * 10**9, 8 * MIB, 40,
    )


def input_body(
    count, plan, meta, *refs,
):
    parts = len(plan)
    grads = refs[:parts]
    weights = refs[parts : parts + 6]
    hidden, out_grad, scale, gain = refs[parts + 6 : parts + 10]
    result, gain_grad, weight, weight_dt, total = refs[parts + 10 :]
    step = pl.program_id(0)
    tokens, width = hidden.shape
    core = meta[0]

    @pl.when(step == 0)
    def _():
        total[...] = jnp.zeros_like(total)

    for (kind, begin, steps), grad in zip(plan, grads):
        @pl.when((step >= begin) & (step < begin + steps))
        def _(kind=kind, grad=grad):
            if kind == 2:
                assemble(weight_dt, weights[4], weights[5], core, count)
                total[...] += dot_nt(grad[...], weight_dt[...])
            else:
                assemble(weight, weights[2 * kind], weights[2 * kind + 1], core, count)
                total[...] += dot_nt(grad[...], weight[...])

    @pl.when(step == pl.num_programs(0) - 1)
    def _():
        gain_grad[...] = jnp.zeros_like(gain_grad)

        def finish(n, carry):
            rows = pl.ds(pl.multiple_of(n * 16, 16), 16)
            r = scale[rows, :]
            value = hidden[rows, :].astype(F32)
            grad = total[rows, :]
            gain_grad[...] += jnp.sum(grad * value * r, axis=0, keepdims=True)
            grad = grad * gain[...]
            mean = jnp.sum(grad * value, axis=1, keepdims=True) / width
            result[rows, :] = r * grad - value * (r * r * r * mean) + out_grad[rows, :].astype(F32)
            return carry

        lax.fori_loop(0, tokens // 16, finish, 0)


def input_backward(meta, grad_gate, grad_parts, grad_raw, weights, hidden, out_grad, scale, gain, count):
    tokens, width = hidden.shape
    half = weights[0].shape[0]
    plan, specs, step = [], [], 0

    def at(begin, steps, rows, columns):
        return pl.BlockSpec((rows, columns), lambda i, meta: (0, jnp.clip(i - begin, 0, steps - 1)))

    for kind, parts in ((0, (grad_gate,)), (1, grad_parts)):
        first = step
        for part in parts:
            steps = part.shape[1] // TILE
            plan.append((kind, step, steps))
            specs.append(at(step, steps, tokens, TILE))
            step += steps
        specs_weight = at(first, step - first, half, TILE)
        if kind == 0:
            weight_specs = [specs_weight] * 2
        else:
            weight_specs = weight_specs + [specs_weight] * 2
    plan.append((2, step, 1))
    specs.append(whole((tokens, LANES)))
    step += 1
    return call(
        functools.partial(input_body, count, tuple(plan)), "input_backward", meta,
        (grad_gate,) + tuple(grad_parts) + (grad_raw,) + tuple(weights)
        + (hidden, out_grad, scale, gain),
        specs + weight_specs + [whole((half, LANES))] * 2
        + [whole((tokens, width))] * 2 + [whole((tokens, 1)), whole((1, width))],
        [shape_of((tokens, width)), shape_of((1, width))],
        [whole((tokens, width)), whole((1, width))],
        [
            pltpu.VMEM((2 * half, TILE), BF), pltpu.VMEM((2 * half, LANES), BF),
            pltpu.VMEM((tokens, width), F32),
        ],
        step, 2 * tokens * width * (DI + CC), 36 * MIB, 48,
    )


def sibling():
    return [(r, r ^ 1) for r in range(lax.axis_size("rep"))]


def swap(x):
    return lax.ppermute(x, "rep", sibling())


def across(x, bit):
    count = lax.axis_size("shard")
    return lax.ppermute(x, "shard", [(k, k ^ bit) for k in range(count)])


def gather_rows(weight, core):
    half = weight.shape[0] // 2
    mine = lax.dynamic_slice_in_dim(weight, core * half, half, 0)
    own = lax.all_gather(mine, "shard", axis=0, tiled=True)
    return own, swap(own)


def pick_half(matrix, core, count):
    rows, width = matrix.shape
    cut = matrix.reshape(rows, count, 2, width // (2 * count))
    return lax.dynamic_index_in_dim(cut, core, 2, keepdims=False).reshape(rows, width // 2)


def bit_order(count, ascending):
    bits = []
    bit = 1
    while bit < count:
        bits.append(bit)
        bit *= 2
    if not ascending:
        bits = bits[::-1]
    order = [0]
    for bit in bits[::-1]:
        order = order + [k | bit for k in order]
    return bits, order


def relative_columns(matrix, shard, order, part):
    count = len(order)
    rows, width = matrix.shape
    group = width // (2 * count)
    return [
        lax.dynamic_slice_in_dim(matrix, (shard ^ k) * (2 * group) + part * group, group, 1)
        for k in order
    ]


def begin_sum(lhs, rhs, shard):
    count = lax.axis_size("shard")
    state = []
    for part in range(2):
        bits, order = bit_order(count, part == 1)
        columns = relative_columns(lhs, shard, order, part)
        send = dot_tn(jnp.concatenate(columns[count // 2 :], axis=1), rhs).astype(BF)
        keep = dot_tn(jnp.concatenate(columns[: count // 2], axis=1), rhs)
        state.append((send, keep, tuple(bits)))
    return state


def fly(state):
    return [across(send, bits[0]) for send, keep, bits in state]


def settle(state, arrived):
    after = []
    for (send, keep, bits), more in zip(state, arrived):
        held = keep + more.astype(F32)
        if len(bits) > 1:
            middle = held.shape[0] // 2
            after.append((held[middle:].astype(BF), held[:middle], bits[1:]))
        else:
            after.append((None, held, ()))
    return after


def finish_sum(state):
    while state[0][2]:
        state = settle(state, fly(state))
    return line_sum(jnp.concatenate([keep for send, keep, bits in state], axis=0))


def line_sum(held):
    chips = lax.axis_size("rep") // 2

    def move(x, pairs):
        return lax.ppermute(x, "rep", [(2 * a + k, 2 * b + k) for a, b in pairs for k in range(2)])

    if chips == 4:
        place = lax.axis_index("rep") // 2
        arrived = move(held.astype(BF), [(0, 1), (3, 2)])
        inner = (held + arrived.astype(F32)).astype(BF)
        arrived = move(inner, [(1, 2), (2, 1)])
        total = (inner.astype(F32) + arrived.astype(F32)).astype(BF)
        arrived = move(total, [(1, 0), (2, 3)])
        return jnp.where((place == 1) | (place == 2), total, arrived)
    total = held.astype(BF)
    bit = 1
    while bit < chips:
        arrived = move(total, [(k, k ^ bit) for k in range(chips)])
        total = (total.astype(F32) + arrived.astype(F32)).astype(BF)
        bit *= 2
    return total


def in_order(own, other, core):
    first = jnp.where(core == 0, own, other)
    second = jnp.where(core == 0, other, own)
    return first, second


def both_tokens(columns, core):
    half = columns.shape[1] // 2
    mine = lax.dynamic_slice_in_dim(columns, core * half, half, 1)
    theirs = swap(lax.dynamic_slice_in_dim(columns, (1 - core) * half, half, 1))
    return jnp.concatenate([mine, theirs], axis=0)


def pair_up(total, core):
    return [part.astype(F32) for part in in_order(total, swap(total), core)]


def pad_lanes(matrix):
    return jnp.pad(matrix, ((0, 0), (0, LANES - matrix.shape[1])))


def shards(
    hidden,
    out_grad,
    norm_gain,
    in_w,
    conv_w,
    conv_b,
    dt_bias,
    a_log,
    skip,
    out_gain,
    out_w,
    lengths,
    offsets,
):
    core = lax.axis_index("rep") % 2
    shard = lax.axis_index("shard")
    count = lax.axis_size("shard")
    small = (norm_gain, conv_w, conv_b, dt_bias, a_log, skip, out_gain)
    packed = jnp.concatenate([part.reshape(-1) for part in small])
    everyone = lax.all_gather(packed, "shard", axis=0, tiled=False)
    parts, start = [], 0
    for part in small:
        cut = everyone[:, start : start + part.size].astype(F32)
        parts.append(cut.reshape((count * part.shape[0],) + part.shape[1:]))
        start += part.size
    gain_one, kernel, bias_conv, bias_step, log_rate, skip_full, gain_two = parts
    decay_rate = -jnp.exp(log_rate)
    conv_own, conv_rest = gather_rows(in_w[:, DI:], core)
    gate_own, gate_rest = gather_rows(in_w[:, :DI], core)
    out_own, out_rest = gather_rows(out_w, core)
    dt_own, dt_rest = pad_lanes(conv_own[:, CC:]), pad_lanes(conv_rest[:, CC:])

    tokens = hidden.shape[0]
    meta = jnp.stack([core, offsets[0], lengths[0]]).astype(jnp.int32)
    taps = jnp.concatenate([kernel.T, bias_conv[None], jnp.zeros((3, CC), F32)], axis=0)
    steps = jnp.concatenate(
        [pad_lanes(jnp.stack([bias_step, decay_rate])), jnp.zeros((6, LANES), F32)], axis=0
    )
    skip_lanes = jnp.repeat(skip_full, HEADDIM)[None]

    positions = jnp.arange(tokens, dtype=jnp.int32)
    live_mask = ((positions >= offsets[0]) & (positions < offsets[0] + lengths[0])).astype(F32)
    hidden_full = hidden.astype(F32)
    inv_rms = lax.rsqrt(jnp.mean(hidden_full * hidden_full, axis=1, keepdims=True) + epsilon)
    normed = (hidden_full * inv_rms * gain_one).astype(BF)
    pulled = (out_grad.astype(F32) * live_mask[:, None]).astype(BF)
    normed_both = jnp.concatenate([normed, swap(normed)], axis=0)
    pulled_both = jnp.concatenate([pulled, swap(pulled)], axis=0)

    masked, signal, columns, rows, trio = conv_forward(
        meta, normed, conv_own, conv_rest, dt_own, dt_rest, taps, steps, count
    )
    mixed, entering = scan_forward(meta, signal, columns, rows, skip_lanes)
    gate, normed_out, scale = gate_forward(
        meta, normed, gate_own, gate_rest, mixed, gain_two[None], count
    )
    normed_out_both = jnp.concatenate(
        [pick_half(normed_out, core, count), swap(pick_half(normed_out, 1 - core, count))], axis=0
    )
    block_out, grad_gate, grad_mixed, grad_gain_two = out_forward(
        meta, normed_out, out_own, out_rest, pulled, hidden, mixed, gate, scale, gain_two[None], count
    )

    out_state = begin_sum(normed_out_both, pulled_both, shard)
    gate_state = begin_sum(normed_both, both_tokens(grad_gate, core), shard)
    out_state, gate_state, grad_mixed = hold((out_state, gate_state, grad_mixed))
    out_there, gate_there = fly(out_state), fly(gate_state)

    kept = (
        jnp.zeros((2, SPAN, SPAN), F32),
        jnp.zeros((SPAN, DSTATE), F32),
        jnp.zeros((SPAN, DSTATE), F32),
    )
    near = GROUPS // 2
    grad_near, sums_near, columns_near, rows_near, *kept = scan_backward(
        meta, signal, grad_mixed, entering, columns, rows, skip_lanes, masked, taps, kept, 0, near
    )
    out_there, gate_there, grad_near, kept, grad_mixed = hold(
        (out_there, gate_there, grad_near, kept, grad_mixed)
    )
    out_state = settle(out_state, out_there)
    gate_state = settle(gate_state, gate_there)
    near_state = begin_sum(normed_both, both_tokens(grad_near, core), shard)
    out_state, gate_state, near_state, kept, grad_mixed = hold(
        (out_state, gate_state, near_state, kept, grad_mixed)
    )
    grad_far, sums_far, columns_far, rows_far, *kept = scan_backward(
        meta, signal, grad_mixed, entering, columns, rows, skip_lanes, masked, taps, kept, near,
        GROUPS - near,
    )
    grad_keys, sums_keys, grad_raw, grad_steps = tail_backward(
        meta, signal, masked, taps, trio, steps, kept, (columns_near, columns_far),
        (rows_near, rows_far),
    )
    far = jnp.concatenate([grad_far, grad_keys], axis=1)
    cut_far, cut_raw = far.shape[1] // 2, HEADS // 2
    later = jnp.concatenate(
        [
            far[:, :cut_far],
            grad_raw[:, :cut_raw],
            far[:, cut_far:],
            grad_raw[:, cut_raw : 2 * cut_raw],
        ],
        axis=1,
    )
    far_state = begin_sum(normed_both, both_tokens(later, core), shard)

    out_w_grad = jnp.concatenate(pair_up(finish_sum(out_state), core), axis=0)
    gate_grads = pair_up(finish_sum(gate_state), core)
    near_grads = pair_up(finish_sum(near_state), core)
    far_grads = pair_up(finish_sum(far_state), core)
    in_w_grad = jnp.concatenate(
        gate_grads
        + near_grads
        + [far_grads[0][:, :cut_far], far_grads[1][:, :cut_far]]
        + [far_grads[0][:, cut_far:], far_grads[1][:, cut_far:]],
        axis=1,
    )

    hidden_grad, grad_gain_one = input_backward(
        meta, grad_gate, (grad_near, grad_far, grad_keys), grad_raw,
        (gate_own, gate_rest, conv_own, conv_rest, dt_own, dt_rest),
        hidden, out_grad, inv_rms, gain_one[None], count,
    )
    sums = jnp.concatenate([sums_near, sums_far, sums_keys], axis=1)
    local = (
        grad_gain_one[0],
        sums[:CONV].T,
        sums[CONV],
        grad_steps[0, :HEADS],
        grad_steps[1, :HEADS],
        jnp.sum(sums[5, :DI].reshape(HEADS, HEADDIM), axis=1),
        grad_gain_two[0],
    )
    summed = lax.psum(jnp.concatenate([part.reshape(-1) for part in local]), ("rep", "shard"))
    mine, start = [], 0
    for part in local:
        cut = summed[start : start + part.size].reshape(part.shape)
        length = part.shape[0] // count
        mine.append(lax.dynamic_slice_in_dim(cut, shard * length, length, 0))
        start += part.size
    return (
        block_out,
        hidden_grad,
        mine[0],
        in_w_grad,
        mine[1],
        mine[2],
        mine[3],
        mine[4],
        mine[5],
        mine[6],
        out_w_grad,
    )


def hold(values):
    leaves, tree = jax.tree.flatten(values)
    arrays = [k for k, leaf in enumerate(leaves) if isinstance(leaf, jax.Array)]
    fixed = lax.optimization_barrier(tuple(leaves[k] for k in arrays))
    for k, leaf in zip(arrays, fixed):
        leaves[k] = leaf
    return jax.tree.unflatten(tree, leaves)


def solution(mesh):
    return jax.shard_map(
        shards,
        mesh=mesh,
        in_specs=(
            P(("rep", "shard"), None),
            P(("rep", "shard"), None),
            P("shard"),
            P("shard", None),
            P("shard", None),
            P("shard"),
            P("shard"),
            P("shard"),
            P("shard"),
            P("shard"),
            P("shard", None),
            P(("rep", "shard")),
            P(("rep", "shard")),
        ),
        out_specs=(
            P(("rep", "shard"), None),
            P(("rep", "shard"), None),
            P("shard"),
            P("shard", None),
            P("shard", None),
            P("shard"),
            P("shard"),
            P("shard"),
            P("shard"),
            P("shard"),
            P("shard", None),
        ),
        check_vma=False,
    )
```

```python
import functools

import jax
import jax.numpy as jnp
from jax import lax
from jax.experimental import pallas as pl
from jax.experimental.pallas import tpu as pltpu
from jax.sharding import PartitionSpec as P

HEADS = 48
HEADDIM = 64
DSTATE = 128
CONV = 4
SPAN = 256
DI = 3072
CC = 3328
TILE = 256
GROUPS = DI // TILE
PER = TILE // HEADDIM
CHUNK = 64
LANES = 128
epsilon = 1e-05
FAR = -1e30

BF = jnp.bfloat16
F32 = jnp.float32
MIB = 1 << 20


def dot(lhs, rhs):
    return jnp.dot(lhs, rhs, preferred_element_type=F32)


def dot_nt(lhs, rhs):
    return lax.dot_general(lhs, rhs, (((1,), (1,)), ((), ())), preferred_element_type=F32)


def dot_tn(lhs, rhs):
    return lax.dot_general(lhs, rhs, (((0,), (0,)), ((), ())), preferred_element_type=F32)


def pieces(value):
    high = value.astype(BF)
    rest = value - high.astype(F32)
    middle = rest.astype(BF)
    low = (rest - middle.astype(F32)).astype(BF)
    return high, middle, low


def fine_dot(lhs, rhs, product):
    high, middle, low = pieces(lhs)
    return product(high, rhs) + (product(middle, rhs) + product(low, rhs))


def row_ids(start, shape):
    return start + lax.broadcasted_iota(jnp.int32, shape, 0)


def live_rows(meta, start, shape):
    ids = row_ids(start, shape)
    return (ids >= meta[1]) & (ids < meta[1] + meta[2])


def gather_lanes(target, blocks, table, at):
    for j, block in enumerate(blocks):
        width = block.shape[1]
        lanes = pl.ds(pl.multiple_of(table[at + j] * width, LANES), width)
        target[0 : block.shape[0], lanes] = block[...]


def call(body, name, meta, operands, in_specs, outs, out_specs, scratch, grid, flops, moved, limit):
    return pl.pallas_call(
        body,
        name=name,
        grid_spec=pltpu.PrefetchScalarGridSpec(
            num_scalar_prefetch=1,
            grid=(grid,),
            in_specs=in_specs,
            out_specs=out_specs,
            scratch_shapes=scratch,
        ),
        out_shape=outs,
        compiler_params=pltpu.CompilerParams(vmem_limit_bytes=limit * MIB),
        cost_estimate=pl.CostEstimate(flops=flops, bytes_accessed=moved, transcendentals=0),
    )(meta, *operands)


def whole(shape):
    rank = len(shape)
    return pl.BlockSpec(shape, lambda i, meta: (0,) * rank)


def tiles(rows, width, shift=0, last=None):
    def index(i, meta):
        at = i + shift
        if last is not None:
            at = jnp.clip(at, 0, last)
        return (0, at)

    return pl.BlockSpec((rows, width), index)


def shape_of(shape, kind=F32):
    return jax.ShapeDtypeStruct(shape, kind)


TABLE = 4
UNITS = 4
OUT_TABLE = TABLE + 2 * UNITS


def own_tile(i, meta):
    half = GROUPS // 2
    return jnp.where(i < half, meta[0] * half + i, (1 - meta[0]) * half + i - half)


def conv_body(meta, x, taps, steps, *refs):
    count = UNITS
    own, rest, dts = refs[:count], refs[count : 2 * count], refs[2 * count : 3 * count]
    masked, signal, columns, rows, trio, weight, weight_dt, shifted = refs[3 * count :]
    tokens = x.shape[0]
    step = pl.program_id(0)

    @pl.when(step <= GROUPS // 2)
    def _():
        gather_lanes(weight, own, meta, TABLE)

    @pl.when(step > GROUPS // 2)
    def _():
        gather_lanes(weight, rest, meta, TABLE + count)

    low = dot_nt(x[...], weight[...]).astype(BF)
    low = jnp.where(live_rows(meta, 0, low.shape), low, jnp.zeros_like(low))
    masked[...] = low
    shifted[0:8, :] = jnp.zeros((8, TILE), F32)
    shifted[8:, :] = low.astype(F32)
    for at in range(0, tokens, CHUNK):
        out = taps[4:5, :]
        for k in range(CONV):
            out = out + shifted[at + 5 + k : at + 5 + k + CHUNK, :] * taps[k : k + 1, :]
        out = out * jax.nn.sigmoid(out)
        out = jnp.where(live_rows(meta, at, out.shape), out, 0.0)
        signal[at : at + CHUNK, :] = out.astype(BF)

    @pl.when(step == 0)
    def _():
        gather_lanes(weight_dt, dts, meta, TABLE)
        raw = dot_nt(x[...], weight_dt[...]).astype(BF).astype(F32)
        raw = jnp.concatenate([raw, jnp.zeros((tokens, LANES - raw.shape[1]), F32)], axis=1)
        pre = raw + steps[0:1, :]
        size = jnp.maximum(pre, 0.0) + jnp.log1p(jnp.exp(-jnp.abs(pre)))
        rate = size * steps[1:2, :]
        lower = row_ids(0, (SPAN, SPAN)) >= lax.broadcasted_iota(jnp.int32, (SPAN, SPAN), 1)
        lower = jnp.where(lower, 1.0, 0.0).astype(BF)
        trio[0] = pre
        trio[1] = size
        for at in range(0, tokens, SPAN):
            high, middle, small = pieces(rate[at : at + SPAN])
            trio[2, at : at + SPAN, :] = dot(lower, high) + (dot(lower, middle) + dot(lower, small))
        log = trio[2]
        size_rows = size.T
        log_rows = log.T
        for g in range(GROUPS):
            a, b = g * PER, (g + 1) * PER
            columns[g] = jnp.concatenate([log[:, a:b], size[:, a:b]], axis=1)
            rows[g] = jnp.concatenate([log_rows[a:b], size_rows[a:b]], axis=0)


def conv_forward(meta, x, taps, steps, own, rest, local):
    tokens, width = x.shape
    count = UNITS
    part = width // count
    half = GROUPS // 2

    def natural(i, meta):
        return jnp.where(i == 0, GROUPS, own_tile(jnp.maximum(i - 1, 0), meta))

    def tile(rows):
        return pl.BlockSpec((rows, TILE), lambda i, meta: (0, natural(i, meta)))

    own_spec = pl.BlockSpec(
        (TILE, part), lambda i, meta: (jnp.where(i == 0, half, jnp.minimum(i - 1, half - 1)), 0)
    )
    rest_spec = pl.BlockSpec((TILE, part), lambda i, meta: (jnp.maximum(i - 1 - half, 0), 0))
    local_spec = pl.BlockSpec(
        (TILE, part),
        lambda i, meta: (GROUPS + (1 - meta[0]) * half + jnp.maximum(i - 1 - half, 0), 0),
    )
    dt_spec = pl.BlockSpec((64, part), lambda i, meta: ((half + 1) * TILE // 64, 0))
    return call(
        conv_body, "conv_forward", meta,
        (x, taps, steps) + tuple(own) + (() if local is None else (local,)) + tuple(rest) + tuple(own),
        [whole((tokens, width)), tile(8), whole((8, LANES))] + [own_spec] * count
        + [rest_spec if local is None else local_spec] + [rest_spec] * (count - 1)
        + [dt_spec] * count,
        [
            shape_of((tokens, CC), BF), shape_of((tokens, CC), BF),
            shape_of((GROUPS, tokens, 2 * PER)), shape_of((GROUPS, 2 * PER, tokens)),
            shape_of((3, tokens, LANES)),
        ],
        [
            tile(tokens), tile(tokens),
            whole((GROUPS, tokens, 2 * PER)), whole((GROUPS, 2 * PER, tokens)),
            whole((3, tokens, LANES)),
        ],
        [
            pltpu.VMEM((TILE, width), BF), pltpu.VMEM((64, width), BF),
            pltpu.VMEM((tokens + 8, TILE), F32),
        ],
        CC // TILE, 2 * tokens * width * CC, 24 * MIB, 40,
    )


def lane_half(shape, half):
    ids = lax.broadcasted_iota(jnp.int32, shape, 1)
    return (ids >= HEADDIM) if half else (ids < HEADDIM)


def scan_body(meta, content, keys, columns, rows, skip, out, entering, scores, write_rows):
    half = SPAN // 2

    @pl.when(pl.program_id(0) == 0)
    def _():
        for span in range(2):
            at = span * SPAN
            scores[span] = dot_nt(keys[at : at + SPAN, DSTATE:], keys[at : at + SPAN, :DSTATE])
        write_rows[...] = keys[0:SPAN, :DSTATE].astype(F32).T

    causal = row_ids(0, (half, half)) >= lax.broadcasted_iota(jnp.int32, (half, half), 1)
    causal_low = row_ids(half, (half, SPAN)) >= lax.broadcasted_iota(jnp.int32, (half, SPAN), 1)
    read = keys[SPAN:, DSTATE:].astype(F32)
    for pair in range(PER // 2):
        lanes = slice(pair * 2 * HEADDIM, (pair + 1) * 2 * HEADDIM)
        first, second, states = [], [], []
        for h in range(2):
            n = 2 * pair + h
            for span in range(2):
                at = span * SPAN
                value = content[at : at + SPAN, lanes]
                log_row = rows[0, n : n + 1, at : at + SPAN]
                step_row = rows[0, PER + n : PER + n + 1, at : at + SPAN]
                upper = columns[0, at : at + half, n : n + 1] - log_row[:, :half]
                upper = jnp.exp(jnp.where(causal, upper, FAR))
                mix = (scores[span, :half, :half] * upper * step_row[:, :half]).astype(BF)
                top = dot(mix, value[:half])
                lower = columns[0, at + half : at + SPAN, n : n + 1] - log_row
                lower = jnp.exp(jnp.where(causal_low, lower, FAR))
                mix = (scores[span, half:, :] * lower * step_row).astype(BF)
                bottom = dot(mix, value)
                both = jnp.concatenate([top, bottom], axis=0)
                if span == 0:
                    spread = jnp.exp(log_row[:, SPAN - 1 :] - log_row) * step_row
                    weight = (write_rows[...] * spread).astype(BF)
                    states.append(dot(weight, value))
                    first.append(both)
                else:
                    second.append(both)
        chosen = lane_half((DSTATE, 2 * HEADDIM), 0)
        state = jnp.where(chosen, states[0], states[1]).astype(BF)
        entering[0, :, lanes] = state
        for h in range(2):
            n = 2 * pair + h
            growth = jnp.exp(columns[0, SPAN:, n : n + 1])
            second[h] = second[h] + dot((read * growth).astype(BF), state)
        chosen = lane_half((SPAN, 2 * HEADDIM), 0)
        for span, parts in ((0, first), (1, second)):
            at = span * SPAN
            mixed = jnp.where(chosen, parts[0], parts[1])
            value = content[at : at + SPAN, lanes].astype(F32)
            out[at : at + SPAN, lanes] = mixed + skip[:, lanes] * value


def scan_forward(meta, signal, columns, rows, skip):
    tokens = signal.shape[0]
    last = DI // TILE
    return call(
        scan_body, "scan_forward", meta, (signal, signal, columns, rows, skip),
        [
            tiles(tokens, TILE), pl.BlockSpec((tokens, TILE), lambda i, meta: (0, last)),
            pl.BlockSpec((1, tokens, 2 * PER), lambda i, meta: (i, 0, 0)),
            pl.BlockSpec((1, 2 * PER, tokens), lambda i, meta: (i, 0, 0)),
            tiles(1, TILE),
        ],
        [shape_of((tokens, DI)), shape_of((GROUPS, DSTATE, TILE), BF)],
        [tiles(tokens, TILE), pl.BlockSpec((1, DSTATE, TILE), lambda i, meta: (i, 0, 0))],
        [pltpu.VMEM((2, SPAN, SPAN), F32), pltpu.VMEM((DSTATE, SPAN), F32)],
        GROUPS, 10 * 10**9, 12 * MIB, 32,
    )


def gate_body(meta, x, mixed, gain, *refs):
    count = UNITS
    own, rest = refs[:count], refs[count : 2 * count]
    gate, normed, theirs, scale, weight, gated, total = refs[2 * count :]
    step = pl.program_id(0)
    tokens = x.shape[0]

    @pl.when(step < GROUPS // 2)
    def _():
        gather_lanes(weight, own, meta, TABLE)

    @pl.when(step >= GROUPS // 2)
    def _():
        gather_lanes(weight, rest, meta, TABLE + count)

    gate[...] = dot_nt(x[...], weight[...]).astype(BF)

    @pl.when(step == 0)
    def _():
        total[...] = jnp.zeros_like(total)

    here = pl.ds(pl.multiple_of(own_tile(step, meta) * TILE, TILE), TILE)
    for at in range(0, tokens, CHUNK):
        part = gate[at : at + CHUNK, :].astype(F32)
        part = mixed[at : at + CHUNK, :] * (part * jax.nn.sigmoid(part))
        gated[at : at + CHUNK, here] = part
        square = part * part
        total[at : at + CHUNK, :] += square[:, :LANES] + square[:, LANES:]

    @pl.when(step == pl.num_programs(0) - 1)
    def _():
        mean = jnp.sum(total[...], axis=1, keepdims=True) / DI
        scale[...] = lax.rsqrt(mean + epsilon)

        def finish(g, carry):
            lanes = pl.ds(pl.multiple_of(g * TILE, TILE), TILE)
            for at in range(0, tokens, CHUNK):
                part = gated[at : at + CHUNK, lanes] * scale[at : at + CHUNK, :] * gain[:, lanes]
                normed[at : at + CHUNK, lanes] = part.astype(BF)
            return carry

        lax.fori_loop(0, GROUPS, finish, 0)
        half = DI // (2 * count)
        for k in range(count):
            other = pl.multiple_of((2 * k + 1 - meta[0]) * half, LANES)
            theirs[:, k * half : (k + 1) * half] = normed[:, pl.ds(other, half)]


def gate_forward(meta, x, mixed, gain, own, rest, local):
    tokens, width = x.shape
    count = UNITS
    part = width // count
    half = GROUPS // 2
    tile_spec = pl.BlockSpec((tokens, TILE), lambda i, meta: (0, own_tile(i, meta)))
    own_spec = pl.BlockSpec((TILE, part), lambda i, meta: (jnp.minimum(i, half - 1), 0))
    rest_spec = pl.BlockSpec((TILE, part), lambda i, meta: (jnp.maximum(i - half, 0), 0))
    local_spec = pl.BlockSpec(
        (TILE, part), lambda i, meta: ((1 - meta[0]) * half + jnp.maximum(i - half, 0), 0)
    )
    return call(
        gate_body, "gate_forward", meta,
        (x, mixed, gain) + tuple(own) + (() if local is None else (local,)) + tuple(rest),
        [whole((tokens, width)), tile_spec, whole((1, DI))] + [own_spec] * count
        + [rest_spec if local is None else local_spec] + [rest_spec] * (count - 1),
        [
            shape_of((tokens, DI), BF), shape_of((tokens, DI), BF), shape_of((tokens, DI // 2), BF),
            shape_of((tokens, 1)),
        ],
        [tile_spec, whole((tokens, DI)), whole((tokens, DI // 2)), whole((tokens, 1))],
        [
            pltpu.VMEM((TILE, width), BF), pltpu.VMEM((tokens, DI), F32),
            pltpu.VMEM((tokens, LANES), F32),
        ],
        GROUPS, 2 * tokens * width * DI, 28 * MIB, 48,
    )


STEPS = 4


def out_body(meta, *refs):
    count = UNITS
    normed, mixed, gate, gain = refs[0:2], refs[2:5], refs[5:8], refs[8:11]
    pulled, hidden, scale = refs[11:14]
    own, rest = refs[14 : 14 + count], refs[14 + count : 14 + 2 * count]
    block, grad_gate, theirs, grad_mixed, grad_gain = refs[14 + 2 * count : 19 + 2 * count]
    weight, branch, back, total = refs[19 + 2 * count :]
    step = pl.program_id(0)
    tokens = pulled.shape[0]
    half = DI // (2 * count)

    @pl.when(step == 0)
    def _():
        branch[...] = jnp.zeros_like(branch)
        total[...] = jnp.zeros_like(total)

    for j in range(count):
        @pl.when(step == j)
        def _(j=j):
            weight[0:half, :] = own[j][...]
            weight[half:, :] = rest[j][...]

    @pl.when(step < count)
    def _():
        branch[...] += dot(jnp.concatenate([normed[0][...], normed[1][...]], axis=1), weight[...])
        grads = dot_nt(pulled[...], weight[...]).astype(BF)
        places = []
        for side in range(2):
            at = meta[OUT_TABLE + side * count + step] * half
            places.append(pl.multiple_of(at, LANES))
            back[:, pl.ds(places[side], half)] = grads[:, side * half : (side + 1) * half]

        def first(n, carry):
            rows = pl.ds(pl.multiple_of(n * CHUNK, CHUNK), CHUNK)
            for side in range(2):
                for at in range(0, half, LANES):
                    cut = slice(at, at + LANES)
                    z = gate[side][rows, cut].astype(F32)
                    gated = mixed[side][rows, cut] * (z * jax.nn.sigmoid(z))
                    grad = back[rows, pl.ds(pl.multiple_of(places[side] + at, LANES), LANES)]
                    total[rows, :] += grad.astype(F32) * gain[side][:, cut] * gated
            return carry

        lax.fori_loop(0, tokens // CHUNK, first, 0)

    @pl.when(step == count - 1)
    def _():
        for at in range(0, tokens, CHUNK):
            part = branch[at : at + CHUNK, :]
            part = jnp.where(live_rows(meta, at, part.shape), part, 0.0)
            block[at : at + CHUNK, :] = (hidden[at : at + CHUNK, :].astype(F32) + part).astype(BF)

    @pl.when(step >= count)
    def _():
        late = step - count
        width = DI // STEPS
        grad_gain[...] = jnp.zeros_like(grad_gain)

        def second(n, carry):
            rows = pl.ds(pl.multiple_of(n * CHUNK, CHUNK), CHUNK)
            r = scale[rows, :]
            mean = jnp.sum(total[rows, :], axis=1, keepdims=True) / DI
            factor = r * r * r * mean
            for at in range(0, width, LANES):
                cut = slice(at, at + LANES)
                z = gate[2][rows, cut].astype(F32)
                sigma = jax.nn.sigmoid(z)
                silu = z * sigma
                out = mixed[2][rows, cut]
                gated = out * silu
                grad = back[rows, pl.ds(pl.multiple_of(late * width + at, LANES), LANES)].astype(F32)
                grad_gain[:, cut] += jnp.sum(grad * gated * r, axis=0, keepdims=True)
                grad = r * (grad * gain[2][:, cut]) - gated * factor
                grad_mixed[rows, cut] = (grad * silu).astype(BF)
                grad = grad * out * sigma * (1.0 + z * (1.0 - sigma))
                grad_gate[rows, cut] = grad.astype(BF)
            return carry

        lax.fori_loop(0, tokens // CHUNK, second, 0)

        @pl.when(late // (STEPS // 2) == 1 - meta[0])
        def _():
            theirs[...] = grad_gate[...]


def out_forward(meta, normed, pulled, hidden, mixed, gate, scale, gain, own, rest, local):
    tokens, width = hidden.shape
    count = UNITS
    half = DI // (2 * count)
    step_width = DI // STEPS

    def early(rows, side):
        def index(i, meta):
            return (0, meta[OUT_TABLE + side * count + jnp.minimum(i, count - 1)])

        return pl.BlockSpec((rows, half), index)

    def late(rows):
        return pl.BlockSpec((rows, step_width), lambda i, meta: (0, jnp.maximum(i - count, 0)))

    def local_spec(side):
        return pl.BlockSpec((half, width), lambda i, meta: (meta[0] if side == 0 else 1 - meta[0], 0))

    first = () if local is None else (local,)

    def weight_specs(side):
        one = whole((half, width)) if local is None else local_spec(side)
        return [one] + [whole((half, width))] * (count - 1)

    theirs_spec = pl.BlockSpec(
        (tokens, step_width),
        lambda i, meta: (0, jnp.clip(i - count - (1 - meta[0]) * (STEPS // 2), 0, STEPS // 2 - 1)),
    )
    return call(
        out_body, "out_forward", meta,
        (normed, normed) + (mixed,) * 3 + (gate,) * 3 + (gain,) * 3 + (pulled, hidden, scale)
        + (first + tuple(own) + first + tuple(rest)),
        [early(tokens, 0), early(tokens, 1), early(tokens, 0), early(tokens, 1), late(tokens),
         early(tokens, 0), early(tokens, 1), late(tokens), early(1, 0), early(1, 1), late(1)]
        + [whole((tokens, width))] * 2 + [whole((tokens, 1))]
        + weight_specs(0) + weight_specs(1),
        [
            shape_of((tokens, width), BF), shape_of((tokens, DI), BF),
            shape_of((tokens, DI // 2), BF), shape_of((tokens, DI), BF), shape_of((1, DI)),
        ],
        [whole((tokens, width)), late(tokens), theirs_spec, late(tokens), late(1)],
        [
            pltpu.VMEM((2 * half, width), BF), pltpu.VMEM((tokens, width), F32),
            pltpu.VMEM((tokens, DI), BF), pltpu.VMEM((tokens, LANES), F32),
        ],
        count + STEPS, 4 * tokens * width * DI, 40 * MIB, 60,
    )


def rows_product_body(meta, mine, theirs, pulled, pulled_rest, out):
    total = dot_tn(mine[...], pulled[...]) + dot_tn(theirs[...], pulled_rest[...])
    out[0] = total.astype(out.dtype)


def rows_product(meta, normed, arrived, arrived_at, pulled, pulled_rest, first, blocks, kind):
    tokens, width = pulled.shape
    unit = DI // (2 * UNITS)
    return call(
        rows_product_body, "rows_product", meta, (normed, arrived, pulled, pulled_rest),
        [
            pl.BlockSpec((tokens, unit), lambda i, meta: (0, meta[OUT_TABLE + first + i])),
            pl.BlockSpec((tokens, unit), lambda i, meta: (0, meta[arrived_at + first + i])),
            whole((tokens, width)), whole((tokens, width)),
        ],
        shape_of((blocks, unit, width), kind),
        pl.BlockSpec((1, unit, width), lambda i, meta: (i, 0, 0)),
        [], blocks, 4 * tokens * width * unit * blocks, 8 * MIB, 40,
    )


def columns_product_body(plan, blocks, meta, *refs):
    parts = len(plan)
    mine, theirs = refs[:parts], refs[parts : 2 * parts]
    here = refs[2 * parts : 2 * parts + blocks]
    there = refs[2 * parts + blocks : 2 * parts + 2 * blocks]
    out = refs[2 * parts + 2 * blocks]
    step = pl.program_id(0)
    width = here[0].shape[1]
    for (begin, steps), a, b in zip(plan, mine, theirs):
        @pl.when((step >= begin) & (step < begin + steps))
        def _(a=a, b=b):
            one = jnp.concatenate([block[...] for block in here], axis=1)
            two = jnp.concatenate([block[...] for block in there], axis=1)
            total = dot_tn(a[...], one) + dot_tn(b[...], two)
            for k in range(blocks):
                out[k] = total[:, k * width : (k + 1) * width].astype(out.dtype)


def columns_product(meta, parts, normed, normed_rest, first, blocks, kind):
    tokens, width = normed.shape
    part = width // UNITS
    plan, step, mine_specs, theirs_specs = [], 0, [], []

    def spec(begin, steps, start):
        return pl.BlockSpec(
            (tokens, TILE), lambda i, meta: (0, start(meta) + jnp.clip(i - begin, 0, steps - 1))
        )

    for matrix, start, steps, arrived in parts:
        plan.append((step, steps))
        mine_specs.append(spec(step, steps, start))
        theirs_specs.append(spec(step, steps, lambda meta: 0))
        step += steps

    def lanes(j):
        return pl.BlockSpec((tokens, part), lambda i, meta: (0, meta[TABLE + first + j]))

    lane_specs = [lanes(j) for j in range(blocks)]
    return call(
        functools.partial(columns_product_body, tuple(plan), blocks), "columns_product", meta,
        tuple(p[0] for p in parts) + tuple(p[3] for p in parts)
        + (normed,) * blocks + (normed_rest,) * blocks,
        mine_specs + theirs_specs + lane_specs + lane_specs,
        shape_of((blocks, step * TILE, part), kind),
        pl.BlockSpec((blocks, TILE, part), lambda i, meta: (0, i, 0)),
        [], step, 4 * tokens * step * TILE * part * blocks, 12 * MIB, 40,
    )


def conv_back(meta, grad, masked, taps, result, sums, shifted, grad_conv):
    tokens = masked.shape[0]
    shifted[0:8, :] = jnp.zeros((8, TILE), F32)
    shifted[8:, :] = masked[...].astype(F32)
    grad_conv[tokens:, :] = jnp.zeros((8, TILE), F32)
    sums[...] = jnp.zeros_like(sums)
    for at in range(0, tokens, CHUNK):
        near = [shifted[at + 5 + k : at + 5 + k + CHUNK, :] for k in range(CONV)]
        out = taps[4:5, :]
        for k in range(CONV):
            out = out + near[k] * taps[k : k + 1, :]
        sigma = jax.nn.sigmoid(out)
        low = grad[at : at + CHUNK, :].astype(BF).astype(F32)
        back = low * sigma * (1.0 + out * (1.0 - sigma))
        back = jnp.where(live_rows(meta, at, back.shape), back, 0.0)
        grad_conv[at : at + CHUNK, :] = back
        for k in range(CONV):
            sums[k : k + 1, :] += jnp.sum(back * near[k], axis=0, keepdims=True)
        sums[4:5, :] += jnp.sum(back, axis=0, keepdims=True)
    for at in range(0, tokens, CHUNK):
        out = grad_conv[at + 3 : at + 3 + CHUNK, :] * taps[0:1, :]
        for k in range(1, CONV):
            out = out + grad_conv[at + 3 - k : at + 3 - k + CHUNK, :] * taps[k : k + 1, :]
        out = jnp.where(live_rows(meta, at, out.shape), out, 0.0)
        result[at : at + CHUNK, :] = out.astype(BF)


def scan_back_body(
    meta, content, keys, grad_out, entering, columns, rows, skip, masked, taps,
    scores_in, write_in, read_in,
    result, theirs, sums, grad_columns, grad_rows, grad_scores, grad_write, grad_read,
    scores, read_rows, grad, shifted, grad_conv,
):
    half = SPAN // 2

    @pl.when(pl.program_id(0) == 0)
    def _():
        for span in range(2):
            at = span * SPAN
            scores[span] = dot_nt(keys[at : at + SPAN, :DSTATE], keys[at : at + SPAN, DSTATE:])
        read_rows[...] = keys[SPAN:, DSTATE:].astype(F32).T
        grad_scores[...] = scores_in[...]
        grad_write[...] = write_in[...]
        grad_read[...] = read_in[...]

    causal = row_ids(0, (half, SPAN)) <= lax.broadcasted_iota(jnp.int32, (half, SPAN), 1)
    causal_low = row_ids(0, (half, half)) <= lax.broadcasted_iota(jnp.int32, (half, half), 1)
    final = row_ids(0, (SPAN, 1)) == SPAN - 1
    write = keys[0:SPAN, :DSTATE].astype(F32)
    read = keys[SPAN:, DSTATE:].astype(F32)
    chosen = [lane_half((SPAN, 2 * HEADDIM), h) for h in range(2)]
    for pair in range(PER // 2):
        lanes = slice(pair * 2 * HEADDIM, (pair + 1) * 2 * HEADDIM)
        found = {}
        log_parts = {}
        step_parts = {}
        for h in range(2):
            n = 2 * pair + h
            for span in range(2):
                at = span * SPAN
                value = content[at : at + SPAN, lanes]
                value = jnp.where(chosen[h], value, jnp.zeros_like(value))
                pull = grad_out[at : at + SPAN, lanes]
                log_row = rows[0, n : n + 1, at : at + SPAN]
                log_col = columns[0, at : at + SPAN, n : n + 1]
                step_col = columns[0, at : at + SPAN, PER + n : PER + n + 1]
                halves, sums_step, flows = [], [], []
                for low in range(2):
                    a = low * half
                    value_part = value[a : a + half]
                    pull_part = pull[a:] if low else pull
                    mix_grad = dot_nt(value_part, pull_part).astype(BF).astype(F32)
                    decay = log_row[:, a:] - log_col[a : a + half]
                    decay = jnp.exp(jnp.where(causal_low if low else causal, decay, FAR))
                    step_part = step_col[a : a + half]
                    through = scores[span, a : a + half, a:] * decay
                    mix = (through * step_part).astype(BF)
                    halves.append(dot(mix, pull_part))
                    grad_scores[span, a : a + half, a:] += mix_grad * (decay * step_part)
                    product = mix_grad * through
                    sums_step.append(jnp.sum(product, axis=1, keepdims=True))
                    flows.append(jnp.sum(product * step_part, axis=0, keepdims=True))
                flow = flows[0]
                flow = jnp.concatenate([flow[:, :half], flow[:, half:] + flows[1]], axis=1)
                grad_rows[0, n : n + 1, at : at + SPAN] = flow
                along = jnp.concatenate(sums_step, axis=0)
                step_parts[h, span] = along
                log_parts[h, span] = -(along * step_col)
                found[h, span] = jnp.concatenate(halves, axis=0)
        state = entering[0, :, lanes]
        grad_states = []
        for h in range(2):
            n = 2 * pair + h
            pull = grad_out[SPAN:, lanes]
            growth = jnp.exp(columns[0, SPAN:, n : n + 1])
            own = jnp.where(chosen[h], pull, jnp.zeros_like(pull))
            back = dot_nt(own, state).astype(BF).astype(F32)
            grown = back * growth
            grad_read[...] += grown
            log_parts[h, 1] = log_parts[h, 1] + jnp.sum(grown * read, axis=1, keepdims=True)
            reader = (read_rows[...] * jnp.exp(rows[0, n : n + 1, SPAN:])).astype(BF)
            grad_states.append(dot(reader, pull))
        grad_state = jnp.where(
            lane_half((DSTATE, 2 * HEADDIM), 0), grad_states[0], grad_states[1]
        ).astype(BF)
        for h in range(2):
            n = 2 * pair + h
            value = content[0:SPAN, lanes]
            value = jnp.where(chosen[h], value, jnp.zeros_like(value))
            log_col = columns[0, 0:SPAN, n : n + 1]
            spread = jnp.exp(log_col[SPAN - 1 :] - log_col)
            scaled = spread * columns[0, 0:SPAN, PER + n : PER + n + 1]
            back = dot_nt(value, grad_state).astype(BF).astype(F32)
            along = jnp.sum(back * write, axis=1, keepdims=True)
            grad_write[...] += back * scaled
            quick = along * scaled
            step_parts[h, 0] = step_parts[h, 0] + along * spread
            ended = jnp.where(final, jnp.sum(quick, axis=0, keepdims=True), 0.0)
            log_parts[h, 0] = log_parts[h, 0] - quick + ended
            weight = (write * scaled).astype(BF)
            found[h, 0] = found[h, 0] + dot(weight, grad_state)
            for span in range(2):
                at = span * SPAN
                grad_columns[0, at : at + SPAN, n : n + 1] = step_parts[h, span]
                grad_columns[0, at : at + SPAN, PER + n : PER + n + 1] = log_parts[h, span]
        for span in range(2):
            at = span * SPAN
            both = jnp.where(chosen[0], found[0, span], found[1, span])
            pull = grad_out[at : at + SPAN, lanes].astype(F32)
            grad[at : at + SPAN, lanes] = both + skip[:, lanes] * pull
    conv_back(meta, grad, masked, taps, result, sums, shifted, grad_conv)
    for at in range(0, content.shape[0], CHUNK):
        value = content[at : at + CHUNK, :].astype(F32) * grad_out[at : at + CHUNK, :].astype(F32)
        sums[5:6, :] += jnp.sum(value, axis=0, keepdims=True)

    half_steps = pl.num_programs(0) // 2
    at_half = pl.program_id(0) // half_steps

    @pl.when(at_half == 1 - meta[0])
    def _():
        theirs[...] = result[...]


def scan_backward(
    meta, signal, grad_out, entering, columns, rows, skip, masked, taps, kept, first, count
):
    tokens = signal.shape[0]
    last = DI // TILE

    def group(*shape):
        return pl.BlockSpec((1,) + shape, lambda i, meta: (i + first, 0, 0))

    def fresh(*shape):
        return pl.BlockSpec((1,) + shape, lambda i, meta: (i, 0, 0))

    kept_specs = [whole((2, SPAN, SPAN)), whole((SPAN, DSTATE)), whole((SPAN, DSTATE))]
    return call(
        scan_back_body, "scan_backward", meta,
        (signal, signal, grad_out, entering, columns, rows, skip, masked, taps) + tuple(kept),
        [
            tiles(tokens, TILE, first), pl.BlockSpec((tokens, TILE), lambda i, meta: (0, last)),
            tiles(tokens, TILE, first), group(DSTATE, TILE), group(tokens, 2 * PER),
            group(2 * PER, tokens), tiles(1, TILE, first), tiles(tokens, TILE, first),
            tiles(8, TILE, first),
        ]
        + kept_specs,
        [
            shape_of((tokens, count * TILE), BF), shape_of((tokens, count // 2 * TILE), BF),
            shape_of((8, count * TILE)),
            shape_of((count, tokens, 2 * PER)), shape_of((count, 2 * PER, tokens)),
            shape_of((2, SPAN, SPAN)), shape_of((SPAN, DSTATE)), shape_of((SPAN, DSTATE)),
        ],
        [
            tiles(tokens, TILE),
            pl.BlockSpec(
                (tokens, TILE),
                lambda i, meta: (0, jnp.clip(i - (1 - meta[0]) * (count // 2), 0, count // 2 - 1)),
            ),
            tiles(8, TILE), fresh(tokens, 2 * PER), fresh(2 * PER, tokens),
        ]
        + kept_specs,
        [
            pltpu.VMEM((2, SPAN, SPAN), F32), pltpu.VMEM((DSTATE, SPAN), F32),
            pltpu.VMEM((tokens, TILE), F32), pltpu.VMEM((tokens + 8, TILE), F32),
            pltpu.VMEM((tokens + 8, TILE), F32),
        ],
        count, 3 * 10**9 * count, count * MIB, 40,
    )


def tail_body(parts, meta, *refs):
    keys, masked, taps, trio, steps, grad_scores, grad_write, grad_read = refs[:8]
    grad_columns = refs[8 : 8 + parts]
    grad_rows = refs[8 + parts : 8 + 2 * parts]
    result, sums, raw, small, packs, grad, shifted, grad_conv = refs[8 + 2 * parts :]
    tokens = keys.shape[0]
    for span in range(2):
        at = span * SPAN
        write = keys[at : at + SPAN, :DSTATE]
        read = keys[at : at + SPAN, DSTATE:]
        to_write = fine_dot(grad_scores[span], read, dot)
        to_read = fine_dot(grad_scores[span], write, dot_tn)
        if span == 0:
            to_write = to_write + grad_write[...]
        else:
            to_read = to_read + grad_read[...]
        grad[at : at + SPAN, :DSTATE] = to_write
        grad[at : at + SPAN, DSTATE:] = to_read
    conv_back(meta, grad, masked, taps, result, sums, shifted, grad_conv)

    blank = jnp.zeros((tokens, LANES - HEADS), F32)
    of_step, of_log, of_row = [], [], []
    for column_ref, row_ref in zip(grad_columns, grad_rows):
        for g in range(column_ref.shape[0]):
            of_step.append(column_ref[g, :, :PER])
            of_log.append(column_ref[g, :, PER:])
            of_row.append(row_ref[g, :PER, :])
    grad_step = jnp.concatenate(of_step + [blank], axis=1)
    grad_log = jnp.concatenate(of_log + [blank], axis=1)
    across = jnp.concatenate(of_row + [jnp.zeros((LANES - HEADS, tokens), F32)], axis=0)
    grad_log = grad_log + across.T
    upper = row_ids(0, (SPAN, SPAN)) <= lax.broadcasted_iota(jnp.int32, (SPAN, SPAN), 1)
    upper = jnp.where(upper, 1.0, 0.0).astype(BF)
    rates = []
    for at in range(0, tokens, SPAN):
        high, middle, low = pieces(grad_log[at : at + SPAN])
        rates.append(dot(upper, high) + (dot(upper, middle) + dot(upper, low)))
    grad_rate = jnp.concatenate(rates, axis=0)
    decay_rate = steps[1:2, :]
    grad_step = grad_step + grad_rate * decay_rate
    grad_raw = grad_step * jax.nn.sigmoid(trio[0])
    raw[...] = grad_raw.astype(BF)
    small[...] = jnp.zeros_like(small)
    small[0:1, :] = jnp.sum(grad_raw, axis=0, keepdims=True)
    small[1:2, :] = jnp.sum(grad_rate * trio[1], axis=0, keepdims=True) * decay_rate
    for side in range(2):
        at = meta[0] if side == 0 else 1 - meta[0]
        packs[side, :, :LANES] = result[:, pl.ds(pl.multiple_of(at * LANES, LANES), LANES)]
        packs[side, :, LANES:] = raw[...]


def tail_backward(meta, signal, masked, taps, trio, steps, kept, grad_columns, grad_rows):
    tokens = signal.shape[0]
    last = DI // TILE
    key_spec = pl.BlockSpec((tokens, TILE), lambda i, meta: (0, last))
    return call(
        functools.partial(tail_body, len(grad_columns)), "tail_backward", meta,
        (signal, masked, taps, trio, steps) + tuple(kept) + tuple(grad_columns) + tuple(grad_rows),
        [
            key_spec, key_spec, pl.BlockSpec((8, TILE), lambda i, meta: (0, last)),
            whole((3, tokens, LANES)), whole((8, LANES)), whole((2, SPAN, SPAN)),
            whole((SPAN, DSTATE)), whole((SPAN, DSTATE)),
        ]
        + [whole(part.shape) for part in tuple(grad_columns) + tuple(grad_rows)],
        [
            shape_of((tokens, TILE), BF), shape_of((8, TILE)), shape_of((tokens, LANES), BF),
            shape_of((8, LANES)), shape_of((2, tokens, TILE), BF),
        ],
        [
            whole((tokens, TILE)), whole((8, TILE)), whole((tokens, LANES)), whole((8, LANES)),
            whole((2, tokens, TILE)),
        ],
        [
            pltpu.VMEM((tokens, TILE), F32), pltpu.VMEM((tokens + 8, TILE), F32),
            pltpu.VMEM((tokens + 8, TILE), F32),
        ],
        1, 2 * 10**9, 8 * MIB, 40,
    )


def input_body(plan, first, last, meta, *refs):
    count = UNITS
    grads = refs[: len(plan)]
    refs = refs[len(plan) :]
    if not first:
        start, refs = refs[0], refs[1:]
    blocks = []
    for begin, steps, half in plan:
        own, refs = refs[:count], refs[count:]
        rest = None
        if half is not None:
            rest, refs = refs[:count], refs[count:]
        blocks.append((own, rest))
    step = pl.program_id(0)

    if last:
        hidden, out_grad, scale, gain, result, gain_grad, weight, weight_dt, total = refs
    else:
        total, weight = refs

    @pl.when(step == 0)
    def _():
        total[...] = jnp.zeros_like(total) if first else start[...]

    for n, (begin, steps, half) in enumerate(plan):
        @pl.when((step >= begin) & (step < begin + steps))
        def _(n=n, half=half):
            own, rest = blocks[n]
            if grads[n].shape[1] == LANES:
                weight_dt[...] = jnp.zeros_like(weight_dt)
                gather_lanes(weight_dt, own, meta, TABLE)
                total[...] += dot(grads[n][...], weight_dt[...])
                return
            if half is None:
                gather_lanes(weight, own, meta, TABLE)
            else:
                @pl.when(meta[0] == half)
                def _():
                    gather_lanes(weight, own, meta, TABLE)

                @pl.when(meta[0] != half)
                def _():
                    gather_lanes(weight, rest, meta, TABLE + count)

            total[...] += dot(grads[n][...], weight[...])

    if not last:
        return

    @pl.when(step == pl.num_programs(0) - 1)
    def _():
        tokens, width = hidden.shape
        gain_grad[...] = jnp.zeros_like(gain_grad)

        def finish(n, carry):
            rows = pl.ds(pl.multiple_of(n * 16, 16), 16)
            r = scale[rows, :]
            value = hidden[rows, :].astype(F32)
            grad = total[rows, :]
            gain_grad[...] += jnp.sum(grad * value * r, axis=0, keepdims=True)
            grad = grad * gain[...]
            mean = jnp.sum(grad * value, axis=1, keepdims=True) / width
            result[rows, :] = r * grad - value * (r * r * r * mean) + out_grad[rows, :].astype(F32)
            return carry

        lax.fori_loop(0, tokens // 16, finish, 0)


def input_backward(meta, start, parts, tokens, width, last=None):
    part = width // UNITS
    plan, step, grad_specs, block_specs, grads, blocks = [], 0, [], [], [], []

    def grad_spec(columns, begin, steps, first):
        return pl.BlockSpec(
            (tokens, columns), lambda i, meta: (0, first + jnp.clip(i - begin, 0, steps - 1))
        )

    def row_spec(rows, begin, steps, first, when):
        def index(i, meta):
            at = first + jnp.clip(i - begin, 0, steps - 1)
            return (at if when is None else jnp.where(when(meta), at, first), 0)

        return pl.BlockSpec((rows, part), index)

    def is_half(half):
        return lambda meta: meta[0] == half

    def not_half(half):
        return lambda meta: meta[0] != half

    for grad, grad_first, steps, half, own, own_first, rest, local_first in parts:
        small = grad.shape[1] == LANES
        plan.append((step, steps, half))
        grads.append(grad)
        grad_specs.append(grad_spec(LANES if small else TILE, step, steps, grad_first))
        when = None if half is None else is_half(half)
        for matrix in own:
            blocks.append(matrix)
            block_specs.append(row_spec(64 if small else TILE, step, steps, own_first, when))
        if half is not None:
            for j, matrix in enumerate(rest):
                blocks.append(matrix)
                row = local_first if j == 0 else 0
                block_specs.append(row_spec(TILE, step, steps, row, not_half(half)))
        step += steps
    more, more_specs = (), []
    outs, out_specs = [shape_of((tokens, width))], [whole((tokens, width))]
    scratch = [pltpu.VMEM((TILE, width), BF)]
    if last is not None:
        more = tuple(last)
        more_specs = [whole((tokens, width))] * 2 + [whole((tokens, 1)), whole((1, width))]
        outs.append(shape_of((1, width)))
        out_specs.append(whole((1, width)))
        scratch += [pltpu.VMEM((LANES, width), BF), pltpu.VMEM((tokens, width), F32)]
    first = start is None
    return call(
        functools.partial(input_body, tuple(plan), first, last is not None),
        "input_backward", meta,
        tuple(grads) + (() if first else (start,)) + tuple(blocks) + more,
        grad_specs + ([] if first else [whole((tokens, width))]) + block_specs + more_specs,
        outs, out_specs, scratch,
        step, 2 * tokens * width * TILE * step, 20 * MIB, 58,
    )


def mirrored(j, count):
    if count != 4:
        return j
    result, bit, other = 0, 1, count // 2
    while bit < count:
        if j & bit:
            result |= other
        bit, other = bit * 2, other // 2
    return result


def hop(x, bit):
    reps, count = lax.axis_size("rep"), lax.axis_size("shard")
    pairs = []
    for r in range(reps):
        flip = bit if r % 2 == 0 else mirrored(bit, count)
        pairs += [(r * count + s, r * count + (s ^ flip)) for s in range(count)]
    return lax.ppermute(x, ("rep", "shard"), pairs)


def swap(x):
    return lax.ppermute(x, "rep", [(r, r ^ 1) for r in range(lax.axis_size("rep"))])


def across(x, bit):
    return lax.ppermute(x, "shard", [(s, s ^ bit) for s in range(lax.axis_size("shard"))])


def along(x, pairs):
    return lax.ppermute(x, "rep", [(2 * a + k, 2 * b + k) for a, b in pairs for k in range(2)])


def settle(keep, arrived):
    held = keep + arrived.astype(F32)
    middle = held.shape[0] // 2
    if middle == 0:
        return None, held
    return held[middle:].astype(BF), held[:middle]


def finish_stages(send, keep):
    while send is not None:
        send, keep = settle(keep, hop(send, send.shape[0]))
    return keep[0]


def inward(held):
    if lax.axis_size("rep") // 2 != 4:
        return held, None
    return held, along(held.astype(BF), [(0, 1), (3, 2)])


def middle(state):
    held, arrived = state
    if arrived is None:
        return held, None
    inner = (held + arrived.astype(F32)).astype(BF)
    return inner, along(inner, [(1, 2), (2, 1)])


def outward(state):
    inner, arrived = state
    if arrived is None:
        chips = lax.axis_size("rep") // 2
        total, bit = inner.astype(BF), 1
        while bit < chips:
            more = along(total, [(k, k ^ bit) for k in range(chips)])
            total = (total.astype(F32) + more.astype(F32)).astype(BF)
            bit *= 2
        return total
    total = (inner.astype(F32) + arrived.astype(F32)).astype(BF)
    place = lax.axis_index("rep") // 2
    return jnp.where((place == 1) | (place == 2), total, along(total, [(1, 0), (2, 3)]))


def in_order(own, other, core):
    return [jnp.where(core == 0, own, other), jnp.where(core == 0, other, own)]


def hold(values):
    leaves, tree = jax.tree.flatten(values)
    return jax.tree.unflatten(tree, lax.optimization_barrier(tuple(leaves)))


def small_sum(vector, shard, count):
    vector = vector + swap(vector)
    rows = jnp.stack([lax.dynamic_index_in_dim(vector, shard ^ j, 0, False) for j in range(count)])
    bit = count // 2
    while bit:
        rows = rows[:bit] + across(rows[bit:], bit)
        bit //= 2
    bit, chips = 1, lax.axis_size("rep") // 2
    while bit < chips:
        rows = rows + along(rows, [(k, k ^ bit) for k in range(chips)])
        bit *= 2
    return rows[0]


def join_lanes(blocks, shard):
    return [
        jnp.concatenate(in_order(blocks[j], blocks[j + 1], shard % 2), axis=1)
        for j in range(0, len(blocks), 2)
    ]


def split_lanes(units, shard):
    half = units.shape[2] // 2
    pairs = in_order(units[:, :, :half], units[:, :, half:], shard % 2)
    return jnp.stack(pairs, axis=1).reshape(2 * units.shape[0], units.shape[1], half)


def pad_lanes(matrix):
    return jnp.pad(matrix, ((0, 0), (0, LANES - matrix.shape[1])))


def shards(
    hidden,
    out_grad,
    norm_gain,
    in_w,
    conv_w,
    conv_b,
    dt_bias,
    a_log,
    skip,
    out_gain,
    out_w,
    lengths,
    offsets,
):
    core = lax.axis_index("rep") % 2
    shard = lax.axis_index("shard")
    count = lax.axis_size("shard")
    tokens, width = hidden.shape
    bits = []
    while 2 ** len(bits) < count:
        bits.append(2 ** len(bits))

    local = in_w.T
    half = DI // 2
    piece = jnp.concatenate(
        [
            lax.dynamic_slice_in_dim(local, DI + core * half, half, 0),
            local[2 * DI :],
            jnp.zeros((16, local.shape[1]), BF),
        ],
        axis=0,
    )
    gate_piece = lax.dynamic_slice_in_dim(local, core * half, half, 0)
    out_piece = lax.dynamic_slice_in_dim(out_w, core * (out_w.shape[0] // 2), out_w.shape[0] // 2, 0)

    def spread(first):
        blocks = [first]
        for bit in bits:
            blocks = blocks + [hop(block, bit) for block in blocks]
        return blocks

    paired = count == 4
    conv_own = spread(piece)
    gate_piece, conv_own = hold((gate_piece, conv_own))
    if paired:
        conv_rest = [swap(block) for block in conv_own[1:]]
        gate_near = hop(gate_piece, 1), hop(gate_piece, 2)
        out_local, in_local = out_w, local
    else:
        gate_own = spread(gate_piece)
        out_piece, gate_own = hold((out_piece, gate_own))
        out_own = spread(out_piece)
        conv_rest = rest_conv = join_lanes([swap(block) for block in conv_own], shard)
        gate_rest = rest_gate = join_lanes([swap(block) for block in gate_own], shard)
        conv_own, gate_own = join_lanes(conv_own, shard), join_lanes(gate_own, shard)
        out_full = [jnp.concatenate(in_order(block, swap(block), core), axis=0) for block in out_own]
        out_one, out_two = out_full[:UNITS], out_full[UNITS:]
        out_local = in_local = None

    small = (norm_gain, conv_w, conv_b, dt_bias, a_log, skip, out_gain)
    packed = jnp.concatenate([part.reshape(-1) for part in small])
    everyone = lax.all_gather(packed, "shard", axis=0, tiled=False)
    parts, start = [], 0
    for part in small:
        cut = everyone[:, start : start + part.size].astype(F32)
        parts.append(cut.reshape((count * part.shape[0],) + part.shape[1:]))
        start += part.size
    gain_one, kernel, bias_conv, bias_step, log_rate, skip_full, gain_two = parts
    decay_rate = -jnp.exp(log_rate)

    mine = [jnp.where(core == 0, j, mirrored(j, count)) for j in range(count)]
    other = [jnp.where(core == 0, mirrored(j, count), j) for j in range(count)]
    mine, other = [shard ^ j for j in mine], [shard ^ j for j in other]
    if paired:
        out_units = [2 * j + core for j in mine] + [2 * j + 1 - core for j in other]
    else:
        out_units = mine
        mine = other = [j // 2 for j in mine[::2]]
    meta = jnp.stack(
        [core, offsets[0], lengths[0], shard] + mine + other + out_units
    ).astype(jnp.int32)
    taps = jnp.concatenate([kernel.T, bias_conv[None], jnp.zeros((3, CC), F32)], axis=0)
    steps = jnp.concatenate(
        [pad_lanes(jnp.stack([bias_step, decay_rate])), jnp.zeros((6, LANES), F32)], axis=0
    )
    skip_lanes = jnp.repeat(skip_full, HEADDIM)[None]

    positions = jnp.arange(tokens, dtype=jnp.int32)
    live_mask = ((positions >= offsets[0]) & (positions < offsets[0] + lengths[0])).astype(F32)
    hidden_full = hidden.astype(F32)
    inv_rms = lax.rsqrt(jnp.mean(hidden_full * hidden_full, axis=1, keepdims=True) + epsilon)
    normed = (hidden_full * inv_rms * gain_one).astype(BF)
    pulled = (out_grad.astype(F32) * live_mask[:, None]).astype(BF)
    normed_rest = swap(normed)
    pulled_rest = swap(pulled)

    masked, signal, columns, rows, trio = conv_forward(
        meta, normed, taps, steps, conv_own, conv_rest, in_local
    )
    if paired:
        gate_near, signal = hold((gate_near, signal))
        gate_own = [gate_piece, *gate_near, hop(gate_near[0], 2)]
    mixed, entering = scan_forward(meta, signal, columns, rows, skip_lanes)
    if paired:
        out_piece, gate_far, mixed = hold((out_piece, gate_own[3], mixed))
        gate_own[3] = gate_far
        gate_rest = [swap(block) for block in gate_own[1:]]
        rest_conv, rest_gate = [local] + conv_rest, [local] + gate_rest
        out_near = hop(out_piece, 1), hop(out_piece, 2)
    gate, normed_out, out_theirs, scale = gate_forward(
        meta, normed, mixed, gain_two[None], gate_own, gate_rest, in_local
    )
    out_arrived = swap(out_theirs if paired else normed_out)
    if paired:
        out_near, normed_out = hold((out_near, normed_out))
        out_one = [*out_near, hop(out_near[0], 2)]
        out_two = [swap(block) for block in out_one]
    block_out, grad_gate, gate_theirs, grad_mixed, grad_gain_two = out_forward(
        meta, normed_out, pulled, hidden, mixed, gate, scale, gain_two[None],
        out_one, out_two, out_local,
    )

    upper = count // 2
    gate_arrived = swap(gate_theirs)

    out_pulls = (pulled, pulled_rest)
    if not paired:
        cut = core * (width // 2)
        out_pulls = [lax.dynamic_slice_in_dim(x, cut, width // 2, 1) for x in out_pulls]

    def out_product(first, kind):
        at = TABLE if paired else OUT_TABLE
        return rows_product(meta, normed_out, out_arrived, at, *out_pulls, first, upper, kind)

    def product(parts, first, kind):
        half_units = UNITS // 2
        first = half_units if first else 0
        units = columns_product(meta, parts, normed, normed_rest, first, half_units, kind)
        return units if paired else split_lanes(units, shard)

    out_send = out_product(upper, BF)
    out_keep = out_product(0, F32)
    gate_parts = [(grad_gate, lambda meta: meta[0] * (GROUPS // 2), GROUPS // 2, gate_arrived)]
    gate_send = product(gate_parts, upper, BF)
    gate_keep = product(gate_parts, 0, F32)
    out_send, gate_send, out_keep, gate_keep, grad_mixed = hold(
        (out_send, gate_send, out_keep, gate_keep, grad_mixed)
    )
    out_there = hop(out_send, upper)
    gate_there = hop(gate_send, upper)

    kept = (
        jnp.zeros((2, SPAN, SPAN), F32),
        jnp.zeros((SPAN, DSTATE), F32),
        jnp.zeros((SPAN, DSTATE), F32),
    )
    near = GROUPS // 2
    grad_near, near_theirs, sums_near, columns_near, rows_near, *kept = scan_backward(
        meta, signal, grad_mixed, entering, columns, rows, skip_lanes, masked, taps, kept, 0, near
    )
    out_there, gate_there, near_theirs = hold((out_there, gate_there, near_theirs))
    near_arrived = swap(near_theirs)
    out_send, out_keep = settle(out_keep, out_there)
    gate_send, gate_keep = settle(gate_keep, gate_there)
    near_parts = [(grad_near, lambda meta: meta[0] * (near // 2), near // 2, near_arrived)]
    near_send = product(near_parts, upper, BF)
    near_keep = product(near_parts, 0, F32)
    out_send, gate_send, near_send, near_keep, kept, grad_mixed = hold(
        (out_send, gate_send, near_send, near_keep, kept, grad_mixed)
    )
    out_there = hop(out_send, upper // 2)
    gate_there = hop(gate_send, upper // 2)
    near_there = hop(near_send, upper)

    grad_far, far_theirs, sums_far, columns_far, rows_far, *kept = scan_backward(
        meta, signal, grad_mixed, entering, columns, rows, skip_lanes, masked, taps, kept, near, near
    )
    out_there, gate_there, near_there, far_theirs, kept = hold(
        (out_there, gate_there, near_there, far_theirs, kept)
    )
    far_arrived = swap(far_theirs)
    out_line = inward(finish_stages(*settle(out_keep, out_there)))
    gate_line = inward(finish_stages(*settle(gate_keep, gate_there)))
    near_send, near_keep = settle(near_keep, near_there)
    near_there = hop(near_send, upper // 2)
    grad_keys, sums_keys, grad_raw, grad_steps, packs = tail_backward(
        meta, signal, masked, taps, trio, steps, kept, (columns_near, columns_far),
        (rows_near, rows_far),
    )
    packs_arrived = swap(packs[1])
    far_parts = [
        (grad_far, lambda meta: meta[0] * (near // 2), near // 2, far_arrived),
        (packs[0], lambda meta: 0, 1, packs_arrived),
    ]
    far_send = product(far_parts, upper, BF)
    far_keep = product(far_parts, 0, F32)
    far_there = hop(far_send, upper)

    part = GROUPS // 2
    early, out_line, gate_line, near_there, far_keep, far_send = hold(
        (grad_gate, out_line, gate_line, near_there, far_keep, far_send)
    )
    out_line = middle(out_line)
    gate_line = middle(gate_line)
    near_line = inward(finish_stages(*settle(near_keep, near_there)))
    (partial,) = input_backward(
        meta, None,
        [
            (early, 0, part, 0, gate_own, 0, rest_gate, 0),
            (early, part, part, 1, gate_own, 0, rest_gate, part if paired else 0),
            (grad_near, 0, part, 0, conv_own, 0, rest_conv, GROUPS if paired else 0),
        ],
        tokens, width,
    )
    partial, out_line, gate_line, near_line, far_there = hold(
        (partial, out_line, gate_line, near_line, far_there)
    )
    out_total = outward(out_line)
    gate_total = outward(gate_line)
    near_line = middle(near_line)
    far_send, far_keep = settle(far_keep, far_there)
    far_there = hop(far_send, upper // 2)
    hidden_grad, grad_gain_one = input_backward(
        meta, partial,
        [
            (grad_far, 0, part, 1, conv_own, 0, rest_conv, GROUPS + part if paired else 0),
            (grad_keys, 0, 1, None, conv_own, part, None, 0),
            (grad_raw, 0, 1, None, conv_own, (part + 1) * TILE // 64, None, 0),
        ],
        tokens, width, (hidden, out_grad, inv_rms, gain_one[None]),
    )
    near_total = outward(near_line)
    far_total = outward(middle(inward(finish_stages(*settle(far_keep, far_there)))))

    out_w_grad = jnp.concatenate(
        in_order(out_total, swap(out_total), core), axis=0 if paired else 1
    ).astype(F32)
    far = in_order(far_total, swap(far_total), core)
    content, keys = near // 2 * TILE, near // 2 * TILE + LANES
    in_w_grad = jnp.concatenate(
        in_order(gate_total, swap(gate_total), core)
        + in_order(near_total, swap(near_total), core)
        + [far[0][:content], far[1][:content], far[0][content:keys], far[1][content:keys]]
        + [far[0][keys : keys + HEADS]],
        axis=0,
    ).astype(F32).T

    sums = jnp.concatenate([sums_near, sums_far, sums_keys], axis=1)
    grads = (
        grad_gain_one[0].reshape(count, -1),
        sums[:CONV].reshape(CONV, count, -1).transpose(1, 0, 2).reshape(count, -1),
        sums[CONV].reshape(count, -1),
        grad_steps[0, :HEADS].reshape(count, -1),
        grad_steps[1, :HEADS].reshape(count, -1),
        jnp.sum(sums[5, :DI].reshape(HEADS, HEADDIM), axis=1).reshape(count, -1),
        grad_gain_two[0].reshape(count, -1),
    )
    summed = small_sum(jnp.concatenate(grads, axis=1), shard, count)
    found, start = [], 0
    for part in grads:
        found.append(summed[start : start + part.shape[1]])
        start += part.shape[1]
    return (
        block_out,
        hidden_grad,
        found[0],
        in_w_grad,
        found[1].reshape(CONV, -1).T,
        found[2],
        found[3],
        found[4],
        found[5],
        found[6],
        out_w_grad,
    )


def solution(mesh):
    return jax.shard_map(
        shards,
        mesh=mesh,
        in_specs=(
            P(("rep", "shard"), None),
            P(("rep", "shard"), None),
            P("shard"),
            P("shard", None),
            P("shard", None),
            P("shard"),
            P("shard"),
            P("shard"),
            P("shard"),
            P("shard"),
            P("shard", None),
            P(("rep", "shard")),
            P(("rep", "shard")),
        ),
        out_specs=(
            P(("rep", "shard"), None),
            P(("rep", "shard"), None),
            P("shard"),
            P("shard", None),
            P("shard", None),
            P("shard"),
            P("shard"),
            P("shard"),
            P("shard"),
            P("shard"),
            P("shard", None),
        ),
        check_vma=False,
    )
```

```python
import functools

import jax
import jax.numpy as jnp
from jax import lax
from jax.experimental import pallas as pl
from jax.experimental.pallas import tpu as pltpu
from jax.sharding import PartitionSpec as P

HEADS = 48
HEADDIM = 64
DSTATE = 128
CONV = 4
SPAN = 256
DI = 3072
CC = 3328
TILE = 256
GROUPS = DI // TILE
PER = TILE // HEADDIM
CHUNK = 64
LANES = 128
epsilon = 1e-05
FAR = -1e30

BF = jnp.bfloat16
F32 = jnp.float32
MIB = 1 << 20


def dot(lhs, rhs):
    return jnp.dot(lhs, rhs, preferred_element_type=F32)


def dot_nt(lhs, rhs):
    return lax.dot_general(lhs, rhs, (((1,), (1,)), ((), ())), preferred_element_type=F32)


def dot_tn(lhs, rhs):
    return lax.dot_general(lhs, rhs, (((0,), (0,)), ((), ())), preferred_element_type=F32)


def pieces(value):
    high = value.astype(BF)
    rest = value - high.astype(F32)
    middle = rest.astype(BF)
    low = (rest - middle.astype(F32)).astype(BF)
    return high, middle, low


def fine_dot(lhs, rhs, product):
    high, middle, low = pieces(lhs)
    return product(high, rhs) + (product(middle, rhs) + product(low, rhs))


def row_ids(start, shape):
    return start + lax.broadcasted_iota(jnp.int32, shape, 0)


def live_rows(meta, start, shape):
    ids = row_ids(start, shape)
    return (ids >= meta[1]) & (ids < meta[1] + meta[2])


def gather_lanes(target, blocks, table, at):
    for j, block in enumerate(blocks):
        width = block.shape[1]
        lanes = pl.ds(pl.multiple_of(table[at + j] * width, LANES), width)
        target[0 : block.shape[0], lanes] = block[...]


def call(body, name, meta, operands, in_specs, outs, out_specs, scratch, grid, flops, moved):
    return pl.pallas_call(
        body,
        name=name,
        grid_spec=pltpu.PrefetchScalarGridSpec(
            num_scalar_prefetch=1,
            grid=(grid,),
            in_specs=in_specs,
            out_specs=out_specs,
            scratch_shapes=scratch,
        ),
        out_shape=outs,
        compiler_params=pltpu.CompilerParams(vmem_limit_bytes=60 * MIB),
        cost_estimate=pl.CostEstimate(flops=flops, bytes_accessed=moved, transcendentals=0),
    )(meta, *operands)


def whole(shape):
    rank = len(shape)
    return pl.BlockSpec(shape, lambda i, meta: (0,) * rank)


def tiles(rows, width, shift=0, last=None):
    def index(i, meta):
        at = i + shift
        if last is not None:
            at = jnp.clip(at, 0, last)
        return (0, at)

    return pl.BlockSpec((rows, width), index)


def shape_of(shape, kind=F32):
    return jax.ShapeDtypeStruct(shape, kind)


TABLE = 4
UNITS = 4
OUT_TABLE = TABLE + 2 * UNITS


def own_tile(i, meta):
    half = GROUPS // 2
    return jnp.where(i < half, meta[0] * half + i, (1 - meta[0]) * half + i - half)


def conv_body(meta, x, taps, steps, *refs):
    count = UNITS
    own, rest, dts = refs[:count], refs[count : 2 * count], refs[2 * count : 3 * count]
    masked, signal, columns, rows, trio, weight, weight_dt, shifted = refs[3 * count :]
    tokens = x.shape[0]
    step = pl.program_id(0)

    @pl.when(step <= GROUPS // 2)
    def _():
        gather_lanes(weight, own, meta, TABLE)

    @pl.when(step > GROUPS // 2)
    def _():
        gather_lanes(weight, rest, meta, TABLE + count)

    low = dot_nt(x[...], weight[...]).astype(BF)
    low = jnp.where(live_rows(meta, 0, low.shape), low, jnp.zeros_like(low))
    masked[...] = low
    shifted[0:8, :] = jnp.zeros((8, TILE), F32)
    shifted[8:, :] = low.astype(F32)
    for at in range(0, tokens, CHUNK):
        out = taps[4:5, :]
        for k in range(CONV):
            out = out + shifted[at + 5 + k : at + 5 + k + CHUNK, :] * taps[k : k + 1, :]
        out = out * jax.nn.sigmoid(out)
        out = jnp.where(live_rows(meta, at, out.shape), out, 0.0)
        signal[at : at + CHUNK, :] = out.astype(BF)

    @pl.when(step == 0)
    def _():
        gather_lanes(weight_dt, dts, meta, TABLE)
        raw = dot_nt(x[...], weight_dt[...]).astype(BF).astype(F32)
        raw = jnp.concatenate([raw, jnp.zeros((tokens, LANES - raw.shape[1]), F32)], axis=1)
        pre = raw + steps[0:1, :]
        size = jnp.maximum(pre, 0.0) + jnp.log1p(jnp.exp(-jnp.abs(pre)))
        rate = size * steps[1:2, :]
        lower = row_ids(0, (SPAN, SPAN)) >= lax.broadcasted_iota(jnp.int32, (SPAN, SPAN), 1)
        lower = jnp.where(lower, 1.0, 0.0).astype(BF)
        trio[0] = pre
        trio[1] = size
        for at in range(0, tokens, SPAN):
            high, middle, small = pieces(rate[at : at + SPAN])
            trio[2, at : at + SPAN, :] = dot(lower, high) + (dot(lower, middle) + dot(lower, small))
        log = trio[2]
        size_rows = size.T
        log_rows = log.T
        for g in range(GROUPS):
            a, b = g * PER, (g + 1) * PER
            columns[g] = jnp.concatenate([log[:, a:b], size[:, a:b]], axis=1)
            rows[g] = jnp.concatenate([log_rows[a:b], size_rows[a:b]], axis=0)


def conv_forward(meta, x, taps, steps, own, rest, local):
    tokens, width = x.shape
    count = UNITS
    part = width // count
    half = GROUPS // 2

    def natural(i, meta):
        return jnp.where(i == 0, GROUPS, own_tile(jnp.maximum(i - 1, 0), meta))

    def tile(rows):
        return pl.BlockSpec((rows, TILE), lambda i, meta: (0, natural(i, meta)))

    own_spec = pl.BlockSpec(
        (TILE, part), lambda i, meta: (jnp.where(i == 0, half, jnp.minimum(i - 1, half - 1)), 0)
    )
    rest_spec = pl.BlockSpec((TILE, part), lambda i, meta: (jnp.maximum(i - 1 - half, 0), 0))
    local_spec = pl.BlockSpec(
        (TILE, part),
        lambda i, meta: (GROUPS + (1 - meta[0]) * half + jnp.maximum(i - 1 - half, 0), 0),
    )
    dt_spec = pl.BlockSpec((64, part), lambda i, meta: ((half + 1) * TILE // 64, 0))
    return call(
        conv_body, "conv_forward", meta,
        (x, taps, steps) + tuple(own) + (() if local is None else (local,)) + tuple(rest) + tuple(own),
        [whole((tokens, width)), tile(8), whole((8, LANES))] + [own_spec] * count
        + [rest_spec if local is None else local_spec] + [rest_spec] * (count - 1)
        + [dt_spec] * count,
        [
            shape_of((tokens, CC), BF), shape_of((tokens, CC), BF),
            shape_of((GROUPS, tokens, 2 * PER)), shape_of((GROUPS, 2 * PER, tokens)),
            shape_of((3, tokens, LANES)),
        ],
        [
            tile(tokens), tile(tokens),
            whole((GROUPS, tokens, 2 * PER)), whole((GROUPS, 2 * PER, tokens)),
            whole((3, tokens, LANES)),
        ],
        [
            pltpu.VMEM((TILE, width), BF), pltpu.VMEM((64, width), BF),
            pltpu.VMEM((tokens + 8, TILE), F32),
        ],
        CC // TILE, 2 * tokens * width * CC, 24 * MIB,
    )


def lane_half(shape, half):
    ids = lax.broadcasted_iota(jnp.int32, shape, 1)
    return (ids >= HEADDIM) if half else (ids < HEADDIM)


def scan_body(meta, content, keys, columns, rows, skip, out, entering, scores, write_rows):
    half = SPAN // 2

    @pl.when(pl.program_id(0) == 0)
    def _():
        for span in range(2):
            at = span * SPAN
            scores[span] = dot_nt(keys[at : at + SPAN, DSTATE:], keys[at : at + SPAN, :DSTATE])
        write_rows[...] = keys[0:SPAN, :DSTATE].astype(F32).T

    causal = row_ids(0, (half, half)) >= lax.broadcasted_iota(jnp.int32, (half, half), 1)
    causal_low = row_ids(half, (half, SPAN)) >= lax.broadcasted_iota(jnp.int32, (half, SPAN), 1)
    read = keys[SPAN:, DSTATE:].astype(F32)
    for pair in range(PER // 2):
        lanes = slice(pair * 2 * HEADDIM, (pair + 1) * 2 * HEADDIM)
        first, second, states = [], [], []
        for h in range(2):
            n = 2 * pair + h
            for span in range(2):
                at = span * SPAN
                value = content[at : at + SPAN, lanes]
                log_row = rows[0, n : n + 1, at : at + SPAN]
                step_row = rows[0, PER + n : PER + n + 1, at : at + SPAN]
                upper = columns[0, at : at + half, n : n + 1] - log_row[:, :half]
                upper = jnp.exp(jnp.where(causal, upper, FAR))
                mix = (scores[span, :half, :half] * upper * step_row[:, :half]).astype(BF)
                top = dot(mix, value[:half])
                lower = columns[0, at + half : at + SPAN, n : n + 1] - log_row
                lower = jnp.exp(jnp.where(causal_low, lower, FAR))
                mix = (scores[span, half:, :] * lower * step_row).astype(BF)
                bottom = dot(mix, value)
                both = jnp.concatenate([top, bottom], axis=0)
                if span == 0:
                    spread = jnp.exp(log_row[:, SPAN - 1 :] - log_row) * step_row
                    weight = (write_rows[...] * spread).astype(BF)
                    states.append(dot(weight, value))
                    first.append(both)
                else:
                    second.append(both)
        chosen = lane_half((DSTATE, 2 * HEADDIM), 0)
        state = jnp.where(chosen, states[0], states[1]).astype(BF)
        entering[0, :, lanes] = state
        for h in range(2):
            n = 2 * pair + h
            growth = jnp.exp(columns[0, SPAN:, n : n + 1])
            second[h] = second[h] + dot((read * growth).astype(BF), state)
        chosen = lane_half((SPAN, 2 * HEADDIM), 0)
        for span, parts in ((0, first), (1, second)):
            at = span * SPAN
            mixed = jnp.where(chosen, parts[0], parts[1])
            value = content[at : at + SPAN, lanes].astype(F32)
            out[at : at + SPAN, lanes] = mixed + skip[:, lanes] * value


def scan_forward(meta, signal, columns, rows, skip):
    tokens = signal.shape[0]
    last = DI // TILE
    return call(
        scan_body, "scan_forward", meta, (signal, signal, columns, rows, skip),
        [
            tiles(tokens, TILE), pl.BlockSpec((tokens, TILE), lambda i, meta: (0, last)),
            pl.BlockSpec((1, tokens, 2 * PER), lambda i, meta: (i, 0, 0)),
            pl.BlockSpec((1, 2 * PER, tokens), lambda i, meta: (i, 0, 0)),
            tiles(1, TILE),
        ],
        [shape_of((tokens, DI)), shape_of((GROUPS, DSTATE, TILE), BF)],
        [tiles(tokens, TILE), pl.BlockSpec((1, DSTATE, TILE), lambda i, meta: (i, 0, 0))],
        [pltpu.VMEM((2, SPAN, SPAN), F32), pltpu.VMEM((DSTATE, SPAN), F32)],
        GROUPS, 10 * 10**9, 12 * MIB,
    )


def gate_body(meta, x, mixed, gain, *refs):
    count = UNITS
    own, rest = refs[:count], refs[count : 2 * count]
    gate, normed, theirs, scale, weight, gated, total = refs[2 * count :]
    step = pl.program_id(0)
    tokens = x.shape[0]

    @pl.when(step < GROUPS // 2)
    def _():
        gather_lanes(weight, own, meta, TABLE)

    @pl.when(step >= GROUPS // 2)
    def _():
        gather_lanes(weight, rest, meta, TABLE + count)

    gate[...] = dot_nt(x[...], weight[...]).astype(BF)

    @pl.when(step == 0)
    def _():
        total[...] = jnp.zeros_like(total)

    here = pl.ds(pl.multiple_of(own_tile(step, meta) * TILE, TILE), TILE)
    for at in range(0, tokens, CHUNK):
        part = gate[at : at + CHUNK, :].astype(F32)
        part = mixed[at : at + CHUNK, :] * (part * jax.nn.sigmoid(part))
        gated[at : at + CHUNK, here] = part
        square = part * part
        total[at : at + CHUNK, :] += square[:, :LANES] + square[:, LANES:]

    @pl.when(step == pl.num_programs(0) - 1)
    def _():
        mean = jnp.sum(total[...], axis=1, keepdims=True) / DI
        scale[...] = lax.rsqrt(mean + epsilon)

        def finish(g, carry):
            lanes = pl.ds(pl.multiple_of(g * TILE, TILE), TILE)
            for at in range(0, tokens, CHUNK):
                part = gated[at : at + CHUNK, lanes] * scale[at : at + CHUNK, :] * gain[:, lanes]
                normed[at : at + CHUNK, lanes] = part.astype(BF)
            return carry

        lax.fori_loop(0, GROUPS, finish, 0)
        half = DI // (2 * count)
        for k in range(count):
            other = pl.multiple_of((2 * k + 1 - meta[0]) * half, LANES)
            theirs[:, k * half : (k + 1) * half] = normed[:, pl.ds(other, half)]


def gate_forward(meta, x, mixed, gain, own, rest, local):
    tokens, width = x.shape
    count = UNITS
    part = width // count
    half = GROUPS // 2
    tile_spec = pl.BlockSpec((tokens, TILE), lambda i, meta: (0, own_tile(i, meta)))
    own_spec = pl.BlockSpec((TILE, part), lambda i, meta: (jnp.minimum(i, half - 1), 0))
    rest_spec = pl.BlockSpec((TILE, part), lambda i, meta: (jnp.maximum(i - half, 0), 0))
    local_spec = pl.BlockSpec(
        (TILE, part), lambda i, meta: ((1 - meta[0]) * half + jnp.maximum(i - half, 0), 0)
    )
    return call(
        gate_body, "gate_forward", meta,
        (x, mixed, gain) + tuple(own) + (() if local is None else (local,)) + tuple(rest),
        [whole((tokens, width)), tile_spec, whole((1, DI))] + [own_spec] * count
        + [rest_spec if local is None else local_spec] + [rest_spec] * (count - 1),
        [
            shape_of((tokens, DI), BF), shape_of((tokens, DI), BF), shape_of((tokens, DI // 2), BF),
            shape_of((tokens, 1)),
        ],
        [tile_spec, whole((tokens, DI)), whole((tokens, DI // 2)), whole((tokens, 1))],
        [
            pltpu.VMEM((TILE, width), BF), pltpu.VMEM((tokens, DI), F32),
            pltpu.VMEM((tokens, LANES), F32),
        ],
        GROUPS, 2 * tokens * width * DI, 28 * MIB,
    )


STEPS = 4


def out_body(meta, *refs):
    count = UNITS
    normed, mixed, gate, gain = refs[0:2], refs[2:5], refs[5:8], refs[8:11]
    pulled, hidden, scale = refs[11:14]
    own, rest = refs[14 : 14 + count], refs[14 + count : 14 + 2 * count]
    block, grad_gate, theirs, grad_mixed, grad_gain = refs[14 + 2 * count : 19 + 2 * count]
    weight, branch, back, total = refs[19 + 2 * count :]
    step = pl.program_id(0)
    tokens = pulled.shape[0]
    half = DI // (2 * count)

    @pl.when(step == 0)
    def _():
        branch[...] = jnp.zeros_like(branch)
        total[...] = jnp.zeros_like(total)

    for j in range(count):
        @pl.when(step == j)
        def _(j=j):
            weight[0:half, :] = own[j][...]
            weight[half:, :] = rest[j][...]

    @pl.when(step < count)
    def _():
        branch[...] += dot(jnp.concatenate([normed[0][...], normed[1][...]], axis=1), weight[...])
        grads = dot_nt(pulled[...], weight[...]).astype(BF)
        places = []
        for side in range(2):
            at = meta[OUT_TABLE + side * count + step] * half
            places.append(pl.multiple_of(at, LANES))
            back[:, pl.ds(places[side], half)] = grads[:, side * half : (side + 1) * half]

        def first(n, carry):
            rows = pl.ds(pl.multiple_of(n * CHUNK, CHUNK), CHUNK)
            for side in range(2):
                for at in range(0, half, LANES):
                    cut = slice(at, at + LANES)
                    z = gate[side][rows, cut].astype(F32)
                    gated = mixed[side][rows, cut] * (z * jax.nn.sigmoid(z))
                    grad = back[rows, pl.ds(pl.multiple_of(places[side] + at, LANES), LANES)]
                    total[rows, :] += grad.astype(F32) * gain[side][:, cut] * gated
            return carry

        lax.fori_loop(0, tokens // CHUNK, first, 0)

    @pl.when(step == count - 1)
    def _():
        for at in range(0, tokens, CHUNK):
            part = branch[at : at + CHUNK, :]
            part = jnp.where(live_rows(meta, at, part.shape), part, 0.0)
            block[at : at + CHUNK, :] = (hidden[at : at + CHUNK, :].astype(F32) + part).astype(BF)

    @pl.when(step >= count)
    def _():
        late = step - count
        width = DI // STEPS
        grad_gain[...] = jnp.zeros_like(grad_gain)

        def second(n, carry):
            rows = pl.ds(pl.multiple_of(n * CHUNK, CHUNK), CHUNK)
            r = scale[rows, :]
            mean = jnp.sum(total[rows, :], axis=1, keepdims=True) / DI
            factor = r * r * r * mean
            for at in range(0, width, LANES):
                cut = slice(at, at + LANES)
                z = gate[2][rows, cut].astype(F32)
                sigma = jax.nn.sigmoid(z)
                silu = z * sigma
                out = mixed[2][rows, cut]
                gated = out * silu
                grad = back[rows, pl.ds(pl.multiple_of(late * width + at, LANES), LANES)].astype(F32)
                grad_gain[:, cut] += jnp.sum(grad * gated * r, axis=0, keepdims=True)
                grad = r * (grad * gain[2][:, cut]) - gated * factor
                grad_mixed[rows, cut] = (grad * silu).astype(BF)
                grad = grad * out * sigma * (1.0 + z * (1.0 - sigma))
                grad_gate[rows, cut] = grad.astype(BF)
            return carry

        lax.fori_loop(0, tokens // CHUNK, second, 0)

        @pl.when(late // (STEPS // 2) == 1 - meta[0])
        def _():
            theirs[...] = grad_gate[...]


def out_forward(meta, normed, pulled, hidden, mixed, gate, scale, gain, own, rest, local):
    tokens, width = hidden.shape
    count = UNITS
    half = DI // (2 * count)
    step_width = DI // STEPS

    def early(rows, side):
        def index(i, meta):
            return (0, meta[OUT_TABLE + side * count + jnp.minimum(i, count - 1)])

        return pl.BlockSpec((rows, half), index)

    def late(rows):
        return pl.BlockSpec((rows, step_width), lambda i, meta: (0, jnp.maximum(i - count, 0)))

    def local_spec(side):
        return pl.BlockSpec((half, width), lambda i, meta: (meta[0] if side == 0 else 1 - meta[0], 0))

    first = () if local is None else (local,)

    def weight_specs(side):
        one = whole((half, width)) if local is None else local_spec(side)
        return [one] + [whole((half, width))] * (count - 1)

    theirs_spec = pl.BlockSpec(
        (tokens, step_width),
        lambda i, meta: (0, jnp.clip(i - count - (1 - meta[0]) * (STEPS // 2), 0, STEPS // 2 - 1)),
    )
    return call(
        out_body, "out_forward", meta,
        (normed, normed) + (mixed,) * 3 + (gate,) * 3 + (gain,) * 3 + (pulled, hidden, scale)
        + (first + tuple(own) + first + tuple(rest)),
        [early(tokens, 0), early(tokens, 1), early(tokens, 0), early(tokens, 1), late(tokens),
         early(tokens, 0), early(tokens, 1), late(tokens), early(1, 0), early(1, 1), late(1)]
        + [whole((tokens, width))] * 2 + [whole((tokens, 1))]
        + weight_specs(0) + weight_specs(1),
        [
            shape_of((tokens, width), BF), shape_of((tokens, DI), BF),
            shape_of((tokens, DI // 2), BF), shape_of((tokens, DI), BF), shape_of((1, DI)),
        ],
        [whole((tokens, width)), late(tokens), theirs_spec, late(tokens), late(1)],
        [
            pltpu.VMEM((2 * half, width), BF), pltpu.VMEM((tokens, width), F32),
            pltpu.VMEM((tokens, DI), BF), pltpu.VMEM((tokens, LANES), F32),
        ],
        count + STEPS, 4 * tokens * width * DI, 40 * MIB,
    )


def rows_product_body(meta, mine, theirs, pulled, pulled_rest, out):
    total = dot_tn(mine[...], pulled[...]) + dot_tn(theirs[...], pulled_rest[...])
    out[0] = total.astype(out.dtype)


def rows_product(meta, normed, arrived, arrived_at, pulled, pulled_rest, first, blocks, kind):
    tokens, width = pulled.shape
    unit = DI // (2 * UNITS)
    return call(
        rows_product_body, "rows_product", meta, (normed, arrived, pulled, pulled_rest),
        [
            pl.BlockSpec((tokens, unit), lambda i, meta: (0, meta[OUT_TABLE + first + i])),
            pl.BlockSpec((tokens, unit), lambda i, meta: (0, meta[arrived_at + first + i])),
            whole((tokens, width)), whole((tokens, width)),
        ],
        shape_of((blocks, unit, width), kind),
        pl.BlockSpec((1, unit, width), lambda i, meta: (i, 0, 0)),
        [], blocks, 4 * tokens * width * unit * blocks, 8 * MIB,
    )


def columns_product_body(plan, blocks, meta, *refs):
    parts = len(plan)
    mine, theirs = refs[:parts], refs[parts : 2 * parts]
    here = refs[2 * parts : 2 * parts + blocks]
    there = refs[2 * parts + blocks : 2 * parts + 2 * blocks]
    out = refs[2 * parts + 2 * blocks]
    step = pl.program_id(0)
    width = here[0].shape[1]
    for (begin, steps), a, b in zip(plan, mine, theirs):
        @pl.when((step >= begin) & (step < begin + steps))
        def _(a=a, b=b):
            one = jnp.concatenate([block[...] for block in here], axis=1)
            two = jnp.concatenate([block[...] for block in there], axis=1)
            total = dot_tn(a[...], one) + dot_tn(b[...], two)
            for k in range(blocks):
                out[k] = total[:, k * width : (k + 1) * width].astype(out.dtype)


def columns_product(meta, parts, normed, normed_rest, first, blocks, kind):
    tokens, width = normed.shape
    part = width // UNITS
    plan, step, mine_specs, theirs_specs = [], 0, [], []

    def spec(begin, steps, start):
        return pl.BlockSpec(
            (tokens, TILE), lambda i, meta: (0, start(meta) + jnp.clip(i - begin, 0, steps - 1))
        )

    for matrix, start, steps, arrived in parts:
        plan.append((step, steps))
        mine_specs.append(spec(step, steps, start))
        theirs_specs.append(spec(step, steps, lambda meta: 0))
        step += steps

    def lanes(j):
        return pl.BlockSpec((tokens, part), lambda i, meta: (0, meta[TABLE + first + j]))

    lane_specs = [lanes(j) for j in range(blocks)]
    return call(
        functools.partial(columns_product_body, tuple(plan), blocks), "columns_product", meta,
        tuple(p[0] for p in parts) + tuple(p[3] for p in parts)
        + (normed,) * blocks + (normed_rest,) * blocks,
        mine_specs + theirs_specs + lane_specs + lane_specs,
        shape_of((blocks, step * TILE, part), kind),
        pl.BlockSpec((blocks, TILE, part), lambda i, meta: (0, i, 0)),
        [], step, 4 * tokens * step * TILE * part * blocks, 12 * MIB,
    )


def conv_back(meta, grad, masked, taps, result, sums, shifted, grad_conv):
    tokens = masked.shape[0]
    shifted[0:8, :] = jnp.zeros((8, TILE), F32)
    shifted[8:, :] = masked[...].astype(F32)
    grad_conv[tokens:, :] = jnp.zeros((8, TILE), F32)
    sums[...] = jnp.zeros_like(sums)
    for at in range(0, tokens, CHUNK):
        near = [shifted[at + 5 + k : at + 5 + k + CHUNK, :] for k in range(CONV)]
        out = taps[4:5, :]
        for k in range(CONV):
            out = out + near[k] * taps[k : k + 1, :]
        sigma = jax.nn.sigmoid(out)
        low = grad[at : at + CHUNK, :].astype(BF).astype(F32)
        back = low * sigma * (1.0 + out * (1.0 - sigma))
        back = jnp.where(live_rows(meta, at, back.shape), back, 0.0)
        grad_conv[at : at + CHUNK, :] = back
        for k in range(CONV):
            sums[k : k + 1, :] += jnp.sum(back * near[k], axis=0, keepdims=True)
        sums[4:5, :] += jnp.sum(back, axis=0, keepdims=True)
    for at in range(0, tokens, CHUNK):
        out = grad_conv[at + 3 : at + 3 + CHUNK, :] * taps[0:1, :]
        for k in range(1, CONV):
            out = out + grad_conv[at + 3 - k : at + 3 - k + CHUNK, :] * taps[k : k + 1, :]
        out = jnp.where(live_rows(meta, at, out.shape), out, 0.0)
        result[at : at + CHUNK, :] = out.astype(BF)


def scan_back_body(
    meta, content, keys, grad_out, entering, columns, rows, skip, masked, taps,
    scores_in, write_in, read_in,
    result, theirs, sums, grad_columns, grad_rows, grad_scores, grad_write, grad_read,
    scores, read_rows, grad, shifted, grad_conv,
):
    half = SPAN // 2

    @pl.when(pl.program_id(0) == 0)
    def _():
        for span in range(2):
            at = span * SPAN
            scores[span] = dot_nt(keys[at : at + SPAN, :DSTATE], keys[at : at + SPAN, DSTATE:])
        read_rows[...] = keys[SPAN:, DSTATE:].astype(F32).T
        grad_scores[...] = scores_in[...]
        grad_write[...] = write_in[...]
        grad_read[...] = read_in[...]

    causal = row_ids(0, (half, SPAN)) <= lax.broadcasted_iota(jnp.int32, (half, SPAN), 1)
    causal_low = row_ids(0, (half, half)) <= lax.broadcasted_iota(jnp.int32, (half, half), 1)
    final = row_ids(0, (SPAN, 1)) == SPAN - 1
    write = keys[0:SPAN, :DSTATE].astype(F32)
    read = keys[SPAN:, DSTATE:].astype(F32)
    chosen = [lane_half((SPAN, 2 * HEADDIM), h) for h in range(2)]
    for pair in range(PER // 2):
        lanes = slice(pair * 2 * HEADDIM, (pair + 1) * 2 * HEADDIM)
        found = {}
        log_parts = {}
        step_parts = {}
        for h in range(2):
            n = 2 * pair + h
            for span in range(2):
                at = span * SPAN
                value = content[at : at + SPAN, lanes]
                value = jnp.where(chosen[h], value, jnp.zeros_like(value))
                pull = grad_out[at : at + SPAN, lanes]
                log_row = rows[0, n : n + 1, at : at + SPAN]
                log_col = columns[0, at : at + SPAN, n : n + 1]
                step_col = columns[0, at : at + SPAN, PER + n : PER + n + 1]
                halves, sums_step, flows = [], [], []
                for low in range(2):
                    a = low * half
                    value_part = value[a : a + half]
                    pull_part = pull[a:] if low else pull
                    mix_grad = dot_nt(value_part, pull_part).astype(BF).astype(F32)
                    decay = log_row[:, a:] - log_col[a : a + half]
                    decay = jnp.exp(jnp.where(causal_low if low else causal, decay, FAR))
                    step_part = step_col[a : a + half]
                    through = scores[span, a : a + half, a:] * decay
                    mix = (through * step_part).astype(BF)
                    halves.append(dot(mix, pull_part))
                    grad_scores[span, a : a + half, a:] += mix_grad * (decay * step_part)
                    product = mix_grad * through
                    sums_step.append(jnp.sum(product, axis=1, keepdims=True))
                    flows.append(jnp.sum(product * step_part, axis=0, keepdims=True))
                flow = flows[0]
                flow = jnp.concatenate([flow[:, :half], flow[:, half:] + flows[1]], axis=1)
                grad_rows[0, n : n + 1, at : at + SPAN] = flow
                along = jnp.concatenate(sums_step, axis=0)
                step_parts[h, span] = along
                log_parts[h, span] = -(along * step_col)
                found[h, span] = jnp.concatenate(halves, axis=0)
        state = entering[0, :, lanes]
        grad_states = []
        for h in range(2):
            n = 2 * pair + h
            pull = grad_out[SPAN:, lanes]
            growth = jnp.exp(columns[0, SPAN:, n : n + 1])
            own = jnp.where(chosen[h], pull, jnp.zeros_like(pull))
            back = dot_nt(own, state).astype(BF).astype(F32)
            grown = back * growth
            grad_read[...] += grown
            log_parts[h, 1] = log_parts[h, 1] + jnp.sum(grown * read, axis=1, keepdims=True)
            reader = (read_rows[...] * jnp.exp(rows[0, n : n + 1, SPAN:])).astype(BF)
            grad_states.append(dot(reader, pull))
        grad_state = jnp.where(
            lane_half((DSTATE, 2 * HEADDIM), 0), grad_states[0], grad_states[1]
        ).astype(BF)
        for h in range(2):
            n = 2 * pair + h
            value = content[0:SPAN, lanes]
            value = jnp.where(chosen[h], value, jnp.zeros_like(value))
            log_col = columns[0, 0:SPAN, n : n + 1]
            spread = jnp.exp(log_col[SPAN - 1 :] - log_col)
            scaled = spread * columns[0, 0:SPAN, PER + n : PER + n + 1]
            back = dot_nt(value, grad_state).astype(BF).astype(F32)
            along = jnp.sum(back * write, axis=1, keepdims=True)
            grad_write[...] += back * scaled
            quick = along * scaled
            step_parts[h, 0] = step_parts[h, 0] + along * spread
            ended = jnp.where(final, jnp.sum(quick, axis=0, keepdims=True), 0.0)
            log_parts[h, 0] = log_parts[h, 0] - quick + ended
            weight = (write * scaled).astype(BF)
            found[h, 0] = found[h, 0] + dot(weight, grad_state)
            for span in range(2):
                at = span * SPAN
                grad_columns[0, at : at + SPAN, n : n + 1] = step_parts[h, span]
                grad_columns[0, at : at + SPAN, PER + n : PER + n + 1] = log_parts[h, span]
        for span in range(2):
            at = span * SPAN
            both = jnp.where(chosen[0], found[0, span], found[1, span])
            pull = grad_out[at : at + SPAN, lanes].astype(F32)
            grad[at : at + SPAN, lanes] = both + skip[:, lanes] * pull
    conv_back(meta, grad, masked, taps, result, sums, shifted, grad_conv)
    for at in range(0, content.shape[0], CHUNK):
        value = content[at : at + CHUNK, :].astype(F32) * grad_out[at : at + CHUNK, :].astype(F32)
        sums[5:6, :] += jnp.sum(value, axis=0, keepdims=True)

    half_steps = pl.num_programs(0) // 2
    at_half = pl.program_id(0) // half_steps

    @pl.when(at_half == 1 - meta[0])
    def _():
        theirs[...] = result[...]


def scan_backward(
    meta, signal, grad_out, entering, columns, rows, skip, masked, taps, kept, first, count
):
    tokens = signal.shape[0]
    last = DI // TILE

    def group(*shape):
        return pl.BlockSpec((1,) + shape, lambda i, meta: (i + first, 0, 0))

    def fresh(*shape):
        return pl.BlockSpec((1,) + shape, lambda i, meta: (i, 0, 0))

    kept_specs = [whole((2, SPAN, SPAN)), whole((SPAN, DSTATE)), whole((SPAN, DSTATE))]
    return call(
        scan_back_body, "scan_backward", meta,
        (signal, signal, grad_out, entering, columns, rows, skip, masked, taps) + tuple(kept),
        [
            tiles(tokens, TILE, first), pl.BlockSpec((tokens, TILE), lambda i, meta: (0, last)),
            tiles(tokens, TILE, first), group(DSTATE, TILE), group(tokens, 2 * PER),
            group(2 * PER, tokens), tiles(1, TILE, first), tiles(tokens, TILE, first),
            tiles(8, TILE, first),
        ]
        + kept_specs,
        [
            shape_of((tokens, count * TILE), BF), shape_of((tokens, count // 2 * TILE), BF),
            shape_of((8, count * TILE)),
            shape_of((count, tokens, 2 * PER)), shape_of((count, 2 * PER, tokens)),
            shape_of((2, SPAN, SPAN)), shape_of((SPAN, DSTATE)), shape_of((SPAN, DSTATE)),
        ],
        [
            tiles(tokens, TILE),
            pl.BlockSpec(
                (tokens, TILE),
                lambda i, meta: (0, jnp.clip(i - (1 - meta[0]) * (count // 2), 0, count // 2 - 1)),
            ),
            tiles(8, TILE), fresh(tokens, 2 * PER), fresh(2 * PER, tokens),
        ]
        + kept_specs,
        [
            pltpu.VMEM((2, SPAN, SPAN), F32), pltpu.VMEM((DSTATE, SPAN), F32),
            pltpu.VMEM((tokens, TILE), F32), pltpu.VMEM((tokens + 8, TILE), F32),
            pltpu.VMEM((tokens + 8, TILE), F32),
        ],
        count, 3 * 10**9 * count, count * MIB,
    )


def tail_body(parts, meta, *refs):
    keys, masked, taps, trio, steps, grad_scores, grad_write, grad_read = refs[:8]
    grad_columns = refs[8 : 8 + parts]
    grad_rows = refs[8 + parts : 8 + 2 * parts]
    result, sums, raw, small, packs, grad, shifted, grad_conv = refs[8 + 2 * parts :]
    tokens = keys.shape[0]
    for span in range(2):
        at = span * SPAN
        write = keys[at : at + SPAN, :DSTATE]
        read = keys[at : at + SPAN, DSTATE:]
        to_write = fine_dot(grad_scores[span], read, dot)
        to_read = fine_dot(grad_scores[span], write, dot_tn)
        if span == 0:
            to_write = to_write + grad_write[...]
        else:
            to_read = to_read + grad_read[...]
        grad[at : at + SPAN, :DSTATE] = to_write
        grad[at : at + SPAN, DSTATE:] = to_read
    conv_back(meta, grad, masked, taps, result, sums, shifted, grad_conv)

    blank = jnp.zeros((tokens, LANES - HEADS), F32)
    of_step, of_log, of_row = [], [], []
    for column_ref, row_ref in zip(grad_columns, grad_rows):
        for g in range(column_ref.shape[0]):
            of_step.append(column_ref[g, :, :PER])
            of_log.append(column_ref[g, :, PER:])
            of_row.append(row_ref[g, :PER, :])
    grad_step = jnp.concatenate(of_step + [blank], axis=1)
    grad_log = jnp.concatenate(of_log + [blank], axis=1)
    across = jnp.concatenate(of_row + [jnp.zeros((LANES - HEADS, tokens), F32)], axis=0)
    grad_log = grad_log + across.T
    upper = row_ids(0, (SPAN, SPAN)) <= lax.broadcasted_iota(jnp.int32, (SPAN, SPAN), 1)
    upper = jnp.where(upper, 1.0, 0.0).astype(BF)
    rates = []
    for at in range(0, tokens, SPAN):
        high, middle, low = pieces(grad_log[at : at + SPAN])
        rates.append(dot(upper, high) + (dot(upper, middle) + dot(upper, low)))
    grad_rate = jnp.concatenate(rates, axis=0)
    decay_rate = steps[1:2, :]
    grad_step = grad_step + grad_rate * decay_rate
    grad_raw = grad_step * jax.nn.sigmoid(trio[0])
    raw[...] = grad_raw.astype(BF)
    small[...] = jnp.zeros_like(small)
    small[0:1, :] = jnp.sum(grad_raw, axis=0, keepdims=True)
    small[1:2, :] = jnp.sum(grad_rate * trio[1], axis=0, keepdims=True) * decay_rate
    for side in range(2):
        at = meta[0] if side == 0 else 1 - meta[0]
        packs[side, :, :LANES] = result[:, pl.ds(pl.multiple_of(at * LANES, LANES), LANES)]
        packs[side, :, LANES:] = raw[...]


def tail_backward(meta, signal, masked, taps, trio, steps, kept, grad_columns, grad_rows):
    tokens = signal.shape[0]
    last = DI // TILE
    key_spec = pl.BlockSpec((tokens, TILE), lambda i, meta: (0, last))
    return call(
        functools.partial(tail_body, len(grad_columns)), "tail_backward", meta,
        (signal, masked, taps, trio, steps) + tuple(kept) + tuple(grad_columns) + tuple(grad_rows),
        [
            key_spec, key_spec, pl.BlockSpec((8, TILE), lambda i, meta: (0, last)),
            whole((3, tokens, LANES)), whole((8, LANES)), whole((2, SPAN, SPAN)),
            whole((SPAN, DSTATE)), whole((SPAN, DSTATE)),
        ]
        + [whole(part.shape) for part in tuple(grad_columns) + tuple(grad_rows)],
        [
            shape_of((tokens, TILE), BF), shape_of((8, TILE)), shape_of((tokens, LANES), BF),
            shape_of((8, LANES)), shape_of((2, tokens, TILE), BF),
        ],
        [
            whole((tokens, TILE)), whole((8, TILE)), whole((tokens, LANES)), whole((8, LANES)),
            whole((2, tokens, TILE)),
        ],
        [
            pltpu.VMEM((tokens, TILE), F32), pltpu.VMEM((tokens + 8, TILE), F32),
            pltpu.VMEM((tokens + 8, TILE), F32),
        ],
        1, 2 * 10**9, 8 * MIB,
    )


def input_body(plan, first, last, meta, *refs):
    count = UNITS
    grads = refs[: len(plan)]
    refs = refs[len(plan) :]
    if not first:
        start, refs = refs[0], refs[1:]
    blocks = []
    for begin, steps, half in plan:
        own, refs = refs[:count], refs[count:]
        rest = None
        if half is not None:
            rest, refs = refs[:count], refs[count:]
        blocks.append((own, rest))
    step = pl.program_id(0)

    if last:
        hidden, out_grad, scale, gain, result, gain_grad, weight, weight_dt, total = refs
    else:
        total, weight = refs

    @pl.when(step == 0)
    def _():
        total[...] = jnp.zeros_like(total) if first else start[...]

    for n, (begin, steps, half) in enumerate(plan):
        @pl.when((step >= begin) & (step < begin + steps))
        def _(n=n, half=half):
            own, rest = blocks[n]
            if grads[n].shape[1] == LANES:
                weight_dt[...] = jnp.zeros_like(weight_dt)
                gather_lanes(weight_dt, own, meta, TABLE)
                total[...] += dot(grads[n][...], weight_dt[...])
                return
            if half is None:
                gather_lanes(weight, own, meta, TABLE)
            else:
                @pl.when(meta[0] == half)
                def _():
                    gather_lanes(weight, own, meta, TABLE)

                @pl.when(meta[0] != half)
                def _():
                    gather_lanes(weight, rest, meta, TABLE + count)

            total[...] += dot(grads[n][...], weight[...])

    if not last:
        return

    @pl.when(step == pl.num_programs(0) - 1)
    def _():
        tokens, width = hidden.shape
        gain_grad[...] = jnp.zeros_like(gain_grad)

        def finish(n, carry):
            rows = pl.ds(pl.multiple_of(n * 16, 16), 16)
            r = scale[rows, :]
            value = hidden[rows, :].astype(F32)
            grad = total[rows, :]
            gain_grad[...] += jnp.sum(grad * value * r, axis=0, keepdims=True)
            grad = grad * gain[...]
            mean = jnp.sum(grad * value, axis=1, keepdims=True) / width
            result[rows, :] = r * grad - value * (r * r * r * mean) + out_grad[rows, :].astype(F32)
            return carry

        lax.fori_loop(0, tokens // 16, finish, 0)


def input_backward(meta, start, parts, tokens, width, last=None):
    part = width // UNITS
    plan, step, grad_specs, block_specs, grads, blocks = [], 0, [], [], [], []

    def grad_spec(columns, begin, steps, first):
        return pl.BlockSpec(
            (tokens, columns), lambda i, meta: (0, first + jnp.clip(i - begin, 0, steps - 1))
        )

    def row_spec(rows, begin, steps, first, when):
        def index(i, meta):
            at = first + jnp.clip(i - begin, 0, steps - 1)
            return (at if when is None else jnp.where(when(meta), at, first), 0)

        return pl.BlockSpec((rows, part), index)

    def is_half(half):
        return lambda meta: meta[0] == half

    def not_half(half):
        return lambda meta: meta[0] != half

    for grad, grad_first, steps, half, own, own_first, rest, local_first in parts:
        small = grad.shape[1] == LANES
        plan.append((step, steps, half))
        grads.append(grad)
        grad_specs.append(grad_spec(LANES if small else TILE, step, steps, grad_first))
        when = None if half is None else is_half(half)
        for matrix in own:
            blocks.append(matrix)
            block_specs.append(row_spec(64 if small else TILE, step, steps, own_first, when))
        if half is not None:
            for j, matrix in enumerate(rest):
                blocks.append(matrix)
                row = local_first if j == 0 else 0
                block_specs.append(row_spec(TILE, step, steps, row, not_half(half)))
        step += steps
    more, more_specs = (), []
    outs, out_specs = [shape_of((tokens, width))], [whole((tokens, width))]
    scratch = [pltpu.VMEM((TILE, width), BF)]
    if last is not None:
        more = tuple(last)
        more_specs = [whole((tokens, width))] * 2 + [whole((tokens, 1)), whole((1, width))]
        outs.append(shape_of((1, width)))
        out_specs.append(whole((1, width)))
        scratch += [pltpu.VMEM((LANES, width), BF), pltpu.VMEM((tokens, width), F32)]
    first = start is None
    return call(
        functools.partial(input_body, tuple(plan), first, last is not None),
        "input_backward", meta,
        tuple(grads) + (() if first else (start,)) + tuple(blocks) + more,
        grad_specs + ([] if first else [whole((tokens, width))]) + block_specs + more_specs,
        outs, out_specs, scratch,
        step, 2 * tokens * width * TILE * step, 20 * MIB,
    )


def mirrored(j, count):
    if count != 4:
        return j
    result, bit, other = 0, 1, count // 2
    while bit < count:
        if j & bit:
            result |= other
        bit, other = bit * 2, other // 2
    return result


def hop(x, bit):
    reps, count = lax.axis_size("rep"), lax.axis_size("shard")
    pairs = []
    for r in range(reps):
        flip = bit if r % 2 == 0 else mirrored(bit, count)
        pairs += [(r * count + s, r * count + (s ^ flip)) for s in range(count)]
    return lax.ppermute(x, ("rep", "shard"), pairs)


def swap(x):
    return lax.ppermute(x, "rep", [(r, r ^ 1) for r in range(lax.axis_size("rep"))])


def across(x, bit):
    return lax.ppermute(x, "shard", [(s, s ^ bit) for s in range(lax.axis_size("shard"))])


def along(x, pairs):
    return lax.ppermute(x, "rep", [(2 * a + k, 2 * b + k) for a, b in pairs for k in range(2)])


def settle(keep, arrived):
    middle = keep.shape[0] // 2
    if middle == 0:
        return None, keep + arrived.astype(F32)
    send = (keep[middle:] + arrived[middle:].astype(F32)).astype(BF)
    return send, keep[:middle] + arrived[:middle].astype(F32)


def finish_stages(send, keep):
    while send is not None:
        send, keep = settle(keep, hop(send, send.shape[0]))
    return keep[0]


def inward(held):
    if lax.axis_size("rep") // 2 != 4:
        return held, None
    return held, along(held.astype(BF), [(0, 1), (3, 2)])


def middle(state):
    held, arrived = state
    if arrived is None:
        return held, None
    inner = (held + arrived.astype(F32)).astype(BF)
    return inner, along(inner, [(1, 2), (2, 1)])


def outward(state):
    inner, arrived = state
    if arrived is None:
        chips = lax.axis_size("rep") // 2
        total, bit = inner.astype(BF), 1
        while bit < chips:
            more = along(total, [(k, k ^ bit) for k in range(chips)])
            total = (total.astype(F32) + more.astype(F32)).astype(BF)
            bit *= 2
        return total, None
    total = (inner.astype(F32) + arrived.astype(F32)).astype(BF)
    return total, along(total, [(1, 0), (2, 3)])


def summed(state):
    total, arrived = state
    if arrived is None:
        return total
    place = lax.axis_index("rep") // 2
    return jnp.where((place == 1) | (place == 2), total, arrived)


def in_order(own, other, core):
    return [jnp.where(core == 0, own, other), jnp.where(core == 0, other, own)]


def hold(values):
    leaves, tree = jax.tree.flatten(values)
    return jax.tree.unflatten(tree, lax.optimization_barrier(tuple(leaves)))


def small_sum(vector, shard, count):
    vector = vector + swap(vector)
    rows = jnp.stack([lax.dynamic_index_in_dim(vector, shard ^ j, 0, False) for j in range(count)])
    bit = count // 2
    while bit:
        rows = rows[:bit] + across(rows[bit:], bit)
        bit //= 2
    bit, chips = 1, lax.axis_size("rep") // 2
    while bit < chips:
        rows = rows + along(rows, [(k, k ^ bit) for k in range(chips)])
        bit *= 2
    return rows[0]


def join_lanes(blocks, shard):
    return [
        jnp.concatenate(in_order(blocks[j], blocks[j + 1], shard % 2), axis=1)
        for j in range(0, len(blocks), 2)
    ]


def split_lanes(units, shard):
    half = units.shape[2] // 2
    pairs = in_order(units[:, :, :half], units[:, :, half:], shard % 2)
    return jnp.stack(pairs, axis=1).reshape(2 * units.shape[0], units.shape[1], half)


def pad_lanes(matrix):
    return jnp.pad(matrix, ((0, 0), (0, LANES - matrix.shape[1])))


def shards(
    hidden,
    out_grad,
    norm_gain,
    in_w,
    conv_w,
    conv_b,
    dt_bias,
    a_log,
    skip,
    out_gain,
    out_w,
    lengths,
    offsets,
):
    core = lax.axis_index("rep") % 2
    shard = lax.axis_index("shard")
    count = lax.axis_size("shard")
    tokens, width = hidden.shape
    bits = []
    while 2 ** len(bits) < count:
        bits.append(2 ** len(bits))

    local = in_w.T
    half = DI // 2
    piece = jnp.concatenate(
        [
            lax.dynamic_slice_in_dim(local, DI + core * half, half, 0),
            local[2 * DI :],
            jnp.zeros((16, local.shape[1]), BF),
        ],
        axis=0,
    )
    gate_piece = lax.dynamic_slice_in_dim(local, core * half, half, 0)
    out_piece = lax.dynamic_slice_in_dim(out_w, core * (out_w.shape[0] // 2), out_w.shape[0] // 2, 0)

    def spread(first):
        blocks = [first]
        for bit in bits:
            blocks = blocks + [hop(block, bit) for block in blocks]
        return blocks

    paired = count == 4
    small = (norm_gain, conv_w.T, conv_b, dt_bias, a_log, skip, out_gain)
    packed = jnp.concatenate([part.reshape(-1) for part in small])
    everyone = jnp.stack(spread(packed)).astype(F32)
    order = [jnp.where(core == 0, j, mirrored(j, count)) for j in range(count)]
    whose = jnp.stack(order)[jnp.arange(count) ^ shard]
    same = (whose[:, None] == jnp.arange(count)[None]).astype(F32)
    everyone = jnp.sum(same[:, :, None] * everyone[None], axis=1)
    parts, start = [], 0
    for part in small:
        cut = everyone[:, start : start + part.size].reshape((count,) + part.shape)
        cut = jnp.moveaxis(cut, 0, -2)
        parts.append(cut.reshape(part.shape[:-1] + (-1,)))
        start += part.size
    conv_own = spread(piece)
    gate_piece, conv_own = hold((gate_piece, conv_own))
    if paired:
        conv_rest = [swap(block) for block in conv_own[1:]]
        gate_near = hop(gate_piece, 1), hop(gate_piece, 2)
        out_local, in_local = out_w, local
    else:
        gate_own = spread(gate_piece)
        out_piece, gate_own = hold((out_piece, gate_own))
        out_own = spread(out_piece)
        conv_rest = rest_conv = join_lanes([swap(block) for block in conv_own], shard)
        gate_rest = rest_gate = join_lanes([swap(block) for block in gate_own], shard)
        conv_own, gate_own = join_lanes(conv_own, shard), join_lanes(gate_own, shard)
        out_full = [jnp.concatenate(in_order(block, swap(block), core), axis=0) for block in out_own]
        out_one, out_two = out_full[:UNITS], out_full[UNITS:]
        out_local = in_local = None

    gain_one, kernel, bias_conv, bias_step, log_rate, skip_full, gain_two = parts
    decay_rate = -jnp.exp(log_rate)

    mine = order
    other = [jnp.where(core == 0, mirrored(j, count), j) for j in range(count)]
    mine, other = [shard ^ j for j in mine], [shard ^ j for j in other]
    if paired:
        out_units = [2 * j + core for j in mine] + [2 * j + 1 - core for j in other]
    else:
        out_units = mine
        mine = other = [j // 2 for j in mine[::2]]
    meta = jnp.stack(
        [core, offsets[0], lengths[0], shard] + mine + other + out_units
    ).astype(jnp.int32)
    taps = jnp.concatenate([kernel, bias_conv[None], jnp.zeros((3, CC), F32)], axis=0)
    steps = jnp.concatenate(
        [pad_lanes(jnp.stack([bias_step, decay_rate])), jnp.zeros((6, LANES), F32)], axis=0
    )
    skip_lanes = jnp.repeat(skip_full, HEADDIM)[None]

    positions = jnp.arange(tokens, dtype=jnp.int32)
    live_mask = ((positions >= offsets[0]) & (positions < offsets[0] + lengths[0])).astype(F32)
    hidden_full = hidden.astype(F32)
    inv_rms = lax.rsqrt(jnp.mean(hidden_full * hidden_full, axis=1, keepdims=True) + epsilon)
    normed = (hidden_full * inv_rms * gain_one).astype(BF)
    pulled = (out_grad.astype(F32) * live_mask[:, None]).astype(BF)
    normed_rest = swap(normed)
    pulled_rest = swap(pulled)

    masked, signal, columns, rows, trio = conv_forward(
        meta, normed, taps, steps, conv_own, conv_rest, in_local
    )
    if paired:
        gate_near, signal = hold((gate_near, signal))
        gate_own = [gate_piece, *gate_near, hop(gate_near[0], 2)]
    mixed, entering = scan_forward(meta, signal, columns, rows, skip_lanes)
    if paired:
        out_piece, gate_far, mixed = hold((out_piece, gate_own[3], mixed))
        gate_own[3] = gate_far
        gate_rest = [swap(block) for block in gate_own[1:]]
        rest_conv, rest_gate = [local] + conv_rest, [local] + gate_rest
        out_near = hop(out_piece, 1), hop(out_piece, 2)
    gate, normed_out, out_theirs, scale = gate_forward(
        meta, normed, mixed, gain_two[None], gate_own, gate_rest, in_local
    )
    out_arrived = swap(out_theirs if paired else normed_out)
    if paired:
        out_near, normed_out = hold((out_near, normed_out))
        out_one = [*out_near, hop(out_near[0], 2)]
        out_two = [swap(block) for block in out_one]

    upper = count // 2
    out_pulls = (pulled, pulled_rest)
    if not paired:
        cut = core * (width // 2)
        out_pulls = [lax.dynamic_slice_in_dim(x, cut, width // 2, 1) for x in out_pulls]

    def out_product(first, kind):
        at = TABLE if paired else OUT_TABLE
        return rows_product(meta, normed_out, out_arrived, at, *out_pulls, first, upper, kind)

    def product(parts, first, kind):
        half_units = UNITS // 2
        first = half_units if first else 0
        units = columns_product(meta, parts, normed, normed_rest, first, half_units, kind)
        return units if paired else split_lanes(units, shard)

    out_send = out_product(upper, BF)
    out_send, normed_out = hold((out_send, normed_out))
    out_keep = out_product(0, F32)
    out_keep, normed_out = hold((out_keep, normed_out))
    out_there = hop(out_send, upper)
    block_out, grad_gate, gate_theirs, grad_mixed, grad_gain_two = out_forward(
        meta, normed_out, pulled, hidden, mixed, gate, scale, gain_two[None],
        out_one, out_two, out_local,
    )
    out_there, gate_theirs = hold((out_there, gate_theirs))

    gate_arrived = swap(gate_theirs)
    out_send, out_keep = settle(out_keep, out_there)
    gate_parts = [(grad_gate, lambda meta: meta[0] * (GROUPS // 2), GROUPS // 2, gate_arrived)]
    gate_send = product(gate_parts, upper, BF)
    gate_send, gate_arrived = hold((gate_send, gate_arrived))
    gate_parts = [gate_parts[0][:3] + (gate_arrived,)]
    gate_keep = product(gate_parts, 0, F32)
    out_send, out_keep, gate_send, gate_keep, grad_mixed = hold(
        (out_send, out_keep, gate_send, gate_keep, grad_mixed)
    )
    out_there = hop(out_send, upper // 2)
    gate_there = hop(gate_send, upper)
    kept = (
        jnp.zeros((2, SPAN, SPAN), F32),
        jnp.zeros((SPAN, DSTATE), F32),
        jnp.zeros((SPAN, DSTATE), F32),
    )
    near = GROUPS // 2
    grad_near, near_theirs, sums_near, columns_near, rows_near, *kept = scan_backward(
        meta, signal, grad_mixed, entering, columns, rows, skip_lanes, masked, taps, kept, 0, near
    )
    out_there, gate_there, near_theirs = hold((out_there, gate_there, near_theirs))
    near_arrived = swap(near_theirs)
    out_line = inward(finish_stages(*settle(out_keep, out_there)))
    gate_send, gate_keep = settle(gate_keep, gate_there)
    near_parts = [(grad_near, lambda meta: meta[0] * (near // 2), near // 2, near_arrived)]
    near_send = product(near_parts, upper, BF)
    near_send, near_arrived = hold((near_send, near_arrived))
    near_parts = [near_parts[0][:3] + (near_arrived,)]
    near_keep = product(near_parts, 0, F32)
    out_held, gate_send, gate_keep, near_send, near_keep, kept, grad_mixed = hold(
        (out_line[0], gate_send, gate_keep, near_send, near_keep, kept, grad_mixed)
    )
    gate_there = hop(gate_send, upper // 2)
    near_there = hop(near_send, upper)
    grad_far, far_theirs, sums_far, columns_far, rows_far, *kept = scan_backward(
        meta, signal, grad_mixed, entering, columns, rows, skip_lanes, masked, taps, kept, near, near
    )
    gate_there, near_there, out_arrived, far_theirs, kept = hold(
        (gate_there, near_there, out_line[1], far_theirs, kept)
    )
    far_arrived = swap(far_theirs)
    gate_line = inward(finish_stages(*settle(gate_keep, gate_there)))
    out_line = middle((out_held, out_arrived))
    near_send, near_keep = settle(near_keep, near_there)
    near_there = hop(near_send, upper // 2)
    grad_keys, sums_keys, grad_raw, grad_steps, packs = tail_backward(
        meta, signal, masked, taps, trio, steps, kept, (columns_near, columns_far),
        (rows_near, rows_far),
    )
    packs_arrived = swap(packs[1])
    far_parts = [
        (grad_far, lambda meta: meta[0] * (near // 2), near // 2, far_arrived),
        (packs[0], lambda meta: 0, 1, packs_arrived),
    ]
    far_send = product(far_parts, upper, BF)
    far_there = hop(far_send, upper)
    far_send, far_arrived = hold((far_send, far_arrived))
    far_parts = [far_parts[0][:3] + (far_arrived,), far_parts[1]]
    far_keep = product(far_parts, 0, F32)
    part = GROUPS // 2
    early, out_inner, gate_held, far_keep, near_keep = hold(
        (grad_gate, out_line[0], gate_line[0], far_keep, near_keep)
    )
    (partial,) = input_backward(
        meta, None,
        [
            (early, 0, part, 0, gate_own, 0, rest_gate, 0),
            (early, part, part, 1, gate_own, 0, rest_gate, part if paired else 0),
        ],
        tokens, width,
    )
    partial, out_arrived, gate_arrived, near_there, far_there = hold(
        (partial, out_line[1], gate_line[1], near_there, far_there)
    )
    far_send, far_keep = settle(far_keep, far_there)
    far_there = hop(far_send, upper // 2)
    gate_line = middle((gate_held, gate_arrived))
    near_line = inward(finish_stages(*settle(near_keep, near_there)))
    out_line = outward((out_inner, out_arrived))
    partial, gate_inner, near_held, far_keep, out_done = hold(
        (partial, gate_line[0], near_line[0], far_keep, out_line[0])
    )
    (partial,) = input_backward(
        meta, partial, [(grad_near, 0, part, 0, conv_own, 0, rest_conv, GROUPS if paired else 0)],
        tokens, width,
    )
    partial, gate_arrived, near_arrived, far_there, out_arrived = hold(
        (partial, gate_line[1], near_line[1], far_there, out_line[1])
    )
    far_line = inward(finish_stages(*settle(far_keep, far_there)))
    near_line = middle((near_held, near_arrived))
    gate_line = outward((gate_inner, gate_arrived))
    out_total = summed((out_done, out_arrived))
    out_other = swap(out_total)
    partial, far_held, near_inner, gate_done, out_total = hold(
        (partial, far_line[0], near_line[0], gate_line[0], out_total)
    )
    hidden_grad, grad_gain_one = input_backward(
        meta, partial,
        [
            (grad_far, 0, part, 1, conv_own, 0, rest_conv, GROUPS + part if paired else 0),
            (grad_keys, 0, 1, None, conv_own, part, None, 0),
            (grad_raw, 0, 1, None, conv_own, (part + 1) * TILE // 64, None, 0),
        ],
        tokens, width, (hidden, out_grad, inv_rms, gain_one[None]),
    )
    grad_gain_one, near_arrived, far_arrived, gate_arrived, out_other = hold(
        (grad_gain_one, near_line[1], far_line[1], gate_line[1], out_other)
    )
    far_line = middle((far_held, far_arrived))
    near_line = outward((near_inner, near_arrived))
    gate_total = summed((gate_done, gate_arrived))
    near_total = summed(near_line)
    far_total = summed(outward(far_line))

    out_w_grad = jnp.concatenate(
        in_order(out_total, out_other, core), axis=0 if paired else 1
    ).astype(F32)
    far = in_order(far_total, swap(far_total), core)
    content, keys = near // 2 * TILE, near // 2 * TILE + LANES
    in_w_grad = jnp.concatenate(
        in_order(gate_total, swap(gate_total), core)
        + in_order(near_total, swap(near_total), core)
        + [far[0][:content], far[1][:content], far[0][content:keys], far[1][content:keys]]
        + [far[0][keys : keys + HEADS]],
        axis=0,
    ).astype(F32).T

    sums = jnp.concatenate([sums_near, sums_far, sums_keys], axis=1)
    grads = (
        grad_gain_one[0].reshape(count, -1),
        sums[:CONV].reshape(CONV, count, -1).transpose(1, 0, 2).reshape(count, -1),
        sums[CONV].reshape(count, -1),
        grad_steps[0, :HEADS].reshape(count, -1),
        grad_steps[1, :HEADS].reshape(count, -1),
        jnp.sum(sums[5, :DI].reshape(HEADS, HEADDIM), axis=1).reshape(count, -1),
        grad_gain_two[0].reshape(count, -1),
    )
    row = small_sum(jnp.concatenate(grads, axis=1), shard, count)
    found, start = [], 0
    for part in grads:
        found.append(row[start : start + part.shape[1]])
        start += part.shape[1]
    return (
        block_out,
        hidden_grad,
        found[0],
        in_w_grad,
        found[1].reshape(CONV, -1).T,
        found[2],
        found[3],
        found[4],
        found[5],
        found[6],
        out_w_grad,
    )


def solution(mesh):
    return jax.shard_map(
        shards,
        mesh=mesh,
        in_specs=(
            P(("rep", "shard"), None),
            P(("rep", "shard"), None),
            P("shard"),
            P("shard", None),
            P("shard", None),
            P("shard"),
            P("shard"),
            P("shard"),
            P("shard"),
            P("shard"),
            P("shard", None),
            P(("rep", "shard")),
            P(("rep", "shard")),
        ),
        out_specs=(
            P(("rep", "shard"), None),
            P(("rep", "shard"), None),
            P("shard"),
            P("shard", None),
            P("shard", None),
            P("shard"),
            P("shard"),
            P("shard"),
            P("shard"),
            P("shard"),
            P("shard", None),
        ),
        check_vma=False,
    )
```

```python
import functools

import jax
import jax.numpy as jnp
from jax import lax
from jax.experimental import pallas as pl
from jax.experimental.pallas import tpu as pltpu
from jax.sharding import PartitionSpec as P

HEADS = 48
HEADDIM = 64
DSTATE = 128
CONV = 4
SPAN = 256
DI = 3072
CC = 3328
TILE = 256
GROUPS = DI // TILE
PER = TILE // HEADDIM
CHUNK = 64
LANES = 128
epsilon = 1e-05
FAR = -1e30

BF = jnp.bfloat16
F32 = jnp.float32
MIB = 1 << 20


def dot(lhs, rhs):
    return jnp.dot(lhs, rhs, preferred_element_type=F32)


def dot_nt(lhs, rhs):
    return lax.dot_general(lhs, rhs, (((1,), (1,)), ((), ())), preferred_element_type=F32)


def dot_tn(lhs, rhs):
    return lax.dot_general(lhs, rhs, (((0,), (0,)), ((), ())), preferred_element_type=F32)


def sigmoid(value):
    return 0.5 * jnp.tanh(0.5 * value) + 0.5


def pieces(value):
    high = value.astype(BF)
    rest = value - high.astype(F32)
    middle = rest.astype(BF)
    low = (rest - middle.astype(F32)).astype(BF)
    return high, middle, low


def fine_dot(lhs, rhs, product):
    high, middle, low = pieces(lhs)
    return product(high, rhs) + (product(middle, rhs) + product(low, rhs))


def row_ids(start, shape):
    return start + lax.broadcasted_iota(jnp.int32, shape, 0)


def live_rows(meta, start, shape):
    ids = row_ids(start, shape)
    return (ids >= meta[1]) & (ids < meta[1] + meta[2])


def gather_lanes(target, blocks, table, at):
    for j, block in enumerate(blocks):
        width = block.shape[1]
        lanes = pl.ds(pl.multiple_of(table[at + j] * width, LANES), width)
        target[0 : block.shape[0], lanes] = block[...]


def call(body, name, meta, operands, in_specs, outs, out_specs, scratch, grid, flops, moved):
    return pl.pallas_call(
        body,
        name=name,
        grid_spec=pltpu.PrefetchScalarGridSpec(
            num_scalar_prefetch=1,
            grid=(grid,),
            in_specs=in_specs,
            out_specs=out_specs,
            scratch_shapes=scratch,
        ),
        out_shape=outs,
        compiler_params=pltpu.CompilerParams(vmem_limit_bytes=60 * MIB),
        cost_estimate=pl.CostEstimate(flops=flops, bytes_accessed=moved, transcendentals=0),
    )(meta, *operands)


def whole(shape):
    rank = len(shape)
    return pl.BlockSpec(shape, lambda i, meta: (0,) * rank)


def tiles(rows, width, shift=0, last=None):
    def index(i, meta):
        at = i + shift
        if last is not None:
            at = jnp.clip(at, 0, last)
        return (0, at)

    return pl.BlockSpec((rows, width), index)


def shape_of(shape, kind=F32):
    return jax.ShapeDtypeStruct(shape, kind)


TABLE = 4
UNITS = 4
OUT_TABLE = TABLE + 2 * UNITS
WIDE = 512
WIDES = DI // WIDE


def own_tile(i, meta):
    half = WIDES // 2
    return jnp.where(i < half, meta[0] * half + i, (1 - meta[0]) * half + i - half)


def convolve(meta, low, taps, shifted, masked, signal, lanes):
    tokens = low.shape[0]
    low = jnp.where(live_rows(meta, 0, low.shape), low.astype(BF), jnp.zeros(low.shape, BF))
    masked[:, lanes] = low
    shifted[8:, lanes] = low.astype(F32)
    for at in range(0, tokens, CHUNK):
        out = taps[4:5, lanes]
        for k in range(CONV):
            out = out + shifted[at + 5 + k : at + 5 + k + CHUNK, lanes] * taps[k : k + 1, lanes]
        out = out * sigmoid(out)
        out = jnp.where(live_rows(meta, at, out.shape), out, 0.0)
        signal[at : at + CHUNK, lanes] = out.astype(BF)


def conv_body(meta, x, taps, taps_keys, steps, *refs):
    count = UNITS
    own, rest, key_rows, dts = (refs[n * count : (n + 1) * count] for n in range(4))
    (masked, signal, masked_keys, keys, columns, rows, trio,
     weight, weight_dt, shifted) = refs[4 * count :]
    tokens = x.shape[0]
    step = pl.program_id(0)

    @pl.when(step == 0)
    def _():
        shifted[0:8, :] = jnp.zeros((8, WIDE), F32)
        gather_lanes(weight, key_rows, meta, TABLE)
        gather_lanes(weight_dt, dts, meta, TABLE)
        lanes = slice(0, TILE)
        low = dot_nt(x[...], weight[0:TILE, :])
        raw = dot_nt(x[...], weight_dt[...]).astype(BF).astype(F32)
        convolve(meta, low, taps_keys, shifted, masked_keys, keys, lanes)
        raw = jnp.concatenate([raw, jnp.zeros((tokens, LANES - raw.shape[1]), F32)], axis=1)
        pre = raw + steps[0:1, :]
        size = jnp.maximum(pre, 0.0) + jnp.log1p(jnp.exp(-jnp.abs(pre)))
        rate = size * steps[1:2, :]
        lower = row_ids(0, (SPAN, SPAN)) >= lax.broadcasted_iota(jnp.int32, (SPAN, SPAN), 1)
        lower = jnp.where(lower, 1.0, 0.0).astype(BF)
        trio[0] = pre
        trio[1] = size
        for at in range(0, tokens, SPAN):
            high, middle, small = pieces(rate[at : at + SPAN])
            trio[2, at : at + SPAN, :] = dot(lower, high) + (dot(lower, middle) + dot(lower, small))
        log = trio[2]
        less = log - jnp.log(size)
        less_rows = less.T
        log_rows = log.T
        for g in range(GROUPS):
            a, b = g * PER, (g + 1) * PER
            columns[g] = jnp.concatenate([log[:, a:b], less[:, a:b]], axis=1)
            rows[g] = jnp.concatenate([log_rows[a:b], less_rows[a:b]], axis=0)

    @pl.when((step > 0) & (step <= WIDES // 2))
    def _():
        gather_lanes(weight, own, meta, TABLE)

    @pl.when(step > WIDES // 2)
    def _():
        gather_lanes(weight, rest, meta, TABLE + count)

    @pl.when(step > 0)
    def _():
        lows = [dot_nt(x[...], weight[at : at + TILE, :]) for at in range(0, WIDE, TILE)]
        for n, low in enumerate(lows):
            lanes = slice(n * TILE, (n + 1) * TILE)
            convolve(meta, low, taps, shifted, masked, signal, lanes)


def conv_forward(meta, x, taps, steps, own, rest, local):
    tokens, width = x.shape
    count = UNITS
    part = width // count
    half = WIDES // 2

    def natural(i, meta):
        return own_tile(jnp.maximum(i - 1, 0), meta)

    def tile(rows):
        return pl.BlockSpec((rows, WIDE), lambda i, meta: (0, natural(i, meta)))

    def late(i):
        return jnp.maximum(i - 1 - half, 0)

    own_spec = pl.BlockSpec((WIDE, part), lambda i, meta: (jnp.clip(i - 1, 0, half - 1), 0))
    rest_spec = pl.BlockSpec((WIDE, part), lambda i, meta: (late(i), 0))
    local_spec = pl.BlockSpec(
        (WIDE, part), lambda i, meta: (WIDES + (1 - meta[0]) * half + late(i), 0)
    )
    key_spec = pl.BlockSpec((TILE, part), lambda i, meta: (half * WIDE // TILE, 0))
    dt_spec = pl.BlockSpec((64, part), lambda i, meta: ((half * WIDE + TILE) // 64, 0))
    return call(
        conv_body, "conv_forward", meta,
        (x, taps, taps, steps) + tuple(own) + (() if local is None else (local,)) + tuple(rest)
        + tuple(own) * 2,
        [
            whole((tokens, width)), tile(8), pl.BlockSpec((8, TILE), lambda i, meta: (0, DI // TILE)),
            whole((8, LANES)),
        ]
        + [own_spec] * count
        + [rest_spec if local is None else local_spec] + [rest_spec] * (count - 1)
        + [key_spec] * count + [dt_spec] * count,
        [
            shape_of((tokens, DI), BF), shape_of((tokens, DI), BF),
            shape_of((tokens, TILE), BF), shape_of((tokens, TILE), BF),
            shape_of((GROUPS, tokens, 2 * PER)), shape_of((GROUPS, 2 * PER, tokens)),
            shape_of((3, tokens, LANES)),
        ],
        [
            tile(tokens), tile(tokens), whole((tokens, TILE)), whole((tokens, TILE)),
            whole((GROUPS, tokens, 2 * PER)), whole((GROUPS, 2 * PER, tokens)),
            whole((3, tokens, LANES)),
        ],
        [
            pltpu.VMEM((WIDE, width), BF), pltpu.VMEM((64, width), BF),
            pltpu.VMEM((tokens + 8, WIDE), F32),
        ],
        1 + WIDES, 2 * tokens * width * CC, 24 * MIB,
    )


def lane_half(shape, half):
    ids = lax.broadcasted_iota(jnp.int32, shape, 1)
    return (ids >= HEADDIM) if half else (ids < HEADDIM)


def heads_apart(value):
    blank = jnp.zeros_like(value)
    first = lane_half(value.shape, 0)
    return jnp.concatenate(
        [jnp.where(first, value, blank), jnp.where(first, blank, value)], axis=0
    )


def heads_together(stacked):
    middle = stacked.shape[0] // 2
    upper = stacked[:middle]
    return jnp.where(lane_half(upper.shape, 0), upper, stacked[middle:])


def scan_body(meta, content, keys, columns, rows, skip, out, entering, scores, write_rows, mixes):
    half = SPAN // 2

    @pl.when(pl.program_id(0) == 0)
    def _():
        for span in range(2):
            at = span * SPAN
            scores[span] = dot_nt(keys[at : at + SPAN, DSTATE:], keys[at : at + SPAN, :DSTATE])
        write_rows[...] = keys[0:SPAN, :DSTATE].astype(F32).T
        mixes[...] = jnp.zeros_like(mixes)

    read = keys[SPAN:, DSTATE:].astype(F32)
    growth = jnp.exp(columns[0, SPAN:, :PER])
    for pair in range(PER // 2):
        lanes = slice(pair * 2 * HEADDIM, (pair + 1) * 2 * HEADDIM)
        weights = []
        for h in range(2):
            n = 2 * pair + h
            less = rows[0, PER + n : PER + n + 1, :]
            for span in range(2):
                for at in range(0, SPAN, CHUNK):
                    row = span * SPAN + at
                    corner = at // half * half
                    log = columns[0, row : row + CHUNK, n : n + 1]
                    for begin in range(0, corner + half, half):
                        cut = slice(begin, begin + half)
                        decay = log - less[:, span * SPAN + begin : span * SPAN + begin + half]
                        if begin == corner:
                            causal = row_ids(at - begin, (CHUNK, half)) >= lax.broadcasted_iota(
                                jnp.int32, (CHUNK, half), 1
                            )
                            decay = jnp.where(causal, decay, FAR)
                        mix = scores[span, at : at + CHUNK, cut] * jnp.exp(decay)
                        mixes[pair, span, h * SPAN + at : h * SPAN + at + CHUNK, cut] = mix.astype(BF)
            total = rows[0, n : n + 1, SPAN - 1 : SPAN]
            weights.append((write_rows[...] * jnp.exp(total - less[:, :SPAN])).astype(BF))
        first = content[0:SPAN, lanes]
        second = content[SPAN:, lanes]
        state = heads_together(dot(jnp.concatenate(weights, axis=0), first)).astype(BF)
        entering[0, :, lanes] = state
        readers = [(read * growth[:, 2 * pair + h : 2 * pair + h + 1]).astype(BF) for h in range(2)]
        one = heads_together(dot(mixes[pair, 0], first))
        two = heads_together(
            dot(mixes[pair, 1], second) + dot(jnp.concatenate(readers, axis=0), state)
        )
        out[0:SPAN, lanes] = one + skip[:, lanes] * first.astype(F32)
        out[SPAN:, lanes] = two + skip[:, lanes] * second.astype(F32)


def scan_forward(meta, signal, keys, columns, rows, skip):
    tokens = signal.shape[0]
    return call(
        scan_body, "scan_forward", meta, (signal, keys, columns, rows, skip),
        [
            tiles(tokens, TILE), whole((tokens, TILE)),
            pl.BlockSpec((1, tokens, 2 * PER), lambda i, meta: (i, 0, 0)),
            pl.BlockSpec((1, 2 * PER, tokens), lambda i, meta: (i, 0, 0)),
            tiles(1, TILE),
        ],
        [shape_of((tokens, DI)), shape_of((GROUPS, DSTATE, TILE), BF)],
        [tiles(tokens, TILE), pl.BlockSpec((1, DSTATE, TILE), lambda i, meta: (i, 0, 0))],
        [
            pltpu.VMEM((2, SPAN, SPAN), F32), pltpu.VMEM((DSTATE, SPAN), F32),
            pltpu.VMEM((PER // 2, 2, 2 * SPAN, SPAN), BF),
        ],
        GROUPS, 10 * 10**9, 12 * MIB,
    )


def gate_body(meta, x, mixed, gain, *refs):
    count = UNITS
    own, rest = refs[:count], refs[count : 2 * count]
    gate, normed, theirs, scale, weight, gated, total = refs[2 * count :]
    step = pl.program_id(0)
    tokens = x.shape[0]

    @pl.when(step < WIDES // 2)
    def _():
        gather_lanes(weight, own, meta, TABLE)

    @pl.when(step >= WIDES // 2)
    def _():
        gather_lanes(weight, rest, meta, TABLE + count)

    @pl.when(step == 0)
    def _():
        total[...] = jnp.zeros_like(total)

    here = own_tile(step, meta) * WIDE
    lows = [dot_nt(x[...], weight[at : at + TILE, :]).astype(BF) for at in range(0, WIDE, TILE)]
    for n, low in enumerate(lows):
        lanes = slice(n * TILE, (n + 1) * TILE)
        place = pl.ds(pl.multiple_of(here + n * TILE, TILE), TILE)
        gate[:, lanes] = low
        for at in range(0, tokens, CHUNK):
            part = low[at : at + CHUNK].astype(F32)
            part = mixed[at : at + CHUNK, lanes] * (part * sigmoid(part))
            gated[at : at + CHUNK, place] = part
            square = part * part
            total[at : at + CHUNK, :] += square[:, :LANES] + square[:, LANES:]

    @pl.when(step == pl.num_programs(0) - 1)
    def _():
        mean = jnp.sum(total[...], axis=1, keepdims=True) / DI
        scale[...] = lax.rsqrt(mean + epsilon)

        def finish(g, carry):
            lanes = pl.ds(pl.multiple_of(g * TILE, TILE), TILE)
            for at in range(0, tokens, CHUNK):
                part = gated[at : at + CHUNK, lanes] * scale[at : at + CHUNK, :] * gain[:, lanes]
                normed[at : at + CHUNK, lanes] = part.astype(BF)
            return carry

        lax.fori_loop(0, GROUPS, finish, 0)
        half = DI // (2 * count)
        for k in range(count):
            other = pl.multiple_of((2 * k + 1 - meta[0]) * half, LANES)
            theirs[:, k * half : (k + 1) * half] = normed[:, pl.ds(other, half)]


def gate_forward(meta, x, mixed, gain, own, rest, local):
    tokens, width = x.shape
    count = UNITS
    part = width // count
    half = WIDES // 2
    tile_spec = pl.BlockSpec((tokens, WIDE), lambda i, meta: (0, own_tile(i, meta)))
    own_spec = pl.BlockSpec((WIDE, part), lambda i, meta: (jnp.minimum(i, half - 1), 0))
    rest_spec = pl.BlockSpec((WIDE, part), lambda i, meta: (jnp.maximum(i - half, 0), 0))
    local_spec = pl.BlockSpec(
        (WIDE, part), lambda i, meta: ((1 - meta[0]) * half + jnp.maximum(i - half, 0), 0)
    )
    return call(
        gate_body, "gate_forward", meta,
        (x, mixed, gain) + tuple(own) + (() if local is None else (local,)) + tuple(rest),
        [whole((tokens, width)), tile_spec, whole((1, DI))] + [own_spec] * count
        + [rest_spec if local is None else local_spec] + [rest_spec] * (count - 1),
        [
            shape_of((tokens, DI), BF), shape_of((tokens, DI), BF), shape_of((tokens, DI // 2), BF),
            shape_of((tokens, 1)),
        ],
        [tile_spec, whole((tokens, DI)), whole((tokens, DI // 2)), whole((tokens, 1))],
        [
            pltpu.VMEM((WIDE, width), BF), pltpu.VMEM((tokens, DI), F32),
            pltpu.VMEM((tokens, LANES), F32),
        ],
        WIDES, 2 * tokens * width * DI, 28 * MIB,
    )


STEPS = 4


def out_body(meta, *refs):
    count = UNITS
    normed, gain = refs[0:2], refs[2]
    mixed, gate, pulled, hidden, scale = refs[3:8]
    own, rest = refs[8 : 8 + count], refs[8 + count : 8 + 2 * count]
    block, grad_gate, theirs, grad_mixed, grad_gain = refs[8 + 2 * count : 13 + 2 * count]
    weight, branch, back, total = refs[13 + 2 * count :]
    step = pl.program_id(0)
    tokens = pulled.shape[0]
    half = DI // (2 * count)

    @pl.when(step == 0)
    def _():
        branch[...] = jnp.zeros_like(branch)
        total[...] = jnp.zeros_like(total)

    for j in range(count):
        @pl.when(step == j)
        def _(j=j):
            weight[0:half, :] = own[j][...]
            weight[half:, :] = rest[j][...]

    @pl.when(step < count)
    def _():
        normed_both = jnp.concatenate([normed[0][...], normed[1][...]], axis=1)
        grads = dot_nt(pulled[...], weight[...]).astype(BF)
        branch[...] += dot(normed_both, weight[...])
        for side in range(2):
            at = meta[OUT_TABLE + side * count + step] * half
            place = pl.ds(pl.multiple_of(at, LANES), half)
            back[:, place] = grads[:, side * half : (side + 1) * half]
        for at in range(0, tokens, CHUNK):
            sums = None
            for lane in range(0, 2 * half, LANES):
                one = grads[at : at + CHUNK, lane : lane + LANES].astype(F32)
                one = one * normed_both[at : at + CHUNK, lane : lane + LANES].astype(F32)
                sums = one if sums is None else sums + one
            total[at : at + CHUNK, :] += sums

    @pl.when(step == count - 1)
    def _():
        for at in range(0, tokens, CHUNK):
            part = branch[at : at + CHUNK, :]
            part = jnp.where(live_rows(meta, at, part.shape), part, 0.0)
            block[at : at + CHUNK, :] = (hidden[at : at + CHUNK, :].astype(F32) + part).astype(BF)

    @pl.when(step >= count)
    def _():
        late = step - count
        width = DI // STEPS
        grad_gain[...] = jnp.zeros_like(grad_gain)

        def second(n, carry):
            rows = pl.ds(pl.multiple_of(n * CHUNK, CHUNK), CHUNK)
            r = scale[rows, :]
            mean = jnp.sum(total[rows, :], axis=1, keepdims=True) / DI
            factor = r * r * mean
            for at in range(0, width, LANES):
                cut = slice(at, at + LANES)
                z = gate[rows, cut].astype(F32)
                sigma = sigmoid(z)
                silu = z * sigma
                out = mixed[rows, cut]
                gated = out * silu
                grad = back[rows, pl.ds(pl.multiple_of(late * width + at, LANES), LANES)].astype(F32)
                grad = grad * r
                grad_gain[:, cut] += jnp.sum(grad * gated, axis=0, keepdims=True)
                grad = grad * gain[:, cut] - gated * factor
                grad_mixed[rows, cut] = (grad * silu).astype(BF)
                grad_gate[rows, cut] = ((grad * out) * (sigma + silu * (1.0 - sigma))).astype(BF)
            return carry

        lax.fori_loop(0, tokens // CHUNK, second, 0)

        @pl.when(late // (STEPS // 2) == 1 - meta[0])
        def _():
            theirs[...] = grad_gate[...]


def out_forward(meta, normed, pulled, hidden, mixed, gate, scale, gain, own, rest, local):
    tokens, width = hidden.shape
    count = UNITS
    half = DI // (2 * count)
    step_width = DI // STEPS

    def early(rows, side):
        def index(i, meta):
            return (0, meta[OUT_TABLE + side * count + jnp.minimum(i, count - 1)])

        return pl.BlockSpec((rows, half), index)

    def late(rows):
        return pl.BlockSpec((rows, step_width), lambda i, meta: (0, jnp.maximum(i - count, 0)))

    def local_spec(side):
        return pl.BlockSpec((half, width), lambda i, meta: (meta[0] if side == 0 else 1 - meta[0], 0))

    first = () if local is None else (local,)

    def weight_specs(side):
        one = whole((half, width)) if local is None else local_spec(side)
        return [one] + [whole((half, width))] * (count - 1)

    theirs_spec = pl.BlockSpec(
        (tokens, step_width),
        lambda i, meta: (0, jnp.clip(i - count - (1 - meta[0]) * (STEPS // 2), 0, STEPS // 2 - 1)),
    )
    return call(
        out_body, "out_forward", meta,
        (normed, normed, gain, mixed, gate, pulled, hidden, scale)
        + (first + tuple(own) + first + tuple(rest)),
        [early(tokens, 0), early(tokens, 1), late(1), late(tokens), late(tokens)]
        + [whole((tokens, width))] * 2 + [whole((tokens, 1))]
        + weight_specs(0) + weight_specs(1),
        [
            shape_of((tokens, width), BF), shape_of((tokens, DI), BF),
            shape_of((tokens, DI // 2), BF), shape_of((tokens, DI), BF), shape_of((1, DI)),
        ],
        [whole((tokens, width)), late(tokens), theirs_spec, late(tokens), late(1)],
        [
            pltpu.VMEM((2 * half, width), BF), pltpu.VMEM((tokens, width), F32),
            pltpu.VMEM((tokens, DI), BF), pltpu.VMEM((tokens, LANES), F32),
        ],
        count + STEPS, 4 * tokens * width * DI, 40 * MIB,
    )


def rows_product_body(meta, mine, theirs, pulled, pulled_rest, send, keep):
    total = dot_tn(mine[...], pulled[...]) + dot_tn(theirs[...], pulled_rest[...])
    total = total.astype(BF)
    sent = pl.num_programs(0) // 2

    @pl.when(pl.program_id(0) < sent)
    def _():
        send[0] = total

    @pl.when(pl.program_id(0) >= sent)
    def _():
        keep[0] = total


def rows_product(meta, normed, arrived, arrived_at, pulled, pulled_rest, units):
    tokens, width = pulled.shape
    unit = DI // (2 * UNITS)
    upper = units // 2

    def which(i):
        return lax.rem(i + upper, units)

    result = shape_of((upper, unit, width), BF)
    return call(
        rows_product_body, "rows_product", meta, (normed, arrived, pulled, pulled_rest),
        [
            pl.BlockSpec((tokens, unit), lambda i, meta: (0, meta[OUT_TABLE + which(i)])),
            pl.BlockSpec((tokens, unit), lambda i, meta: (0, meta[arrived_at + which(i)])),
            whole((tokens, width)), whole((tokens, width)),
        ],
        [result, result],
        [
            pl.BlockSpec((1, unit, width), lambda i, meta: (jnp.minimum(i, upper - 1), 0, 0)),
            pl.BlockSpec((1, unit, width), lambda i, meta: (jnp.maximum(i - upper, 0), 0, 0)),
        ],
        [], units, 4 * tokens * width * unit * units, 12 * MIB,
    )


def columns_product_body(plan, meta, *refs):
    parts = len(plan)
    mine, theirs = refs[:parts], refs[parts : 2 * parts]
    here, there, send, keep, right, right_rest = refs[2 * parts :]
    step = pl.program_id(0)
    width = here.shape[1] // UNITS

    @pl.when(step == 0)
    def _():
        for j in range(UNITS):
            lanes = pl.ds(pl.multiple_of(meta[TABLE + j] * width, LANES), width)
            right[:, j * width : (j + 1) * width] = here[:, lanes]
            right_rest[:, j * width : (j + 1) * width] = there[:, lanes]

    for (begin, steps), a, b in zip(plan, mine, theirs):
        @pl.when((step >= begin) & (step < begin + steps))
        def _(a=a, b=b):
            total = (dot_tn(a[...], right[...]) + dot_tn(b[...], right_rest[...])).astype(BF)
            for k in range(UNITS // 2):
                keep[k] = total[:, k * width : (k + 1) * width]
                other = UNITS // 2 + k
                send[k] = total[:, other * width : (other + 1) * width]


def columns_product(meta, parts, normed, normed_rest):
    tokens, width = normed.shape
    part = width // UNITS
    plan, step, mine_specs, theirs_specs = [], 0, [], []

    def spec(begin, steps, start):
        return pl.BlockSpec(
            (tokens, TILE), lambda i, meta: (0, start(meta) + jnp.clip(i - begin, 0, steps - 1))
        )

    for matrix, start, steps, arrived in parts:
        plan.append((step, steps))
        mine_specs.append(spec(step, steps, start))
        theirs_specs.append(spec(step, steps, lambda meta: 0))
        step += steps
    result = shape_of((UNITS // 2, step * TILE, part), BF)
    result_spec = pl.BlockSpec((UNITS // 2, TILE, part), lambda i, meta: (0, i, 0))
    return call(
        functools.partial(columns_product_body, tuple(plan)), "columns_product", meta,
        tuple(p[0] for p in parts) + tuple(p[3] for p in parts) + (normed, normed_rest),
        mine_specs + theirs_specs + [whole((tokens, width))] * 2,
        [result, result], [result_spec, result_spec],
        [pltpu.VMEM((tokens, width), BF), pltpu.VMEM((tokens, width), BF)],
        step, 4 * tokens * step * TILE * width, 12 * MIB,
    )


def conv_back(meta, grad, masked, taps, result, sums, shifted, grad_conv):
    tokens = masked.shape[0]
    shifted[0:8, :] = jnp.zeros((8, TILE), F32)
    shifted[8:, :] = masked[...].astype(F32)
    grad_conv[tokens:, :] = jnp.zeros((8, TILE), F32)
    sums[...] = jnp.zeros_like(sums)
    chunk = CHUNK // 2

    def fold(value):
        return jnp.sum(value.reshape(chunk // 8, 8, TILE), axis=0)

    totals = [jnp.zeros((8, TILE), F32) for _ in range(CONV + 1)]
    for at in range(0, tokens, chunk):
        near = [shifted[at + 5 + k : at + 5 + k + chunk, :] for k in range(CONV)]
        out = taps[4:5, :]
        for k in range(CONV):
            out = out + near[k] * taps[k : k + 1, :]
        sigma = sigmoid(out)
        low = grad[at : at + chunk, :].astype(BF).astype(F32)
        back = low * (sigma + out * sigma * (1.0 - sigma))
        back = jnp.where(live_rows(meta, at, back.shape), back, 0.0)
        grad_conv[at : at + chunk, :] = back
        for k in range(CONV):
            totals[k] = totals[k] + fold(back * near[k])
        totals[CONV] = totals[CONV] + fold(back)
    for k in range(CONV + 1):
        sums[k : k + 1, :] = jnp.sum(totals[k], axis=0, keepdims=True)
    for at in range(0, tokens, chunk):
        out = grad_conv[at + 3 : at + 3 + chunk, :] * taps[0:1, :]
        for k in range(1, CONV):
            out = out + grad_conv[at + 3 - k : at + 3 - k + chunk, :] * taps[k : k + 1, :]
        out = jnp.where(live_rows(meta, at, out.shape), out, 0.0)
        result[at : at + chunk, :] = out.astype(BF)


def scan_back_body(
    meta, content, keys, grad_out, entering, columns, rows, skip, masked, taps,
    scores_in, write_in, read_in,
    result, theirs, sums, grad_columns, grad_rows, grad_scores, grad_write, grad_read,
    scores, read_rows, grad, shifted, grad_conv, mixes, mix_grads,
):
    half = SPAN // 2

    @pl.when(pl.program_id(0) == 0)
    def _():
        for span in range(2):
            at = span * SPAN
            scores[span] = dot_nt(keys[at : at + SPAN, :DSTATE], keys[at : at + SPAN, DSTATE:])
        read_rows[...] = keys[SPAN:, DSTATE:].astype(F32).T
        grad_scores[...] = scores_in[...]
        grad_write[...] = write_in[...]
        grad_read[...] = read_in[...]
        mixes[...] = jnp.zeros_like(mixes)

    final = row_ids(0, (SPAN, 1)) == SPAN - 1
    write = keys[0:SPAN, :DSTATE].astype(F32)
    read = keys[SPAN:, DSTATE:].astype(F32)
    growth = jnp.exp(columns[0, SPAN:, :PER])
    scaled = jnp.exp(columns[0, SPAN - 1 : SPAN, :PER] - columns[0, 0:SPAN, PER:])
    for pair in range(PER // 2):
        lanes = slice(pair * 2 * HEADDIM, (pair + 1) * 2 * HEADDIM)
        pulls = [grad_out[span * SPAN : (span + 1) * SPAN, lanes] for span in range(2)]
        values = [heads_apart(content[span * SPAN : (span + 1) * SPAN, lanes]) for span in range(2)]
        for span in range(2):
            mix_grads[pair, span] = dot_nt(values[span], pulls[span])
        state = entering[0, :, lanes]
        readers = [
            (read_rows[...] * jnp.exp(rows[0, 2 * pair + h : 2 * pair + h + 1, SPAN:])).astype(BF)
            for h in range(2)
        ]
        grad_state = heads_together(dot(jnp.concatenate(readers, axis=0), pulls[1])).astype(BF)
        from_state = dot_nt(heads_apart(pulls[1]), state)
        to_weight = dot_nt(values[0], grad_state)
        weights = []
        extra = []
        for h in range(2):
            n = 2 * pair + h
            grown = from_state[h * SPAN : (h + 1) * SPAN] * growth[:, n : n + 1]
            grad_read[...] += grown
            along = jnp.sum(grown * read, axis=1, keepdims=True)
            grad_columns[0, SPAN:, PER + n : PER + n + 1] = along
            scale = scaled[:, n : n + 1]
            back = to_weight[h * SPAN : (h + 1) * SPAN] * scale
            grad_write[...] += back
            back = back * write
            extra.append(back)
            total = jnp.sum(jnp.sum(back, axis=0, keepdims=True), axis=1, keepdims=True)
            grad_columns[0, 0:SPAN, PER + n : PER + n + 1] = jnp.where(final, total, 0.0)
            weights.append((write * scale).astype(BF))
        from_weight = heads_together(dot(jnp.concatenate(weights, axis=0), grad_state))
        for h in range(2):
            n = 2 * pair + h
            for span in range(2):
                top = span * SPAN
                flows = [jnp.zeros((8, half), F32), jnp.zeros((8, half), F32)]
                for at in range(0, SPAN, CHUNK):
                    less = columns[0, top + at : top + at + CHUNK, PER + n : PER + n + 1]
                    corner = at // half * half
                    across = extra[h][at : at + CHUNK] if span == 0 else None
                    for begin in range(corner, SPAN, half):
                        cut = slice(begin, begin + half)
                        decay = rows[0, n : n + 1, top + begin : top + begin + half] - less
                        if begin == corner:
                            causal = row_ids(at - begin, (CHUNK, half)) <= lax.broadcasted_iota(
                                jnp.int32, (CHUNK, half), 1
                            )
                            decay = jnp.where(causal, decay, FAR)
                        decay = jnp.exp(decay)
                        score = scores[span, at : at + CHUNK, cut]
                        row = h * SPAN + at
                        mixes[pair, span, row : row + CHUNK, cut] = (score * decay).astype(BF)
                        change = mix_grads[pair, span, row : row + CHUNK, cut] * decay
                        grad_scores[span, at : at + CHUNK, cut] += change
                        flow = change * score
                        across = flow if across is None else across + flow
                        flows[begin // half] = flows[begin // half] + jnp.sum(
                            flow.reshape(CHUNK // 8, 8, half), axis=0
                        )
                    along = jnp.sum(across, axis=1, keepdims=True)
                    grad_columns[0, top + at : top + at + CHUNK, n : n + 1] = along
                for k in range(2):
                    begin = top + k * half
                    grad_rows[0, n : n + 1, begin : begin + half] = jnp.sum(
                        flows[k], axis=0, keepdims=True
                    )
        for span in range(2):
            both = heads_together(dot(mixes[pair, span], pulls[span]))
            if span == 0:
                both = both + from_weight
            grad[span * SPAN : (span + 1) * SPAN, lanes] = (
                both + skip[:, lanes] * pulls[span].astype(F32)
            )
    conv_back(meta, grad, masked, taps, result, sums, shifted, grad_conv)
    skips = jnp.zeros((8, TILE), F32)
    for at in range(0, content.shape[0], CHUNK):
        value = content[at : at + CHUNK, :].astype(F32) * grad_out[at : at + CHUNK, :].astype(F32)
        skips = skips + jnp.sum(value.reshape(CHUNK // 8, 8, TILE), axis=0)
    sums[5:6, :] = jnp.sum(skips, axis=0, keepdims=True)

    half_steps = pl.num_programs(0) // 2
    at_half = pl.program_id(0) // half_steps

    @pl.when(at_half == 1 - meta[0])
    def _():
        theirs[...] = result[...]


def scan_backward(
    meta, signal, keys, grad_out, entering, columns, rows, skip, masked, taps, kept, first, count
):
    tokens = signal.shape[0]

    def group(*shape):
        return pl.BlockSpec((1,) + shape, lambda i, meta: (i + first, 0, 0))

    def fresh(*shape):
        return pl.BlockSpec((1,) + shape, lambda i, meta: (i, 0, 0))

    kept_specs = [whole((2, SPAN, SPAN)), whole((SPAN, DSTATE)), whole((SPAN, DSTATE))]
    return call(
        scan_back_body, "scan_backward", meta,
        (signal, keys, grad_out, entering, columns, rows, skip, masked, taps) + tuple(kept),
        [
            tiles(tokens, TILE, first), whole((tokens, TILE)),
            tiles(tokens, TILE, first), group(DSTATE, TILE), group(tokens, 2 * PER),
            group(2 * PER, tokens), tiles(1, TILE, first), tiles(tokens, TILE, first),
            tiles(8, TILE, first),
        ]
        + kept_specs,
        [
            shape_of((tokens, count * TILE), BF), shape_of((tokens, count // 2 * TILE), BF),
            shape_of((8, count * TILE)),
            shape_of((count, tokens, 2 * PER)), shape_of((count, 2 * PER, tokens)),
            shape_of((2, SPAN, SPAN)), shape_of((SPAN, DSTATE)), shape_of((SPAN, DSTATE)),
        ],
        [
            tiles(tokens, TILE),
            pl.BlockSpec(
                (tokens, TILE),
                lambda i, meta: (0, jnp.clip(i - (1 - meta[0]) * (count // 2), 0, count // 2 - 1)),
            ),
            tiles(8, TILE), fresh(tokens, 2 * PER), fresh(2 * PER, tokens),
        ]
        + kept_specs,
        [
            pltpu.VMEM((2, SPAN, SPAN), F32), pltpu.VMEM((DSTATE, SPAN), F32),
            pltpu.VMEM((tokens, TILE), F32), pltpu.VMEM((tokens + 8, TILE), F32),
            pltpu.VMEM((tokens + 8, TILE), F32), pltpu.VMEM((PER // 2, 2, 2 * SPAN, SPAN), BF),
            pltpu.VMEM((PER // 2, 2, 2 * SPAN, SPAN), F32),
        ],
        count, 3 * 10**9 * count, count * MIB,
    )


def tail_body(parts, meta, *refs):
    keys, masked, taps, trio, steps, grad_scores, grad_write, grad_read = refs[:8]
    grad_columns = refs[8 : 8 + parts]
    grad_rows = refs[8 + parts : 8 + 2 * parts]
    result, sums, raw, small, packs, grad, shifted, grad_conv = refs[8 + 2 * parts :]
    tokens = keys.shape[0]
    for span in range(2):
        at = span * SPAN
        write = keys[at : at + SPAN, :DSTATE]
        read = keys[at : at + SPAN, DSTATE:]
        to_write = fine_dot(grad_scores[span], read, dot)
        to_read = fine_dot(grad_scores[span], write, dot_tn)
        if span == 0:
            to_write = to_write + grad_write[...]
        else:
            to_read = to_read + grad_read[...]
        grad[at : at + SPAN, :DSTATE] = to_write
        grad[at : at + SPAN, DSTATE:] = to_read
    conv_back(meta, grad, masked, taps, result, sums, shifted, grad_conv)

    blank = jnp.zeros((tokens, LANES - HEADS), F32)
    of_step, of_log, of_row = [], [], []
    for column_ref, row_ref in zip(grad_columns, grad_rows):
        for g in range(column_ref.shape[0]):
            of_step.append(column_ref[g, :, :PER])
            of_log.append(column_ref[g, :, PER:])
            of_row.append(row_ref[g, :PER, :])
    grad_size = jnp.concatenate(of_step + [blank], axis=1)
    grad_log = jnp.concatenate(of_log + [blank], axis=1) - grad_size
    across = jnp.concatenate(of_row + [jnp.zeros((LANES - HEADS, tokens), F32)], axis=0)
    grad_log = grad_log + across.T
    upper = row_ids(0, (SPAN, SPAN)) <= lax.broadcasted_iota(jnp.int32, (SPAN, SPAN), 1)
    upper = jnp.where(upper, 1.0, 0.0).astype(BF)
    rates = []
    for at in range(0, tokens, SPAN):
        high, middle, low = pieces(grad_log[at : at + SPAN])
        rates.append(dot(upper, high) + (dot(upper, middle) + dot(upper, low)))
    grad_rate = jnp.concatenate(rates, axis=0)
    decay_rate = steps[1:2, :]
    sigma = jax.nn.sigmoid(trio[0])
    size = trio[1]
    tiny = size > 0.0
    share = jnp.where(tiny, sigma / jnp.where(tiny, size, 1.0), 1.0)
    grad_raw = grad_size * share + grad_rate * decay_rate * sigma
    raw[...] = grad_raw.astype(BF)
    small[...] = jnp.zeros_like(small)
    small[0:1, :] = jnp.sum(grad_raw, axis=0, keepdims=True)
    small[1:2, :] = jnp.sum(grad_rate * trio[1], axis=0, keepdims=True) * decay_rate
    for side in range(2):
        at = meta[0] if side == 0 else 1 - meta[0]
        packs[side, :, :LANES] = result[:, pl.ds(pl.multiple_of(at * LANES, LANES), LANES)]
        packs[side, :, LANES:] = raw[...]


def tail_backward(meta, keys, masked, taps, trio, steps, kept, grad_columns, grad_rows):
    tokens = keys.shape[0]
    last = DI // TILE
    key_spec = whole((tokens, TILE))
    return call(
        functools.partial(tail_body, len(grad_columns)), "tail_backward", meta,
        (keys, masked, taps, trio, steps) + tuple(kept) + tuple(grad_columns) + tuple(grad_rows),
        [
            key_spec, key_spec, pl.BlockSpec((8, TILE), lambda i, meta: (0, last)),
            whole((3, tokens, LANES)), whole((8, LANES)), whole((2, SPAN, SPAN)),
            whole((SPAN, DSTATE)), whole((SPAN, DSTATE)),
        ]
        + [whole(part.shape) for part in tuple(grad_columns) + tuple(grad_rows)],
        [
            shape_of((tokens, TILE), BF), shape_of((8, TILE)), shape_of((tokens, LANES), BF),
            shape_of((8, LANES)), shape_of((2, tokens, TILE), BF),
        ],
        [
            whole((tokens, TILE)), whole((8, TILE)), whole((tokens, LANES)), whole((8, LANES)),
            whole((2, tokens, TILE)),
        ],
        [
            pltpu.VMEM((tokens, TILE), F32), pltpu.VMEM((tokens + 8, TILE), F32),
            pltpu.VMEM((tokens + 8, TILE), F32),
        ],
        1, 2 * 10**9, 8 * MIB,
    )


def input_body(plan, first, last, meta, *refs):
    count = UNITS
    grads = refs[: len(plan)]
    refs = refs[len(plan) :]
    if not first:
        start, refs = refs[0], refs[1:]
    blocks = []
    for begin, steps, half in plan:
        own, refs = refs[:count], refs[count:]
        rest = None
        if half is not None:
            rest, refs = refs[:count], refs[count:]
        blocks.append((own, rest))
    step = pl.program_id(0)

    if last:
        hidden, out_grad, scale, gain, result, gain_grad, weight, weight_dt, total = refs
    else:
        total, weight = refs

    @pl.when(step == 0)
    def _():
        total[...] = jnp.zeros_like(total) if first else start[...]

    for n, (begin, steps, half) in enumerate(plan):
        @pl.when((step >= begin) & (step < begin + steps))
        def _(n=n, half=half):
            own, rest = blocks[n]
            rows = own[0].shape[0]
            if grads[n].shape[1] == LANES:
                weight_dt[...] = jnp.zeros_like(weight_dt)
                gather_lanes(weight_dt, own, meta, TABLE)
                total[...] += dot(grads[n][...], weight_dt[...])
                return
            if half is None:
                gather_lanes(weight, own, meta, TABLE)
            else:
                @pl.when(meta[0] == half)
                def _():
                    gather_lanes(weight, own, meta, TABLE)

                @pl.when(meta[0] != half)
                def _():
                    gather_lanes(weight, rest, meta, TABLE + count)

            total[...] += dot(grads[n][...], weight[0:rows, :])

    if not last:
        return

    @pl.when(step == pl.num_programs(0) - 1)
    def _():
        tokens, width = hidden.shape
        gain_grad[...] = jnp.zeros_like(gain_grad)

        def finish(n, carry):
            rows = pl.ds(pl.multiple_of(n * 16, 16), 16)
            r = scale[rows, :]
            value = hidden[rows, :].astype(F32)
            grad = total[rows, :]
            gain_grad[...] += jnp.sum(grad * value * r, axis=0, keepdims=True)
            grad = grad * gain[...]
            mean = jnp.sum(grad * value, axis=1, keepdims=True) / width
            result[rows, :] = r * grad - value * (r * r * r * mean) + out_grad[rows, :].astype(F32)
            return carry

        lax.fori_loop(0, tokens // 16, finish, 0)


def input_backward(meta, start, parts, tokens, width, last=None):
    part = width // UNITS
    plan, step, grad_specs, block_specs, grads, blocks = [], 0, [], [], [], []

    def grad_spec(columns, begin, steps, first):
        return pl.BlockSpec(
            (tokens, columns), lambda i, meta: (0, first + jnp.clip(i - begin, 0, steps - 1))
        )

    def row_spec(rows, begin, steps, first, when):
        def index(i, meta):
            at = first + jnp.clip(i - begin, 0, steps - 1)
            return (at if when is None else jnp.where(when(meta), at, first), 0)

        return pl.BlockSpec((rows, part), index)

    def is_half(half):
        return lambda meta: meta[0] == half

    def not_half(half):
        return lambda meta: meta[0] != half

    for grad, grad_first, steps, half, own, own_first, rest, local_first in parts:
        columns = WIDE if half is not None else grad.shape[1]
        row_tile = 64 if columns == LANES else columns
        plan.append((step, steps, half))
        grads.append(grad)
        grad_specs.append(grad_spec(columns, step, steps, grad_first))
        when = None if half is None else is_half(half)
        for matrix in own:
            blocks.append(matrix)
            block_specs.append(row_spec(row_tile, step, steps, own_first, when))
        if half is not None:
            for j, matrix in enumerate(rest):
                blocks.append(matrix)
                row = local_first if j == 0 else 0
                block_specs.append(row_spec(row_tile, step, steps, row, not_half(half)))
        step += steps
    more, more_specs = (), []
    outs, out_specs = [shape_of((tokens, width))], [whole((tokens, width))]
    scratch = [pltpu.VMEM((WIDE, width), BF)]
    if last is not None:
        more = tuple(last)
        more_specs = [whole((tokens, width))] * 2 + [whole((tokens, 1)), whole((1, width))]
        outs.append(shape_of((1, width)))
        out_specs.append(whole((1, width)))
        scratch += [pltpu.VMEM((LANES, width), BF), pltpu.VMEM((tokens, width), F32)]
    first = start is None
    return call(
        functools.partial(input_body, tuple(plan), first, last is not None),
        "input_backward", meta,
        tuple(grads) + (() if first else (start,)) + tuple(blocks) + more,
        grad_specs + ([] if first else [whole((tokens, width))]) + block_specs + more_specs,
        outs, out_specs, scratch,
        step, 2 * tokens * width * WIDE * step, 20 * MIB,
    )


def mirrored(j, count):
    if count != 4:
        return j
    result, bit, other = 0, 1, count // 2
    while bit < count:
        if j & bit:
            result |= other
        bit, other = bit * 2, other // 2
    return result


def hop(x, bit):
    reps, count = lax.axis_size("rep"), lax.axis_size("shard")
    pairs = []
    for r in range(reps):
        flip = bit if r % 2 == 0 else mirrored(bit, count)
        pairs += [(r * count + s, r * count + (s ^ flip)) for s in range(count)]
    return lax.ppermute(x, ("rep", "shard"), pairs)


def swap(x):
    return lax.ppermute(x, "rep", [(r, r ^ 1) for r in range(lax.axis_size("rep"))])


def across(x, bit):
    return lax.ppermute(x, "shard", [(s, s ^ bit) for s in range(lax.axis_size("shard"))])


def along(x, pairs):
    return lax.ppermute(x, "rep", [(2 * a + k, 2 * b + k) for a, b in pairs for k in range(2)])


def settle(keep, arrived):
    middle = keep.shape[0] // 2
    if middle == 0:
        return None, keep.astype(F32) + arrived.astype(F32)
    held = (keep.astype(F32) + arrived.astype(F32)).astype(BF)
    return held[middle:], held[:middle]


def finish_stages(send, keep):
    while send is not None:
        send, keep = settle(keep, hop(send, send.shape[0]))
    return keep[0]


def inward(held):
    if lax.axis_size("rep") // 2 != 4:
        return held, None
    return held, along(held.astype(BF), [(0, 1), (3, 2)])


def middle(state):
    held, arrived = state
    if arrived is None:
        return held, None
    inner = (held + arrived.astype(F32)).astype(BF)
    return inner, along(inner, [(1, 2), (2, 1)])


def outward(state):
    inner, arrived = state
    if arrived is None:
        chips = lax.axis_size("rep") // 2
        total, bit = inner.astype(BF), 1
        while bit < chips:
            more = along(total, [(k, k ^ bit) for k in range(chips)])
            total = (total.astype(F32) + more.astype(F32)).astype(BF)
            bit *= 2
        return total, None
    total = (inner.astype(F32) + arrived.astype(F32)).astype(BF)
    return total, along(total, [(1, 0), (2, 3)])


def summed(state):
    total, arrived = state
    if arrived is None:
        return total
    place = lax.axis_index("rep") // 2
    return jnp.where((place == 1) | (place == 2), total, arrived)


def in_order(own, other, core):
    return [jnp.where(core == 0, own, other), jnp.where(core == 0, other, own)]


def hold(values):
    leaves, tree = jax.tree.flatten(values)
    return jax.tree.unflatten(tree, lax.optimization_barrier(tuple(leaves)))


def small_sum(vector, shard, count):
    vector = vector + swap(vector)
    rows = jnp.stack([lax.dynamic_index_in_dim(vector, shard ^ j, 0, False) for j in range(count)])
    bit = count // 2
    while bit:
        rows = rows[:bit] + across(rows[bit:], bit)
        bit //= 2
    bit, chips = 1, lax.axis_size("rep") // 2
    while bit < chips:
        rows = rows + along(rows, [(k, k ^ bit) for k in range(chips)])
        bit *= 2
    return rows[0]


def join_lanes(blocks, shard):
    return [
        jnp.concatenate(in_order(blocks[j], blocks[j + 1], shard % 2), axis=1)
        for j in range(0, len(blocks), 2)
    ]


def split_lanes(units, shard):
    half = units.shape[2] // 2
    pairs = in_order(units[:, :, :half], units[:, :, half:], shard % 2)
    return jnp.stack(pairs, axis=1).reshape(2 * units.shape[0], units.shape[1], half)


def pad_lanes(matrix):
    return jnp.pad(matrix, ((0, 0), (0, LANES - matrix.shape[1])))


def shards(
    hidden,
    out_grad,
    norm_gain,
    in_w,
    conv_w,
    conv_b,
    dt_bias,
    a_log,
    skip,
    out_gain,
    out_w,
    lengths,
    offsets,
):
    core = lax.axis_index("rep") % 2
    shard = lax.axis_index("shard")
    count = lax.axis_size("shard")
    tokens, width = hidden.shape
    bits = []
    while 2 ** len(bits) < count:
        bits.append(2 ** len(bits))

    local = in_w.T
    half = DI // 2
    piece = jnp.concatenate(
        [
            lax.dynamic_slice_in_dim(local, DI + core * half, half, 0),
            local[2 * DI :],
            jnp.zeros((16, local.shape[1]), BF),
        ],
        axis=0,
    )
    gate_piece = lax.dynamic_slice_in_dim(local, core * half, half, 0)
    out_piece = lax.dynamic_slice_in_dim(out_w, core * (out_w.shape[0] // 2), out_w.shape[0] // 2, 0)

    def spread(first):
        blocks = [first]
        for bit in bits:
            blocks = blocks + [hop(block, bit) for block in blocks]
        return blocks

    paired = count == 4
    small = (norm_gain, conv_w.T, conv_b, dt_bias, a_log, skip, out_gain)
    packed = jnp.concatenate([part.reshape(-1) for part in small])
    everyone = [packed] + [
        lax.ppermute(
            packed, ("rep", "shard"),
            [
                (r * count + s, r * count + (s ^ (j if r % 2 == 0 else mirrored(j, count))))
                for r in range(lax.axis_size("rep"))
                for s in range(count)
            ],
        )
        for j in range(1, count)
    ]
    piece, everyone = hold((piece, everyone))
    everyone = jnp.stack(everyone).astype(F32)
    order = [jnp.where(core == 0, j, mirrored(j, count)) for j in range(count)]
    whose = jnp.stack(order)[jnp.arange(count) ^ shard]
    same = (whose[:, None] == jnp.arange(count)[None]).astype(F32)
    everyone = jnp.sum(same[:, :, None] * everyone[None], axis=1)
    parts, start = [], 0
    for part in small:
        cut = everyone[:, start : start + part.size].reshape((count,) + part.shape)
        cut = jnp.moveaxis(cut, 0, -2)
        parts.append(cut.reshape(part.shape[:-1] + (-1,)))
        start += part.size
    conv_own = spread(piece)
    gate_piece, conv_own = hold((gate_piece, conv_own))
    if paired:
        conv_rest = [swap(block) for block in conv_own[1:]]
        gate_near = hop(gate_piece, 1), hop(gate_piece, 2)
        out_local, in_local = out_w, local
    else:
        gate_own = spread(gate_piece)
        out_piece, gate_own = hold((out_piece, gate_own))
        out_own = spread(out_piece)
        conv_rest = rest_conv = join_lanes([swap(block) for block in conv_own], shard)
        gate_rest = rest_gate = join_lanes([swap(block) for block in gate_own], shard)
        conv_own, gate_own = join_lanes(conv_own, shard), join_lanes(gate_own, shard)
        out_full = [jnp.concatenate(in_order(block, swap(block), core), axis=0) for block in out_own]
        out_one, out_two = out_full[:UNITS], out_full[UNITS:]
        out_local = in_local = None

    gain_one, kernel, bias_conv, bias_step, log_rate, skip_full, gain_two = parts
    decay_rate = -jnp.exp(log_rate)

    mine = order
    other = [jnp.where(core == 0, mirrored(j, count), j) for j in range(count)]
    mine, other = [shard ^ j for j in mine], [shard ^ j for j in other]
    if paired:
        out_units = [2 * j + core for j in mine] + [2 * j + 1 - core for j in other]
    else:
        out_units = mine
        mine = other = [j // 2 for j in mine[::2]]
    meta = jnp.stack(
        [core, offsets[0], lengths[0], shard] + mine + other + out_units
    ).astype(jnp.int32)
    taps = jnp.concatenate([kernel, bias_conv[None], jnp.zeros((3, CC), F32)], axis=0)
    steps = jnp.concatenate(
        [pad_lanes(jnp.stack([bias_step, decay_rate])), jnp.zeros((6, LANES), F32)], axis=0
    )
    skip_lanes = jnp.repeat(skip_full, HEADDIM)[None]

    positions = jnp.arange(tokens, dtype=jnp.int32)
    live_mask = ((positions >= offsets[0]) & (positions < offsets[0] + lengths[0])).astype(F32)
    hidden_full = hidden.astype(F32)
    inv_rms = lax.rsqrt(jnp.mean(hidden_full * hidden_full, axis=1, keepdims=True) + epsilon)
    normed = (hidden_full * inv_rms * gain_one).astype(BF)
    pulled = (out_grad.astype(F32) * live_mask[:, None]).astype(BF)
    normed_rest = swap(normed)
    pulled_rest = swap(pulled)

    masked, signal, masked_keys, keys, columns, rows, trio = conv_forward(
        meta, normed, taps, steps, conv_own, conv_rest, in_local
    )
    if paired:
        gate_near, signal = hold((gate_near, signal))
        gate_own = [gate_piece, *gate_near, hop(gate_near[0], 2)]
    mixed, entering = scan_forward(meta, signal, keys, columns, rows, skip_lanes)
    if paired:
        out_piece, gate_far, mixed = hold((out_piece, gate_own[3], mixed))
        gate_own[3] = gate_far
        gate_rest = [swap(block) for block in gate_own[1:]]
        rest_conv, rest_gate = [local] + conv_rest, [local] + gate_rest
        out_near = hop(out_piece, 1), hop(out_piece, 2)
    gate, normed_out, out_theirs, scale = gate_forward(
        meta, normed, mixed, gain_two[None], gate_own, gate_rest, in_local
    )
    out_arrived = swap(out_theirs if paired else normed_out)
    if paired:
        out_near, normed_out = hold((out_near, normed_out))
        out_one = [*out_near, hop(out_near[0], 2)]
        out_two = [swap(block) for block in out_one]

    upper = count // 2
    out_pulls = (pulled, pulled_rest)
    if not paired:
        cut = core * (width // 2)
        out_pulls = [lax.dynamic_slice_in_dim(x, cut, width // 2, 1) for x in out_pulls]

    def product(parts):
        send, keep = columns_product(meta, parts, normed, normed_rest)
        return (send, keep) if paired else (split_lanes(send, shard), split_lanes(keep, shard))

    out_send, out_keep = rows_product(
        meta, normed_out, out_arrived, TABLE if paired else OUT_TABLE, *out_pulls, count
    )
    out_send, out_keep, normed_out = hold((out_send, out_keep, normed_out))
    out_there = hop(out_send, upper)
    block_out, grad_gate, gate_theirs, grad_mixed, grad_gain_two = out_forward(
        meta, normed_out, pulled, hidden, mixed, gate, scale, gain_two[None],
        out_one, out_two, out_local,
    )
    out_there, gate_theirs = hold((out_there, gate_theirs))

    gate_arrived = swap(gate_theirs)
    out_send, out_keep = settle(out_keep, out_there)
    gate_parts = [(grad_gate, lambda meta: meta[0] * (GROUPS // 2), GROUPS // 2, gate_arrived)]
    gate_send, gate_keep = product(gate_parts)
    out_send, out_keep, gate_send, gate_keep, grad_mixed = hold(
        (out_send, out_keep, gate_send, gate_keep, grad_mixed)
    )
    out_there = hop(out_send, upper // 2)
    gate_there = hop(gate_send, upper)
    kept = (
        jnp.zeros((2, SPAN, SPAN), F32),
        jnp.zeros((SPAN, DSTATE), F32),
        jnp.zeros((SPAN, DSTATE), F32),
    )
    near = GROUPS // 2
    grad_near, near_theirs, sums_near, columns_near, rows_near, *kept = scan_backward(
        meta, signal, keys, grad_mixed, entering, columns, rows, skip_lanes, masked, taps, kept, 0, near
    )
    out_there, gate_there, near_theirs = hold((out_there, gate_there, near_theirs))
    near_arrived = swap(near_theirs)
    out_line = inward(finish_stages(*settle(out_keep, out_there)))
    gate_send, gate_keep = settle(gate_keep, gate_there)
    near_parts = [(grad_near, lambda meta: meta[0] * (near // 2), near // 2, near_arrived)]
    near_send, near_keep = product(near_parts)
    out_held, gate_send, gate_keep, near_send, near_keep, kept, grad_mixed = hold(
        (out_line[0], gate_send, gate_keep, near_send, near_keep, kept, grad_mixed)
    )
    gate_there = hop(gate_send, upper // 2)
    near_there = hop(near_send, upper)
    grad_far, far_theirs, sums_far, columns_far, rows_far, *kept = scan_backward(
        meta, signal, keys, grad_mixed, entering, columns, rows, skip_lanes, masked, taps, kept, near,
        near,
    )
    gate_there, near_there, out_arrived, far_theirs, kept = hold(
        (gate_there, near_there, out_line[1], far_theirs, kept)
    )
    far_arrived = swap(far_theirs)
    gate_line = inward(finish_stages(*settle(gate_keep, gate_there)))
    out_line = middle((out_held, out_arrived))
    near_send, near_keep = settle(near_keep, near_there)
    near_there = hop(near_send, upper // 2)
    grad_keys, sums_keys, grad_raw, grad_steps, packs = tail_backward(
        meta, keys, masked_keys, taps, trio, steps, kept, (columns_near, columns_far),
        (rows_near, rows_far),
    )
    packs_arrived = swap(packs[1])
    far_parts = [
        (grad_far, lambda meta: meta[0] * (near // 2), near // 2, far_arrived),
        (packs[0], lambda meta: 0, 1, packs_arrived),
    ]
    far_send, far_keep = product(far_parts)
    far_there = hop(far_send, upper)
    part = WIDES // 2
    early, out_inner, gate_held, far_keep, near_keep = hold(
        (grad_gate, out_line[0], gate_line[0], far_keep, near_keep)
    )
    (partial,) = input_backward(
        meta, None,
        [
            (early, 0, part, 0, gate_own, 0, rest_gate, 0),
            (early, part, part, 1, gate_own, 0, rest_gate, part if paired else 0),
        ],
        tokens, width,
    )
    partial, out_arrived, gate_arrived, near_there, far_there = hold(
        (partial, out_line[1], gate_line[1], near_there, far_there)
    )
    far_send, far_keep = settle(far_keep, far_there)
    far_there = hop(far_send, upper // 2)
    gate_line = middle((gate_held, gate_arrived))
    near_line = inward(finish_stages(*settle(near_keep, near_there)))
    out_line = outward((out_inner, out_arrived))
    partial, gate_inner, near_held, far_keep, out_done = hold(
        (partial, gate_line[0], near_line[0], far_keep, out_line[0])
    )
    (partial,) = input_backward(
        meta, partial, [(grad_near, 0, part, 0, conv_own, 0, rest_conv, WIDES if paired else 0)],
        tokens, width,
    )
    partial, gate_arrived, near_arrived, far_there, out_arrived = hold(
        (partial, gate_line[1], near_line[1], far_there, out_line[1])
    )
    far_line = inward(finish_stages(*settle(far_keep, far_there)))
    near_line = middle((near_held, near_arrived))
    gate_line = outward((gate_inner, gate_arrived))
    out_total = summed((out_done, out_arrived))
    out_other = swap(out_total)
    partial, far_held, near_inner, gate_done, out_total = hold(
        (partial, far_line[0], near_line[0], gate_line[0], out_total)
    )
    hidden_grad, grad_gain_one = input_backward(
        meta, partial,
        [
            (grad_far, 0, part, 1, conv_own, 0, rest_conv, WIDES + part if paired else 0),
            (grad_keys, 0, 1, None, conv_own, DI // 2 // TILE, None, 0),
            (grad_raw, 0, 1, None, conv_own, (DI // 2 + TILE) // 64, None, 0),
        ],
        tokens, width, (hidden, out_grad, inv_rms, gain_one[None]),
    )
    grad_gain_one, near_arrived, far_arrived, gate_arrived, out_other = hold(
        (grad_gain_one, near_line[1], far_line[1], gate_line[1], out_other)
    )
    far_line = middle((far_held, far_arrived))
    near_line = outward((near_inner, near_arrived))
    gate_total = summed((gate_done, gate_arrived))
    near_total = summed(near_line)
    far_total = summed(outward(far_line))

    out_w_grad = jnp.concatenate(
        in_order(out_total, out_other, core), axis=0 if paired else 1
    ).astype(F32)
    far = in_order(far_total, swap(far_total), core)
    content, keys = near // 2 * TILE, near // 2 * TILE + LANES
    in_w_grad = jnp.concatenate(
        in_order(gate_total, swap(gate_total), core)
        + in_order(near_total, swap(near_total), core)
        + [far[0][:content], far[1][:content], far[0][content:keys], far[1][content:keys]]
        + [far[0][keys : keys + HEADS]],
        axis=0,
    ).astype(F32).T

    sums = jnp.concatenate([sums_near, sums_far, sums_keys], axis=1)
    grads = (
        grad_gain_one[0].reshape(count, -1),
        sums[:CONV].reshape(CONV, count, -1).transpose(1, 0, 2).reshape(count, -1),
        sums[CONV].reshape(count, -1),
        grad_steps[0, :HEADS].reshape(count, -1),
        grad_steps[1, :HEADS].reshape(count, -1),
        jnp.sum(sums[5, :DI].reshape(HEADS, HEADDIM), axis=1).reshape(count, -1),
        grad_gain_two[0].reshape(count, -1),
    )
    row = small_sum(jnp.concatenate(grads, axis=1), shard, count)
    found, start = [], 0
    for part in grads:
        found.append(row[start : start + part.shape[1]])
        start += part.shape[1]
    return (
        block_out,
        hidden_grad,
        found[0],
        in_w_grad,
        found[1].reshape(CONV, -1).T,
        found[2],
        found[3],
        found[4],
        found[5],
        found[6],
        out_w_grad,
    )


def solution(mesh):
    return jax.shard_map(
        shards,
        mesh=mesh,
        in_specs=(
            P(("rep", "shard"), None),
            P(("rep", "shard"), None),
            P("shard"),
            P("shard", None),
            P("shard", None),
            P("shard"),
            P("shard"),
            P("shard"),
            P("shard"),
            P("shard"),
            P("shard", None),
            P(("rep", "shard")),
            P(("rep", "shard")),
        ),
        out_specs=(
            P(("rep", "shard"), None),
            P(("rep", "shard"), None),
            P("shard"),
            P("shard", None),
            P("shard", None),
            P("shard"),
            P("shard"),
            P("shard"),
            P("shard"),
            P("shard"),
            P("shard", None),
        ),
        check_vma=False,
    )
```

```python
import functools

import jax
import jax.numpy as jnp
from jax import lax
from jax.experimental import pallas as pl
from jax.experimental.pallas import tpu as pltpu
from jax.sharding import PartitionSpec as P

HEADS = 48
HEADDIM = 64
DSTATE = 128
CONV = 4
SPAN = 256
DI = 3072
CC = 3328
TILE = 256
GROUPS = DI // TILE
PER = TILE // HEADDIM
CHUNK = 64
LANES = 128
epsilon = 1e-05
FAR = -1e30
LOG2E = 1.4426950408889634
PACK = 4 * PER

BF = jnp.bfloat16
F32 = jnp.float32
MIB = 1 << 20


def dot(lhs, rhs):
    return jnp.dot(lhs, rhs, preferred_element_type=F32)


def dot_nt(lhs, rhs):
    return lax.dot_general(lhs, rhs, (((1,), (1,)), ((), ())), preferred_element_type=F32)


def dot_tn(lhs, rhs):
    return lax.dot_general(lhs, rhs, (((0,), (0,)), ((), ())), preferred_element_type=F32)


def sigmoid(value):
    return 0.5 * jnp.tanh(0.5 * value) + 0.5


def pieces(value):
    high = value.astype(BF)
    rest = value - high.astype(F32)
    middle = rest.astype(BF)
    low = (rest - middle.astype(F32)).astype(BF)
    return high, middle, low


def fine_dot(lhs, rhs, product):
    high, middle, low = pieces(lhs)
    return product(high, rhs) + (product(middle, rhs) + product(low, rhs))


def row_ids(start, shape):
    return start + lax.broadcasted_iota(jnp.int32, shape, 0)


def live_rows(meta, start, shape):
    ids = row_ids(start, shape)
    return (ids >= meta[1]) & (ids < meta[1] + meta[2])


def gather_lanes(target, blocks, table, at):
    for j, block in enumerate(blocks):
        width = block.shape[1]
        lanes = pl.ds(pl.multiple_of(table[at + j] * width, LANES), width)
        target[0 : block.shape[0], lanes] = block[...]


def call(body, name, meta, operands, in_specs, outs, out_specs, scratch, grid, flops, moved):
    return pl.pallas_call(
        body,
        name=name,
        grid_spec=pltpu.PrefetchScalarGridSpec(
            num_scalar_prefetch=1,
            grid=(grid,),
            in_specs=in_specs,
            out_specs=out_specs,
            scratch_shapes=scratch,
        ),
        out_shape=outs,
        compiler_params=pltpu.CompilerParams(vmem_limit_bytes=60 * MIB),
        cost_estimate=pl.CostEstimate(flops=flops, bytes_accessed=moved, transcendentals=0),
    )(meta, *operands)


def whole(shape):
    rank = len(shape)
    return pl.BlockSpec(shape, lambda i, meta: (0,) * rank)


def tiles(rows, width, shift=0, last=None):
    def index(i, meta):
        at = i + shift
        if last is not None:
            at = jnp.clip(at, 0, last)
        return (0, at)

    return pl.BlockSpec((rows, width), index)


def shape_of(shape, kind=F32):
    return jax.ShapeDtypeStruct(shape, kind)


TABLE = 4
UNITS = 4
OUT_TABLE = TABLE + 2 * UNITS
WIDE = 512
WIDES = DI // WIDE


def own_tile(i, meta):
    half = WIDES // 2
    return jnp.where(i < half, meta[0] * half + i, (1 - meta[0]) * half + i - half)


def live_lanes(meta, live):
    live[...] = jnp.where(live_rows(meta, 0, live.shape), 1.0, 0.0)


def convolve(low, taps, live, shifted, masked, signal, slope, begin):
    for lane in range(0, low.shape[1], LANES):
        cut = slice(begin + lane, begin + lane + LANES)
        for at in range(0, low.shape[0], CHUNK):
            part = low[at : at + CHUNK, lane : lane + LANES].astype(BF).astype(F32)
            part = part * live[at : at + CHUNK, :]
            masked[at : at + CHUNK, cut] = part.astype(BF)
            shifted[8 + at : 8 + at + CHUNK, cut] = part
        for at in range(0, low.shape[0], CHUNK):
            out = taps[4:5, cut]
            for k in range(CONV):
                out = out + shifted[at + 5 + k : at + 5 + k + CHUNK, cut] * taps[k : k + 1, cut]
            sigma = sigmoid(out)
            out = out * sigma
            here = live[at : at + CHUNK, :]
            signal[at : at + CHUNK, cut] = (out * here).astype(BF)
            slope[at : at + CHUNK, cut] = (sigma + out * (1.0 - sigma)) * here


def conv_body(meta, x, taps, taps_keys, steps, *refs):
    count = UNITS
    own, rest, key_rows, dts = (refs[n * count : (n + 1) * count] for n in range(4))
    (masked, signal, slope, masked_keys, keys, slope_keys, columns, rows, trio,
     weight, weight_dt, shifted, live) = refs[4 * count :]
    tokens = x.shape[0]
    step = pl.program_id(0)

    @pl.when(step == 0)
    def _():
        shifted[0:8, :] = jnp.zeros((8, WIDE), F32)
        live_lanes(meta, live)
        gather_lanes(weight, key_rows, meta, TABLE)
        gather_lanes(weight_dt, dts, meta, TABLE)
        low = dot_nt(x[...], weight[0:TILE, :])
        raw = dot_nt(x[...], weight_dt[...]).astype(BF).astype(F32)
        convolve(low, taps_keys, live, shifted, masked_keys, keys, slope_keys, 0)
        raw = jnp.concatenate([raw, jnp.zeros((tokens, LANES - raw.shape[1]), F32)], axis=1)
        pre = raw + steps[0:1, :]
        size = jnp.maximum(pre, 0.0) + jnp.log1p(jnp.exp(-jnp.abs(pre)))
        rate = size * steps[1:2, :]
        lower = row_ids(0, (SPAN, SPAN)) >= lax.broadcasted_iota(jnp.int32, (SPAN, SPAN), 1)
        lower = jnp.where(lower, 1.0, 0.0).astype(BF)
        trio[0] = pre
        trio[1] = size
        for at in range(0, tokens, SPAN):
            high, middle, small = pieces(rate[at : at + SPAN])
            trio[2, at : at + SPAN, :] = dot(lower, high) + (dot(lower, middle) + dot(lower, small))
        log = trio[2] * LOG2E
        less = log - jnp.log(size) * LOG2E
        factor = jnp.concatenate(
            [jnp.exp2(log[SPAN - 1 : SPAN] - less[:SPAN]), jnp.exp2(log[SPAN:])], axis=0
        )
        high = factor.astype(BF).astype(F32)
        rest_factor = factor - high
        less_rows = less.T
        log_rows = log.T
        for g in range(GROUPS):
            a, b = g * PER, (g + 1) * PER
            columns[g] = jnp.concatenate(
                [log[:, a:b], less[:, a:b], high[:, a:b], rest_factor[:, a:b]], axis=1
            )
            rows[g] = jnp.concatenate([log_rows[a:b], less_rows[a:b]], axis=0)

    @pl.when((step > 0) & (step <= WIDES // 2))
    def _():
        gather_lanes(weight, own, meta, TABLE)

    @pl.when(step > WIDES // 2)
    def _():
        gather_lanes(weight, rest, meta, TABLE + count)

    @pl.when(step > 0)
    def _():
        lows = [dot_nt(x[...], weight[at : at + TILE, :]) for at in range(0, WIDE, TILE)]
        for n, low in enumerate(lows):
            convolve(low, taps, live, shifted, masked, signal, slope, n * TILE)


def conv_forward(meta, x, taps, steps, own, rest, local):
    tokens, width = x.shape
    count = UNITS
    part = width // count
    half = WIDES // 2

    def natural(i, meta):
        return own_tile(jnp.maximum(i - 1, 0), meta)

    def tile(rows):
        return pl.BlockSpec((rows, WIDE), lambda i, meta: (0, natural(i, meta)))

    def late(i):
        return jnp.maximum(i - 1 - half, 0)

    own_spec = pl.BlockSpec((WIDE, part), lambda i, meta: (jnp.clip(i - 1, 0, half - 1), 0))
    rest_spec = pl.BlockSpec((WIDE, part), lambda i, meta: (late(i), 0))
    local_spec = pl.BlockSpec(
        (WIDE, part), lambda i, meta: (WIDES + (1 - meta[0]) * half + late(i), 0)
    )
    key_spec = pl.BlockSpec((TILE, part), lambda i, meta: (half * WIDE // TILE, 0))
    dt_spec = pl.BlockSpec((64, part), lambda i, meta: ((half * WIDE + TILE) // 64, 0))
    return call(
        conv_body, "conv_forward", meta,
        (x, taps, taps, steps) + tuple(own) + (() if local is None else (local,)) + tuple(rest)
        + tuple(own) * 2,
        [
            whole((tokens, width)), tile(8), pl.BlockSpec((8, TILE), lambda i, meta: (0, DI // TILE)),
            whole((8, LANES)),
        ]
        + [own_spec] * count
        + [rest_spec if local is None else local_spec] + [rest_spec] * (count - 1)
        + [key_spec] * count + [dt_spec] * count,
        [
            shape_of((tokens, DI), BF), shape_of((tokens, DI), BF), shape_of((tokens, DI)),
            shape_of((tokens, TILE), BF), shape_of((tokens, TILE), BF), shape_of((tokens, TILE)),
            shape_of((GROUPS, tokens, PACK)), shape_of((GROUPS, 2 * PER, tokens)),
            shape_of((3, tokens, LANES)),
        ],
        [
            tile(tokens), tile(tokens), tile(tokens),
            whole((tokens, TILE)), whole((tokens, TILE)), whole((tokens, TILE)),
            whole((GROUPS, tokens, PACK)), whole((GROUPS, 2 * PER, tokens)),
            whole((3, tokens, LANES)),
        ],
        [
            pltpu.VMEM((WIDE, width), BF), pltpu.VMEM((64, width), BF),
            pltpu.VMEM((tokens + 8, WIDE), F32), pltpu.VMEM((tokens, LANES), F32),
        ],
        1 + WIDES, 2 * tokens * width * CC, 24 * MIB,
    )


def lane_half(shape, half):
    ids = lax.broadcasted_iota(jnp.int32, shape, 1)
    return (ids >= HEADDIM) if half else (ids < HEADDIM)


def heads_apart(value):
    blank = jnp.zeros_like(value)
    first = lane_half(value.shape, 0)
    return jnp.concatenate(
        [jnp.where(first, value, blank), jnp.where(first, blank, value)], axis=0
    )


def heads_together(stacked):
    middle = stacked.shape[0] // 2
    upper = stacked[:middle]
    return jnp.where(lane_half(upper.shape, 0), upper, stacked[middle:])


def head_lanes(shape, width):
    lane = lax.broadcasted_iota(jnp.int32, shape, 1) // width
    row = lax.broadcasted_iota(jnp.int32, shape, 0) % PER
    return jnp.where(lane == row, 1.0, 0.0).astype(BF)


def scan_body(
    meta, content, keys, columns, rows, skip, out, entering,
    scores, write_rows, mixes, blocked, spread,
):
    half = SPAN // 2

    @pl.when(pl.program_id(0) == 0)
    def _():
        for span in range(2):
            at = span * SPAN
            scores[span] = dot_nt(keys[at : at + SPAN, DSTATE:], keys[at : at + SPAN, :DSTATE])
        write_rows[...] = keys[0:SPAN, :DSTATE].astype(F32).T.astype(BF)
        mixes[...] = jnp.zeros_like(mixes)
        after = row_ids(0, blocked.shape) >= lax.broadcasted_iota(jnp.int32, blocked.shape, 1)
        blocked[...] = jnp.where(after, 0.0, FAR)
        spread[...] = head_lanes(spread.shape, HEADDIM)

    factor = dot(columns[0, :, 2 * PER :].astype(BF), spread[...])
    first = content[0:SPAN, :].astype(F32)
    state = dot(write_rows[...], (first * factor[:SPAN]).astype(BF)).astype(BF)
    entering[0] = state
    out[0:SPAN, :] = skip[...] * first
    carried = dot(keys[SPAN:, DSTATE:], state) * factor[SPAN:]
    out[SPAN:, :] = carried + skip[...] * content[SPAN:, :].astype(F32)
    for pair in range(PER // 2):
        lanes = slice(pair * 2 * HEADDIM, (pair + 1) * 2 * HEADDIM)
        for h in range(2):
            n = 2 * pair + h
            for span in range(2):
                for at in range(0, SPAN, CHUNK):
                    row = span * SPAN + at
                    corner = at // half * half
                    log = columns[0, row : row + CHUNK, n : n + 1]
                    for begin in range(0, corner + half, half):
                        cut = slice(begin, begin + half)
                        less = rows[0, PER + n : PER + n + 1, span * SPAN + begin : span * SPAN + begin + half]
                        decay = log - less
                        if begin == corner:
                            decay = decay + blocked[at - begin : at - begin + CHUNK, :]
                        mix = scores[span, at : at + CHUNK, cut] * jnp.exp2(decay)
                        mixes[pair, span, h * SPAN + at : h * SPAN + at + CHUNK, cut] = mix.astype(BF)
        for span in range(2):
            at = span * SPAN
            value = content[at : at + SPAN, lanes]
            out[at : at + SPAN, lanes] += heads_together(dot(mixes[pair, span], value))


def scan_forward(meta, signal, keys, columns, rows, skip):
    tokens = signal.shape[0]
    return call(
        scan_body, "scan_forward", meta, (signal, keys, columns, rows, skip),
        [
            tiles(tokens, TILE), whole((tokens, TILE)),
            pl.BlockSpec((1, tokens, PACK), lambda i, meta: (i, 0, 0)),
            pl.BlockSpec((1, 2 * PER, tokens), lambda i, meta: (i, 0, 0)),
            tiles(1, TILE),
        ],
        [shape_of((tokens, DI)), shape_of((GROUPS, DSTATE, TILE), BF)],
        [tiles(tokens, TILE), pl.BlockSpec((1, DSTATE, TILE), lambda i, meta: (i, 0, 0))],
        [
            pltpu.VMEM((2, SPAN, SPAN), F32), pltpu.VMEM((DSTATE, SPAN), BF),
            pltpu.VMEM((PER // 2, 2, 2 * SPAN, SPAN), BF), pltpu.VMEM((SPAN // 2, SPAN // 2), F32),
            pltpu.VMEM((2 * PER, TILE), BF),
        ],
        GROUPS, 10 * 10**9, 12 * MIB,
    )


def gate_body(meta, x, mixed, gain, *refs):
    count = UNITS
    own, rest = refs[:count], refs[count : 2 * count]
    gate, normed, theirs, scale, weight, gated, total = refs[2 * count :]
    step = pl.program_id(0)
    tokens = x.shape[0]

    @pl.when(step < WIDES // 2)
    def _():
        gather_lanes(weight, own, meta, TABLE)

    @pl.when(step >= WIDES // 2)
    def _():
        gather_lanes(weight, rest, meta, TABLE + count)

    @pl.when(step == 0)
    def _():
        total[...] = jnp.zeros_like(total)

    here = own_tile(step, meta) * WIDE
    lows = [dot_nt(x[...], weight[at : at + TILE, :]).astype(BF) for at in range(0, WIDE, TILE)]
    for n, low in enumerate(lows):
        lanes = slice(n * TILE, (n + 1) * TILE)
        place = pl.ds(pl.multiple_of(here + n * TILE, TILE), TILE)
        gate[:, lanes] = low
        for at in range(0, tokens, CHUNK):
            part = low[at : at + CHUNK].astype(F32)
            part = mixed[at : at + CHUNK, lanes] * (part * sigmoid(part))
            gated[at : at + CHUNK, place] = part
            square = part * part
            total[at : at + CHUNK, :] += square[:, :LANES] + square[:, LANES:]

    @pl.when(step == pl.num_programs(0) - 1)
    def _():
        mean = jnp.sum(total[...], axis=1, keepdims=True) / DI
        scale[...] = lax.rsqrt(mean + epsilon)

        def finish(n, carry):
            place = pl.ds(pl.multiple_of(n * CHUNK, CHUNK), CHUNK)
            factor = jnp.broadcast_to(scale[place, :], (CHUNK, LANES))
            for at in range(0, DI, LANES):
                part = gated[place, at : at + LANES] * factor * gain[:, at : at + LANES]
                normed[place, at : at + LANES] = part.astype(BF)
            return carry

        lax.fori_loop(0, tokens // CHUNK, finish, 0)
        half = DI // (2 * count)
        for k in range(count):
            other = pl.multiple_of((2 * k + 1 - meta[0]) * half, LANES)
            theirs[:, k * half : (k + 1) * half] = normed[:, pl.ds(other, half)]


def gate_forward(meta, x, mixed, gain, own, rest, local):
    tokens, width = x.shape
    count = UNITS
    part = width // count
    half = WIDES // 2
    tile_spec = pl.BlockSpec((tokens, WIDE), lambda i, meta: (0, own_tile(i, meta)))
    own_spec = pl.BlockSpec((WIDE, part), lambda i, meta: (jnp.minimum(i, half - 1), 0))
    rest_spec = pl.BlockSpec((WIDE, part), lambda i, meta: (jnp.maximum(i - half, 0), 0))
    local_spec = pl.BlockSpec(
        (WIDE, part), lambda i, meta: ((1 - meta[0]) * half + jnp.maximum(i - half, 0), 0)
    )
    return call(
        gate_body, "gate_forward", meta,
        (x, mixed, gain) + tuple(own) + (() if local is None else (local,)) + tuple(rest),
        [whole((tokens, width)), tile_spec, whole((1, DI))] + [own_spec] * count
        + [rest_spec if local is None else local_spec] + [rest_spec] * (count - 1),
        [
            shape_of((tokens, DI), BF), shape_of((tokens, DI), BF), shape_of((tokens, DI // 2), BF),
            shape_of((tokens, 1)),
        ],
        [tile_spec, whole((tokens, DI)), whole((tokens, DI // 2)), whole((tokens, 1))],
        [
            pltpu.VMEM((WIDE, width), BF), pltpu.VMEM((tokens, DI), F32),
            pltpu.VMEM((tokens, LANES), F32),
        ],
        WIDES, 2 * tokens * width * DI, 28 * MIB,
    )


STEPS = 4


def out_body(meta, *refs):
    count = UNITS
    normed, gain = refs[0:2], refs[2]
    mixed, gate, pulled, hidden, scale = refs[3:8]
    own, rest = refs[8 : 8 + count], refs[8 + count : 8 + 2 * count]
    block, grad_gate, theirs, grad_mixed, grad_gain = refs[8 + 2 * count : 13 + 2 * count]
    weight, branch, back, total = refs[13 + 2 * count :]
    step = pl.program_id(0)
    tokens = pulled.shape[0]
    half = DI // (2 * count)

    @pl.when(step == 0)
    def _():
        branch[...] = jnp.zeros_like(branch)
        total[...] = jnp.zeros_like(total)

    for j in range(count):
        @pl.when(step == j)
        def _(j=j):
            weight[0:half, :] = own[j][...]
            weight[half:, :] = rest[j][...]

    @pl.when(step < count)
    def _():
        normed_both = jnp.concatenate([normed[0][...], normed[1][...]], axis=1)
        grads = dot_nt(pulled[...], weight[...]).astype(BF)
        branch[...] += dot(normed_both, weight[...])
        for side in range(2):
            at = meta[OUT_TABLE + side * count + step] * half
            place = pl.ds(pl.multiple_of(at, LANES), half)
            back[:, place] = grads[:, side * half : (side + 1) * half]
        for at in range(0, tokens, CHUNK):
            sums = None
            for lane in range(0, 2 * half, LANES):
                one = grads[at : at + CHUNK, lane : lane + LANES].astype(F32)
                one = one * normed_both[at : at + CHUNK, lane : lane + LANES].astype(F32)
                sums = one if sums is None else sums + one
            total[at : at + CHUNK, :] += sums

    @pl.when(step == count - 1)
    def _():
        for at in range(0, tokens, CHUNK):
            part = branch[at : at + CHUNK, :]
            part = jnp.where(live_rows(meta, at, part.shape), part, 0.0)
            block[at : at + CHUNK, :] = (hidden[at : at + CHUNK, :].astype(F32) + part).astype(BF)

    @pl.when(step >= count)
    def _():
        late = step - count
        width = DI // STEPS
        grad_gain[...] = jnp.zeros_like(grad_gain)

        def second(n, carry):
            rows = pl.ds(pl.multiple_of(n * CHUNK, CHUNK), CHUNK)
            r = jnp.broadcast_to(scale[rows, :], (CHUNK, LANES))
            mean = jnp.sum(total[rows, :], axis=1, keepdims=True) / DI
            factor = r * r * mean
            for at in range(0, width, LANES):
                cut = slice(at, at + LANES)
                z = gate[rows, cut].astype(F32)
                sigma = sigmoid(z)
                silu = z * sigma
                out = mixed[rows, cut]
                gated = out * silu
                grad = back[rows, pl.ds(pl.multiple_of(late * width + at, LANES), LANES)].astype(F32)
                grad = grad * r
                grad_gain[:, cut] += jnp.sum(grad * gated, axis=0, keepdims=True)
                grad = grad * gain[:, cut] - gated * factor
                grad_mixed[rows, cut] = (grad * silu).astype(BF)
                grad_gate[rows, cut] = ((grad * out) * (sigma + silu * (1.0 - sigma))).astype(BF)
            return carry

        lax.fori_loop(0, tokens // CHUNK, second, 0)

        @pl.when(late // (STEPS // 2) == 1 - meta[0])
        def _():
            theirs[...] = grad_gate[...]


def out_forward(meta, normed, pulled, hidden, mixed, gate, scale, gain, own, rest, local):
    tokens, width = hidden.shape
    count = UNITS
    half = DI // (2 * count)
    step_width = DI // STEPS

    def early(rows, side):
        def index(i, meta):
            return (0, meta[OUT_TABLE + side * count + jnp.minimum(i, count - 1)])

        return pl.BlockSpec((rows, half), index)

    def late(rows):
        return pl.BlockSpec((rows, step_width), lambda i, meta: (0, jnp.maximum(i - count, 0)))

    def local_spec(side):
        return pl.BlockSpec((half, width), lambda i, meta: (meta[0] if side == 0 else 1 - meta[0], 0))

    first = () if local is None else (local,)

    def weight_specs(side):
        one = whole((half, width)) if local is None else local_spec(side)
        return [one] + [whole((half, width))] * (count - 1)

    theirs_spec = pl.BlockSpec(
        (tokens, step_width),
        lambda i, meta: (0, jnp.clip(i - count - (1 - meta[0]) * (STEPS // 2), 0, STEPS // 2 - 1)),
    )
    return call(
        out_body, "out_forward", meta,
        (normed, normed, gain, mixed, gate, pulled, hidden, scale)
        + (first + tuple(own) + first + tuple(rest)),
        [early(tokens, 0), early(tokens, 1), late(1), late(tokens), late(tokens)]
        + [whole((tokens, width))] * 2 + [whole((tokens, 1))]
        + weight_specs(0) + weight_specs(1),
        [
            shape_of((tokens, width), BF), shape_of((tokens, DI), BF),
            shape_of((tokens, DI // 2), BF), shape_of((tokens, DI), BF), shape_of((1, DI)),
        ],
        [whole((tokens, width)), late(tokens), theirs_spec, late(tokens), late(1)],
        [
            pltpu.VMEM((2 * half, width), BF), pltpu.VMEM((tokens, width), F32),
            pltpu.VMEM((tokens, DI), BF), pltpu.VMEM((tokens, LANES), F32),
        ],
        count + STEPS, 4 * tokens * width * DI, 40 * MIB,
    )


def rows_product_body(meta, mine, theirs, pulled, pulled_rest, send, keep):
    total = dot_tn(mine[...], pulled[...]) + dot_tn(theirs[...], pulled_rest[...])
    total = total.astype(BF)
    sent = pl.num_programs(0) // 2

    @pl.when(pl.program_id(0) < sent)
    def _():
        send[0] = total

    @pl.when(pl.program_id(0) >= sent)
    def _():
        keep[0] = total


def rows_product(meta, normed, arrived, arrived_at, pulled, pulled_rest, units):
    tokens, width = pulled.shape
    unit = DI // (2 * UNITS)
    upper = units // 2

    def which(i):
        return lax.rem(i + upper, units)

    result = shape_of((upper, unit, width), BF)
    return call(
        rows_product_body, "rows_product", meta, (normed, arrived, pulled, pulled_rest),
        [
            pl.BlockSpec((tokens, unit), lambda i, meta: (0, meta[OUT_TABLE + which(i)])),
            pl.BlockSpec((tokens, unit), lambda i, meta: (0, meta[arrived_at + which(i)])),
            whole((tokens, width)), whole((tokens, width)),
        ],
        [result, result],
        [
            pl.BlockSpec((1, unit, width), lambda i, meta: (jnp.minimum(i, upper - 1), 0, 0)),
            pl.BlockSpec((1, unit, width), lambda i, meta: (jnp.maximum(i - upper, 0), 0, 0)),
        ],
        [], units, 4 * tokens * width * unit * units, 12 * MIB,
    )


def columns_product_body(plan, meta, *refs):
    parts = len(plan)
    mine, theirs = refs[:parts], refs[parts : 2 * parts]
    here, there, send, keep, right, right_rest = refs[2 * parts :]
    step = pl.program_id(0)
    width = here.shape[1] // UNITS

    @pl.when(step == 0)
    def _():
        for j in range(UNITS):
            lanes = pl.ds(pl.multiple_of(meta[TABLE + j] * width, LANES), width)
            right[:, j * width : (j + 1) * width] = here[:, lanes]
            right_rest[:, j * width : (j + 1) * width] = there[:, lanes]

    for (begin, steps), a, b in zip(plan, mine, theirs):
        @pl.when((step >= begin) & (step < begin + steps))
        def _(a=a, b=b):
            total = (dot_tn(a[...], right[...]) + dot_tn(b[...], right_rest[...])).astype(BF)
            for k in range(UNITS // 2):
                keep[k] = total[:, k * width : (k + 1) * width]
                other = UNITS // 2 + k
                send[k] = total[:, other * width : (other + 1) * width]


def columns_product(meta, parts, normed, normed_rest):
    tokens, width = normed.shape
    part = width // UNITS
    plan, step, mine_specs, theirs_specs = [], 0, [], []

    def spec(begin, steps, start):
        return pl.BlockSpec(
            (tokens, TILE), lambda i, meta: (0, start(meta) + jnp.clip(i - begin, 0, steps - 1))
        )

    for matrix, start, steps, arrived in parts:
        plan.append((step, steps))
        mine_specs.append(spec(step, steps, start))
        theirs_specs.append(spec(step, steps, lambda meta: 0))
        step += steps
    result = shape_of((UNITS // 2, step * TILE, part), BF)
    result_spec = pl.BlockSpec((UNITS // 2, TILE, part), lambda i, meta: (0, i, 0))
    return call(
        functools.partial(columns_product_body, tuple(plan)), "columns_product", meta,
        tuple(p[0] for p in parts) + tuple(p[3] for p in parts) + (normed, normed_rest),
        mine_specs + theirs_specs + [whole((tokens, width))] * 2,
        [result, result], [result_spec, result_spec],
        [pltpu.VMEM((tokens, width), BF), pltpu.VMEM((tokens, width), BF)],
        step, 4 * tokens * step * TILE * width, 12 * MIB,
    )


def conv_back(meta, masked, taps, result, sums, live, grad_conv):
    tokens = masked.shape[0]
    grad_conv[tokens:, :] = jnp.zeros((8, TILE), F32)
    sums[...] = jnp.zeros_like(sums)
    for lane in range(0, TILE, LANES):
        cut = slice(lane, lane + LANES)
        totals = [jnp.zeros((8, LANES), F32) for _ in range(CONV + 1)]
        for at in range(0, tokens, CHUNK):
            near = [grad_conv[at + 3 - k : at + 3 - k + CHUNK, cut] for k in range(CONV)]
            value = masked[at : at + CHUNK, cut].astype(F32)
            out = near[0] * taps[0:1, cut]
            for k in range(1, CONV):
                out = out + near[k] * taps[k : k + 1, cut]
            result[at : at + CHUNK, cut] = (out * live[at : at + CHUNK, :]).astype(BF)
            for k in range(CONV):
                totals[k] = totals[k] + fold(near[k] * value)
            totals[CONV] = totals[CONV] + fold(near[CONV - 1])
        for k in range(CONV + 1):
            sums[k : k + 1, cut] = jnp.sum(totals[k], axis=0, keepdims=True)


def fold(value):
    return jnp.sum(value.reshape(value.shape[0] // 8, 8, value.shape[1]), axis=0)


def scan_back_body(
    meta, content, keys, grad_out, entering, columns, rows, skip, masked, slope, taps,
    scores_in, write_in, read_in,
    result, theirs, sums, grad_columns, grad_rows, grad_scores, grad_write, grad_read,
    scores, read_rows, live, grad_conv, mixes, mix_grads, blocked, spread,
):
    half = SPAN // 2

    @pl.when(pl.program_id(0) == 0)
    def _():
        for span in range(2):
            at = span * SPAN
            scores[span] = dot_nt(keys[at : at + SPAN, :DSTATE], keys[at : at + SPAN, DSTATE:])
        read_rows[...] = keys[SPAN:, DSTATE:].astype(F32).T.astype(BF)
        grad_scores[...] = scores_in[...]
        grad_write[...] = write_in[...]
        grad_read[...] = read_in[...]
        mixes[...] = jnp.zeros_like(mixes)
        live_lanes(meta, live)
        after = row_ids(0, blocked.shape) <= lax.broadcasted_iota(jnp.int32, blocked.shape, 1)
        blocked[...] = jnp.where(after, 0.0, FAR)
        spread[...] = head_lanes(spread.shape, HEADDIM)

    for pair in range(PER // 2):
        lanes = slice(pair * 2 * HEADDIM, (pair + 1) * 2 * HEADDIM)
        for span in range(2):
            cut = slice(span * SPAN, (span + 1) * SPAN)
            mix_grads[pair, span] = dot_nt(heads_apart(content[cut, lanes]), grad_out[cut, lanes])

    factor = dot(columns[0, :, 2 * PER :].astype(BF), spread[...])
    state = entering[0]
    pull = grad_out[SPAN:, :].astype(F32)
    grown = (pull * factor[SPAN:]).astype(BF)
    grad_state = dot(read_rows[...], grown).astype(BF)
    grad_read[...] += dot_nt(grown, state)
    carried = dot(keys[SPAN:, DSTATE:], state) * factor[SPAN:]
    of_read = dot_nt((pull * carried).astype(BF), spread[...])
    value = content[0:SPAN, :].astype(F32)
    grad_write[...] += dot_nt((value * factor[:SPAN]).astype(BF), grad_state)
    from_state = dot(keys[0:SPAN, :DSTATE], grad_state) * factor[:SPAN]
    of_write = dot_nt((value * from_state).astype(BF), spread[...])
    skips = fold(pull * content[SPAN:, :].astype(F32))
    grad_conv[SPAN : 2 * SPAN, :] = skip[...] * pull
    pull = grad_out[0:SPAN, :].astype(F32)
    skips = skips + fold(pull * value)
    grad_conv[0:SPAN, :] = skip[...] * pull + from_state

    for pair in range(PER // 2):
        lanes = slice(pair * 2 * HEADDIM, (pair + 1) * 2 * HEADDIM)
        for h in range(2):
            n = 2 * pair + h
            for span in range(2):
                top = span * SPAN
                flows = [jnp.zeros((8, half), F32), jnp.zeros((8, half), F32)]
                for at in range(0, SPAN, CHUNK):
                    less = columns[0, top + at : top + at + CHUNK, PER + n : PER + n + 1]
                    corner = at // half * half
                    across = None
                    for begin in range(corner, SPAN, half):
                        cut = slice(begin, begin + half)
                        decay = rows[0, n : n + 1, top + begin : top + begin + half] - less
                        if begin == corner:
                            decay = decay + blocked[at - begin : at - begin + CHUNK, :]
                        decay = jnp.exp2(decay)
                        score = scores[span, at : at + CHUNK, cut]
                        row = h * SPAN + at
                        mixes[pair, span, row : row + CHUNK, cut] = (score * decay).astype(BF)
                        change = mix_grads[pair, span, row : row + CHUNK, cut] * decay
                        grad_scores[span, at : at + CHUNK, cut] += change
                        flow = change * score
                        across = flow if across is None else across + flow
                        flows[begin // half] = flows[begin // half] + fold(flow)
                    along = jnp.sum(across, axis=1, keepdims=True)
                    grad_columns[0, top + at : top + at + CHUNK, n : n + 1] = along
                for k in range(2):
                    begin = top + k * half
                    grad_rows[0, n : n + 1, begin : begin + half] = jnp.sum(
                        flows[k], axis=0, keepdims=True
                    )
        for span in range(2):
            cut = slice(span * SPAN, (span + 1) * SPAN)
            both = heads_together(dot(mixes[pair, span], grad_out[cut, lanes]))
            grad_conv[cut, lanes] = (grad_conv[cut, lanes] + both) * slope[cut, lanes]

    lane = lax.broadcasted_iota(jnp.int32, of_write.shape, 1) < PER
    final = row_ids(0, of_write.shape) == SPAN - 1
    ended = jnp.where(final, jnp.sum(of_write, axis=0, keepdims=True), 0.0)
    grad_columns[0, 0:SPAN, :] = jnp.where(lane, grad_columns[0, 0:SPAN, :] + of_write, ended)
    grad_columns[0, SPAN:, :] = jnp.where(lane, grad_columns[0, SPAN:, :], of_read)

    conv_back(meta, masked, taps, result, sums, live, grad_conv)
    sums[5:6, :] = jnp.sum(skips, axis=0, keepdims=True)
    half_steps = pl.num_programs(0) // 2
    at_half = pl.program_id(0) // half_steps

    @pl.when(at_half == 1 - meta[0])
    def _():
        theirs[...] = result[...]


def scan_backward(
    meta, signal, keys, grad_out, entering, columns, rows, skip, masked, slope, taps, kept, first, count
):
    tokens = signal.shape[0]

    def group(*shape):
        return pl.BlockSpec((1,) + shape, lambda i, meta: (i + first, 0, 0))

    def fresh(*shape):
        return pl.BlockSpec((1,) + shape, lambda i, meta: (i, 0, 0))

    kept_specs = [whole((2, SPAN, SPAN)), whole((SPAN, DSTATE)), whole((SPAN, DSTATE))]
    return call(
        scan_back_body, "scan_backward", meta,
        (signal, keys, grad_out, entering, columns, rows, skip, masked, slope, taps) + tuple(kept),
        [
            tiles(tokens, TILE, first), whole((tokens, TILE)),
            tiles(tokens, TILE, first), group(DSTATE, TILE), group(tokens, PACK),
            group(2 * PER, tokens), tiles(1, TILE, first), tiles(tokens, TILE, first),
            tiles(tokens, TILE, first), tiles(8, TILE, first),
        ]
        + kept_specs,
        [
            shape_of((tokens, count * TILE), BF), shape_of((tokens, count // 2 * TILE), BF),
            shape_of((8, count * TILE)),
            shape_of((count, tokens, 2 * PER)), shape_of((count, 2 * PER, tokens)),
            shape_of((2, SPAN, SPAN)), shape_of((SPAN, DSTATE)), shape_of((SPAN, DSTATE)),
        ],
        [
            tiles(tokens, TILE),
            pl.BlockSpec(
                (tokens, TILE),
                lambda i, meta: (0, jnp.clip(i - (1 - meta[0]) * (count // 2), 0, count // 2 - 1)),
            ),
            tiles(8, TILE), fresh(tokens, 2 * PER), fresh(2 * PER, tokens),
        ]
        + kept_specs,
        [
            pltpu.VMEM((2, SPAN, SPAN), F32), pltpu.VMEM((DSTATE, SPAN), BF),
            pltpu.VMEM((tokens, LANES), F32), pltpu.VMEM((tokens + 8, TILE), F32),
            pltpu.VMEM((PER // 2, 2, 2 * SPAN, SPAN), BF),
            pltpu.VMEM((PER // 2, 2, 2 * SPAN, SPAN), F32),
            pltpu.VMEM((SPAN // 2, SPAN // 2), F32), pltpu.VMEM((2 * PER, TILE), BF),
        ],
        count, 3 * 10**9 * count, count * MIB,
    )


def tail_body(parts, meta, *refs):
    keys, masked, slope, taps, trio, steps, grad_scores, grad_write, grad_read = refs[:9]
    grad_columns = refs[9 : 9 + parts]
    grad_rows = refs[9 + parts : 9 + 2 * parts]
    result, sums, raw, small, packs, live, grad_conv = refs[9 + 2 * parts :]
    tokens = keys.shape[0]
    for span in range(2):
        at = span * SPAN
        write = keys[at : at + SPAN, :DSTATE]
        read = keys[at : at + SPAN, DSTATE:]
        to_write = fine_dot(grad_scores[span], read, dot)
        to_read = fine_dot(grad_scores[span], write, dot_tn)
        if span == 0:
            to_write = to_write + grad_write[...]
        else:
            to_read = to_read + grad_read[...]
        cut = slice(at, at + SPAN)
        grad_conv[cut, :DSTATE] = to_write * slope[cut, :DSTATE]
        grad_conv[cut, DSTATE:] = to_read * slope[cut, DSTATE:]
    live_lanes(meta, live)
    conv_back(meta, masked, taps, result, sums, live, grad_conv)

    blank = jnp.zeros((tokens, LANES - HEADS), F32)
    of_step, of_log, of_row = [], [], []
    for column_ref, row_ref in zip(grad_columns, grad_rows):
        for g in range(column_ref.shape[0]):
            of_step.append(column_ref[g, :, :PER])
            of_log.append(column_ref[g, :, PER:])
            of_row.append(row_ref[g, :PER, :])
    grad_size = jnp.concatenate(of_step + [blank], axis=1)
    grad_log = jnp.concatenate(of_log + [blank], axis=1) - grad_size
    across = jnp.concatenate(of_row + [jnp.zeros((LANES - HEADS, tokens), F32)], axis=0)
    grad_log = grad_log + across.T
    upper = row_ids(0, (SPAN, SPAN)) <= lax.broadcasted_iota(jnp.int32, (SPAN, SPAN), 1)
    upper = jnp.where(upper, 1.0, 0.0).astype(BF)
    rates = []
    for at in range(0, tokens, SPAN):
        high, middle, low = pieces(grad_log[at : at + SPAN])
        rates.append(dot(upper, high) + (dot(upper, middle) + dot(upper, low)))
    grad_rate = jnp.concatenate(rates, axis=0)
    decay_rate = steps[1:2, :]
    sigma = jax.nn.sigmoid(trio[0])
    size = trio[1]
    tiny = size > 0.0
    share = jnp.where(tiny, sigma / jnp.where(tiny, size, 1.0), 1.0)
    grad_raw = grad_size * share + grad_rate * decay_rate * sigma
    raw[...] = grad_raw.astype(BF)
    small[...] = jnp.zeros_like(small)
    small[0:1, :] = jnp.sum(grad_raw, axis=0, keepdims=True)
    small[1:2, :] = jnp.sum(grad_rate * trio[1], axis=0, keepdims=True) * decay_rate
    for side in range(2):
        at = meta[0] if side == 0 else 1 - meta[0]
        packs[side, :, :LANES] = result[:, pl.ds(pl.multiple_of(at * LANES, LANES), LANES)]
        packs[side, :, LANES:] = raw[...]


def tail_backward(meta, keys, masked, slope, taps, trio, steps, kept, grad_columns, grad_rows):
    tokens = keys.shape[0]
    last = DI // TILE
    key_spec = whole((tokens, TILE))
    return call(
        functools.partial(tail_body, len(grad_columns)), "tail_backward", meta,
        (keys, masked, slope, taps, trio, steps) + tuple(kept) + tuple(grad_columns) + tuple(grad_rows),
        [
            key_spec, key_spec, key_spec, pl.BlockSpec((8, TILE), lambda i, meta: (0, last)),
            whole((3, tokens, LANES)), whole((8, LANES)), whole((2, SPAN, SPAN)),
            whole((SPAN, DSTATE)), whole((SPAN, DSTATE)),
        ]
        + [whole(part.shape) for part in tuple(grad_columns) + tuple(grad_rows)],
        [
            shape_of((tokens, TILE), BF), shape_of((8, TILE)), shape_of((tokens, LANES), BF),
            shape_of((8, LANES)), shape_of((2, tokens, TILE), BF),
        ],
        [
            whole((tokens, TILE)), whole((8, TILE)), whole((tokens, LANES)), whole((8, LANES)),
            whole((2, tokens, TILE)),
        ],
        [pltpu.VMEM((tokens, LANES), F32), pltpu.VMEM((tokens + 8, TILE), F32)],
        1, 2 * 10**9, 8 * MIB,
    )


def cut_body(chips, meta, place, keep, arrived, mine, *sends):
    rows = mine.shape[0]
    for d in range(chips):
        at = pl.multiple_of((place[0] ^ d) * rows, 16)
        held = keep[0, pl.ds(at, rows), :].astype(F32) + arrived[0, pl.ds(at, rows), :].astype(F32)
        if d == 0:
            mine[...] = held
        else:
            sends[d - 1][...] = held.astype(BF)


def cut_parts(meta, place, keep, arrived, chips):
    _, length, width = keep.shape
    part = (length // chips, width)
    return call(
        functools.partial(cut_body, chips), "cut_parts", meta, (place, keep, arrived),
        [pl.BlockSpec(memory_space=pltpu.SMEM), whole(keep.shape), whole(keep.shape)],
        [shape_of(part)] + [shape_of(part, BF)] * (chips - 1),
        [whole(part)] * chips, [], 1, 10**8, 4 * MIB,
    )


def join_body(chips, meta, place, *refs):
    out = refs[chips]
    rows = refs[0].shape[0]
    for d in range(chips):
        at = pl.multiple_of((place[0] ^ d) * rows, 16)
        out[pl.ds(at, rows), :] = refs[d][...]


def join_parts(meta, place, parts):
    chips = len(parts)
    rows, width = parts[0].shape
    return call(
        functools.partial(join_body, chips), "join_parts", meta, (place,) + tuple(parts),
        [pl.BlockSpec(memory_space=pltpu.SMEM)] + [whole((rows, width))] * chips,
        shape_of((chips * rows, width), BF), whole((chips * rows, width)),
        [], 1, 10**8, 4 * MIB,
    )


def input_body(plan, first, last, meta, *refs):
    count = UNITS
    grads = refs[: len(plan)]
    refs = refs[len(plan) :]
    if not first:
        start, refs = refs[0], refs[1:]
    blocks = []
    for begin, steps, half in plan:
        own, refs = refs[:count], refs[count:]
        rest = None
        if half is not None:
            rest, refs = refs[:count], refs[count:]
        blocks.append((own, rest))
    step = pl.program_id(0)

    if last:
        hidden, out_grad, scale, gain, result, gain_grad, weight, weight_dt, total, folded = refs
    else:
        total, weight = refs

    @pl.when(step == 0)
    def _():
        total[...] = jnp.zeros_like(total) if first else start[...]

    for n, (begin, steps, half) in enumerate(plan):
        @pl.when((step >= begin) & (step < begin + steps))
        def _(n=n, half=half):
            own, rest = blocks[n]
            rows = own[0].shape[0]
            if grads[n].shape[1] == LANES:
                weight_dt[...] = jnp.zeros_like(weight_dt)
                gather_lanes(weight_dt, own, meta, TABLE)
                total[...] += dot(grads[n][...], weight_dt[...])
                return
            if half is None:
                gather_lanes(weight, own, meta, TABLE)
            else:
                @pl.when(meta[0] == half)
                def _():
                    gather_lanes(weight, own, meta, TABLE)

                @pl.when(meta[0] != half)
                def _():
                    gather_lanes(weight, rest, meta, TABLE + count)

            total[...] += dot(grads[n][...], weight[0:rows, :])

    if not last:
        return

    @pl.when(step == pl.num_programs(0) - 1)
    def _():
        tokens, width = hidden.shape
        folded[...] = jnp.zeros_like(folded)

        def finish(n, carry):
            rows = pl.ds(pl.multiple_of(n * 32, 32), 32)
            r = jnp.broadcast_to(scale[rows, :], (32, LANES))
            sums = jnp.zeros((32, LANES), F32)
            for at in range(0, width, LANES):
                cut = slice(at, at + LANES)
                both = total[rows, cut] * hidden[rows, cut].astype(F32)
                folded[:, cut] += fold(both * r)
                sums = sums + both * gain[:, cut]
            mean = jnp.sum(sums, axis=1, keepdims=True) / width
            factor = r * r * r * mean
            for at in range(0, width, LANES):
                cut = slice(at, at + LANES)
                value = r * (total[rows, cut] * gain[:, cut]) - hidden[rows, cut].astype(F32) * factor
                result[rows, cut] = value + out_grad[rows, cut].astype(F32)
            return carry

        lax.fori_loop(0, tokens // 32, finish, 0)
        gain_grad[...] = jnp.sum(folded[...], axis=0, keepdims=True)


def input_backward(meta, start, parts, tokens, width, last=None):
    part = width // UNITS
    plan, step, grad_specs, block_specs, grads, blocks = [], 0, [], [], [], []

    def grad_spec(columns, begin, steps, first):
        return pl.BlockSpec(
            (tokens, columns), lambda i, meta: (0, first + jnp.clip(i - begin, 0, steps - 1))
        )

    def row_spec(rows, begin, steps, first, when):
        def index(i, meta):
            at = first + jnp.clip(i - begin, 0, steps - 1)
            return (at if when is None else jnp.where(when(meta), at, first), 0)

        return pl.BlockSpec((rows, part), index)

    def is_half(half):
        return lambda meta: meta[0] == half

    def not_half(half):
        return lambda meta: meta[0] != half

    for grad, grad_first, steps, half, own, own_first, rest, rest_first, local_first in parts:
        columns = WIDE if half is not None else grad.shape[1]
        row_tile = 64 if columns == LANES else columns
        plan.append((step, steps, half))
        grads.append(grad)
        grad_specs.append(grad_spec(columns, step, steps, grad_first))
        when = None if half is None else is_half(half)
        for matrix in own:
            blocks.append(matrix)
            block_specs.append(row_spec(row_tile, step, steps, own_first, when))
        if half is not None:
            for j, matrix in enumerate(rest):
                blocks.append(matrix)
                row = local_first if j == 0 else rest_first
                block_specs.append(row_spec(row_tile, step, steps, row, not_half(half)))
        step += steps
    more, more_specs = (), []
    outs, out_specs = [shape_of((tokens, width))], [whole((tokens, width))]
    scratch = [pltpu.VMEM((WIDE, width), BF)]
    if last is not None:
        more = tuple(last)
        more_specs = [whole((tokens, width))] * 2 + [whole((tokens, 1)), whole((1, width))]
        outs.append(shape_of((1, width)))
        out_specs.append(whole((1, width)))
        scratch += [
            pltpu.VMEM((LANES, width), BF), pltpu.VMEM((tokens, width), F32),
            pltpu.VMEM((8, width), F32),
        ]
    first = start is None
    return call(
        functools.partial(input_body, tuple(plan), first, last is not None),
        "input_backward", meta,
        tuple(grads) + (() if first else (start,)) + tuple(blocks) + more,
        grad_specs + ([] if first else [whole((tokens, width))]) + block_specs + more_specs,
        outs, out_specs, scratch,
        step, 2 * tokens * width * WIDE * step, 20 * MIB,
    )


NEAR = 8


def mirrored(j, count):
    if count != 4:
        return j
    result, bit, other = 0, 1, count // 2
    while bit < count:
        if j & bit:
            result |= other
        bit, other = bit * 2, other // 2
    return result


def hop(x, bit):
    reps, count = lax.axis_size("rep"), lax.axis_size("shard")
    pairs = []
    for r in range(reps):
        flip = bit if r % 2 == 0 else mirrored(bit, count)
        pairs += [(r * count + s, r * count + (s ^ flip)) for s in range(count)]
    return lax.ppermute(x, ("rep", "shard"), pairs)


def swap(x):
    return lax.ppermute(x, "rep", [(r, r ^ 1) for r in range(lax.axis_size("rep"))])


def across(x, bit):
    return lax.ppermute(x, "shard", [(s, s ^ bit) for s in range(lax.axis_size("shard"))])


def along(x, pairs):
    return lax.ppermute(x, "rep", [(2 * a + k, 2 * b + k) for a, b in pairs for k in range(2)])


def settle(keep, arrived):
    middle = keep.shape[0] // 2
    if middle == 0:
        return None, keep.astype(F32) + arrived.astype(F32)
    held = (keep.astype(F32) + arrived.astype(F32)).astype(BF)
    return held[middle:], held[:middle]


def finish_stages(send, keep):
    while send is not None:
        send, keep = settle(keep, hop(send, send.shape[0]))
    return keep[0]


def inward(held):
    if lax.axis_size("rep") // 2 != 4:
        return held, None
    return held, along(held.astype(BF), [(0, 1), (3, 2)])


def middle(state):
    held, arrived = state
    if arrived is None:
        return held, None
    inner = (held + arrived.astype(F32)).astype(BF)
    return inner, along(inner, [(1, 2), (2, 1)])


def outward(state):
    inner, arrived = state
    if arrived is None:
        chips = lax.axis_size("rep") // 2
        total, bit = inner.astype(BF), 1
        while bit < chips:
            more = along(total, [(k, k ^ bit) for k in range(chips)])
            total = (total.astype(F32) + more.astype(F32)).astype(BF)
            bit *= 2
        return total, None
    total = (inner.astype(F32) + arrived.astype(F32)).astype(BF)
    return total, along(total, [(1, 0), (2, 3)])


def summed(state):
    total, arrived = state
    if arrived is None:
        return total
    place = lax.axis_index("rep") // 2
    return jnp.where((place == 1) | (place == 2), total, arrived)


def in_order(own, other, core):
    return [jnp.where(core == 0, own, other), jnp.where(core == 0, other, own)]


def hold(values):
    leaves, tree = jax.tree.flatten(values)
    return jax.tree.unflatten(tree, lax.optimization_barrier(tuple(leaves)))


def small_sum(vector, shard, count):
    vector = vector + swap(vector)
    rows = jnp.stack([lax.dynamic_index_in_dim(vector, shard ^ j, 0, False) for j in range(count)])
    bit = count // 2
    while bit:
        rows = rows[:bit] + across(rows[bit:], bit)
        bit //= 2
    bit, chips = 1, lax.axis_size("rep") // 2
    while bit < chips:
        rows = rows + along(rows, [(k, k ^ bit) for k in range(chips)])
        bit *= 2
    return rows[0]


def join_lanes(blocks, shard):
    return [
        jnp.concatenate(in_order(blocks[j], blocks[j + 1], shard % 2), axis=1)
        for j in range(0, len(blocks), 2)
    ]


def split_lanes(units, shard):
    half = units.shape[2] // 2
    pairs = in_order(units[:, :, :half], units[:, :, half:], shard % 2)
    return jnp.stack(pairs, axis=1).reshape(2 * units.shape[0], units.shape[1], half)


def pad_lanes(matrix):
    return jnp.pad(matrix, ((0, 0), (0, LANES - matrix.shape[1])))


def shards(
    hidden,
    out_grad,
    norm_gain,
    in_w,
    conv_w,
    conv_b,
    dt_bias,
    a_log,
    skip,
    out_gain,
    out_w,
    lengths,
    offsets,
):
    core = lax.axis_index("rep") % 2
    shard = lax.axis_index("shard")
    count = lax.axis_size("shard")
    tokens, width = hidden.shape
    bits = []
    while 2 ** len(bits) < count:
        bits.append(2 ** len(bits))

    local = in_w.T
    half = DI // 2
    piece = jnp.concatenate(
        [
            lax.dynamic_slice_in_dim(local, DI + core * half, half, 0),
            local[2 * DI :],
            jnp.zeros((16, local.shape[1]), BF),
        ],
        axis=0,
    )
    gate_piece = lax.dynamic_slice_in_dim(local, core * half, half, 0)
    out_piece = lax.dynamic_slice_in_dim(out_w, core * (out_w.shape[0] // 2), out_w.shape[0] // 2, 0)

    def spread(first):
        blocks = [first]
        for bit in bits:
            blocks = blocks + [hop(block, bit) for block in blocks]
        return blocks

    paired = count == 4
    small = (norm_gain, conv_w.T, conv_b, dt_bias, a_log, skip, out_gain)
    packed = jnp.concatenate([part.reshape(-1) for part in small])
    everyone = [packed] + [
        lax.ppermute(
            packed, ("rep", "shard"),
            [
                (r * count + s, r * count + (s ^ (j if r % 2 == 0 else mirrored(j, count))))
                for r in range(lax.axis_size("rep"))
                for s in range(count)
            ],
        )
        for j in range(1, count)
    ]
    piece, everyone = hold((piece, everyone))
    everyone = jnp.stack(everyone).astype(F32)
    order = [jnp.where(core == 0, j, mirrored(j, count)) for j in range(count)]
    whose = jnp.stack(order)[jnp.arange(count) ^ shard]
    same = (whose[:, None] == jnp.arange(count)[None]).astype(F32)
    everyone = jnp.sum(same[:, :, None] * everyone[None], axis=1)
    parts, start = [], 0
    for part in small:
        cut = everyone[:, start : start + part.size].reshape((count,) + part.shape)
        cut = jnp.moveaxis(cut, 0, -2)
        parts.append(cut.reshape(part.shape[:-1] + (-1,)))
        start += part.size
    conv_own = spread(piece)
    gate_piece, conv_own = hold((gate_piece, conv_own))
    if paired:
        conv_rest = [swap(block) for block in conv_own[1:]]
        gate_near = hop(gate_piece, 1), hop(gate_piece, 2)
        out_local, in_local = out_w, local
    else:
        gate_own = spread(gate_piece)
        out_piece, gate_own = hold((out_piece, gate_own))
        out_own = spread(out_piece)
        conv_rest = rest_conv = join_lanes([swap(block) for block in conv_own], shard)
        gate_rest = rest_gate = join_lanes([swap(block) for block in gate_own], shard)
        conv_own, gate_own = join_lanes(conv_own, shard), join_lanes(gate_own, shard)
        out_full = [jnp.concatenate(in_order(block, swap(block), core), axis=0) for block in out_own]
        out_one, out_two = out_full[:UNITS], out_full[UNITS:]
        out_local = in_local = None

    gain_one, kernel, bias_conv, bias_step, log_rate, skip_full, gain_two = parts
    decay_rate = -jnp.exp(log_rate)

    mine = order
    other = [jnp.where(core == 0, mirrored(j, count), j) for j in range(count)]
    mine, other = [shard ^ j for j in mine], [shard ^ j for j in other]
    if paired:
        out_units = [2 * j + core for j in mine] + [2 * j + 1 - core for j in other]
    else:
        out_units = mine
        mine = other = [j // 2 for j in mine[::2]]
    meta = jnp.stack(
        [core, offsets[0], lengths[0], shard] + mine + other + out_units
    ).astype(jnp.int32)
    taps = jnp.concatenate([kernel, bias_conv[None], jnp.zeros((3, CC), F32)], axis=0)
    steps = jnp.concatenate(
        [pad_lanes(jnp.stack([bias_step, decay_rate])), jnp.zeros((6, LANES), F32)], axis=0
    )
    skip_lanes = jnp.repeat(skip_full, HEADDIM)[None]

    positions = jnp.arange(tokens, dtype=jnp.int32)
    live_mask = ((positions >= offsets[0]) & (positions < offsets[0] + lengths[0])).astype(F32)
    hidden_full = hidden.astype(F32)
    inv_rms = lax.rsqrt(jnp.mean(hidden_full * hidden_full, axis=1, keepdims=True) + epsilon)
    normed = (hidden_full * inv_rms * gain_one).astype(BF)
    pulled = (out_grad.astype(F32) * live_mask[:, None]).astype(BF)
    normed_rest = swap(normed)
    pulled_rest = swap(pulled)

    (masked, signal, slope, masked_keys, keys, slope_keys, columns, rows, trio) = conv_forward(
        meta, normed, taps, steps, conv_own, conv_rest, in_local
    )
    if paired:
        gate_near, signal = hold((gate_near, signal))
        gate_own = [gate_piece, *gate_near, hop(gate_near[0], 2)]
    mixed, entering = scan_forward(meta, signal, keys, columns, rows, skip_lanes)
    if paired:
        out_piece, gate_far, mixed = hold((out_piece, gate_own[3], mixed))
        gate_own[3] = gate_far
        gate_rest = [swap(block) for block in gate_own[1:]]
        rest_conv, rest_gate = [local] + conv_rest, [local] + gate_rest
        out_near = hop(out_piece, 1), hop(out_piece, 2)
    gate, normed_out, out_theirs, scale = gate_forward(
        meta, normed, mixed, gain_two[None], gate_own, gate_rest, in_local
    )
    out_arrived = swap(out_theirs if paired else normed_out)
    if paired:
        out_near, normed_out = hold((out_near, normed_out))
        out_one = [*out_near, hop(out_near[0], 2)]
        out_two = [swap(block) for block in out_one]

    upper = count // 2
    out_pulls = (pulled, pulled_rest)
    if not paired:
        cut = core * (width // 2)
        out_pulls = [lax.dynamic_slice_in_dim(x, cut, width // 2, 1) for x in out_pulls]

    def product(parts):
        send, keep = columns_product(meta, parts, normed, normed_rest)
        return (send, keep) if paired else (split_lanes(send, shard), split_lanes(keep, shard))

    out_send, out_keep = rows_product(
        meta, normed_out, out_arrived, TABLE if paired else OUT_TABLE, *out_pulls, count
    )
    out_send, out_keep, normed_out = hold((out_send, out_keep, normed_out))
    out_there = hop(out_send, upper)
    block_out, grad_gate, gate_theirs, grad_mixed, grad_gain_two = out_forward(
        meta, normed_out, pulled, hidden, mixed, gate, scale, gain_two[None],
        out_one, out_two, out_local,
    )
    out_there, gate_theirs = hold((out_there, gate_theirs))

    gate_arrived = swap(gate_theirs)
    out_send, out_keep = settle(out_keep, out_there)
    gate_parts = [(grad_gate, lambda meta: meta[0] * (GROUPS // 2), GROUPS // 2, gate_arrived)]
    gate_send, gate_keep = product(gate_parts)
    out_send, out_keep, gate_send, gate_keep, grad_mixed = hold(
        (out_send, out_keep, gate_send, gate_keep, grad_mixed)
    )
    out_there = hop(out_send, upper // 2)
    gate_there = hop(gate_send, upper)
    kept = (
        jnp.zeros((2, SPAN, SPAN), F32),
        jnp.zeros((SPAN, DSTATE), F32),
        jnp.zeros((SPAN, DSTATE), F32),
    )
    near, far = NEAR, GROUPS - NEAR
    grad_near, near_theirs, sums_near, columns_near, rows_near, *kept = scan_backward(
        meta, signal, keys, grad_mixed, entering, columns, rows, skip_lanes, masked, slope, taps, kept,
        0, near,
    )
    out_there, gate_there, near_theirs = hold((out_there, gate_there, near_theirs))
    near_arrived = swap(near_theirs)
    out_line = inward(finish_stages(*settle(out_keep, out_there)))
    gate_send, gate_keep = settle(gate_keep, gate_there)
    near_parts = [(grad_near, lambda meta: meta[0] * (near // 2), near // 2, near_arrived)]
    near_send, near_keep = product(near_parts)
    out_held, gate_send, gate_keep, near_send, near_keep, kept, grad_mixed = hold(
        (out_line[0], gate_send, gate_keep, near_send, near_keep, kept, grad_mixed)
    )
    gate_there = hop(gate_send, upper // 2)
    near_there = hop(near_send, upper)
    grad_far, far_theirs, sums_far, columns_far, rows_far, *kept = scan_backward(
        meta, signal, keys, grad_mixed, entering, columns, rows, skip_lanes, masked, slope, taps, kept,
        near, far,
    )
    gate_there, near_there, out_arrived, far_theirs, kept = hold(
        (gate_there, near_there, out_line[1], far_theirs, kept)
    )
    far_arrived = swap(far_theirs)
    gate_line = inward(finish_stages(*settle(gate_keep, gate_there)))
    out_line = middle((out_held, out_arrived))
    near_send, near_keep = settle(near_keep, near_there)
    near_there = hop(near_send, upper // 2)
    grad_keys, sums_keys, grad_raw, grad_steps, packs = tail_backward(
        meta, keys, masked_keys, slope_keys, taps, trio, steps, kept, (columns_near, columns_far),
        (rows_near, rows_far),
    )
    packs_arrived = swap(packs[1])
    far_parts = [
        (grad_far, lambda meta: meta[0] * (far // 2), far // 2, far_arrived),
        (packs[0], lambda meta: 0, 1, packs_arrived),
    ]
    far_send, far_keep = product(far_parts)
    far_there = hop(far_send, upper)
    part = WIDES // 2
    over = near * TILE // WIDE - part
    early, out_inner, gate_held, far_keep, near_keep = hold(
        (grad_gate, out_line[0], gate_line[0], far_keep, near_keep)
    )
    (partial,) = input_backward(
        meta, None,
        [
            (early, 0, part, 0, gate_own, 0, rest_gate, 0, 0),
            (early, part, part, 1, gate_own, 0, rest_gate, 0, part if paired else 0),
        ],
        tokens, width,
    )
    partial, out_arrived, gate_arrived, near_there, far_there = hold(
        (partial, out_line[1], gate_line[1], near_there, far_there)
    )
    far_send, far_keep = settle(far_keep, far_there)
    far_there = hop(far_send, upper // 2)
    gate_line = middle((gate_held, gate_arrived))
    near_line = inward(finish_stages(*settle(near_keep, near_there)))
    out_line = outward((out_inner, out_arrived))
    partial, gate_inner, near_held, far_keep, out_done = hold(
        (partial, gate_line[0], near_line[0], far_keep, out_line[0])
    )
    (partial,) = input_backward(
        meta, partial,
        [
            (grad_near, 0, part, 0, conv_own, 0, rest_conv, 0, WIDES if paired else 0),
            (
                grad_near, part, over, 1, conv_own, 0, rest_conv, 0,
                WIDES + part if paired else 0,
            ),
        ],
        tokens, width,
    )
    partial, gate_arrived, near_arrived, far_there, out_arrived = hold(
        (partial, gate_line[1], near_line[1], far_there, out_line[1])
    )
    while far_keep.shape[0] > 1:
        far_send, far_keep = settle(far_keep, far_there)
        far_there = hop(far_send, far_send.shape[0])
    chips = lax.axis_size("rep") // 2
    place = (lax.axis_index("rep") // 2).astype(jnp.int32).reshape(1)
    far_mine, *far_parts = cut_parts(meta, place, far_keep, far_there, chips)
    far_parts = [
        along(part_sent, [(k, k ^ (d + 1)) for k in range(chips)])
        for d, part_sent in enumerate(far_parts)
    ]
    near_line = middle((near_held, near_arrived))
    gate_line = outward((gate_inner, gate_arrived))
    out_total = summed((out_done, out_arrived))
    out_other = swap(out_total)
    partial, far_mine, near_inner, gate_done, out_total = hold(
        (partial, far_mine, near_line[0], gate_line[0], out_total)
    )
    hidden_grad, grad_gain_one = input_backward(
        meta, partial,
        [
            (
                grad_far, 0, part - over, 1, conv_own, over, rest_conv, over,
                WIDES + part + over if paired else over,
            ),
            (grad_keys, 0, 1, None, conv_own, DI // 2 // TILE, None, 0, 0),
            (grad_raw, 0, 1, None, conv_own, (DI // 2 + TILE) // 64, None, 0, 0),
        ],
        tokens, width, (hidden, out_grad, inv_rms, gain_one[None]),
    )
    grad_gain_one, near_arrived, far_parts, gate_arrived, out_other = hold(
        (grad_gain_one, near_line[1], far_parts, gate_line[1], out_other)
    )
    for arrived in far_parts:
        far_mine = far_mine + arrived.astype(F32)
    far_mine = far_mine.astype(BF)
    far_parts = [
        along(far_mine, [(k, k ^ d) for k in range(chips)]) for d in range(1, chips)
    ]
    near_line = outward((near_inner, near_arrived))
    gate_total = summed((gate_done, gate_arrived))
    near_total = summed(near_line)
    far_total = join_parts(meta, place, [far_mine] + far_parts)

    out_w_grad = jnp.concatenate(
        in_order(out_total, out_other, core), axis=0 if paired else 1
    ).astype(F32)
    far_rows = in_order(far_total, swap(far_total), core)
    content, keys = far // 2 * TILE, far // 2 * TILE + LANES
    in_w_grad = jnp.concatenate(
        in_order(gate_total, swap(gate_total), core)
        + in_order(near_total, swap(near_total), core)
        + [far_rows[0][:content], far_rows[1][:content]]
        + [far_rows[0][content:keys], far_rows[1][content:keys], far_rows[0][keys : keys + HEADS]],
        axis=0,
    ).astype(F32).T

    sums = jnp.concatenate([sums_near, sums_far, sums_keys], axis=1)
    grads = (
        grad_gain_one[0].reshape(count, -1),
        sums[:CONV].reshape(CONV, count, -1).transpose(1, 0, 2).reshape(count, -1),
        sums[CONV].reshape(count, -1),
        grad_steps[0, :HEADS].reshape(count, -1),
        grad_steps[1, :HEADS].reshape(count, -1),
        jnp.sum(sums[5, :DI].reshape(HEADS, HEADDIM), axis=1).reshape(count, -1),
        grad_gain_two[0].reshape(count, -1),
    )
    row = small_sum(jnp.concatenate(grads, axis=1), shard, count)
    found, start = [], 0
    for part in grads:
        found.append(row[start : start + part.shape[1]])
        start += part.shape[1]
    return (
        block_out,
        hidden_grad,
        found[0],
        in_w_grad,
        found[1].reshape(CONV, -1).T,
        found[2],
        found[3],
        found[4],
        found[5],
        found[6],
        out_w_grad,
    )


def solution(mesh):
    return jax.shard_map(
        shards,
        mesh=mesh,
        in_specs=(
            P(("rep", "shard"), None),
            P(("rep", "shard"), None),
            P("shard"),
            P("shard", None),
            P("shard", None),
            P("shard"),
            P("shard"),
            P("shard"),
            P("shard"),
            P("shard"),
            P("shard", None),
            P(("rep", "shard")),
            P(("rep", "shard")),
        ),
        out_specs=(
            P(("rep", "shard"), None),
            P(("rep", "shard"), None),
            P("shard"),
            P("shard", None),
            P("shard", None),
            P("shard"),
            P("shard"),
            P("shard"),
            P("shard"),
            P("shard"),
            P("shard", None),
        ),
        check_vma=False,
    )
```

```python
import functools

import jax
import jax.numpy as jnp
from jax import lax
from jax.experimental import pallas as pl
from jax.experimental.pallas import tpu as pltpu
from jax.sharding import PartitionSpec as P

HEADS = 48
HEADDIM = 64
DSTATE = 128
CONV = 4
SPAN = 256
DI = 3072
CC = 3328
TILE = 256
GROUPS = DI // TILE
PER = TILE // HEADDIM
CHUNK = 64
LANES = 128
epsilon = 1e-05
FAR = -1e30
LOG2E = 1.4426950408889634
PACK = 4 * PER

BF = jnp.bfloat16
F32 = jnp.float32
MIB = 1 << 20


def dot(lhs, rhs):
    return jnp.dot(lhs, rhs, preferred_element_type=F32)


def dot_nt(lhs, rhs):
    return lax.dot_general(lhs, rhs, (((1,), (1,)), ((), ())), preferred_element_type=F32)


def dot_tn(lhs, rhs):
    return lax.dot_general(lhs, rhs, (((0,), (0,)), ((), ())), preferred_element_type=F32)


def sigmoid(value):
    return 0.5 * jnp.tanh(0.5 * value) + 0.5


def pieces(value):
    high = value.astype(BF)
    rest = value - high.astype(F32)
    middle = rest.astype(BF)
    low = (rest - middle.astype(F32)).astype(BF)
    return high, middle, low


def fine_dot(lhs, rhs, product):
    high, middle, low = pieces(lhs)
    return product(high, rhs) + (product(middle, rhs) + product(low, rhs))


def row_ids(start, shape):
    return start + lax.broadcasted_iota(jnp.int32, shape, 0)


def live_rows(meta, start, shape):
    ids = row_ids(start, shape)
    return (ids >= meta[1]) & (ids < meta[1] + meta[2])


def gather_lanes(target, blocks, table, at):
    for j, block in enumerate(blocks):
        width = block.shape[1]
        lanes = pl.ds(pl.multiple_of(table[at + j] * width, LANES), width)
        target[0 : block.shape[0], lanes] = block[...]


def call(body, name, meta, operands, in_specs, outs, out_specs, scratch, grid, flops, moved):
    return pl.pallas_call(
        body,
        name=name,
        grid_spec=pltpu.PrefetchScalarGridSpec(
            num_scalar_prefetch=1,
            grid=(grid,),
            in_specs=in_specs,
            out_specs=out_specs,
            scratch_shapes=scratch,
        ),
        out_shape=outs,
        compiler_params=pltpu.CompilerParams(vmem_limit_bytes=60 * MIB),
        cost_estimate=pl.CostEstimate(flops=flops, bytes_accessed=moved, transcendentals=0),
    )(meta, *operands)


def whole(shape):
    rank = len(shape)
    return pl.BlockSpec(shape, lambda i, meta: (0,) * rank)


def tiles(rows, width, shift=0, last=None):
    def index(i, meta):
        at = i + shift
        if last is not None:
            at = jnp.clip(at, 0, last)
        return (0, at)

    return pl.BlockSpec((rows, width), index)


def shape_of(shape, kind=F32):
    return jax.ShapeDtypeStruct(shape, kind)


TABLE = 4
UNITS = 4
OUT_TABLE = TABLE + 2 * UNITS
WIDE = 512
WIDES = DI // WIDE


def own_tile(i, meta):
    half = WIDES // 2
    return jnp.where(i < half, meta[0] * half + i, (1 - meta[0]) * half + i - half)


def live_lanes(meta, live):
    live[...] = jnp.where(live_rows(meta, 0, live.shape), 1.0, 0.0)


def convolve(low, taps, live, shifted, masked, signal, slope, begin):
    for lane in range(0, low.shape[1], LANES):
        cut = slice(begin + lane, begin + lane + LANES)
        tile = (begin + lane) // LANES
        for at in range(0, low.shape[0], CHUNK):
            part = low[at : at + CHUNK, lane : lane + LANES].astype(BF).astype(F32)
            part = part * live[at : at + CHUNK, :]
            masked[at : at + CHUNK, cut] = part.astype(BF)
            shifted[tile, 8 + at : 8 + at + CHUNK, :] = part
        for at in range(0, low.shape[0], CHUNK):
            out = taps[4:5, cut]
            for k in range(CONV):
                out = out + shifted[tile, at + 5 + k : at + 5 + k + CHUNK, :] * taps[k : k + 1, cut]
            sigma = sigmoid(out)
            out = out * sigma
            here = live[at : at + CHUNK, :]
            signal[at : at + CHUNK, cut] = (out * here).astype(BF)
            slope[at : at + CHUNK, cut] = (sigma + out * (1.0 - sigma)) * here


def conv_body(meta, x, taps, taps_keys, steps, *refs):
    count = UNITS
    own, rest, key_rows, dts = (refs[n * count : (n + 1) * count] for n in range(4))
    (masked, signal, slope, masked_keys, keys, slope_keys, columns, rows, trio,
     weight, weight_dt, shifted, live) = refs[4 * count :]
    tokens = x.shape[0]
    step = pl.program_id(0)

    @pl.when(step == 0)
    def _():
        shifted[:, 0:8, :] = jnp.zeros((WIDE // LANES, 8, LANES), F32)
        live_lanes(meta, live)
        gather_lanes(weight, key_rows, meta, TABLE)
        gather_lanes(weight_dt, dts, meta, TABLE)
        low = dot_nt(x[...], weight[0:TILE, :])
        raw = dot_nt(x[...], weight_dt[...]).astype(BF).astype(F32)
        convolve(low, taps_keys, live, shifted, masked_keys, keys, slope_keys, 0)
        raw = jnp.concatenate([raw, jnp.zeros((tokens, LANES - raw.shape[1]), F32)], axis=1)
        pre = raw + steps[0:1, :]
        size = jnp.maximum(pre, 0.0) + jnp.log1p(jnp.exp(-jnp.abs(pre)))
        rate = size * steps[1:2, :]
        lower = row_ids(0, (SPAN, SPAN)) >= lax.broadcasted_iota(jnp.int32, (SPAN, SPAN), 1)
        lower = jnp.where(lower, 1.0, 0.0).astype(BF)
        trio[0] = pre
        trio[1] = size
        for at in range(0, tokens, SPAN):
            high, middle, small = pieces(rate[at : at + SPAN])
            trio[2, at : at + SPAN, :] = dot(lower, high) + (dot(lower, middle) + dot(lower, small))
        log = trio[2] * LOG2E
        less = log - jnp.log(size) * LOG2E
        factor = jnp.concatenate(
            [jnp.exp2(log[SPAN - 1 : SPAN] - less[:SPAN]), jnp.exp2(log[SPAN:])], axis=0
        )
        high = factor.astype(BF).astype(F32)
        rest_factor = factor - high
        less_rows = less.T
        log_rows = log.T
        for g in range(GROUPS):
            a, b = g * PER, (g + 1) * PER
            columns[g] = jnp.concatenate(
                [log[:, a:b], less[:, a:b], high[:, a:b], rest_factor[:, a:b]], axis=1
            )
            rows[g] = jnp.concatenate([log_rows[a:b], less_rows[a:b]], axis=0)

    @pl.when((step > 0) & (step <= WIDES // 2))
    def _():
        gather_lanes(weight, own, meta, TABLE)

    @pl.when(step > WIDES // 2)
    def _():
        gather_lanes(weight, rest, meta, TABLE + count)

    @pl.when(step > 0)
    def _():
        lows = [dot_nt(x[...], weight[at : at + TILE, :]) for at in range(0, WIDE, TILE)]
        for n, low in enumerate(lows):
            convolve(low, taps, live, shifted, masked, signal, slope, n * TILE)


def conv_forward(meta, x, taps, steps, own, rest, local):
    tokens, width = x.shape
    count = UNITS
    part = width // count
    half = WIDES // 2

    def natural(i, meta):
        return own_tile(jnp.maximum(i - 1, 0), meta)

    def tile(rows):
        return pl.BlockSpec((rows, WIDE), lambda i, meta: (0, natural(i, meta)))

    def late(i):
        return jnp.maximum(i - 1 - half, 0)

    own_spec = pl.BlockSpec((WIDE, part), lambda i, meta: (jnp.clip(i - 1, 0, half - 1), 0))
    rest_spec = pl.BlockSpec((WIDE, part), lambda i, meta: (late(i), 0))
    local_spec = pl.BlockSpec(
        (WIDE, part), lambda i, meta: (WIDES + (1 - meta[0]) * half + late(i), 0)
    )
    key_spec = pl.BlockSpec((TILE, part), lambda i, meta: (half * WIDE // TILE, 0))
    dt_spec = pl.BlockSpec((64, part), lambda i, meta: ((half * WIDE + TILE) // 64, 0))
    return call(
        conv_body, "conv_forward", meta,
        (x, taps, taps, steps) + tuple(own) + (() if local is None else (local,)) + tuple(rest)
        + tuple(own) * 2,
        [
            whole((tokens, width)), tile(8), pl.BlockSpec((8, TILE), lambda i, meta: (0, DI // TILE)),
            whole((8, LANES)),
        ]
        + [own_spec] * count
        + [rest_spec if local is None else local_spec] + [rest_spec] * (count - 1)
        + [key_spec] * count + [dt_spec] * count,
        [
            shape_of((tokens, DI), BF), shape_of((tokens, DI), BF), shape_of((tokens, DI)),
            shape_of((tokens, TILE), BF), shape_of((tokens, TILE), BF), shape_of((tokens, TILE)),
            shape_of((GROUPS, tokens, PACK)), shape_of((GROUPS, 2 * PER, tokens)),
            shape_of((3, tokens, LANES)),
        ],
        [
            tile(tokens), tile(tokens), tile(tokens),
            whole((tokens, TILE)), whole((tokens, TILE)), whole((tokens, TILE)),
            whole((GROUPS, tokens, PACK)), whole((GROUPS, 2 * PER, tokens)),
            whole((3, tokens, LANES)),
        ],
        [
            pltpu.VMEM((WIDE, width), BF), pltpu.VMEM((64, width), BF),
            pltpu.VMEM((WIDE // LANES, tokens + 8, LANES), F32), pltpu.VMEM((tokens, LANES), F32),
        ],
        1 + WIDES, 2 * tokens * width * CC, 24 * MIB,
    )


def lane_half(shape, half):
    ids = lax.broadcasted_iota(jnp.int32, shape, 1)
    return (ids >= HEADDIM) if half else (ids < HEADDIM)


def heads_apart(value, ones):
    return jnp.concatenate([value * ones[0:1], value * ones[1:2]], axis=0)


def heads_together(stacked):
    middle = stacked.shape[0] // 2
    upper = stacked[:middle]
    return jnp.where(lane_half(upper.shape, 0), upper, stacked[middle:])


def head_lanes(shape, width):
    lane = lax.broadcasted_iota(jnp.int32, shape, 1) // width
    row = lax.broadcasted_iota(jnp.int32, shape, 0) % PER
    return jnp.where(lane == row, 1.0, 0.0).astype(BF)


def scan_body(
    meta, content, keys, columns, rows, skip, out, entering,
    scores, write_rows, mixes, blocked, spread,
):
    half = SPAN // 2

    @pl.when(pl.program_id(0) == 0)
    def _():
        for span in range(2):
            at = span * SPAN
            scores[span] = dot_nt(keys[at : at + SPAN, DSTATE:], keys[at : at + SPAN, :DSTATE])
        write_rows[...] = keys[0:SPAN, :DSTATE].astype(F32).T.astype(BF)
        mixes[...] = jnp.zeros_like(mixes)
        after = row_ids(0, blocked.shape) >= lax.broadcasted_iota(jnp.int32, blocked.shape, 1)
        blocked[...] = jnp.where(after, 0.0, FAR)
        spread[...] = head_lanes(spread.shape, HEADDIM)

    factor = dot(columns[0, :, 2 * PER :].astype(BF), spread[...])
    first = content[0:SPAN, :].astype(F32)
    state = dot(write_rows[...], (first * factor[:SPAN]).astype(BF)).astype(BF)
    entering[0] = state
    out[0:SPAN, :] = skip[...] * first
    carried = dot(keys[SPAN:, DSTATE:], state) * factor[SPAN:]
    out[SPAN:, :] = carried + skip[...] * content[SPAN:, :].astype(F32)
    for pair in range(PER // 2):
        lanes = slice(pair * 2 * HEADDIM, (pair + 1) * 2 * HEADDIM)
        for h in range(2):
            n = 2 * pair + h
            for span in range(2):
                for at in range(0, SPAN, CHUNK):
                    row = span * SPAN + at
                    corner = at // half * half
                    log = columns[0, row : row + CHUNK, n : n + 1]
                    for begin in range(0, corner + half, half):
                        cut = slice(begin, begin + half)
                        less = rows[0, PER + n : PER + n + 1, span * SPAN + begin : span * SPAN + begin + half]
                        decay = log - less
                        if begin == corner:
                            decay = decay + blocked[at - begin : at - begin + CHUNK, :]
                        mix = scores[span, at : at + CHUNK, cut] * jnp.exp2(decay)
                        mixes[pair, span, h * SPAN + at : h * SPAN + at + CHUNK, cut] = mix.astype(BF)
        for span in range(2):
            at = span * SPAN
            value = content[at : at + SPAN, lanes]
            out[at : at + SPAN, lanes] += heads_together(dot(mixes[pair, span], value))


def scan_forward(meta, signal, keys, columns, rows, skip):
    tokens = signal.shape[0]
    return call(
        scan_body, "scan_forward", meta, (signal, keys, columns, rows, skip),
        [
            tiles(tokens, TILE), whole((tokens, TILE)),
            pl.BlockSpec((1, tokens, PACK), lambda i, meta: (i, 0, 0)),
            pl.BlockSpec((1, 2 * PER, tokens), lambda i, meta: (i, 0, 0)),
            tiles(1, TILE),
        ],
        [shape_of((tokens, DI)), shape_of((GROUPS, DSTATE, TILE), BF)],
        [tiles(tokens, TILE), pl.BlockSpec((1, DSTATE, TILE), lambda i, meta: (i, 0, 0))],
        [
            pltpu.VMEM((2, SPAN, SPAN), F32), pltpu.VMEM((DSTATE, SPAN), BF),
            pltpu.VMEM((PER // 2, 2, 2 * SPAN, SPAN), BF), pltpu.VMEM((SPAN // 2, SPAN // 2), F32),
            pltpu.VMEM((2 * PER, TILE), BF),
        ],
        GROUPS, 10 * 10**9, 12 * MIB,
    )


def gate_body(meta, x, mixed, gain, *refs):
    count = UNITS
    own, rest = refs[:count], refs[count : 2 * count]
    gate, normed, theirs, scale, weight, gated, total = refs[2 * count :]
    step = pl.program_id(0)
    tokens = x.shape[0]

    @pl.when(step < WIDES // 2)
    def _():
        gather_lanes(weight, own, meta, TABLE)

    @pl.when(step >= WIDES // 2)
    def _():
        gather_lanes(weight, rest, meta, TABLE + count)

    @pl.when(step == 0)
    def _():
        total[...] = jnp.zeros_like(total)

    here = own_tile(step, meta) * WIDE
    lows = [dot_nt(x[...], weight[at : at + TILE, :]).astype(BF) for at in range(0, WIDE, TILE)]
    for n, low in enumerate(lows):
        lanes = slice(n * TILE, (n + 1) * TILE)
        place = pl.ds(pl.multiple_of(here + n * TILE, TILE), TILE)
        gate[:, lanes] = low
        for at in range(0, tokens, CHUNK):
            part = low[at : at + CHUNK].astype(F32)
            part = mixed[at : at + CHUNK, lanes] * (part * sigmoid(part))
            gated[at : at + CHUNK, place] = part
            square = part * part
            total[at : at + CHUNK, :] += square[:, :LANES] + square[:, LANES:]

    @pl.when(step == pl.num_programs(0) - 1)
    def _():
        mean = jnp.sum(total[...], axis=1, keepdims=True) / DI
        scale[...] = lax.rsqrt(mean + epsilon)

        def finish(n, carry):
            place = pl.ds(pl.multiple_of(n * CHUNK, CHUNK), CHUNK)
            factor = jnp.broadcast_to(scale[place, :], (CHUNK, LANES))
            for at in range(0, DI, LANES):
                part = gated[place, at : at + LANES] * factor * gain[:, at : at + LANES]
                normed[place, at : at + LANES] = part.astype(BF)
            return carry

        lax.fori_loop(0, tokens // CHUNK, finish, 0)
        half = DI // (2 * count)
        for k in range(count):
            other = pl.multiple_of((2 * k + 1 - meta[0]) * half, LANES)
            theirs[:, k * half : (k + 1) * half] = normed[:, pl.ds(other, half)]


def gate_forward(meta, x, mixed, gain, own, rest, local):
    tokens, width = x.shape
    count = UNITS
    part = width // count
    half = WIDES // 2
    tile_spec = pl.BlockSpec((tokens, WIDE), lambda i, meta: (0, own_tile(i, meta)))
    own_spec = pl.BlockSpec((WIDE, part), lambda i, meta: (jnp.minimum(i, half - 1), 0))
    rest_spec = pl.BlockSpec((WIDE, part), lambda i, meta: (jnp.maximum(i - half, 0), 0))
    local_spec = pl.BlockSpec(
        (WIDE, part), lambda i, meta: ((1 - meta[0]) * half + jnp.maximum(i - half, 0), 0)
    )
    return call(
        gate_body, "gate_forward", meta,
        (x, mixed, gain) + tuple(own) + (() if local is None else (local,)) + tuple(rest),
        [whole((tokens, width)), tile_spec, whole((1, DI))] + [own_spec] * count
        + [rest_spec if local is None else local_spec] + [rest_spec] * (count - 1),
        [
            shape_of((tokens, DI), BF), shape_of((tokens, DI), BF), shape_of((tokens, DI // 2), BF),
            shape_of((tokens, 1)),
        ],
        [tile_spec, whole((tokens, DI)), whole((tokens, DI // 2)), whole((tokens, 1))],
        [
            pltpu.VMEM((WIDE, width), BF), pltpu.VMEM((tokens, DI), F32),
            pltpu.VMEM((tokens, LANES), F32),
        ],
        WIDES, 2 * tokens * width * DI, 28 * MIB,
    )


STEPS = 4


def out_body(meta, *refs):
    count = UNITS
    normed, gain = refs[0:2], refs[2]
    mixed, gate, pulled, hidden, scale = refs[3:8]
    own, rest = refs[8 : 8 + count], refs[8 + count : 8 + 2 * count]
    block, grad_gate, theirs, grad_mixed, grad_gain = refs[8 + 2 * count : 13 + 2 * count]
    weight, branch, back, total = refs[13 + 2 * count :]
    step = pl.program_id(0)
    tokens = pulled.shape[0]
    half = DI // (2 * count)

    @pl.when(step == 0)
    def _():
        branch[...] = jnp.zeros_like(branch)
        total[...] = jnp.zeros_like(total)

    for j in range(count):
        @pl.when(step == j)
        def _(j=j):
            weight[0:half, :] = own[j][...]
            weight[half:, :] = rest[j][...]

    @pl.when(step < count)
    def _():
        normed_both = jnp.concatenate([normed[0][...], normed[1][...]], axis=1)
        grads = dot_nt(pulled[...], weight[...]).astype(BF)
        branch[...] += dot(normed_both, weight[...])
        for side in range(2):
            at = meta[OUT_TABLE + side * count + step] * half
            place = pl.ds(pl.multiple_of(at, LANES), half)
            back[:, place] = grads[:, side * half : (side + 1) * half]
        for at in range(0, tokens, CHUNK):
            sums = None
            for lane in range(0, 2 * half, LANES):
                one = grads[at : at + CHUNK, lane : lane + LANES].astype(F32)
                one = one * normed_both[at : at + CHUNK, lane : lane + LANES].astype(F32)
                sums = one if sums is None else sums + one
            total[at : at + CHUNK, :] += sums

    @pl.when(step == count - 1)
    def _():
        for at in range(0, tokens, CHUNK):
            part = branch[at : at + CHUNK, :]
            part = jnp.where(live_rows(meta, at, part.shape), part, 0.0)
            block[at : at + CHUNK, :] = (hidden[at : at + CHUNK, :].astype(F32) + part).astype(BF)

    @pl.when(step >= count)
    def _():
        late = step - count
        width = DI // STEPS
        grad_gain[...] = jnp.zeros_like(grad_gain)

        def second(n, carry):
            rows = pl.ds(pl.multiple_of(n * CHUNK, CHUNK), CHUNK)
            r = jnp.broadcast_to(scale[rows, :], (CHUNK, LANES))
            mean = jnp.sum(total[rows, :], axis=1, keepdims=True) / DI
            factor = r * r * mean
            for at in range(0, width, LANES):
                cut = slice(at, at + LANES)
                z = gate[rows, cut].astype(F32)
                sigma = sigmoid(z)
                silu = z * sigma
                out = mixed[rows, cut]
                gated = out * silu
                grad = back[rows, pl.ds(pl.multiple_of(late * width + at, LANES), LANES)].astype(F32)
                grad = grad * r
                grad_gain[:, cut] += jnp.sum(grad * gated, axis=0, keepdims=True)
                grad = grad * gain[:, cut] - gated * factor
                grad_mixed[rows, cut] = (grad * silu).astype(BF)
                grad_gate[rows, cut] = ((grad * out) * (sigma + silu * (1.0 - sigma))).astype(BF)
            return carry

        lax.fori_loop(0, tokens // CHUNK, second, 0)

        @pl.when(late // (STEPS // 2) == 1 - meta[0])
        def _():
            theirs[...] = grad_gate[...]


def out_forward(meta, normed, pulled, hidden, mixed, gate, scale, gain, own, rest, local):
    tokens, width = hidden.shape
    count = UNITS
    half = DI // (2 * count)
    step_width = DI // STEPS

    def early(rows, side):
        def index(i, meta):
            return (0, meta[OUT_TABLE + side * count + jnp.minimum(i, count - 1)])

        return pl.BlockSpec((rows, half), index)

    def late(rows):
        return pl.BlockSpec((rows, step_width), lambda i, meta: (0, jnp.maximum(i - count, 0)))

    def local_spec(side):
        return pl.BlockSpec((half, width), lambda i, meta: (meta[0] if side == 0 else 1 - meta[0], 0))

    first = () if local is None else (local,)

    def weight_specs(side):
        one = whole((half, width)) if local is None else local_spec(side)
        return [one] + [whole((half, width))] * (count - 1)

    theirs_spec = pl.BlockSpec(
        (tokens, step_width),
        lambda i, meta: (0, jnp.clip(i - count - (1 - meta[0]) * (STEPS // 2), 0, STEPS // 2 - 1)),
    )
    return call(
        out_body, "out_forward", meta,
        (normed, normed, gain, mixed, gate, pulled, hidden, scale)
        + (first + tuple(own) + first + tuple(rest)),
        [early(tokens, 0), early(tokens, 1), late(1), late(tokens), late(tokens)]
        + [whole((tokens, width))] * 2 + [whole((tokens, 1))]
        + weight_specs(0) + weight_specs(1),
        [
            shape_of((tokens, width), BF), shape_of((tokens, DI), BF),
            shape_of((tokens, DI // 2), BF), shape_of((tokens, DI), BF), shape_of((1, DI)),
        ],
        [whole((tokens, width)), late(tokens), theirs_spec, late(tokens), late(1)],
        [
            pltpu.VMEM((2 * half, width), BF), pltpu.VMEM((tokens, width), F32),
            pltpu.VMEM((tokens, DI), BF), pltpu.VMEM((tokens, LANES), F32),
        ],
        count + STEPS, 4 * tokens * width * DI, 40 * MIB,
    )


def rows_product_body(meta, mine, theirs, pulled, pulled_rest, send, keep):
    total = dot_tn(mine[...], pulled[...]) + dot_tn(theirs[...], pulled_rest[...])
    total = total.astype(BF)
    sent = pl.num_programs(0) // 2

    @pl.when(pl.program_id(0) < sent)
    def _():
        send[0] = total

    @pl.when(pl.program_id(0) >= sent)
    def _():
        keep[0] = total


def rows_product(meta, normed, arrived, arrived_at, pulled, pulled_rest, units):
    tokens, width = pulled.shape
    unit = DI // (2 * UNITS)
    upper = units // 2

    def which(i):
        return lax.rem(i + upper, units)

    result = shape_of((upper, unit, width), BF)
    return call(
        rows_product_body, "rows_product", meta, (normed, arrived, pulled, pulled_rest),
        [
            pl.BlockSpec((tokens, unit), lambda i, meta: (0, meta[OUT_TABLE + which(i)])),
            pl.BlockSpec((tokens, unit), lambda i, meta: (0, meta[arrived_at + which(i)])),
            whole((tokens, width)), whole((tokens, width)),
        ],
        [result, result],
        [
            pl.BlockSpec((1, unit, width), lambda i, meta: (jnp.minimum(i, upper - 1), 0, 0)),
            pl.BlockSpec((1, unit, width), lambda i, meta: (jnp.maximum(i - upper, 0), 0, 0)),
        ],
        [], units, 4 * tokens * width * unit * units, 12 * MIB,
    )


def columns_product_body(plan, meta, *refs):
    parts = len(plan)
    mine, theirs = refs[:parts], refs[parts : 2 * parts]
    here, there, send, keep, right, right_rest = refs[2 * parts :]
    step = pl.program_id(0)
    width = here.shape[1] // UNITS

    @pl.when(step == 0)
    def _():
        for j in range(UNITS):
            lanes = pl.ds(pl.multiple_of(meta[TABLE + j] * width, LANES), width)
            right[:, j * width : (j + 1) * width] = here[:, lanes]
            right_rest[:, j * width : (j + 1) * width] = there[:, lanes]

    for (begin, steps), a, b in zip(plan, mine, theirs):
        @pl.when((step >= begin) & (step < begin + steps))
        def _(a=a, b=b):
            total = (dot_tn(a[...], right[...]) + dot_tn(b[...], right_rest[...])).astype(BF)
            for k in range(UNITS // 2):
                keep[k] = total[:, k * width : (k + 1) * width]
                other = UNITS // 2 + k
                send[k] = total[:, other * width : (other + 1) * width]


def columns_product(meta, parts, normed, normed_rest):
    tokens, width = normed.shape
    part = width // UNITS
    plan, step, mine_specs, theirs_specs = [], 0, [], []

    def spec(begin, steps, start):
        return pl.BlockSpec(
            (tokens, TILE), lambda i, meta: (0, start(meta) + jnp.clip(i - begin, 0, steps - 1))
        )

    for matrix, start, steps, arrived in parts:
        plan.append((step, steps))
        mine_specs.append(spec(step, steps, start))
        theirs_specs.append(spec(step, steps, lambda meta: 0))
        step += steps
    result = shape_of((UNITS // 2, step * TILE, part), BF)
    result_spec = pl.BlockSpec((UNITS // 2, TILE, part), lambda i, meta: (0, i, 0))
    return call(
        functools.partial(columns_product_body, tuple(plan)), "columns_product", meta,
        tuple(p[0] for p in parts) + tuple(p[3] for p in parts) + (normed, normed_rest),
        mine_specs + theirs_specs + [whole((tokens, width))] * 2,
        [result, result], [result_spec, result_spec],
        [pltpu.VMEM((tokens, width), BF), pltpu.VMEM((tokens, width), BF)],
        step, 4 * tokens * step * TILE * width, 12 * MIB,
    )


def conv_back(meta, masked, taps, result, sums, live, grad_conv):
    tokens = masked.shape[0]
    grad_conv[:, tokens:, :] = jnp.zeros((TILE // LANES, 8, LANES), F32)
    sums[...] = jnp.zeros_like(sums)
    for lane in range(0, TILE, LANES):
        cut = slice(lane, lane + LANES)
        totals = [jnp.zeros((8, LANES), F32) for _ in range(CONV + 1)]
        for at in range(0, tokens, CHUNK):
            near = [
                grad_conv[lane // LANES, at + 3 - k : at + 3 - k + CHUNK, :] for k in range(CONV)
            ]
            value = masked[at : at + CHUNK, cut].astype(F32)
            out = near[0] * taps[0:1, cut]
            for k in range(1, CONV):
                out = out + near[k] * taps[k : k + 1, cut]
            result[at : at + CHUNK, cut] = (out * live[at : at + CHUNK, :]).astype(BF)
            for k in range(CONV):
                totals[k] = totals[k] + fold(near[k] * value)
            totals[CONV] = totals[CONV] + fold(near[CONV - 1])
        for k in range(CONV + 1):
            sums[k : k + 1, cut] = jnp.sum(totals[k], axis=0, keepdims=True)


def fold(value):
    return jnp.sum(value.reshape(value.shape[0] // 8, 8, value.shape[1]), axis=0)


def scan_back_body(
    meta, content, keys, grad_out, mixed, entering, columns, rows, skip, masked, slope, taps,
    scores_in, write_in, read_in,
    result, theirs, sums, grad_columns, grad_scores, grad_write, grad_read,
    scores, read_rows, live, grad_conv, mixes, mix_grads, blocked, spread,
):
    half = SPAN // 2

    @pl.when(pl.program_id(0) == 0)
    def _():
        for span in range(2):
            at = span * SPAN
            scores[span] = dot_nt(keys[at : at + SPAN, :DSTATE], keys[at : at + SPAN, DSTATE:])
        read_rows[...] = keys[SPAN:, DSTATE:].astype(F32).T.astype(BF)
        grad_scores[...] = scores_in[...]
        grad_write[...] = write_in[...]
        grad_read[...] = read_in[...]
        mixes[...] = jnp.zeros_like(mixes)
        live_lanes(meta, live)
        after = row_ids(0, blocked.shape) <= lax.broadcasted_iota(jnp.int32, blocked.shape, 1)
        blocked[...] = jnp.where(after, 0.0, FAR)
        spread[...] = head_lanes(spread.shape, HEADDIM)

    def heads_sum(value):
        high = value.astype(BF)
        low = (value - high.astype(F32)).astype(BF)
        return dot_nt(high, spread[...]) + dot_nt(low, spread[...])

    for pair in range(PER // 2):
        lanes = slice(pair * 2 * HEADDIM, (pair + 1) * 2 * HEADDIM)
        ones = spread[2 * pair : 2 * pair + 2, lanes]
        for span in range(2):
            cut = slice(span * SPAN, (span + 1) * SPAN)
            mix_grads[pair, span] = dot_nt(heads_apart(content[cut, lanes], ones), grad_out[cut, lanes])

    factor = dot(columns[0, :, 2 * PER :].astype(BF), spread[...])
    grown = (grad_out[SPAN:, :].astype(F32) * factor[SPAN:]).astype(BF)
    grad_state = dot(read_rows[...], grown).astype(BF)
    grad_read[...] += dot_nt(grown, entering[0])
    worth = (content[0:SPAN, :].astype(F32) * factor[:SPAN]).astype(BF)
    grad_write[...] += dot_nt(worth, grad_state)
    from_state = dot(keys[0:SPAN, :DSTATE], grad_state) * factor[:SPAN]

    for pair in range(PER // 2):
        for h in range(2):
            n = 2 * pair + h
            for span in range(2):
                top = span * SPAN
                for at in range(0, SPAN, CHUNK):
                    less = columns[0, top + at : top + at + CHUNK, PER + n : PER + n + 1]
                    corner = at // half * half
                    for begin in range(corner, SPAN, half):
                        cut = slice(begin, begin + half)
                        decay = rows[0, n : n + 1, top + begin : top + begin + half] - less
                        if begin == corner:
                            decay = decay + blocked[at - begin : at - begin + CHUNK, :]
                        decay = jnp.exp2(decay)
                        row = h * SPAN + at
                        mix = scores[span, at : at + CHUNK, cut] * decay
                        mixes[pair, span, row : row + CHUNK, cut] = mix.astype(BF)
                        change = mix_grads[pair, span, row : row + CHUNK, cut] * decay
                        grad_scores[span, at : at + CHUNK, cut] += change

    lane = lax.broadcasted_iota(jnp.int32, (SPAN, 2 * PER), 1) < PER
    final = row_ids(0, lane.shape) == SPAN - 1
    skips = jnp.zeros((8, TILE), F32)
    for span in range(2):
        cut = slice(span * SPAN, (span + 1) * SPAN)
        value = content[cut, :].astype(F32)
        pull = grad_out[cut, :].astype(F32)
        both = []
        for pair in range(PER // 2):
            lanes = slice(pair * 2 * HEADDIM, (pair + 1) * 2 * HEADDIM)
            both.append(heads_together(dot(mixes[pair, span], grad_out[cut, lanes])))
        both = jnp.concatenate(both, axis=1)
        if span == 0:
            ended = jnp.sum(fold(value * from_state), axis=0, keepdims=True)
            both = both + from_state
        skipped = skip[...] * value
        skips = skips + fold(pull * value)
        written = heads_sum(value * both)
        read = heads_sum(pull * (mixed[cut, :] - skipped))
        if span == 0:
            ended = heads_sum(jnp.broadcast_to(ended, (8, TILE)))[0:1]
            read = read + jnp.where(final, ended, 0.0)
        grad_columns[0, cut, :] = jnp.where(lane, written, read)
        both = (both + skip[...] * pull) * slope[cut, :]
        for k in range(TILE // LANES):
            grad_conv[k, cut, :] = both[:, k * LANES : (k + 1) * LANES]

    conv_back(meta, masked, taps, result, sums, live, grad_conv)
    sums[5:6, :] = jnp.sum(skips, axis=0, keepdims=True)
    half_steps = pl.num_programs(0) // 2
    at_half = pl.program_id(0) // half_steps

    @pl.when(at_half == 1 - meta[0])
    def _():
        theirs[...] = result[...]


def scan_backward(
    meta, signal, keys, grad_out, mixed, entering, columns, rows, skip, masked, slope, taps, kept,
    first, count,
):
    tokens = signal.shape[0]

    def group(*shape):
        return pl.BlockSpec((1,) + shape, lambda i, meta: (i + first, 0, 0))

    def fresh(*shape):
        return pl.BlockSpec((1,) + shape, lambda i, meta: (i, 0, 0))

    kept_specs = [whole((2, SPAN, SPAN)), whole((SPAN, DSTATE)), whole((SPAN, DSTATE))]
    return call(
        scan_back_body, "scan_backward", meta,
        (signal, keys, grad_out, mixed, entering, columns, rows, skip, masked, slope, taps)
        + tuple(kept),
        [
            tiles(tokens, TILE, first), whole((tokens, TILE)),
            tiles(tokens, TILE, first), tiles(tokens, TILE, first), group(DSTATE, TILE),
            group(tokens, PACK),
            group(2 * PER, tokens), tiles(1, TILE, first), tiles(tokens, TILE, first),
            tiles(tokens, TILE, first), tiles(8, TILE, first),
        ]
        + kept_specs,
        [
            shape_of((tokens, count * TILE), BF), shape_of((tokens, count // 2 * TILE), BF),
            shape_of((8, count * TILE)),
            shape_of((count, tokens, 2 * PER)),
            shape_of((2, SPAN, SPAN)), shape_of((SPAN, DSTATE)), shape_of((SPAN, DSTATE)),
        ],
        [
            tiles(tokens, TILE),
            pl.BlockSpec(
                (tokens, TILE),
                lambda i, meta: (0, jnp.clip(i - (1 - meta[0]) * (count // 2), 0, count // 2 - 1)),
            ),
            tiles(8, TILE), fresh(tokens, 2 * PER),
        ]
        + kept_specs,
        [
            pltpu.VMEM((2, SPAN, SPAN), F32), pltpu.VMEM((DSTATE, SPAN), BF),
            pltpu.VMEM((tokens, LANES), F32), pltpu.VMEM((TILE // LANES, tokens + 8, LANES), F32),
            pltpu.VMEM((PER // 2, 2, 2 * SPAN, SPAN), BF),
            pltpu.VMEM((PER // 2, 2, 2 * SPAN, SPAN), F32),
            pltpu.VMEM((SPAN // 2, SPAN // 2), F32), pltpu.VMEM((2 * PER, TILE), BF),
        ],
        count, 3 * 10**9 * count, count * MIB,
    )


def tail_body(parts, meta, *refs):
    keys, masked, slope, taps, trio, steps, grad_scores, grad_write, grad_read = refs[:9]
    grad_columns = refs[9 : 9 + parts]
    result, sums, raw, small, packs, live, grad_conv = refs[9 + parts :]
    tokens = keys.shape[0]
    for span in range(2):
        at = span * SPAN
        write = keys[at : at + SPAN, :DSTATE]
        read = keys[at : at + SPAN, DSTATE:]
        to_write = fine_dot(grad_scores[span], read, dot)
        to_read = fine_dot(grad_scores[span], write, dot_tn)
        if span == 0:
            to_write = to_write + grad_write[...]
        else:
            to_read = to_read + grad_read[...]
        cut = slice(at, at + SPAN)
        grad_conv[0, cut, :] = to_write * slope[cut, :DSTATE]
        grad_conv[1, cut, :] = to_read * slope[cut, DSTATE:]
    live_lanes(meta, live)
    conv_back(meta, masked, taps, result, sums, live, grad_conv)

    blank = jnp.zeros((tokens, LANES - HEADS), F32)
    of_step, of_log = [], []
    for column_ref in grad_columns:
        for g in range(column_ref.shape[0]):
            of_step.append(column_ref[g, :, :PER])
            of_log.append(column_ref[g, :, PER:])
    grad_size = jnp.concatenate(of_step + [blank], axis=1)
    grad_log = jnp.concatenate(of_log + [blank], axis=1) - grad_size
    upper = row_ids(0, (SPAN, SPAN)) <= lax.broadcasted_iota(jnp.int32, (SPAN, SPAN), 1)
    upper = jnp.where(upper, 1.0, 0.0).astype(BF)
    rates = []
    for at in range(0, tokens, SPAN):
        high, middle, low = pieces(grad_log[at : at + SPAN])
        rates.append(dot(upper, high) + (dot(upper, middle) + dot(upper, low)))
    grad_rate = jnp.concatenate(rates, axis=0)
    decay_rate = steps[1:2, :]
    sigma = jax.nn.sigmoid(trio[0])
    size = trio[1]
    tiny = size > 0.0
    share = jnp.where(tiny, sigma / jnp.where(tiny, size, 1.0), 1.0)
    grad_raw = grad_size * share + grad_rate * decay_rate * sigma
    raw[...] = grad_raw.astype(BF)
    small[...] = jnp.zeros_like(small)
    small[0:1, :] = jnp.sum(grad_raw, axis=0, keepdims=True)
    small[1:2, :] = jnp.sum(grad_rate * trio[1], axis=0, keepdims=True) * decay_rate
    for side in range(2):
        at = meta[0] if side == 0 else 1 - meta[0]
        packs[side, :, :LANES] = result[:, pl.ds(pl.multiple_of(at * LANES, LANES), LANES)]
        packs[side, :, LANES:] = raw[...]


def tail_backward(meta, keys, masked, slope, taps, trio, steps, kept, grad_columns):
    tokens = keys.shape[0]
    last = DI // TILE
    key_spec = whole((tokens, TILE))
    return call(
        functools.partial(tail_body, len(grad_columns)), "tail_backward", meta,
        (keys, masked, slope, taps, trio, steps) + tuple(kept) + tuple(grad_columns),
        [
            key_spec, key_spec, key_spec, pl.BlockSpec((8, TILE), lambda i, meta: (0, last)),
            whole((3, tokens, LANES)), whole((8, LANES)), whole((2, SPAN, SPAN)),
            whole((SPAN, DSTATE)), whole((SPAN, DSTATE)),
        ]
        + [whole(part.shape) for part in grad_columns],
        [
            shape_of((tokens, TILE), BF), shape_of((8, TILE)), shape_of((tokens, LANES), BF),
            shape_of((8, LANES)), shape_of((2, tokens, TILE), BF),
        ],
        [
            whole((tokens, TILE)), whole((8, TILE)), whole((tokens, LANES)), whole((8, LANES)),
            whole((2, tokens, TILE)),
        ],
        [pltpu.VMEM((tokens, LANES), F32), pltpu.VMEM((TILE // LANES, tokens + 8, LANES), F32)],
        1, 2 * 10**9, 8 * MIB,
    )


def input_body(plan, first, last, meta, *refs):
    count = UNITS
    grads = refs[: len(plan)]
    refs = refs[len(plan) :]
    if not first:
        start, refs = refs[0], refs[1:]
    blocks = []
    for begin, steps, half in plan:
        own, refs = refs[:count], refs[count:]
        rest = None
        if half is not None:
            rest, refs = refs[:count], refs[count:]
        blocks.append((own, rest))
    step = pl.program_id(0)

    if last:
        hidden, out_grad, scale, gain, result, gain_grad, weight, weight_dt, total, folded = refs
    else:
        total, weight = refs

    @pl.when(step == 0)
    def _():
        total[...] = jnp.zeros_like(total) if first else start[...]

    for n, (begin, steps, half) in enumerate(plan):
        @pl.when((step >= begin) & (step < begin + steps))
        def _(n=n, half=half):
            own, rest = blocks[n]
            rows = own[0].shape[0]
            if grads[n].shape[1] == LANES:
                weight_dt[...] = jnp.zeros_like(weight_dt)
                gather_lanes(weight_dt, own, meta, TABLE)
                total[...] += dot(grads[n][...], weight_dt[...])
                return
            if half is None:
                gather_lanes(weight, own, meta, TABLE)
            else:
                @pl.when(meta[0] == half)
                def _():
                    gather_lanes(weight, own, meta, TABLE)

                @pl.when(meta[0] != half)
                def _():
                    gather_lanes(weight, rest, meta, TABLE + count)

            total[...] += dot(grads[n][...], weight[0:rows, :])

    if not last:
        return

    @pl.when(step == pl.num_programs(0) - 1)
    def _():
        tokens, width = hidden.shape
        folded[...] = jnp.zeros_like(folded)

        def finish(n, carry):
            rows = pl.ds(pl.multiple_of(n * 32, 32), 32)
            r = jnp.broadcast_to(scale[rows, :], (32, LANES))
            sums = jnp.zeros((32, LANES), F32)
            for at in range(0, width, LANES):
                cut = slice(at, at + LANES)
                both = total[rows, cut] * hidden[rows, cut].astype(F32)
                folded[:, cut] += fold(both * r)
                sums = sums + both * gain[:, cut]
            mean = jnp.sum(sums, axis=1, keepdims=True) / width
            factor = r * r * r * mean
            for at in range(0, width, LANES):
                cut = slice(at, at + LANES)
                value = r * (total[rows, cut] * gain[:, cut]) - hidden[rows, cut].astype(F32) * factor
                result[rows, cut] = value + out_grad[rows, cut].astype(F32)
            return carry

        lax.fori_loop(0, tokens // 32, finish, 0)
        gain_grad[...] = jnp.sum(folded[...], axis=0, keepdims=True)


def input_backward(meta, start, parts, tokens, width, last=None):
    part = width // UNITS
    plan, step, grad_specs, block_specs, grads, blocks = [], 0, [], [], [], []

    def grad_spec(columns, begin, steps, first):
        return pl.BlockSpec(
            (tokens, columns), lambda i, meta: (0, first + jnp.clip(i - begin, 0, steps - 1))
        )

    def row_spec(rows, begin, steps, first, when):
        def index(i, meta):
            at = first + jnp.clip(i - begin, 0, steps - 1)
            return (at if when is None else jnp.where(when(meta), at, first), 0)

        return pl.BlockSpec((rows, part), index)

    def is_half(half):
        return lambda meta: meta[0] == half

    def not_half(half):
        return lambda meta: meta[0] != half

    for grad, grad_first, steps, half, own, own_first, rest, rest_first, local_first in parts:
        columns = WIDE if half is not None else grad.shape[1]
        row_tile = 64 if columns == LANES else columns
        plan.append((step, steps, half))
        grads.append(grad)
        grad_specs.append(grad_spec(columns, step, steps, grad_first))
        when = None if half is None else is_half(half)
        for matrix in own:
            blocks.append(matrix)
            block_specs.append(row_spec(row_tile, step, steps, own_first, when))
        if half is not None:
            for j, matrix in enumerate(rest):
                blocks.append(matrix)
                row = local_first if j == 0 else rest_first
                block_specs.append(row_spec(row_tile, step, steps, row, not_half(half)))
        step += steps
    more, more_specs = (), []
    outs, out_specs = [shape_of((tokens, width))], [whole((tokens, width))]
    scratch = [pltpu.VMEM((WIDE, width), BF)]
    if last is not None:
        more = tuple(last)
        more_specs = [whole((tokens, width))] * 2 + [whole((tokens, 1)), whole((1, width))]
        outs.append(shape_of((1, width)))
        out_specs.append(whole((1, width)))
        scratch += [
            pltpu.VMEM((LANES, width), BF), pltpu.VMEM((tokens, width), F32),
            pltpu.VMEM((8, width), F32),
        ]
    first = start is None
    return call(
        functools.partial(input_body, tuple(plan), first, last is not None),
        "input_backward", meta,
        tuple(grads) + (() if first else (start,)) + tuple(blocks) + more,
        grad_specs + ([] if first else [whole((tokens, width))]) + block_specs + more_specs,
        outs, out_specs, scratch,
        step, 2 * tokens * width * WIDE * step, 20 * MIB,
    )


NEAR = 8


def mirrored(j, count):
    if count != 4:
        return j
    result, bit, other = 0, 1, count // 2
    while bit < count:
        if j & bit:
            result |= other
        bit, other = bit * 2, other // 2
    return result


def hop(x, bit):
    reps, count = lax.axis_size("rep"), lax.axis_size("shard")
    pairs = []
    for r in range(reps):
        flip = bit if r % 2 == 0 else mirrored(bit, count)
        pairs += [(r * count + s, r * count + (s ^ flip)) for s in range(count)]
    return lax.ppermute(x, ("rep", "shard"), pairs)


def swap(x):
    return lax.ppermute(x, "rep", [(r, r ^ 1) for r in range(lax.axis_size("rep"))])


def across(x, bit):
    return lax.ppermute(x, "shard", [(s, s ^ bit) for s in range(lax.axis_size("shard"))])


def along(x, pairs):
    return lax.ppermute(x, "rep", [(2 * a + k, 2 * b + k) for a, b in pairs for k in range(2)])


def settle(keep, arrived):
    middle = keep.shape[0] // 2
    if middle == 0:
        return None, keep.astype(F32) + arrived.astype(F32)
    held = (keep.astype(F32) + arrived.astype(F32)).astype(BF)
    return held[middle:], held[:middle]


def finish_stages(send, keep):
    while send is not None:
        send, keep = settle(keep, hop(send, send.shape[0]))
    return keep[0]


def inward(held):
    if lax.axis_size("rep") // 2 != 4:
        return held, None
    return held, along(held.astype(BF), [(0, 1), (3, 2)])


def middle(state):
    held, arrived = state
    if arrived is None:
        return held, None
    inner = (held + arrived.astype(F32)).astype(BF)
    return inner, along(inner, [(1, 2), (2, 1)])


def outward(state):
    inner, arrived = state
    if arrived is None:
        chips = lax.axis_size("rep") // 2
        total, bit = inner.astype(BF), 1
        while bit < chips:
            more = along(total, [(k, k ^ bit) for k in range(chips)])
            total = (total.astype(F32) + more.astype(F32)).astype(BF)
            bit *= 2
        return total, None
    total = (inner.astype(F32) + arrived.astype(F32)).astype(BF)
    return total, along(total, [(1, 0), (2, 3)])


def summed(state):
    total, arrived = state
    if arrived is None:
        return total
    place = lax.axis_index("rep") // 2
    return jnp.where((place == 1) | (place == 2), total, arrived)


def in_order(own, other, core):
    return [jnp.where(core == 0, own, other), jnp.where(core == 0, other, own)]


def hold(values):
    leaves, tree = jax.tree.flatten(values)
    return jax.tree.unflatten(tree, lax.optimization_barrier(tuple(leaves)))


def small_sum(vector, shard, count):
    vector = vector + swap(vector)
    rows = [lax.dynamic_slice_in_dim(vector, shard ^ j, 1, 0) for j in range(count)]
    rows = rows[:1] + [across(row, j) for j, row in enumerate(rows) if j]
    while len(rows) > 1:
        rows = [a + b for a, b in zip(rows[::2], rows[1::2])]
    chips = lax.axis_size("rep") // 2
    rows = rows + [along(rows[0], [(k, k ^ d) for k in range(chips)]) for d in range(1, chips)]
    while len(rows) > 1:
        rows = [a + b for a, b in zip(rows[::2], rows[1::2])]
    return rows[0][0]


def join_lanes(blocks, shard):
    return [
        jnp.concatenate(in_order(blocks[j], blocks[j + 1], shard % 2), axis=1)
        for j in range(0, len(blocks), 2)
    ]


def split_lanes(units, shard):
    half = units.shape[2] // 2
    pairs = in_order(units[:, :, :half], units[:, :, half:], shard % 2)
    return jnp.stack(pairs, axis=1).reshape(2 * units.shape[0], units.shape[1], half)


def pad_lanes(matrix):
    return jnp.pad(matrix, ((0, 0), (0, LANES - matrix.shape[1])))


def shards(
    hidden,
    out_grad,
    norm_gain,
    in_w,
    conv_w,
    conv_b,
    dt_bias,
    a_log,
    skip,
    out_gain,
    out_w,
    lengths,
    offsets,
):
    core = lax.axis_index("rep") % 2
    shard = lax.axis_index("shard")
    count = lax.axis_size("shard")
    tokens, width = hidden.shape
    bits = []
    while 2 ** len(bits) < count:
        bits.append(2 ** len(bits))

    local = in_w.T
    half = DI // 2
    piece = jnp.concatenate(
        [
            lax.dynamic_slice_in_dim(local, DI + core * half, half, 0),
            local[2 * DI :],
            jnp.zeros((16, local.shape[1]), BF),
        ],
        axis=0,
    )
    gate_piece = lax.dynamic_slice_in_dim(local, core * half, half, 0)
    out_piece = lax.dynamic_slice_in_dim(out_w, core * (out_w.shape[0] // 2), out_w.shape[0] // 2, 0)

    def spread(first):
        blocks = [first]
        for bit in bits:
            blocks = blocks + [hop(block, bit) for block in blocks]
        return blocks

    paired = count == 4
    small = (norm_gain, conv_w.T, conv_b, dt_bias, a_log, skip, out_gain)
    packed = jnp.concatenate([part.reshape(-1) for part in small])
    everyone = [packed] + [
        lax.ppermute(
            packed, ("rep", "shard"),
            [
                (r * count + s, r * count + (s ^ (j if r % 2 == 0 else mirrored(j, count))))
                for r in range(lax.axis_size("rep"))
                for s in range(count)
            ],
        )
        for j in range(1, count)
    ]
    piece, everyone = hold((piece, everyone))
    everyone = jnp.stack(everyone).astype(F32)
    order = [jnp.where(core == 0, j, mirrored(j, count)) for j in range(count)]
    whose = jnp.stack(order)[jnp.arange(count) ^ shard]
    same = (whose[:, None] == jnp.arange(count)[None]).astype(F32)
    everyone = jnp.sum(same[:, :, None] * everyone[None], axis=1)
    parts, start = [], 0
    for part in small:
        cut = everyone[:, start : start + part.size].reshape((count,) + part.shape)
        cut = jnp.moveaxis(cut, 0, -2)
        parts.append(cut.reshape(part.shape[:-1] + (-1,)))
        start += part.size
    conv_own = spread(piece)
    gate_piece, conv_own = hold((gate_piece, conv_own))
    if paired:
        conv_rest = [swap(block) for block in conv_own[1:]]
        gate_near = hop(gate_piece, 1), hop(gate_piece, 2)
        out_local, in_local = out_w, local
    else:
        gate_own = spread(gate_piece)
        out_piece, gate_own = hold((out_piece, gate_own))
        out_own = spread(out_piece)
        conv_rest = rest_conv = join_lanes([swap(block) for block in conv_own], shard)
        gate_rest = rest_gate = join_lanes([swap(block) for block in gate_own], shard)
        conv_own, gate_own = join_lanes(conv_own, shard), join_lanes(gate_own, shard)
        out_full = [jnp.concatenate(in_order(block, swap(block), core), axis=0) for block in out_own]
        out_one, out_two = out_full[:UNITS], out_full[UNITS:]
        out_local = in_local = None

    gain_one, kernel, bias_conv, bias_step, log_rate, skip_full, gain_two = parts
    decay_rate = -jnp.exp(log_rate)

    mine = order
    other = [jnp.where(core == 0, mirrored(j, count), j) for j in range(count)]
    mine, other = [shard ^ j for j in mine], [shard ^ j for j in other]
    if paired:
        out_units = [2 * j + core for j in mine] + [2 * j + 1 - core for j in other]
    else:
        out_units = mine
        mine = other = [j // 2 for j in mine[::2]]
    meta = jnp.stack(
        [core, offsets[0], lengths[0], shard] + mine + other + out_units
    ).astype(jnp.int32)
    taps = jnp.concatenate([kernel, bias_conv[None], jnp.zeros((3, CC), F32)], axis=0)
    steps = jnp.concatenate(
        [pad_lanes(jnp.stack([bias_step, decay_rate])), jnp.zeros((6, LANES), F32)], axis=0
    )
    skip_lanes = jnp.repeat(skip_full, HEADDIM)[None]

    positions = jnp.arange(tokens, dtype=jnp.int32)
    live_mask = ((positions >= offsets[0]) & (positions < offsets[0] + lengths[0])).astype(F32)
    hidden_full = hidden.astype(F32)
    inv_rms = lax.rsqrt(jnp.mean(hidden_full * hidden_full, axis=1, keepdims=True) + epsilon)
    normed = (hidden_full * inv_rms * gain_one).astype(BF)
    pulled = (out_grad.astype(F32) * live_mask[:, None]).astype(BF)
    normed_rest = swap(normed)
    pulled_rest = swap(pulled)

    (masked, signal, slope, masked_keys, keys, slope_keys, columns, rows, trio) = conv_forward(
        meta, normed, taps, steps, conv_own, conv_rest, in_local
    )
    if paired:
        gate_near, signal = hold((gate_near, signal))
        gate_own = [gate_piece, *gate_near, hop(gate_near[0], 2)]
    mixed, entering = scan_forward(meta, signal, keys, columns, rows, skip_lanes)
    if paired:
        out_piece, gate_far, mixed = hold((out_piece, gate_own[3], mixed))
        gate_own[3] = gate_far
        gate_rest = [swap(block) for block in gate_own[1:]]
        rest_conv, rest_gate = [local] + conv_rest, [local] + gate_rest
        out_near = hop(out_piece, 1), hop(out_piece, 2)
    gate, normed_out, out_theirs, scale = gate_forward(
        meta, normed, mixed, gain_two[None], gate_own, gate_rest, in_local
    )
    out_arrived = swap(out_theirs if paired else normed_out)
    if paired:
        out_near, normed_out = hold((out_near, normed_out))
        out_one = [*out_near, hop(out_near[0], 2)]
        out_two = [swap(block) for block in out_one]

    upper = count // 2
    out_pulls = (pulled, pulled_rest)
    if not paired:
        cut = core * (width // 2)
        out_pulls = [lax.dynamic_slice_in_dim(x, cut, width // 2, 1) for x in out_pulls]

    def product(parts):
        send, keep = columns_product(meta, parts, normed, normed_rest)
        return (send, keep) if paired else (split_lanes(send, shard), split_lanes(keep, shard))

    out_send, out_keep = rows_product(
        meta, normed_out, out_arrived, TABLE if paired else OUT_TABLE, *out_pulls, count
    )
    out_send, out_keep, normed_out = hold((out_send, out_keep, normed_out))
    out_there = hop(out_send, upper)
    block_out, grad_gate, gate_theirs, grad_mixed, grad_gain_two = out_forward(
        meta, normed_out, pulled, hidden, mixed, gate, scale, gain_two[None],
        out_one, out_two, out_local,
    )
    out_there, gate_theirs = hold((out_there, gate_theirs))

    gate_arrived = swap(gate_theirs)
    out_send, out_keep = settle(out_keep, out_there)
    gate_parts = [(grad_gate, lambda meta: meta[0] * (GROUPS // 2), GROUPS // 2, gate_arrived)]
    gate_send, gate_keep = product(gate_parts)
    out_send, out_keep, gate_send, gate_keep, grad_mixed = hold(
        (out_send, out_keep, gate_send, gate_keep, grad_mixed)
    )
    out_there = hop(out_send, upper // 2)
    gate_there = hop(gate_send, upper)
    kept = (
        jnp.zeros((2, SPAN, SPAN), F32),
        jnp.zeros((SPAN, DSTATE), F32),
        jnp.zeros((SPAN, DSTATE), F32),
    )
    near, far = NEAR, GROUPS - NEAR
    grad_near, near_theirs, sums_near, columns_near, *kept = scan_backward(
        meta, signal, keys, grad_mixed, mixed, entering, columns, rows, skip_lanes, masked, slope, taps,
        kept, 0, near,
    )
    out_there, gate_there, near_theirs = hold((out_there, gate_there, near_theirs))
    near_arrived = swap(near_theirs)
    out_line = inward(finish_stages(*settle(out_keep, out_there)))
    gate_send, gate_keep = settle(gate_keep, gate_there)
    near_parts = [(grad_near, lambda meta: meta[0] * (near // 2), near // 2, near_arrived)]
    near_send, near_keep = product(near_parts)
    out_held, gate_send, gate_keep, near_send, near_keep, kept, grad_mixed = hold(
        (out_line[0], gate_send, gate_keep, near_send, near_keep, kept, grad_mixed)
    )
    gate_there = hop(gate_send, upper // 2)
    near_there = hop(near_send, upper)
    grad_far, far_theirs, sums_far, columns_far, *kept = scan_backward(
        meta, signal, keys, grad_mixed, mixed, entering, columns, rows, skip_lanes, masked, slope, taps,
        kept, near, far,
    )
    gate_there, near_there, out_arrived, far_theirs, kept = hold(
        (gate_there, near_there, out_line[1], far_theirs, kept)
    )
    far_arrived = swap(far_theirs)
    gate_line = inward(finish_stages(*settle(gate_keep, gate_there)))
    near_send, near_keep = settle(near_keep, near_there)
    near_there = hop(near_send, upper // 2)
    kept, gate_held, near_keep, out_held = hold((kept, gate_line[0], near_keep, out_held))
    grad_keys, sums_keys, grad_raw, grad_steps, packs = tail_backward(
        meta, keys, masked_keys, slope_keys, taps, trio, steps, kept, (columns_near, columns_far),
    )
    packs_arrived = swap(packs[1])
    out_line = middle((out_held, out_arrived))
    far_parts = [
        (grad_far, lambda meta: meta[0] * (far // 2), far // 2, far_arrived),
        (packs[0], lambda meta: 0, 1, packs_arrived),
    ]
    far_send, far_keep = product(far_parts)
    far_there = hop(far_send, upper)
    part = WIDES // 2
    over = near * TILE // WIDE - part

    def gate_part(half):
        return [(grad_gate, half * part, part, half, gate_own, 0, rest_gate, 0, half * part if paired else 0)]

    def conv_part(grad, grad_first, steps, half, first):
        local_first = WIDES + half * part + first if paired else first
        return (grad, grad_first, steps, half, conv_own, first, rest_conv, first, local_first)

    grad_gate, far_keep, out_inner = hold((grad_gate, far_keep, out_line[0]))
    (partial,) = input_backward(meta, None, gate_part(0) + gate_part(1), tokens, width)
    partial, far_there = hold((partial, far_there))
    far_send, far_keep = settle(far_keep, far_there)
    far_there = hop(far_send, upper // 2)
    far_keep, near_there, gate_arrived = hold((far_keep, near_there, gate_line[1]))
    near_line = inward(finish_stages(*settle(near_keep, near_there)))
    gate_line = middle((gate_held, gate_arrived))
    partial, near_held, gate_inner, far_keep = hold((partial, near_line[0], gate_line[0], far_keep))
    (partial,) = input_backward(
        meta, partial, [conv_part(grad_near, 0, part, 0, 0)], tokens, width
    )
    partial, far_there = hold((partial, far_there))
    far_line = inward(finish_stages(*settle(far_keep, far_there)))
    far_held, out_arrived = hold((far_line[0], out_line[1]))
    out_line = outward((out_inner, out_arrived))
    partial, out_done, far_held = hold((partial, out_line[0], far_held))
    (partial,) = input_backward(
        meta, partial,
        [conv_part(grad_near, part, over, 1, 0), conv_part(grad_far, 0, part - over, 1, over)],
        tokens, width,
    )
    partial, far_arrived = hold((partial, far_line[1]))
    far_line = middle((far_held, far_arrived))
    far_inner, near_arrived, gate_arrived, out_arrived = hold(
        (far_line[0], near_line[1], gate_line[1], out_line[1])
    )
    near_line = middle((near_held, near_arrived))
    gate_line = outward((gate_inner, gate_arrived))
    out_total = summed((out_done, out_arrived))
    out_other = swap(out_total)
    partial, far_inner, near_inner, gate_done, out_total = hold(
        (partial, far_inner, near_line[0], gate_line[0], out_total)
    )
    hidden_grad, grad_gain_one = input_backward(
        meta, partial,
        [
            (grad_keys, 0, 1, None, conv_own, DI // 2 // TILE, None, 0, 0),
            (grad_raw, 0, 1, None, conv_own, (DI // 2 + TILE) // 64, None, 0, 0),
        ],
        tokens, width, (hidden, out_grad, inv_rms, gain_one[None]),
    )
    grad_gain_one, far_arrived = hold((grad_gain_one, far_line[1]))
    far_line = outward((far_inner, far_arrived))
    far_done, near_arrived, gate_arrived, out_other, grad_gain_one = hold(
        (far_line[0], near_line[1], gate_line[1], out_other, grad_gain_one)
    )
    near_line = outward((near_inner, near_arrived))
    gate_total = summed((gate_done, gate_arrived))
    near_total = summed(near_line)
    sums = jnp.concatenate([sums_near, sums_far, sums_keys], axis=1)
    grads = (
        grad_gain_one[0].reshape(count, -1),
        sums[:CONV].reshape(CONV, count, -1).transpose(1, 0, 2).reshape(count, -1),
        sums[CONV].reshape(count, -1),
        grad_steps[0, :HEADS].reshape(count, -1),
        grad_steps[1, :HEADS].reshape(count, -1),
        jnp.sum(sums[5, :DI].reshape(HEADS, HEADDIM), axis=1).reshape(count, -1),
        grad_gain_two[0].reshape(count, -1),
    )
    row = small_sum(jnp.concatenate(grads, axis=1), shard, count)
    row, far_arrived = hold((row, far_line[1]))
    far_total = summed((far_done, far_arrived))

    out_w_grad = jnp.concatenate(
        in_order(out_total, out_other, core), axis=0 if paired else 1
    ).astype(F32)
    far_rows = in_order(far_total, swap(far_total), core)
    content, keys = far // 2 * TILE, far // 2 * TILE + LANES
    in_w_grad = jnp.concatenate(
        in_order(gate_total, swap(gate_total), core)
        + in_order(near_total, swap(near_total), core)
        + [far_rows[0][:content], far_rows[1][:content]]
        + [far_rows[0][content:keys], far_rows[1][content:keys], far_rows[0][keys : keys + HEADS]],
        axis=0,
    ).astype(F32).T

    found, start = [], 0
    for part in grads:
        found.append(row[start : start + part.shape[1]])
        start += part.shape[1]
    return (
        block_out,
        hidden_grad,
        found[0],
        in_w_grad,
        found[1].reshape(CONV, -1).T,
        found[2],
        found[3],
        found[4],
        found[5],
        found[6],
        out_w_grad,
    )


def solution(mesh):
    return jax.shard_map(
        shards,
        mesh=mesh,
        in_specs=(
            P(("rep", "shard"), None),
            P(("rep", "shard"), None),
            P("shard"),
            P("shard", None),
            P("shard", None),
            P("shard"),
            P("shard"),
            P("shard"),
            P("shard"),
            P("shard"),
            P("shard", None),
            P(("rep", "shard")),
            P(("rep", "shard")),
        ),
        out_specs=(
            P(("rep", "shard"), None),
            P(("rep", "shard"), None),
            P("shard"),
            P("shard", None),
            P("shard", None),
            P("shard"),
            P("shard"),
            P("shard"),
            P("shard"),
            P("shard"),
            P("shard", None),
        ),
        check_vma=False,
    )
```

```python
import functools

import jax
import jax.numpy as jnp
from jax import lax
from jax.experimental import pallas as pl
from jax.experimental.pallas import tpu as pltpu
from jax.sharding import PartitionSpec as P

HEADS = 48
HEADDIM = 64
DSTATE = 128
CONV = 4
SPAN = 256
DI = 3072
CC = 3328
TILE = 256
GROUPS = DI // TILE
PER = TILE // HEADDIM
CHUNK = 64
LANES = 128
epsilon = 1e-05
FAR = -1e30
LOG2E = 1.4426950408889634
PACK = 4 * PER

BF = jnp.bfloat16
F32 = jnp.float32
MIB = 1 << 20


def dot(lhs, rhs):
    return jnp.dot(lhs, rhs, preferred_element_type=F32)


def dot_nt(lhs, rhs):
    return lax.dot_general(lhs, rhs, (((1,), (1,)), ((), ())), preferred_element_type=F32)


def dot_tn(lhs, rhs):
    return lax.dot_general(lhs, rhs, (((0,), (0,)), ((), ())), preferred_element_type=F32)


def sigmoid(value):
    return 0.5 * jnp.tanh(0.5 * value) + 0.5


def pieces(value):
    high = value.astype(BF)
    rest = value - high.astype(F32)
    middle = rest.astype(BF)
    low = (rest - middle.astype(F32)).astype(BF)
    return high, middle, low


def fine_dot(lhs, rhs, product):
    high, middle, low = pieces(lhs)
    return product(high, rhs) + (product(middle, rhs) + product(low, rhs))


def row_ids(start, shape):
    return start + lax.broadcasted_iota(jnp.int32, shape, 0)


def live_rows(meta, start, shape):
    ids = row_ids(start, shape)
    return (ids >= meta[1]) & (ids < meta[1] + meta[2])


def gather_lanes(target, blocks, table, at):
    for j, block in enumerate(blocks):
        width = block.shape[1]
        lanes = pl.ds(pl.multiple_of(table[at + j] * width, LANES), width)
        target[0 : block.shape[0], lanes] = block[...]


def call(
    body, name, meta, operands, in_specs, outs, out_specs, scratch, grid, flops, moved, filled=None
):
    if filled:
        first = len(operands) + 1
        operands, extra = operands + tuple(filled.values()), len(filled)
        in_specs = in_specs + [pl.BlockSpec(memory_space=pl.ANY)] * extra
        aliases = {first + n: place for n, place in enumerate(filled)}
        inner, many = body, first - 1

        def body(meta, *refs):
            return inner(meta, *refs[:many], *refs[many + extra :])
    else:
        aliases = {}
    return pl.pallas_call(
        body,
        name=name,
        grid_spec=pltpu.PrefetchScalarGridSpec(
            num_scalar_prefetch=1,
            grid=(grid,),
            in_specs=in_specs,
            out_specs=out_specs,
            scratch_shapes=scratch,
        ),
        out_shape=outs,
        input_output_aliases=aliases,
        compiler_params=pltpu.CompilerParams(vmem_limit_bytes=60 * MIB),
        cost_estimate=pl.CostEstimate(flops=flops, bytes_accessed=moved, transcendentals=0),
    )(meta, *operands)


def whole(shape):
    rank = len(shape)
    return pl.BlockSpec(shape, lambda i, meta: (0,) * rank)


def tiles(rows, width, shift=0, last=None):
    def index(i, meta):
        at = i + shift
        if last is not None:
            at = jnp.clip(at, 0, last)
        return (0, at)

    return pl.BlockSpec((rows, width), index)


def shape_of(shape, kind=F32):
    return jax.ShapeDtypeStruct(shape, kind)


TABLE = 4
UNITS = 4
OUT_TABLE = TABLE + 2 * UNITS
WIDE = 512
WIDES = DI // WIDE


def own_tile(i, meta):
    half = WIDES // 2
    return jnp.where(i < half, meta[0] * half + i, (1 - meta[0]) * half + i - half)


def live_lanes(meta, live):
    live[...] = jnp.where(live_rows(meta, 0, live.shape), 1.0, 0.0)


def convolve(low, taps, live, shifted, masked, signal, slope, begin):
    for lane in range(0, low.shape[1], LANES):
        cut = slice(begin + lane, begin + lane + LANES)
        tile = (begin + lane) // LANES
        for at in range(0, low.shape[0], CHUNK):
            part = low[at : at + CHUNK, lane : lane + LANES].astype(BF).astype(F32)
            part = part * live[at : at + CHUNK, :]
            masked[at : at + CHUNK, cut] = part.astype(BF)
            shifted[tile, 8 + at : 8 + at + CHUNK, :] = part
        for at in range(0, low.shape[0], CHUNK):
            out = taps[4:5, cut]
            for k in range(CONV):
                out = out + shifted[tile, at + 5 + k : at + 5 + k + CHUNK, :] * taps[k : k + 1, cut]
            sigma = sigmoid(out)
            out = out * sigma
            here = live[at : at + CHUNK, :]
            signal[at : at + CHUNK, cut] = (out * here).astype(BF)
            slope[at : at + CHUNK, cut] = (sigma + out * (1.0 - sigma)) * here


def conv_body(meta, x, taps, taps_keys, steps, *refs):
    count = UNITS
    own, rest, key_rows, dts = (refs[n * count : (n + 1) * count] for n in range(4))
    (masked, signal, slope, masked_keys, keys, slope_keys, columns, rows, trio,
     weight, weight_dt, shifted, live) = refs[4 * count :]
    tokens = x.shape[0]
    step = pl.program_id(0)

    @pl.when(step == 0)
    def _():
        conv_start(meta, shifted, live)
        gather_lanes(weight, key_rows, meta, TABLE)
        gather_lanes(weight_dt, dts, meta, TABLE)
        low = dot_nt(x[...], weight[0:TILE, :])
        raw = dot_nt(x[...], weight_dt[...]).astype(BF).astype(F32)
        convolve(low, taps_keys, live, shifted, masked_keys, keys, slope_keys, 0)
        raw = jnp.concatenate([raw, jnp.zeros((tokens, LANES - raw.shape[1]), F32)], axis=1)
        pre = raw + steps[0:1, :]
        size = jnp.maximum(pre, 0.0) + jnp.log1p(jnp.exp(-jnp.abs(pre)))
        rate = size * steps[1:2, :]
        lower = row_ids(0, (SPAN, SPAN)) >= lax.broadcasted_iota(jnp.int32, (SPAN, SPAN), 1)
        lower = jnp.where(lower, 1.0, 0.0).astype(BF)
        trio[0] = pre
        trio[1] = size
        for at in range(0, tokens, SPAN):
            high, middle, small = pieces(rate[at : at + SPAN])
            trio[2, at : at + SPAN, :] = dot(lower, high) + (dot(lower, middle) + dot(lower, small))
        log = trio[2] * LOG2E
        less = log - jnp.log(size) * LOG2E
        factor = jnp.concatenate(
            [jnp.exp2(log[SPAN - 1 : SPAN] - less[:SPAN]), jnp.exp2(log[SPAN:])], axis=0
        )
        high = factor.astype(BF).astype(F32)
        rest_factor = factor - high
        less_rows = less.T
        log_rows = log.T
        for g in range(GROUPS):
            a, b = g * PER, (g + 1) * PER
            columns[g] = jnp.concatenate(
                [log[:, a:b], less[:, a:b], high[:, a:b], rest_factor[:, a:b]], axis=1
            )
            rows[g] = jnp.concatenate([log_rows[a:b], less_rows[a:b]], axis=0)

    @pl.when(step > 0)
    def _():
        conv_tile(
            meta, step == 1, x, taps, own, rest, masked, signal, slope, weight, shifted, live
        )


def conv_start(meta, shifted, live):
    shifted[:, 0:8, :] = jnp.zeros((WIDE // LANES, 8, LANES), F32)
    live_lanes(meta, live)


def conv_tile(
    meta, is_own, x, taps, own, rest, masked, signal, slope, weight, shifted, live
):
    @pl.when(is_own)
    def _():
        gather_lanes(weight, own, meta, TABLE)

    @pl.when(jnp.logical_not(is_own))
    def _():
        gather_lanes(weight, rest, meta, TABLE + UNITS)

    lows = [dot_nt(x[...], weight[at : at + TILE, :]) for at in range(0, WIDE, TILE)]
    for n, low in enumerate(lows):
        convolve(low, taps, live, shifted, masked, signal, slope, n * TILE)


def conv_more_body(meta, x, taps, *refs):
    own, rest = refs[:UNITS], refs[UNITS : 2 * UNITS]
    masked, signal, slope, weight, shifted, live = refs[2 * UNITS :]
    step = pl.program_id(0)

    @pl.when(step == 0)
    def _():
        conv_start(meta, shifted, live)

    conv_tile(
        meta, step < WIDES // 2 - 1, x, taps, own, rest, masked, signal, slope, weight, shifted, live
    )


def conv_forward(meta, x, taps, steps, own, rest, local):
    tokens, width = x.shape
    count = UNITS
    part = width // count
    half = WIDES // 2

    def tile(rows):
        def index(i, meta):
            return (0, jnp.where(i < 2, meta[0], 1 - meta[0]) * half)

        return pl.BlockSpec((rows, WIDE), index)

    first_spec = pl.BlockSpec((WIDE, part), lambda i, meta: (0, 0))
    local_spec = pl.BlockSpec((WIDE, part), lambda i, meta: (WIDES + (1 - meta[0]) * half, 0))
    key_spec = pl.BlockSpec((TILE, part), lambda i, meta: (WIDE // TILE, 0))
    dt_spec = pl.BlockSpec((64, part), lambda i, meta: ((WIDE + TILE) // 64, 0))
    return call(
        conv_body, "conv_forward", meta,
        (x, taps, taps, steps) + tuple(own) + (() if local is None else (local,)) + tuple(rest)
        + tuple(own) * 2,
        [
            whole((tokens, width)), tile(8), pl.BlockSpec((8, TILE), lambda i, meta: (0, DI // TILE)),
            whole((8, LANES)),
        ]
        + [first_spec] * count
        + [first_spec if local is None else local_spec] + [first_spec] * (count - 1)
        + [key_spec] * count + [dt_spec] * count,
        [
            shape_of((tokens, DI), BF), shape_of((tokens, DI), BF), shape_of((tokens, DI)),
            shape_of((tokens, TILE), BF), shape_of((tokens, TILE), BF), shape_of((tokens, TILE)),
            shape_of((GROUPS, tokens, PACK)), shape_of((GROUPS, 2 * PER, tokens)),
            shape_of((3, tokens, LANES)),
        ],
        [
            tile(tokens), tile(tokens), tile(tokens),
            whole((tokens, TILE)), whole((tokens, TILE)), whole((tokens, TILE)),
            whole((GROUPS, tokens, PACK)), whole((GROUPS, 2 * PER, tokens)),
            whole((3, tokens, LANES)),
        ],
        [
            pltpu.VMEM((WIDE, width), BF), pltpu.VMEM((64, width), BF),
            pltpu.VMEM((WIDE // LANES, tokens + 8, LANES), F32), pltpu.VMEM((tokens, LANES), F32),
        ],
        3, 2 * tokens * width * 3 * WIDE, 24 * MIB,
    )


def conv_more(meta, x, taps, own, rest, local, filled):
    tokens, width = x.shape
    part = width // UNITS
    half = WIDES // 2
    tail = half - 1

    def natural(i, meta):
        own_half = jnp.where(i < tail, meta[0], 1 - meta[0])
        return own_half * half + 1 + jnp.where(i < tail, i, i - tail)

    def tile(rows):
        return pl.BlockSpec((rows, WIDE), lambda i, meta: (0, natural(i, meta)))

    own_spec = pl.BlockSpec((WIDE, part), lambda i, meta: (jnp.minimum(i, tail - 1), 0))
    rest_spec = pl.BlockSpec((WIDE, part), lambda i, meta: (jnp.maximum(i - tail, 0), 0))
    local_spec = pl.BlockSpec(
        (WIDE, part),
        lambda i, meta: (WIDES + (1 - meta[0]) * half + 1 + jnp.maximum(i - tail, 0), 0),
    )
    return call(
        conv_more_body, "conv_more", meta,
        (x, taps) + tuple(own) + (() if local is None else (local,)) + tuple(rest),
        [whole((tokens, width)), tile(8)] + [own_spec] * UNITS
        + [rest_spec if local is None else local_spec] + [rest_spec] * (UNITS - 1),
        [shape_of((tokens, DI), BF), shape_of((tokens, DI), BF), shape_of((tokens, DI))],
        [tile(tokens)] * 3,
        [
            pltpu.VMEM((WIDE, width), BF), pltpu.VMEM((WIDE // LANES, tokens + 8, LANES), F32),
            pltpu.VMEM((tokens, LANES), F32),
        ],
        2 * tail, 2 * tokens * width * 2 * tail * WIDE, 20 * MIB,
        dict(enumerate(filled)),
    )


def lane_half(shape, half):
    ids = lax.broadcasted_iota(jnp.int32, shape, 1)
    return (ids >= HEADDIM) if half else (ids < HEADDIM)


def heads_apart(value, ones):
    return jnp.concatenate([value * ones[0:1], value * ones[1:2]], axis=0)


def heads_together(stacked):
    middle = stacked.shape[0] // 2
    upper = stacked[:middle]
    return jnp.where(lane_half(upper.shape, 0), upper, stacked[middle:])


def head_lanes(shape, width):
    lane = lax.broadcasted_iota(jnp.int32, shape, 1) // width
    row = lax.broadcasted_iota(jnp.int32, shape, 0) % PER
    return jnp.where(lane == row, 1.0, 0.0).astype(BF)


def scan_body(
    meta, content, keys, columns, rows, skip, out, entering,
    scores, write_rows, mixes, blocked, spread,
):
    half = SPAN // 2

    @pl.when(pl.program_id(0) == 0)
    def _():
        for span in range(2):
            at = span * SPAN
            scores[span] = dot_nt(keys[at : at + SPAN, DSTATE:], keys[at : at + SPAN, :DSTATE])
        write_rows[...] = keys[0:SPAN, :DSTATE].astype(F32).T.astype(BF)
        mixes[...] = jnp.zeros_like(mixes)
        after = row_ids(0, blocked.shape) >= lax.broadcasted_iota(jnp.int32, blocked.shape, 1)
        blocked[...] = jnp.where(after, 0.0, FAR)
        spread[...] = head_lanes(spread.shape, HEADDIM)

    factor = dot(columns[0, :, 2 * PER :].astype(BF), spread[...])
    first = content[0:SPAN, :].astype(F32)
    state = dot(write_rows[...], (first * factor[:SPAN]).astype(BF)).astype(BF)
    entering[0] = state
    out[0:SPAN, :] = skip[...] * first
    carried = dot(keys[SPAN:, DSTATE:], state) * factor[SPAN:]
    out[SPAN:, :] = carried + skip[...] * content[SPAN:, :].astype(F32)
    for pair in range(PER // 2):
        lanes = slice(pair * 2 * HEADDIM, (pair + 1) * 2 * HEADDIM)
        for h in range(2):
            n = 2 * pair + h
            for span in range(2):
                for at in range(0, SPAN, CHUNK):
                    row = span * SPAN + at
                    corner = at // half * half
                    log = columns[0, row : row + CHUNK, n : n + 1]
                    for begin in range(0, corner + half, half):
                        cut = slice(begin, begin + half)
                        less = rows[0, PER + n : PER + n + 1, span * SPAN + begin : span * SPAN + begin + half]
                        decay = log - less
                        if begin == corner:
                            decay = decay + blocked[at - begin : at - begin + CHUNK, :]
                        mix = scores[span, at : at + CHUNK, cut] * jnp.exp2(decay)
                        mixes[pair, span, h * SPAN + at : h * SPAN + at + CHUNK, cut] = mix.astype(BF)
        for span in range(2):
            at = span * SPAN
            value = content[at : at + SPAN, lanes]
            out[at : at + SPAN, lanes] += heads_together(dot(mixes[pair, span], value))


def scan_forward(meta, signal, keys, columns, rows, skip):
    tokens = signal.shape[0]
    return call(
        scan_body, "scan_forward", meta, (signal, keys, columns, rows, skip),
        [
            tiles(tokens, TILE), whole((tokens, TILE)),
            pl.BlockSpec((1, tokens, PACK), lambda i, meta: (i, 0, 0)),
            pl.BlockSpec((1, 2 * PER, tokens), lambda i, meta: (i, 0, 0)),
            tiles(1, TILE),
        ],
        [shape_of((tokens, DI)), shape_of((GROUPS, DSTATE, TILE), BF)],
        [tiles(tokens, TILE), pl.BlockSpec((1, DSTATE, TILE), lambda i, meta: (i, 0, 0))],
        [
            pltpu.VMEM((2, SPAN, SPAN), F32), pltpu.VMEM((DSTATE, SPAN), BF),
            pltpu.VMEM((PER // 2, 2, 2 * SPAN, SPAN), BF), pltpu.VMEM((SPAN // 2, SPAN // 2), F32),
            pltpu.VMEM((2 * PER, TILE), BF),
        ],
        GROUPS, 10 * 10**9, 12 * MIB,
    )


def gate_body(meta, x, mixed, gain, *refs):
    count = UNITS
    own, rest = refs[:count], refs[count : 2 * count]
    gate, normed, theirs, scale, weight, gated, total = refs[2 * count :]
    step = pl.program_id(0)
    tokens = x.shape[0]

    @pl.when(step < WIDES // 2)
    def _():
        gather_lanes(weight, own, meta, TABLE)

    @pl.when(step >= WIDES // 2)
    def _():
        gather_lanes(weight, rest, meta, TABLE + count)

    @pl.when(step == 0)
    def _():
        total[...] = jnp.zeros_like(total)

    here = own_tile(step, meta) * WIDE
    lows = [dot_nt(x[...], weight[at : at + TILE, :]).astype(BF) for at in range(0, WIDE, TILE)]
    for n, low in enumerate(lows):
        lanes = slice(n * TILE, (n + 1) * TILE)
        place = pl.ds(pl.multiple_of(here + n * TILE, TILE), TILE)
        gate[:, lanes] = low
        for at in range(0, tokens, CHUNK):
            part = low[at : at + CHUNK].astype(F32)
            part = mixed[at : at + CHUNK, lanes] * (part * sigmoid(part))
            gated[at : at + CHUNK, place] = part
            square = part * part
            total[at : at + CHUNK, :] += square[:, :LANES] + square[:, LANES:]

    @pl.when(step == pl.num_programs(0) - 1)
    def _():
        mean = jnp.sum(total[...], axis=1, keepdims=True) / DI
        scale[...] = lax.rsqrt(mean + epsilon)

        def finish(n, carry):
            place = pl.ds(pl.multiple_of(n * CHUNK, CHUNK), CHUNK)
            factor = jnp.broadcast_to(scale[place, :], (CHUNK, LANES))
            for at in range(0, DI, LANES):
                part = gated[place, at : at + LANES] * factor * gain[:, at : at + LANES]
                normed[place, at : at + LANES] = part.astype(BF)
            return carry

        lax.fori_loop(0, tokens // CHUNK, finish, 0)
        half = DI // (2 * count)
        for k in range(count):
            other = pl.multiple_of((2 * k + 1 - meta[0]) * half, LANES)
            theirs[:, k * half : (k + 1) * half] = normed[:, pl.ds(other, half)]


def gate_forward(meta, x, mixed, gain, own, rest, local):
    tokens, width = x.shape
    count = UNITS
    part = width // count
    half = WIDES // 2
    tile_spec = pl.BlockSpec((tokens, WIDE), lambda i, meta: (0, own_tile(i, meta)))
    own_spec = pl.BlockSpec((WIDE, part), lambda i, meta: (jnp.minimum(i, half - 1), 0))
    rest_spec = pl.BlockSpec((WIDE, part), lambda i, meta: (jnp.maximum(i - half, 0), 0))
    local_spec = pl.BlockSpec(
        (WIDE, part), lambda i, meta: ((1 - meta[0]) * half + jnp.maximum(i - half, 0), 0)
    )
    return call(
        gate_body, "gate_forward", meta,
        (x, mixed, gain) + tuple(own) + (() if local is None else (local,)) + tuple(rest),
        [whole((tokens, width)), tile_spec, whole((1, DI))] + [own_spec] * count
        + [rest_spec if local is None else local_spec] + [rest_spec] * (count - 1),
        [
            shape_of((tokens, DI), BF), shape_of((tokens, DI), BF), shape_of((tokens, DI // 2), BF),
            shape_of((tokens, 1)),
        ],
        [tile_spec, whole((tokens, DI)), whole((tokens, DI // 2)), whole((tokens, 1))],
        [
            pltpu.VMEM((WIDE, width), BF), pltpu.VMEM((tokens, DI), F32),
            pltpu.VMEM((tokens, LANES), F32),
        ],
        WIDES, 2 * tokens * width * DI, 28 * MIB,
    )


def out_body(meta, *refs):
    count = UNITS
    normed, pulled, hidden = refs[0:2], refs[2], refs[3]
    own, rest = refs[4 : 4 + count], refs[4 + count : 4 + 2 * count]
    block, back, total, weight, branch = refs[4 + 2 * count :]
    step = pl.program_id(0)
    tokens = pulled.shape[0]
    half = DI // (2 * count)

    @pl.when(step == 0)
    def _():
        total[...] = jnp.zeros_like(total)

    for j in range(count):
        @pl.when(step == j)
        def _(j=j):
            weight[0:half, :] = own[j][...]
            weight[half:, :] = rest[j][...]

    normed_both = jnp.concatenate([normed[0][...], normed[1][...]], axis=1)
    grads = dot_nt(pulled[...], weight[...]).astype(BF)
    more = dot(normed_both, weight[...])

    @pl.when(step == 0)
    def _():
        branch[...] = more

    @pl.when((step > 0) & (step < count - 1))
    def _():
        branch[...] += more

    for side in range(2):
        at = meta[OUT_TABLE + side * count + step] * half
        back[:, pl.ds(pl.multiple_of(at, LANES), half)] = grads[:, side * half : (side + 1) * half]
    for at in range(0, tokens, CHUNK):
        sums = None
        for lane in range(0, 2 * half, LANES):
            one = grads[at : at + CHUNK, lane : lane + LANES].astype(F32)
            one = one * normed_both[at : at + CHUNK, lane : lane + LANES].astype(F32)
            sums = one if sums is None else sums + one
        total[at : at + CHUNK, :] += sums

    @pl.when(step == count - 1)
    def _():
        for at in range(0, tokens, CHUNK):
            part = branch[at : at + CHUNK, :] + more[at : at + CHUNK, :]
            part = jnp.where(live_rows(meta, at, part.shape), part, 0.0)
            block[at : at + CHUNK, :] = (hidden[at : at + CHUNK, :].astype(F32) + part).astype(BF)


def out_forward(meta, normed, pulled, hidden, own, rest, local):
    tokens, width = hidden.shape
    count = UNITS
    half = DI // (2 * count)

    def columns(side):
        return pl.BlockSpec(
            (tokens, half), lambda i, meta: (0, meta[OUT_TABLE + side * count + i])
        )

    def local_spec(side):
        return pl.BlockSpec((half, width), lambda i, meta: (meta[0] if side == 0 else 1 - meta[0], 0))

    first = () if local is None else (local,)

    def weight_specs(side):
        one = whole((half, width)) if local is None else local_spec(side)
        return [one] + [whole((half, width))] * (count - 1)

    return call(
        out_body, "out_forward", meta,
        (normed, normed, pulled, hidden) + (first + tuple(own) + first + tuple(rest)),
        [columns(0), columns(1), whole((tokens, width)), whole((tokens, width))]
        + weight_specs(0) + weight_specs(1),
        [shape_of((tokens, width), BF), shape_of((tokens, DI), BF), shape_of((tokens, LANES))],
        [whole((tokens, width)), whole((tokens, DI)), whole((tokens, LANES))],
        [pltpu.VMEM((2 * half, width), BF), pltpu.VMEM((tokens, width), F32)],
        count, 4 * tokens * width * DI, 24 * MIB,
    )


STEPS = 4


def norm_back_body(
    meta, back, total, mixed, gate, scale, gain, grad_gate, theirs, grad_mixed, grad_gain
):
    step = pl.program_id(0)
    tokens, width = back.shape
    grad_gain[...] = jnp.zeros_like(grad_gain)

    def one(n, carry):
        rows = pl.ds(pl.multiple_of(n * CHUNK, CHUNK), CHUNK)
        r = jnp.broadcast_to(scale[rows, :], (CHUNK, LANES))
        mean = jnp.sum(total[rows, :], axis=1, keepdims=True) / DI
        factor = r * r * mean
        for at in range(0, width, LANES):
            cut = slice(at, at + LANES)
            z = gate[rows, cut].astype(F32)
            sigma = sigmoid(z)
            silu = z * sigma
            out = mixed[rows, cut]
            gated = out * silu
            grad = back[rows, cut].astype(F32) * r
            grad_gain[:, cut] += fold(grad * gated)
            grad = grad * gain[:, cut] - gated * factor
            grad_mixed[rows, cut] = (grad * silu).astype(BF)
            grad_gate[rows, cut] = ((grad * out) * (sigma + silu * (1.0 - sigma))).astype(BF)
        return carry

    lax.fori_loop(0, tokens // CHUNK, one, 0)

    @pl.when(step // (STEPS // 2) == 1 - meta[0])
    def _():
        theirs[...] = grad_gate[...]


def norm_back(meta, back, total, mixed, gate, scale, gain):
    tokens = back.shape[0]
    width = DI // STEPS

    def tile(rows):
        return pl.BlockSpec((rows, width), lambda i, meta: (0, i))

    theirs_spec = pl.BlockSpec(
        (tokens, width),
        lambda i, meta: (0, jnp.clip(i - (1 - meta[0]) * (STEPS // 2), 0, STEPS // 2 - 1)),
    )
    return call(
        norm_back_body, "norm_back", meta, (back, total, mixed, gate, scale, gain),
        [tile(tokens), whole((tokens, LANES)), tile(tokens), tile(tokens), whole((tokens, 1)), tile(1)],
        [
            shape_of((tokens, DI), BF), shape_of((tokens, DI // 2), BF), shape_of((tokens, DI), BF),
            shape_of((8, DI)),
        ],
        [tile(tokens), theirs_spec, tile(tokens), tile(8)],
        [], STEPS, 10**9, 24 * MIB,
    )


def rows_product_body(meta, mine, theirs, pulled, pulled_rest, send, keep):
    total = dot_tn(mine[...], pulled[...]) + dot_tn(theirs[...], pulled_rest[...])
    total = total.astype(BF)
    sent = pl.num_programs(0) // 2

    @pl.when(pl.program_id(0) < sent)
    def _():
        send[0] = total

    @pl.when(pl.program_id(0) >= sent)
    def _():
        keep[0] = total


def rows_product(meta, normed, arrived, arrived_at, pulled, pulled_rest, units):
    tokens, width = pulled.shape
    unit = DI // (2 * UNITS)
    upper = units // 2

    def which(i):
        return lax.rem(i + upper, units)

    result = shape_of((upper, unit, width), BF)
    return call(
        rows_product_body, "rows_product", meta, (normed, arrived, pulled, pulled_rest),
        [
            pl.BlockSpec((tokens, unit), lambda i, meta: (0, meta[OUT_TABLE + which(i)])),
            pl.BlockSpec((tokens, unit), lambda i, meta: (0, meta[arrived_at + which(i)])),
            whole((tokens, width)), whole((tokens, width)),
        ],
        [result, result],
        [
            pl.BlockSpec((1, unit, width), lambda i, meta: (jnp.minimum(i, upper - 1), 0, 0)),
            pl.BlockSpec((1, unit, width), lambda i, meta: (jnp.maximum(i - upper, 0), 0, 0)),
        ],
        [], units, 4 * tokens * width * unit * units, 12 * MIB,
    )


def columns_product_body(plan, meta, *refs):
    parts = len(plan)
    mine, theirs = refs[:parts], refs[parts : 2 * parts]
    here, there, send, keep, right, right_rest = refs[2 * parts :]
    step = pl.program_id(0)
    width = here.shape[1] // UNITS

    @pl.when(step == 0)
    def _():
        for j in range(UNITS):
            lanes = pl.ds(pl.multiple_of(meta[TABLE + j] * width, LANES), width)
            right[:, j * width : (j + 1) * width] = here[:, lanes]
            right_rest[:, j * width : (j + 1) * width] = there[:, lanes]

    for (begin, steps), a, b in zip(plan, mine, theirs):
        @pl.when((step >= begin) & (step < begin + steps))
        def _(a=a, b=b):
            total = (dot_tn(a[...], right[...]) + dot_tn(b[...], right_rest[...])).astype(BF)
            for k in range(UNITS // 2):
                keep[k] = total[:, k * width : (k + 1) * width]
                other = UNITS // 2 + k
                send[k] = total[:, other * width : (other + 1) * width]


def columns_product(meta, parts, normed, normed_rest):
    tokens, width = normed.shape
    part = width // UNITS
    plan, step, mine_specs, theirs_specs = [], 0, [], []

    def spec(begin, steps, start):
        return pl.BlockSpec(
            (tokens, TILE), lambda i, meta: (0, start(meta) + jnp.clip(i - begin, 0, steps - 1))
        )

    for matrix, start, steps, arrived in parts:
        plan.append((step, steps))
        mine_specs.append(spec(step, steps, start))
        theirs_specs.append(spec(step, steps, lambda meta: 0))
        step += steps
    result = shape_of((UNITS // 2, step * TILE, part), BF)
    result_spec = pl.BlockSpec((UNITS // 2, TILE, part), lambda i, meta: (0, i, 0))
    return call(
        functools.partial(columns_product_body, tuple(plan)), "columns_product", meta,
        tuple(p[0] for p in parts) + tuple(p[3] for p in parts) + (normed, normed_rest),
        mine_specs + theirs_specs + [whole((tokens, width))] * 2,
        [result, result], [result_spec, result_spec],
        [pltpu.VMEM((tokens, width), BF), pltpu.VMEM((tokens, width), BF)],
        step, 4 * tokens * step * TILE * width, 12 * MIB,
    )


def conv_back(meta, masked, taps, result, sums, live, grad_conv):
    tokens = masked.shape[0]
    grad_conv[:, tokens:, :] = jnp.zeros((TILE // LANES, 8, LANES), F32)
    sums[...] = jnp.zeros_like(sums)
    for lane in range(0, TILE, LANES):
        cut = slice(lane, lane + LANES)
        totals = [jnp.zeros((8, LANES), F32) for _ in range(CONV + 1)]
        for at in range(0, tokens, CHUNK):
            near = [
                grad_conv[lane // LANES, at + 3 - k : at + 3 - k + CHUNK, :] for k in range(CONV)
            ]
            value = masked[at : at + CHUNK, cut].astype(F32)
            out = near[0] * taps[0:1, cut]
            for k in range(1, CONV):
                out = out + near[k] * taps[k : k + 1, cut]
            result[at : at + CHUNK, cut] = (out * live[at : at + CHUNK, :]).astype(BF)
            for k in range(CONV):
                totals[k] = totals[k] + fold(near[k] * value)
            totals[CONV] = totals[CONV] + fold(near[CONV - 1])
        for k in range(CONV + 1):
            sums[k : k + 1, cut] = jnp.sum(totals[k], axis=0, keepdims=True)


def fold(value):
    return jnp.sum(value.reshape(value.shape[0] // 8, 8, value.shape[1]), axis=0)


def scan_back_body(
    meta, content, keys, grad_out, mixed, entering, columns, rows, skip, masked, slope, taps,
    scores_in, write_in, read_in,
    result, theirs, sums, grad_columns, grad_scores, grad_write, grad_read,
    scores, read_rows, live, grad_conv, mixes, mix_grads, blocked, spread,
):
    half = SPAN // 2

    @pl.when(pl.program_id(0) == 0)
    def _():
        for span in range(2):
            at = span * SPAN
            scores[span] = dot_nt(keys[at : at + SPAN, :DSTATE], keys[at : at + SPAN, DSTATE:])
        read_rows[...] = keys[SPAN:, DSTATE:].astype(F32).T.astype(BF)
        grad_scores[...] = scores_in[...]
        grad_write[...] = write_in[...]
        grad_read[...] = read_in[...]
        mixes[...] = jnp.zeros_like(mixes)
        live_lanes(meta, live)
        after = row_ids(0, blocked.shape) <= lax.broadcasted_iota(jnp.int32, blocked.shape, 1)
        blocked[...] = jnp.where(after, 0.0, FAR)
        spread[...] = head_lanes(spread.shape, HEADDIM)

    def heads_sum(value):
        high = value.astype(BF)
        low = (value - high.astype(F32)).astype(BF)
        return dot_nt(high, spread[...]) + dot_nt(low, spread[...])

    for pair in range(PER // 2):
        lanes = slice(pair * 2 * HEADDIM, (pair + 1) * 2 * HEADDIM)
        ones = spread[2 * pair : 2 * pair + 2, lanes]
        for span in range(2):
            cut = slice(span * SPAN, (span + 1) * SPAN)
            mix_grads[pair, span] = dot_nt(heads_apart(content[cut, lanes], ones), grad_out[cut, lanes])

    factor = dot(columns[0, :, 2 * PER :].astype(BF), spread[...])
    grown = (grad_out[SPAN:, :].astype(F32) * factor[SPAN:]).astype(BF)
    grad_state = dot(read_rows[...], grown).astype(BF)
    grad_read[...] += dot_nt(grown, entering[0])
    worth = (content[0:SPAN, :].astype(F32) * factor[:SPAN]).astype(BF)
    grad_write[...] += dot_nt(worth, grad_state)
    from_state = dot(keys[0:SPAN, :DSTATE], grad_state) * factor[:SPAN]

    for pair in range(PER // 2):
        for h in range(2):
            n = 2 * pair + h
            for span in range(2):
                top = span * SPAN
                for at in range(0, SPAN, CHUNK):
                    less = columns[0, top + at : top + at + CHUNK, PER + n : PER + n + 1]
                    corner = at // half * half
                    for begin in range(corner, SPAN, half):
                        cut = slice(begin, begin + half)
                        decay = rows[0, n : n + 1, top + begin : top + begin + half] - less
                        if begin == corner:
                            decay = decay + blocked[at - begin : at - begin + CHUNK, :]
                        decay = jnp.exp2(decay)
                        row = h * SPAN + at
                        mix = scores[span, at : at + CHUNK, cut] * decay
                        mixes[pair, span, row : row + CHUNK, cut] = mix.astype(BF)
                        change = mix_grads[pair, span, row : row + CHUNK, cut] * decay
                        grad_scores[span, at : at + CHUNK, cut] += change

    lane = lax.broadcasted_iota(jnp.int32, (SPAN, 2 * PER), 1) < PER
    final = row_ids(0, lane.shape) == SPAN - 1
    skips = jnp.zeros((8, TILE), F32)
    for span in range(2):
        cut = slice(span * SPAN, (span + 1) * SPAN)
        value = content[cut, :].astype(F32)
        pull = grad_out[cut, :].astype(F32)
        both = []
        for pair in range(PER // 2):
            lanes = slice(pair * 2 * HEADDIM, (pair + 1) * 2 * HEADDIM)
            both.append(heads_together(dot(mixes[pair, span], grad_out[cut, lanes])))
        both = jnp.concatenate(both, axis=1)
        if span == 0:
            ended = jnp.sum(fold(value * from_state), axis=0, keepdims=True)
            both = both + from_state
        skipped = skip[...] * value
        skips = skips + fold(pull * value)
        written = heads_sum(value * both)
        read = heads_sum(pull * (mixed[cut, :] - skipped))
        if span == 0:
            ended = heads_sum(jnp.broadcast_to(ended, (8, TILE)))[0:1]
            read = read + jnp.where(final, ended, 0.0)
        grad_columns[0, cut, :] = jnp.where(lane, written, read)
        both = (both + skip[...] * pull) * slope[cut, :]
        for k in range(TILE // LANES):
            grad_conv[k, cut, :] = both[:, k * LANES : (k + 1) * LANES]

    conv_back(meta, masked, taps, result, sums, live, grad_conv)
    sums[5:6, :] = jnp.sum(skips, axis=0, keepdims=True)
    half_steps = pl.num_programs(0) // 2
    at_half = pl.program_id(0) // half_steps

    @pl.when(at_half == 1 - meta[0])
    def _():
        theirs[...] = result[...]


def scan_backward(
    meta, signal, keys, grad_out, mixed, entering, columns, rows, skip, masked, slope, taps, kept,
    first, count,
):
    tokens = signal.shape[0]

    def group(*shape):
        return pl.BlockSpec((1,) + shape, lambda i, meta: (i + first, 0, 0))

    def fresh(*shape):
        return pl.BlockSpec((1,) + shape, lambda i, meta: (i, 0, 0))

    kept_specs = [whole((2, SPAN, SPAN)), whole((SPAN, DSTATE)), whole((SPAN, DSTATE))]
    return call(
        scan_back_body, "scan_backward", meta,
        (signal, keys, grad_out, mixed, entering, columns, rows, skip, masked, slope, taps)
        + tuple(kept),
        [
            tiles(tokens, TILE, first), whole((tokens, TILE)),
            tiles(tokens, TILE, first), tiles(tokens, TILE, first), group(DSTATE, TILE),
            group(tokens, PACK),
            group(2 * PER, tokens), tiles(1, TILE, first), tiles(tokens, TILE, first),
            tiles(tokens, TILE, first), tiles(8, TILE, first),
        ]
        + kept_specs,
        [
            shape_of((tokens, count * TILE), BF), shape_of((tokens, count // 2 * TILE), BF),
            shape_of((8, count * TILE)),
            shape_of((count, tokens, 2 * PER)),
            shape_of((2, SPAN, SPAN)), shape_of((SPAN, DSTATE)), shape_of((SPAN, DSTATE)),
        ],
        [
            tiles(tokens, TILE),
            pl.BlockSpec(
                (tokens, TILE),
                lambda i, meta: (0, jnp.clip(i - (1 - meta[0]) * (count // 2), 0, count // 2 - 1)),
            ),
            tiles(8, TILE), fresh(tokens, 2 * PER),
        ]
        + kept_specs,
        [
            pltpu.VMEM((2, SPAN, SPAN), F32), pltpu.VMEM((DSTATE, SPAN), BF),
            pltpu.VMEM((tokens, LANES), F32), pltpu.VMEM((TILE // LANES, tokens + 8, LANES), F32),
            pltpu.VMEM((PER // 2, 2, 2 * SPAN, SPAN), BF),
            pltpu.VMEM((PER // 2, 2, 2 * SPAN, SPAN), F32),
            pltpu.VMEM((SPAN // 2, SPAN // 2), F32), pltpu.VMEM((2 * PER, TILE), BF),
        ],
        count, 3 * 10**9 * count, count * MIB,
    )


def tail_body(parts, meta, *refs):
    keys, masked, slope, taps, trio, steps, grad_scores, grad_write, grad_read = refs[:9]
    grad_columns = refs[9 : 9 + parts]
    result, sums, raw, small, packs, live, grad_conv = refs[9 + parts :]
    tokens = keys.shape[0]
    for span in range(2):
        at = span * SPAN
        write = keys[at : at + SPAN, :DSTATE]
        read = keys[at : at + SPAN, DSTATE:]
        to_write = fine_dot(grad_scores[span], read, dot)
        to_read = fine_dot(grad_scores[span], write, dot_tn)
        if span == 0:
            to_write = to_write + grad_write[...]
        else:
            to_read = to_read + grad_read[...]
        cut = slice(at, at + SPAN)
        grad_conv[0, cut, :] = to_write * slope[cut, :DSTATE]
        grad_conv[1, cut, :] = to_read * slope[cut, DSTATE:]
    live_lanes(meta, live)
    conv_back(meta, masked, taps, result, sums, live, grad_conv)

    blank = jnp.zeros((tokens, LANES - HEADS), F32)
    of_step, of_log = [], []
    for column_ref in grad_columns:
        for g in range(column_ref.shape[0]):
            of_step.append(column_ref[g, :, :PER])
            of_log.append(column_ref[g, :, PER:])
    grad_size = jnp.concatenate(of_step + [blank], axis=1)
    grad_log = jnp.concatenate(of_log + [blank], axis=1) - grad_size
    upper = row_ids(0, (SPAN, SPAN)) <= lax.broadcasted_iota(jnp.int32, (SPAN, SPAN), 1)
    upper = jnp.where(upper, 1.0, 0.0).astype(BF)
    rates = []
    for at in range(0, tokens, SPAN):
        high, middle, low = pieces(grad_log[at : at + SPAN])
        rates.append(dot(upper, high) + (dot(upper, middle) + dot(upper, low)))
    grad_rate = jnp.concatenate(rates, axis=0)
    decay_rate = steps[1:2, :]
    sigma = jax.nn.sigmoid(trio[0])
    size = trio[1]
    tiny = size > 0.0
    share = jnp.where(tiny, sigma / jnp.where(tiny, size, 1.0), 1.0)
    grad_raw = grad_size * share + grad_rate * decay_rate * sigma
    raw[...] = grad_raw.astype(BF)
    small[...] = jnp.zeros_like(small)
    small[0:1, :] = jnp.sum(grad_raw, axis=0, keepdims=True)
    small[1:2, :] = jnp.sum(grad_rate * trio[1], axis=0, keepdims=True) * decay_rate
    for side in range(2):
        at = meta[0] if side == 0 else 1 - meta[0]
        packs[side, :, :LANES] = result[:, pl.ds(pl.multiple_of(at * LANES, LANES), LANES)]
        packs[side, :, LANES:] = raw[...]


def tail_backward(meta, keys, masked, slope, taps, trio, steps, kept, grad_columns):
    tokens = keys.shape[0]
    last = DI // TILE
    key_spec = whole((tokens, TILE))
    return call(
        functools.partial(tail_body, len(grad_columns)), "tail_backward", meta,
        (keys, masked, slope, taps, trio, steps) + tuple(kept) + tuple(grad_columns),
        [
            key_spec, key_spec, key_spec, pl.BlockSpec((8, TILE), lambda i, meta: (0, last)),
            whole((3, tokens, LANES)), whole((8, LANES)), whole((2, SPAN, SPAN)),
            whole((SPAN, DSTATE)), whole((SPAN, DSTATE)),
        ]
        + [whole(part.shape) for part in grad_columns],
        [
            shape_of((tokens, TILE), BF), shape_of((8, TILE)), shape_of((tokens, LANES), BF),
            shape_of((8, LANES)), shape_of((2, tokens, TILE), BF),
        ],
        [
            whole((tokens, TILE)), whole((8, TILE)), whole((tokens, LANES)), whole((8, LANES)),
            whole((2, tokens, TILE)),
        ],
        [pltpu.VMEM((tokens, LANES), F32), pltpu.VMEM((TILE // LANES, tokens + 8, LANES), F32)],
        1, 1, 1,
    )


def input_body(plan, first, last, meta, *refs):
    count = UNITS
    grads = refs[: len(plan)]
    refs = refs[len(plan) :]
    if not first:
        start, refs = refs[0], refs[1:]
    blocks = []
    for begin, steps, half in plan:
        own, refs = refs[:count], refs[count:]
        rest = None
        if half is not None:
            rest, refs = refs[:count], refs[count:]
        blocks.append((own, rest))
    step = pl.program_id(0)

    if last:
        hidden, out_grad, scale, gain, result, gain_grad, weight, weight_dt, total, folded = refs
    else:
        total, weight = refs

    @pl.when(step == 0)
    def _():
        total[...] = jnp.zeros_like(total) if first else start[...]

    for n, (begin, steps, half) in enumerate(plan):
        @pl.when((step >= begin) & (step < begin + steps))
        def _(n=n, half=half):
            own, rest = blocks[n]
            rows = own[0].shape[0]
            if grads[n].shape[1] == LANES:
                weight_dt[...] = jnp.zeros_like(weight_dt)
                gather_lanes(weight_dt, own, meta, TABLE)
                total[...] += dot(grads[n][...], weight_dt[...])
                return
            if half is None:
                gather_lanes(weight, own, meta, TABLE)
            else:
                @pl.when(meta[0] == half)
                def _():
                    gather_lanes(weight, own, meta, TABLE)

                @pl.when(meta[0] != half)
                def _():
                    gather_lanes(weight, rest, meta, TABLE + count)

            total[...] += dot(grads[n][...], weight[0:rows, :])

    if not last:
        return

    @pl.when(step == pl.num_programs(0) - 1)
    def _():
        tokens, width = hidden.shape
        folded[...] = jnp.zeros_like(folded)

        def finish(n, carry):
            rows = pl.ds(pl.multiple_of(n * 32, 32), 32)
            r = jnp.broadcast_to(scale[rows, :], (32, LANES))
            sums = jnp.zeros((32, LANES), F32)
            for at in range(0, width, LANES):
                cut = slice(at, at + LANES)
                both = total[rows, cut] * hidden[rows, cut].astype(F32)
                folded[:, cut] += fold(both * r)
                sums = sums + both * gain[:, cut]
            mean = jnp.sum(sums, axis=1, keepdims=True) / width
            factor = r * r * r * mean
            for at in range(0, width, LANES):
                cut = slice(at, at + LANES)
                value = r * (total[rows, cut] * gain[:, cut]) - hidden[rows, cut].astype(F32) * factor
                result[rows, cut] = value + out_grad[rows, cut].astype(F32)
            return carry

        lax.fori_loop(0, tokens // 32, finish, 0)
        gain_grad[...] = jnp.sum(folded[...], axis=0, keepdims=True)


def input_backward(meta, start, parts, tokens, width, last=None):
    part = width // UNITS
    plan, step, grad_specs, block_specs, grads, blocks = [], 0, [], [], [], []

    def grad_spec(columns, begin, steps, first):
        return pl.BlockSpec(
            (tokens, columns), lambda i, meta: (0, first + jnp.clip(i - begin, 0, steps - 1))
        )

    def row_spec(rows, begin, steps, first, when):
        def index(i, meta):
            at = first + jnp.clip(i - begin, 0, steps - 1)
            return (at if when is None else jnp.where(when(meta), at, first), 0)

        return pl.BlockSpec((rows, part), index)

    def is_half(half):
        return lambda meta: meta[0] == half

    def not_half(half):
        return lambda meta: meta[0] != half

    for grad, grad_first, steps, half, own, own_first, rest, rest_first, local_first in parts:
        columns = WIDE if half is not None else grad.shape[1]
        row_tile = 64 if columns == LANES else columns
        plan.append((step, steps, half))
        grads.append(grad)
        grad_specs.append(grad_spec(columns, step, steps, grad_first))
        when = None if half is None else is_half(half)
        for matrix in own:
            blocks.append(matrix)
            block_specs.append(row_spec(row_tile, step, steps, own_first, when))
        if half is not None:
            for j, matrix in enumerate(rest):
                blocks.append(matrix)
                row = local_first if j == 0 else rest_first
                block_specs.append(row_spec(row_tile, step, steps, row, not_half(half)))
        step += steps
    more, more_specs = (), []
    outs, out_specs = [shape_of((tokens, width))], [whole((tokens, width))]
    scratch = [pltpu.VMEM((WIDE, width), BF)]
    if last is not None:
        more = tuple(last)
        more_specs = [whole((tokens, width))] * 2 + [whole((tokens, 1)), whole((1, width))]
        outs.append(shape_of((1, width)))
        out_specs.append(whole((1, width)))
        scratch += [
            pltpu.VMEM((LANES, width), BF), pltpu.VMEM((tokens, width), F32),
            pltpu.VMEM((8, width), F32),
        ]
    first = start is None
    return call(
        functools.partial(input_body, tuple(plan), first, last is not None),
        "input_backward", meta,
        tuple(grads) + (() if first else (start,)) + tuple(blocks) + more,
        grad_specs + ([] if first else [whole((tokens, width))]) + block_specs + more_specs,
        outs, out_specs, scratch,
        step, 2 * tokens * width * WIDE * step, 20 * MIB,
    )


def place_body(plan, meta, own, other, out):
    step = pl.program_id(0)
    for begin, steps, half, at in plan:
        @pl.when((step >= begin) & (step < begin + steps))
        def _(begin=begin, half=half, at=at):
            row = at if isinstance(at, int) else at(step - begin)
            rows = out.shape[0] if half is not None else LANES
            row = pl.multiple_of(row, 16)

            def put(source):
                out[0:rows, :] = source[pl.ds(row, rows), :].astype(F32)

            if half == "keys":
                @pl.when(meta[0] == 0)
                def _():
                    out[0:LANES, :] = own[pl.ds(row, LANES), :].astype(F32)
                    out[LANES:, :] = other[pl.ds(row, LANES), :].astype(F32)

                @pl.when(meta[0] == 1)
                def _():
                    out[0:LANES, :] = other[pl.ds(row, LANES), :].astype(F32)
                    out[LANES:, :] = own[pl.ds(row, LANES), :].astype(F32)

                return
            which = 0 if half is None else half

            @pl.when(meta[0] == which)
            def _():
                put(own)

            @pl.when(meta[0] != which)
            def _():
                put(other)


def place_rows(meta, own, other, halves, first, total, filled, last):
    length, width = own.shape
    steps = halves // TILE
    plan = [(h * steps, steps, h, lambda k: k * TILE) for h in range(2)]
    count = 2 * steps
    if last:
        plan += [(count, 1, "keys", halves), (count + 1, 1, None, halves + LANES)]
        count += 2
    return call(
        functools.partial(place_body, plan), "place_rows", meta, (own, other),
        [whole((length, width)), whole((length, width))],
        shape_of((total, width)),
        pl.BlockSpec((TILE, width), lambda i, meta: (first + i, 0)),
        [], count, 10**8, 8 * MIB, None if filled is None else {0: filled},
    )


NEAR = 8


def mirrored(j, count):
    if count != 4:
        return j
    result, bit, other = 0, 1, count // 2
    while bit < count:
        if j & bit:
            result |= other
        bit, other = bit * 2, other // 2
    return result


def hop(x, bit):
    reps, count = lax.axis_size("rep"), lax.axis_size("shard")
    pairs = []
    for r in range(reps):
        flip = bit if r % 2 == 0 else mirrored(bit, count)
        pairs += [(r * count + s, r * count + (s ^ flip)) for s in range(count)]
    return lax.ppermute(x, ("rep", "shard"), pairs)


def swap(x):
    return lax.ppermute(x, "rep", [(r, r ^ 1) for r in range(lax.axis_size("rep"))])


def across(x, bit):
    return lax.ppermute(x, "shard", [(s, s ^ bit) for s in range(lax.axis_size("shard"))])


def along(x, pairs):
    return lax.ppermute(x, "rep", [(2 * a + k, 2 * b + k) for a, b in pairs for k in range(2)])


def settle(keep, arrived):
    middle = keep.shape[0] // 2
    if middle == 0:
        return None, keep.astype(F32) + arrived.astype(F32)
    held = (keep.astype(F32) + arrived.astype(F32)).astype(BF)
    return held[middle:], held[:middle]


def finish_stages(send, keep):
    while send is not None:
        send, keep = settle(keep, hop(send, send.shape[0]))
    return keep[0]


def inward(held):
    if lax.axis_size("rep") // 2 != 4:
        return held, None
    return held, along(held.astype(BF), [(0, 1), (3, 2)])


def middle(state):
    held, arrived = state
    if arrived is None:
        return held, None
    inner = (held + arrived.astype(F32)).astype(BF)
    return inner, along(inner, [(1, 2), (2, 1)])


def outward(state):
    inner, arrived = state
    if arrived is None:
        chips = lax.axis_size("rep") // 2
        total, bit = inner.astype(BF), 1
        while bit < chips:
            more = along(total, [(k, k ^ bit) for k in range(chips)])
            total = (total.astype(F32) + more.astype(F32)).astype(BF)
            bit *= 2
        return total, None
    total = (inner.astype(F32) + arrived.astype(F32)).astype(BF)
    return total, along(total, [(1, 0), (2, 3)])


def summed(state):
    total, arrived = state
    if arrived is None:
        return total
    place = lax.axis_index("rep") // 2
    return jnp.where((place == 1) | (place == 2), total, arrived)


def in_order(own, other, core):
    return [jnp.where(core == 0, own, other), jnp.where(core == 0, other, own)]


def hold(values):
    leaves, tree = jax.tree.flatten(values)
    return jax.tree.unflatten(tree, lax.optimization_barrier(tuple(leaves)))


def add_up(rows):
    while len(rows) > 1:
        rows = [a + b for a, b in zip(rows[::2], rows[1::2])]
    return rows[0]


def group_sum(vector, shard, count):
    vector = vector + swap(vector)
    rows = [lax.dynamic_slice_in_dim(vector, shard ^ j, 1, 0) for j in range(count)]
    return add_up(rows[:1] + [across(row, j) for j, row in enumerate(rows) if j])


def chips_sum(row):
    chips = lax.axis_size("rep") // 2
    return add_up(
        [row] + [along(row, [(k, k ^ d) for k in range(chips)]) for d in range(1, chips)]
    )


def join_lanes(blocks, shard):
    return [
        jnp.concatenate(in_order(blocks[j], blocks[j + 1], shard % 2), axis=1)
        for j in range(0, len(blocks), 2)
    ]


def split_lanes(units, shard):
    half = units.shape[2] // 2
    pairs = in_order(units[:, :, :half], units[:, :, half:], shard % 2)
    return jnp.stack(pairs, axis=1).reshape(2 * units.shape[0], units.shape[1], half)


def pad_lanes(matrix):
    return jnp.pad(matrix, ((0, 0), (0, LANES - matrix.shape[1])))


def shards(
    hidden,
    out_grad,
    norm_gain,
    in_w,
    conv_w,
    conv_b,
    dt_bias,
    a_log,
    skip,
    out_gain,
    out_w,
    lengths,
    offsets,
):
    core = lax.axis_index("rep") % 2
    shard = lax.axis_index("shard")
    count = lax.axis_size("shard")
    tokens, width = hidden.shape
    bits = []
    while 2 ** len(bits) < count:
        bits.append(2 ** len(bits))

    local = in_w.T
    half = DI // 2
    piece = jnp.concatenate(
        [
            lax.dynamic_slice_in_dim(local, DI + core * half, WIDE, 0),
            local[2 * DI :],
            jnp.zeros((16, local.shape[1]), BF),
        ],
        axis=0,
    )
    more_piece = lax.dynamic_slice_in_dim(local, DI + core * half + WIDE, half - WIDE, 0)
    gate_piece = lax.dynamic_slice_in_dim(local, core * half, half, 0)
    out_piece = lax.dynamic_slice_in_dim(out_w, core * (out_w.shape[0] // 2), out_w.shape[0] // 2, 0)

    def spread(first):
        blocks = [first]
        for bit in bits:
            blocks = blocks + [hop(block, bit) for block in blocks]
        return blocks

    paired = count == 4
    small = (norm_gain, conv_w.T, conv_b, dt_bias, a_log, skip, out_gain)
    packed = jnp.concatenate([part.reshape(-1) for part in small])
    everyone = [packed] + [
        lax.ppermute(
            packed, ("rep", "shard"),
            [
                (r * count + s, r * count + (s ^ (j if r % 2 == 0 else mirrored(j, count))))
                for r in range(lax.axis_size("rep"))
                for s in range(count)
            ],
        )
        for j in range(1, count)
    ]
    piece, everyone = hold((piece, everyone))
    everyone = jnp.stack(everyone).astype(F32)
    order = [jnp.where(core == 0, j, mirrored(j, count)) for j in range(count)]
    whose = jnp.stack(order)[jnp.arange(count) ^ shard]
    same = (whose[:, None] == jnp.arange(count)[None]).astype(F32)
    everyone = jnp.sum(same[:, :, None] * everyone[None], axis=1)
    parts, start = [], 0
    for part in small:
        cut = everyone[:, start : start + part.size].reshape((count,) + part.shape)
        cut = jnp.moveaxis(cut, 0, -2)
        parts.append(cut.reshape(part.shape[:-1] + (-1,)))
        start += part.size
    conv_own = spread(piece)
    if paired:
        conv_own[3], more_piece = hold((conv_own[3], more_piece))
        conv_rest = [swap(block) for block in conv_own[1:]]
        more_near = hop(more_piece, 1), hop(more_piece, 2)
        out_local, in_local = out_w, local
    else:
        gate_own = spread(gate_piece)
        out_piece, gate_own = hold((out_piece, gate_own))
        out_own = spread(out_piece)
        more_own = spread(more_piece)
        more_rest = rest_more = join_lanes([swap(block) for block in more_own], shard)
        more_own = join_lanes(more_own, shard)
        conv_rest = rest_conv = join_lanes([swap(block) for block in conv_own], shard)
        gate_rest = rest_gate = join_lanes([swap(block) for block in gate_own], shard)
        conv_own, gate_own = join_lanes(conv_own, shard), join_lanes(gate_own, shard)
        out_full = [jnp.concatenate(in_order(block, swap(block), core), axis=0) for block in out_own]
        out_one, out_two = out_full[:UNITS], out_full[UNITS:]
        out_local = in_local = None

    gain_one, kernel, bias_conv, bias_step, log_rate, skip_full, gain_two = parts
    decay_rate = -jnp.exp(log_rate)

    mine = order
    other = [jnp.where(core == 0, mirrored(j, count), j) for j in range(count)]
    mine, other = [shard ^ j for j in mine], [shard ^ j for j in other]
    if paired:
        out_units = [2 * j + core for j in mine] + [2 * j + 1 - core for j in other]
    else:
        out_units = mine
        mine = other = [j // 2 for j in mine[::2]]
    meta = jnp.stack(
        [core, offsets[0], lengths[0], shard] + mine + other + out_units
    ).astype(jnp.int32)
    taps = jnp.concatenate([kernel, bias_conv[None], jnp.zeros((3, CC), F32)], axis=0)
    steps = jnp.concatenate(
        [pad_lanes(jnp.stack([bias_step, decay_rate])), jnp.zeros((6, LANES), F32)], axis=0
    )
    skip_lanes = jnp.repeat(skip_full, HEADDIM)[None]

    positions = jnp.arange(tokens, dtype=jnp.int32)
    live_mask = ((positions >= offsets[0]) & (positions < offsets[0] + lengths[0])).astype(F32)
    hidden_full = hidden.astype(F32)
    inv_rms = lax.rsqrt(jnp.mean(hidden_full * hidden_full, axis=1, keepdims=True) + epsilon)
    normed = (hidden_full * inv_rms * gain_one).astype(BF)
    pulled = (out_grad.astype(F32) * live_mask[:, None]).astype(BF)
    normed_rest = swap(normed)
    pulled_rest = swap(pulled)

    (masked, signal, slope, masked_keys, keys, slope_keys, columns, rows, trio) = conv_forward(
        meta, normed, taps, steps, conv_own, conv_rest, in_local
    )
    content = [masked, signal, slope]
    if paired:
        more_near, content = hold((more_near, content))
        more_far = hop(more_near[0], 2)
        more_rest = [swap(block) for block in more_near]
        more_far, gate_piece = hold((more_far, gate_piece))
        more_own = [more_piece, *more_near, more_far]
        more_rest.append(swap(more_far))
        gate_near = hop(gate_piece, 1), hop(gate_piece, 2)
    masked, signal, slope = conv_more(meta, normed, taps, more_own, more_rest, in_local, content)
    if paired:
        gate_near, signal = hold((gate_near, signal))
        gate_own = [gate_piece, *gate_near, hop(gate_near[0], 2)]
    mixed, entering = scan_forward(meta, signal, keys, columns, rows, skip_lanes)
    if paired:
        out_piece, gate_far, mixed = hold((out_piece, gate_own[3], mixed))
        gate_own[3] = gate_far
        gate_rest = [swap(block) for block in gate_own[1:]]
        rest_conv, rest_gate = [local] + conv_rest, [local] + gate_rest
        rest_more = [local] + more_rest
        out_near = hop(out_piece, 1), hop(out_piece, 2)
    gate, normed_out, out_theirs, scale = gate_forward(
        meta, normed, mixed, gain_two[None], gate_own, gate_rest, in_local
    )
    out_arrived = swap(out_theirs if paired else normed_out)
    if paired:
        out_near, normed_out = hold((out_near, normed_out))
        out_one = [*out_near, hop(out_near[0], 2)]
        out_two = [swap(block) for block in out_one]

    upper = count // 2
    out_pulls = (pulled, pulled_rest)
    if not paired:
        cut = core * (width // 2)
        out_pulls = [lax.dynamic_slice_in_dim(x, cut, width // 2, 1) for x in out_pulls]

    def product(parts):
        send, keep = columns_product(meta, parts, normed, normed_rest)
        return (send, keep) if paired else (split_lanes(send, shard), split_lanes(keep, shard))

    out_send, out_keep = rows_product(
        meta, normed_out, out_arrived, TABLE if paired else OUT_TABLE, *out_pulls, count
    )
    out_send, out_keep, normed_out = hold((out_send, out_keep, normed_out))
    out_there = hop(out_send, upper)
    block_out, back, total = out_forward(
        meta, normed_out, pulled, hidden, out_one, out_two, out_local
    )
    out_there, total = hold((out_there, total))
    out_send, out_keep = settle(out_keep, out_there)
    out_there = hop(out_send, upper // 2)
    out_keep, total = hold((out_keep, total))
    grad_gate, gate_theirs, grad_mixed, grad_gain_two = norm_back(
        meta, back, total, mixed, gate, scale, gain_two[None]
    )

    gate_theirs, out_there = hold((gate_theirs, out_there))
    gate_arrived = swap(gate_theirs)
    out_line = inward(finish_stages(*settle(out_keep, out_there)))
    out_held, gate_arrived = hold((out_line[0], gate_arrived))
    gate_parts = [(grad_gate, lambda meta: meta[0] * (GROUPS // 2), GROUPS // 2, gate_arrived)]
    gate_send, gate_keep = product(gate_parts)
    gate_send, gate_keep, grad_mixed = hold((gate_send, gate_keep, grad_mixed))
    gate_there = hop(gate_send, upper)
    kept = (
        jnp.zeros((2, SPAN, SPAN), F32),
        jnp.zeros((SPAN, DSTATE), F32),
        jnp.zeros((SPAN, DSTATE), F32),
    )
    near, far = NEAR, GROUPS - NEAR
    part = WIDES // 2
    over = near * TILE // WIDE - part

    def gate_part(half):
        at = half * part
        return [(grad_gate, at, part, half, gate_own, 0, rest_gate, 0, at if paired else 0)]

    def conv_part(grad, grad_first, steps, half, first):
        parts = []
        if first == 0:
            local_first = WIDES + half * part if paired else 0
            parts.append((grad, grad_first, 1, half, conv_own, 0, rest_conv, 0, local_first))
            grad_first, steps, first = grad_first + 1, steps - 1, 1
        if steps:
            local_first = WIDES + half * part + first if paired else first - 1
            parts.append(
                (grad, grad_first, steps, half, more_own, first - 1, rest_more, first - 1, local_first)
            )
        return parts

    grad_near, near_theirs, sums_near, columns_near, *kept = scan_backward(
        meta, signal, keys, grad_mixed, mixed, entering, columns, rows, skip_lanes, masked, slope, taps,
        kept, 0, near,
    )
    near_theirs, out_arrived = hold((near_theirs, out_line[1]))
    near_arrived = swap(near_theirs)
    out_line = middle((out_held, out_arrived))
    kept, grad_gate, out_inner = hold((kept, grad_gate, out_line[0]))
    (partial,) = input_backward(meta, None, gate_part(0), tokens, width)
    gate_there, partial, near_arrived = hold((gate_there, partial, near_arrived))
    gate_send, gate_keep = settle(gate_keep, gate_there)
    gate_there = hop(gate_send, upper // 2)
    gate_keep, near_arrived = hold((gate_keep, near_arrived))
    near_parts = [(grad_near, lambda meta: meta[0] * (near // 2), near // 2, near_arrived)]
    near_send, near_keep = product(near_parts)
    near_there = hop(near_send, upper)
    near_keep, kept, grad_mixed = hold((near_keep, kept, grad_mixed))
    grad_far, far_theirs, sums_far, columns_far, *kept = scan_backward(
        meta, signal, keys, grad_mixed, mixed, entering, columns, rows, skip_lanes, masked, slope, taps,
        kept, near, far,
    )
    far_theirs, out_arrived = hold((far_theirs, out_line[1]))
    far_arrived = swap(far_theirs)
    out_line = outward((out_inner, out_arrived))
    out_done, kept = hold((out_line[0], kept))
    grad_keys, sums_keys, grad_raw, grad_steps, packs = tail_backward(
        meta, keys, masked_keys, slope_keys, taps, trio, steps, kept, (columns_near, columns_far),
    )
    packs_arrived = swap(packs[1])
    packs, gate_there, near_there = hold((packs, gate_there, near_there))
    gate_line = inward(finish_stages(*settle(gate_keep, gate_there)))
    gate_held, packs = hold((gate_line[0], packs))
    far_parts = [
        (grad_far, lambda meta: meta[0] * (far // 2), far // 2, far_arrived),
        (packs[0], lambda meta: 0, 1, packs_arrived),
    ]
    far_send, far_keep = product(far_parts)
    far_there = hop(far_send, upper)
    near_there, far_keep = hold((near_there, far_keep))
    near_send, near_keep = settle(near_keep, near_there)
    near_there = hop(near_send, upper // 2)
    partial, near_keep = hold((partial, near_keep))
    (partial,) = input_backward(meta, partial, gate_part(1), tokens, width)
    partial, far_there = hold((partial, far_there))
    far_send, far_keep = settle(far_keep, far_there)
    far_there = hop(far_send, upper // 2)
    far_keep, near_there, out_arrived = hold((far_keep, near_there, out_line[1]))
    near_line = inward(finish_stages(*settle(near_keep, near_there)))
    out_total = summed((out_done, out_arrived))
    out_other = swap(out_total)
    partial, near_held, far_keep, out_total = hold((partial, near_line[0], far_keep, out_total))
    (partial,) = input_backward(meta, partial, conv_part(grad_near, 0, part, 0, 0), tokens, width)
    partial, far_there = hold((partial, far_there))
    far_line = inward(finish_stages(*settle(far_keep, far_there)))
    far_held, gate_arrived, out_other = hold((far_line[0], gate_line[1], out_other))
    gate_line = middle((gate_held, gate_arrived))
    partial, gate_inner, far_held, out_other = hold((partial, gate_line[0], far_held, out_other))
    (partial,) = input_backward(
        meta, partial,
        conv_part(grad_near, part, over, 1, 0) + conv_part(grad_far, 0, part - over, 1, over),
        tokens, width,
    )
    partial, far_arrived = hold((partial, far_line[1]))
    far_line = middle((far_held, far_arrived))
    far_inner, near_arrived, gate_arrived = hold((far_line[0], near_line[1], gate_line[1]))
    near_line = middle((near_held, near_arrived))
    gate_line = outward((gate_inner, gate_arrived))
    partial, far_inner, near_inner, gate_done = hold((partial, far_inner, near_line[0], gate_line[0]))
    hidden_grad, grad_gain_one = input_backward(
        meta, partial,
        [
            (grad_keys, 0, 1, None, conv_own, WIDE // TILE, None, 0, 0),
            (grad_raw, 0, 1, None, conv_own, (WIDE + TILE) // 64, None, 0, 0),
        ],
        tokens, width, (hidden, out_grad, inv_rms, gain_one[None]),
    )
    grad_gain_one, far_arrived = hold((grad_gain_one, far_line[1]))
    far_line = outward((far_inner, far_arrived))
    far_done, near_arrived, gate_arrived, grad_gain_one = hold(
        (far_line[0], near_line[1], gate_line[1], grad_gain_one)
    )
    near_line = outward((near_inner, near_arrived))
    gate_total = summed((gate_done, gate_arrived))
    gate_other = swap(gate_total)
    sums = jnp.concatenate([sums_near, sums_far, sums_keys], axis=1)
    grads = (
        grad_gain_one[0].reshape(count, -1),
        sums[:CONV].reshape(CONV, count, -1).transpose(1, 0, 2).reshape(count, -1),
        sums[CONV].reshape(count, -1),
        grad_steps[0, :HEADS].reshape(count, -1),
        grad_steps[1, :HEADS].reshape(count, -1),
        jnp.sum(sums[5, :DI].reshape(HEADS, HEADDIM), axis=1).reshape(count, -1),
        jnp.sum(grad_gain_two, axis=0).reshape(count, -1),
    )
    row = group_sum(jnp.concatenate(grads, axis=1), shard, count)
    row, far_arrived, gate_other = hold((row, far_line[1], gate_other))
    far_total = summed((far_done, far_arrived))
    far_other = swap(far_total)
    row = chips_sum(row)[0]
    near_total = summed(near_line)
    near_other = swap(near_total)
    all_rows = local.shape[0]
    rows_so_far = place_rows(meta, gate_total, gate_other, DI // 2, 0, all_rows, None, False)
    rows_so_far = place_rows(
        meta, near_total, near_other, near // 2 * TILE, GROUPS, all_rows, rows_so_far, False
    )
    rows_so_far = place_rows(
        meta, far_total, far_other, far // 2 * TILE, GROUPS + near, all_rows, rows_so_far, True
    )
    in_w_grad = rows_so_far.T

    out_w_grad = jnp.concatenate(
        in_order(out_total, out_other, core), axis=0 if paired else 1
    ).astype(F32)
    found, start = [], 0
    for part in grads:
        found.append(row[start : start + part.shape[1]])
        start += part.shape[1]
    return (
        block_out,
        hidden_grad,
        found[0],
        in_w_grad,
        found[1].reshape(CONV, -1).T,
        found[2],
        found[3],
        found[4],
        found[5],
        found[6],
        out_w_grad,
    )


def solution(mesh):
    return jax.shard_map(
        shards,
        mesh=mesh,
        in_specs=(
            P(("rep", "shard"), None),
            P(("rep", "shard"), None),
            P("shard"),
            P("shard", None),
            P("shard", None),
            P("shard"),
            P("shard"),
            P("shard"),
            P("shard"),
            P("shard"),
            P("shard", None),
            P(("rep", "shard")),
            P(("rep", "shard")),
        ),
        out_specs=(
            P(("rep", "shard"), None),
            P(("rep", "shard"), None),
            P("shard"),
            P("shard", None),
            P("shard", None),
            P("shard"),
            P("shard"),
            P("shard"),
            P("shard"),
            P("shard"),
            P("shard", None),
        ),
        check_vma=False,
    )
```

```python
import functools

import jax
import jax.numpy as jnp
from jax import lax
from jax.experimental import pallas as pl
from jax.experimental.pallas import tpu as pltpu
from jax.sharding import PartitionSpec as P

HEADS = 48
HEADDIM = 64
DSTATE = 128
CONV = 4
SPAN = 256
DI = 3072
CC = 3328
TILE = 256
GROUPS = DI // TILE
PER = TILE // HEADDIM
CHUNK = 64
LANES = 128
epsilon = 1e-05
FAR = -1e30
LOG2E = 1.4426950408889634
PACK = 4 * PER

BF = jnp.bfloat16
F32 = jnp.float32
MIB = 1 << 20


def dot(lhs, rhs):
    return jnp.dot(lhs, rhs, preferred_element_type=F32)


def dot_nt(lhs, rhs):
    return lax.dot_general(lhs, rhs, (((1,), (1,)), ((), ())), preferred_element_type=F32)


def dot_tn(lhs, rhs):
    return lax.dot_general(lhs, rhs, (((0,), (0,)), ((), ())), preferred_element_type=F32)


def sigmoid(value):
    return 0.5 * jnp.tanh(0.5 * value) + 0.5


def pieces(value):
    high = value.astype(BF)
    rest = value - high.astype(F32)
    middle = rest.astype(BF)
    low = (rest - middle.astype(F32)).astype(BF)
    return high, middle, low


def fine_dot(lhs, rhs, product):
    high, middle, low = pieces(lhs)
    return product(high, rhs) + (product(middle, rhs) + product(low, rhs))


def row_ids(start, shape):
    return start + lax.broadcasted_iota(jnp.int32, shape, 0)


def live_rows(meta, start, shape):
    ids = row_ids(start, shape)
    return (ids >= meta[1]) & (ids < meta[1] + meta[2])


def gather_lanes(target, blocks, table, at):
    for j, block in enumerate(blocks):
        width = block.shape[1]
        lanes = pl.ds(pl.multiple_of(table[at + j] * width, LANES), width)
        target[0 : block.shape[0], lanes] = block[...]


def call(
    body, name, meta, operands, in_specs, outs, out_specs, scratch, grid, flops, moved, filled=None
):
    if filled:
        first = len(operands) + 1
        operands, extra = operands + tuple(filled.values()), len(filled)
        in_specs = in_specs + [pl.BlockSpec(memory_space=pl.ANY)] * extra
        aliases = {first + n: place for n, place in enumerate(filled)}
        inner, many = body, first - 1

        def body(meta, *refs):
            return inner(meta, *refs[:many], *refs[many + extra :])
    else:
        aliases = {}
    return pl.pallas_call(
        body,
        name=name,
        grid_spec=pltpu.PrefetchScalarGridSpec(
            num_scalar_prefetch=1,
            grid=(grid,),
            in_specs=in_specs,
            out_specs=out_specs,
            scratch_shapes=scratch,
        ),
        out_shape=outs,
        input_output_aliases=aliases,
        compiler_params=pltpu.CompilerParams(vmem_limit_bytes=60 * MIB),
        cost_estimate=pl.CostEstimate(flops=flops, bytes_accessed=moved, transcendentals=0),
    )(meta, *operands)


def whole(shape):
    rank = len(shape)
    return pl.BlockSpec(shape, lambda i, meta: (0,) * rank)


def tiles(rows, width, shift=0, last=None):
    def index(i, meta):
        at = i + shift
        if last is not None:
            at = jnp.clip(at, 0, last)
        return (0, at)

    return pl.BlockSpec((rows, width), index)


def shape_of(shape, kind=F32):
    return jax.ShapeDtypeStruct(shape, kind)


TABLE = 4
UNITS = 4
OUT_TABLE = TABLE + 2 * UNITS
WIDE = 512
WIDES = DI // WIDE


def own_tile(i, meta):
    half = WIDES // 2
    return jnp.where(i < half, meta[0] * half + i, (1 - meta[0]) * half + i - half)


def live_lanes(meta, live):
    live[...] = jnp.where(live_rows(meta, 0, live.shape), 1.0, 0.0)


def convolve(low, taps, live, shifted, masked, signal, slope, begin):
    for lane in range(0, low.shape[1], LANES):
        cut = slice(begin + lane, begin + lane + LANES)
        tile = (begin + lane) // LANES
        for at in range(0, low.shape[0], CHUNK):
            part = low[at : at + CHUNK, lane : lane + LANES].astype(BF).astype(F32)
            part = part * live[at : at + CHUNK, :]
            masked[at : at + CHUNK, cut] = part.astype(BF)
            shifted[tile, 8 + at : 8 + at + CHUNK, :] = part
        for at in range(0, low.shape[0], CHUNK):
            out = taps[4:5, cut]
            for k in range(CONV):
                out = out + shifted[tile, at + 5 + k : at + 5 + k + CHUNK, :] * taps[k : k + 1, cut]
            sigma = sigmoid(out)
            out = out * sigma
            here = live[at : at + CHUNK, :]
            signal[at : at + CHUNK, cut] = (out * here).astype(BF)
            slope[at : at + CHUNK, cut] = (sigma + out * (1.0 - sigma)) * here


def conv_body(meta, x, taps, taps_keys, steps, *refs):
    count = UNITS
    own, rest, key_rows, dts = (refs[n * count : (n + 1) * count] for n in range(4))
    (masked, signal, slope, masked_keys, keys, slope_keys, columns, rows, trio,
     weight, weight_dt, shifted, live) = refs[4 * count :]
    tokens = x.shape[0]
    step = pl.program_id(0)

    @pl.when(step == 0)
    def _():
        shifted[:, 0:8, :] = jnp.zeros((WIDE // LANES, 8, LANES), F32)
        live_lanes(meta, live)
        gather_lanes(weight, key_rows, meta, TABLE)
        gather_lanes(weight_dt, dts, meta, TABLE)
        low = dot_nt(x[...], weight[0:TILE, :])
        raw = dot_nt(x[...], weight_dt[...]).astype(BF).astype(F32)
        convolve(low, taps_keys, live, shifted, masked_keys, keys, slope_keys, 0)
        raw = jnp.concatenate([raw, jnp.zeros((tokens, LANES - raw.shape[1]), F32)], axis=1)
        pre = raw + steps[0:1, :]
        size = jnp.maximum(pre, 0.0) + jnp.log1p(jnp.exp(-jnp.abs(pre)))
        rate = size * steps[1:2, :]
        lower = row_ids(0, (SPAN, SPAN)) >= lax.broadcasted_iota(jnp.int32, (SPAN, SPAN), 1)
        lower = jnp.where(lower, 1.0, 0.0).astype(BF)
        trio[0] = pre
        trio[1] = size
        for at in range(0, tokens, SPAN):
            high, middle, small = pieces(rate[at : at + SPAN])
            trio[2, at : at + SPAN, :] = dot(lower, high) + (dot(lower, middle) + dot(lower, small))
        log = trio[2] * LOG2E
        less = log - jnp.log(size) * LOG2E
        factor = jnp.concatenate(
            [jnp.exp2(log[SPAN - 1 : SPAN] - less[:SPAN]), jnp.exp2(log[SPAN:])], axis=0
        )
        high = factor.astype(BF).astype(F32)
        rest_factor = factor - high
        less_rows = less.T
        log_rows = log.T
        for g in range(GROUPS):
            a, b = g * PER, (g + 1) * PER
            columns[g] = jnp.concatenate(
                [log[:, a:b], less[:, a:b], high[:, a:b], rest_factor[:, a:b]], axis=1
            )
            rows[g] = jnp.concatenate([log_rows[a:b], less_rows[a:b]], axis=0)

    @pl.when((step > 0) & (step <= WIDES // 2))
    def _():
        gather_lanes(weight, own, meta, TABLE)

    @pl.when(step > WIDES // 2)
    def _():
        gather_lanes(weight, rest, meta, TABLE + count)

    @pl.when(step > 0)
    def _():
        lows = [dot_nt(x[...], weight[at : at + TILE, :]) for at in range(0, WIDE, TILE)]
        for n, low in enumerate(lows):
            convolve(low, taps, live, shifted, masked, signal, slope, n * TILE)


def conv_forward(meta, x, taps, steps, own, rest, local):
    tokens, width = x.shape
    count = UNITS
    part = width // count
    half = WIDES // 2

    def natural(i, meta):
        return own_tile(jnp.maximum(i - 1, 0), meta)

    def tile(rows):
        return pl.BlockSpec((rows, WIDE), lambda i, meta: (0, natural(i, meta)))

    def late(i):
        return jnp.maximum(i - 1 - half, 0)

    own_spec = pl.BlockSpec((WIDE, part), lambda i, meta: (jnp.clip(i - 1, 0, half - 1), 0))
    rest_spec = pl.BlockSpec((WIDE, part), lambda i, meta: (late(i), 0))
    local_spec = pl.BlockSpec(
        (WIDE, part), lambda i, meta: (WIDES + (1 - meta[0]) * half + late(i), 0)
    )
    key_spec = pl.BlockSpec((TILE, part), lambda i, meta: (half * WIDE // TILE, 0))
    dt_spec = pl.BlockSpec((64, part), lambda i, meta: ((half * WIDE + TILE) // 64, 0))
    return call(
        conv_body, "conv_forward", meta,
        (x, taps, taps, steps) + tuple(own) + (() if local is None else (local,)) + tuple(rest)
        + tuple(own) * 2,
        [
            whole((tokens, width)), tile(8), pl.BlockSpec((8, TILE), lambda i, meta: (0, DI // TILE)),
            whole((8, LANES)),
        ]
        + [own_spec] * count
        + [rest_spec if local is None else local_spec] + [rest_spec] * (count - 1)
        + [key_spec] * count + [dt_spec] * count,
        [
            shape_of((tokens, DI), BF), shape_of((tokens, DI), BF), shape_of((tokens, DI)),
            shape_of((tokens, TILE), BF), shape_of((tokens, TILE), BF), shape_of((tokens, TILE)),
            shape_of((GROUPS, tokens, PACK)), shape_of((GROUPS, 2 * PER, tokens)),
            shape_of((3, tokens, LANES)),
        ],
        [
            tile(tokens), tile(tokens), tile(tokens),
            whole((tokens, TILE)), whole((tokens, TILE)), whole((tokens, TILE)),
            whole((GROUPS, tokens, PACK)), whole((GROUPS, 2 * PER, tokens)),
            whole((3, tokens, LANES)),
        ],
        [
            pltpu.VMEM((WIDE, width), BF), pltpu.VMEM((64, width), BF),
            pltpu.VMEM((WIDE // LANES, tokens + 8, LANES), F32), pltpu.VMEM((tokens, LANES), F32),
        ],
        1 + WIDES, 2 * tokens * width * CC, 24 * MIB,
    )


def lane_half(shape, half):
    ids = lax.broadcasted_iota(jnp.int32, shape, 1)
    return (ids >= HEADDIM) if half else (ids < HEADDIM)


def heads_apart(value, ones):
    return jnp.concatenate([value * ones[0:1], value * ones[1:2]], axis=0)


def heads_together(stacked):
    middle = stacked.shape[0] // 2
    upper = stacked[:middle]
    return jnp.where(lane_half(upper.shape, 0), upper, stacked[middle:])


def head_lanes(shape, width):
    lane = lax.broadcasted_iota(jnp.int32, shape, 1) // width
    row = lax.broadcasted_iota(jnp.int32, shape, 0) % PER
    return jnp.where(lane == row, 1.0, 0.0).astype(BF)


def scan_body(
    meta, content, keys, columns, rows, skip, out, entering,
    scores, write_rows, mixes, blocked, spread,
):
    half = SPAN // 2

    @pl.when(pl.program_id(0) == 0)
    def _():
        for span in range(2):
            at = span * SPAN
            scores[span] = dot_nt(keys[at : at + SPAN, DSTATE:], keys[at : at + SPAN, :DSTATE])
        write_rows[...] = keys[0:SPAN, :DSTATE].astype(F32).T.astype(BF)
        mixes[...] = jnp.zeros_like(mixes)
        after = row_ids(0, blocked.shape) >= lax.broadcasted_iota(jnp.int32, blocked.shape, 1)
        blocked[...] = jnp.where(after, 0.0, FAR)
        spread[...] = head_lanes(spread.shape, HEADDIM)

    factor = dot(columns[0, :, 2 * PER :].astype(BF), spread[...])
    first = content[0:SPAN, :].astype(F32)
    state = dot(write_rows[...], (first * factor[:SPAN]).astype(BF)).astype(BF)
    entering[0] = state
    out[0:SPAN, :] = skip[...] * first
    carried = dot(keys[SPAN:, DSTATE:], state) * factor[SPAN:]
    out[SPAN:, :] = carried + skip[...] * content[SPAN:, :].astype(F32)
    for pair in range(PER // 2):
        lanes = slice(pair * 2 * HEADDIM, (pair + 1) * 2 * HEADDIM)
        for h in range(2):
            n = 2 * pair + h
            for span in range(2):
                for at in range(0, SPAN, CHUNK):
                    row = span * SPAN + at
                    corner = at // half * half
                    log = columns[0, row : row + CHUNK, n : n + 1]
                    for begin in range(0, corner + half, half):
                        cut = slice(begin, begin + half)
                        less = rows[0, PER + n : PER + n + 1, span * SPAN + begin : span * SPAN + begin + half]
                        decay = log - less
                        if begin == corner:
                            decay = decay + blocked[at - begin : at - begin + CHUNK, :]
                        mix = scores[span, at : at + CHUNK, cut] * jnp.exp2(decay)
                        mixes[pair, span, h * SPAN + at : h * SPAN + at + CHUNK, cut] = mix.astype(BF)
        for span in range(2):
            at = span * SPAN
            value = content[at : at + SPAN, lanes]
            out[at : at + SPAN, lanes] += heads_together(dot(mixes[pair, span], value))


def scan_forward(meta, signal, keys, columns, rows, skip):
    tokens = signal.shape[0]
    return call(
        scan_body, "scan_forward", meta, (signal, keys, columns, rows, skip),
        [
            tiles(tokens, TILE), whole((tokens, TILE)),
            pl.BlockSpec((1, tokens, PACK), lambda i, meta: (i, 0, 0)),
            pl.BlockSpec((1, 2 * PER, tokens), lambda i, meta: (i, 0, 0)),
            tiles(1, TILE),
        ],
        [shape_of((tokens, DI)), shape_of((GROUPS, DSTATE, TILE), BF)],
        [tiles(tokens, TILE), pl.BlockSpec((1, DSTATE, TILE), lambda i, meta: (i, 0, 0))],
        [
            pltpu.VMEM((2, SPAN, SPAN), F32), pltpu.VMEM((DSTATE, SPAN), BF),
            pltpu.VMEM((PER // 2, 2, 2 * SPAN, SPAN), BF), pltpu.VMEM((SPAN // 2, SPAN // 2), F32),
            pltpu.VMEM((2 * PER, TILE), BF),
        ],
        GROUPS, 10 * 10**9, 12 * MIB,
    )


def gate_body(meta, x, mixed, gain, *refs):
    count = UNITS
    own, rest = refs[:count], refs[count : 2 * count]
    gate, normed, theirs, scale, weight, gated, total = refs[2 * count :]
    step = pl.program_id(0)
    tokens = x.shape[0]

    @pl.when(step < WIDES // 2)
    def _():
        gather_lanes(weight, own, meta, TABLE)

    @pl.when(step >= WIDES // 2)
    def _():
        gather_lanes(weight, rest, meta, TABLE + count)

    @pl.when(step == 0)
    def _():
        total[...] = jnp.zeros_like(total)

    here = own_tile(step, meta) * WIDE
    lows = [dot_nt(x[...], weight[at : at + TILE, :]).astype(BF) for at in range(0, WIDE, TILE)]
    for n, low in enumerate(lows):
        lanes = slice(n * TILE, (n + 1) * TILE)
        place = pl.ds(pl.multiple_of(here + n * TILE, TILE), TILE)
        gate[:, lanes] = low
        for at in range(0, tokens, CHUNK):
            part = low[at : at + CHUNK].astype(F32)
            part = mixed[at : at + CHUNK, lanes] * (part * sigmoid(part))
            gated[at : at + CHUNK, place] = part
            square = part * part
            total[at : at + CHUNK, :] += square[:, :LANES] + square[:, LANES:]

    @pl.when(step == pl.num_programs(0) - 1)
    def _():
        mean = jnp.sum(total[...], axis=1, keepdims=True) / DI
        scale[...] = lax.rsqrt(mean + epsilon)

        def finish(n, carry):
            place = pl.ds(pl.multiple_of(n * CHUNK, CHUNK), CHUNK)
            factor = jnp.broadcast_to(scale[place, :], (CHUNK, LANES))
            for at in range(0, DI, LANES):
                part = gated[place, at : at + LANES] * factor * gain[:, at : at + LANES]
                normed[place, at : at + LANES] = part.astype(BF)
            return carry

        lax.fori_loop(0, tokens // CHUNK, finish, 0)
        half = DI // (2 * count)
        for k in range(count):
            other = pl.multiple_of((2 * k + 1 - meta[0]) * half, LANES)
            theirs[:, k * half : (k + 1) * half] = normed[:, pl.ds(other, half)]


def gate_forward(meta, x, mixed, gain, own, rest, local):
    tokens, width = x.shape
    count = UNITS
    part = width // count
    half = WIDES // 2
    tile_spec = pl.BlockSpec((tokens, WIDE), lambda i, meta: (0, own_tile(i, meta)))
    own_spec = pl.BlockSpec((WIDE, part), lambda i, meta: (jnp.minimum(i, half - 1), 0))
    rest_spec = pl.BlockSpec((WIDE, part), lambda i, meta: (jnp.maximum(i - half, 0), 0))
    local_spec = pl.BlockSpec(
        (WIDE, part), lambda i, meta: ((1 - meta[0]) * half + jnp.maximum(i - half, 0), 0)
    )
    return call(
        gate_body, "gate_forward", meta,
        (x, mixed, gain) + tuple(own) + (() if local is None else (local,)) + tuple(rest),
        [whole((tokens, width)), tile_spec, whole((1, DI))] + [own_spec] * count
        + [rest_spec if local is None else local_spec] + [rest_spec] * (count - 1),
        [
            shape_of((tokens, DI), BF), shape_of((tokens, DI), BF), shape_of((tokens, DI // 2), BF),
            shape_of((tokens, 1)),
        ],
        [tile_spec, whole((tokens, DI)), whole((tokens, DI // 2)), whole((tokens, 1))],
        [
            pltpu.VMEM((WIDE, width), BF), pltpu.VMEM((tokens, DI), F32),
            pltpu.VMEM((tokens, LANES), F32),
        ],
        WIDES, 2 * tokens * width * DI, 28 * MIB,
    )


def out_body(meta, *refs):
    count = UNITS
    normed, pulled, hidden = refs[0:2], refs[2], refs[3]
    block, back, total, weight, branch = refs[-5:]
    refs = refs[4:-5]
    many = len(refs) // 2
    sides = refs[:many], refs[many:]
    step = pl.program_id(0)
    tokens = pulled.shape[0]
    half = DI // (2 * count)

    @pl.when(step == 0)
    def _():
        total[...] = jnp.zeros_like(total)

    for j in range(count):
        @pl.when(step == j)
        def _(j=j):
            for side, parts in enumerate(sides):
                weight[side * half : (side + 1) * half, :] = parts[j][...]

    normed_both = jnp.concatenate([normed[0][...], normed[1][...]], axis=1)
    grads = dot_nt(pulled[...], weight[...]).astype(BF)
    more = dot(normed_both, weight[...])

    @pl.when(step == 0)
    def _():
        branch[...] = more

    @pl.when((step > 0) & (step < count - 1))
    def _():
        branch[...] += more

    for side in range(2):
        at = meta[OUT_TABLE + side * count + step] * half
        back[:, pl.ds(pl.multiple_of(at, LANES), half)] = grads[:, side * half : (side + 1) * half]
    for at in range(0, tokens, CHUNK):
        sums = None
        for lane in range(0, 2 * half, LANES):
            one = grads[at : at + CHUNK, lane : lane + LANES].astype(F32)
            one = one * normed_both[at : at + CHUNK, lane : lane + LANES].astype(F32)
            sums = one if sums is None else sums + one
        total[at : at + CHUNK, :] += sums

    @pl.when(step == count - 1)
    def _():
        for at in range(0, tokens, CHUNK):
            part = branch[at : at + CHUNK, :] + more[at : at + CHUNK, :]
            part = jnp.where(live_rows(meta, at, part.shape), part, 0.0)
            block[at : at + CHUNK, :] = (hidden[at : at + CHUNK, :].astype(F32) + part).astype(BF)


def out_forward(meta, normed, pulled, hidden, own, rest, local):
    tokens, width = hidden.shape
    count = UNITS
    half = DI // (2 * count)

    def columns(side):
        return pl.BlockSpec(
            (tokens, half), lambda i, meta: (0, meta[OUT_TABLE + side * count + i])
        )

    def local_spec(side):
        return pl.BlockSpec((half, width), lambda i, meta: (meta[0] if side == 0 else 1 - meta[0], 0))

    first = () if local is None else (local,)

    def weight_specs(side):
        if local is None:
            return [whole((half, width))] * count
        return [local_spec(side)] + [whole(part.shape) for part in own]

    return call(
        out_body, "out_forward", meta,
        (normed, normed, pulled, hidden) + (first + tuple(own) + first + tuple(rest)),
        [columns(0), columns(1), whole((tokens, width)), whole((tokens, width))]
        + weight_specs(0) + weight_specs(1),
        [shape_of((tokens, width), BF), shape_of((tokens, DI), BF), shape_of((tokens, LANES))],
        [whole((tokens, width)), whole((tokens, DI)), whole((tokens, LANES))],
        [pltpu.VMEM((2 * half, width), BF), pltpu.VMEM((tokens, width), F32)],
        count, 4 * tokens * width * DI, 24 * MIB,
    )


STEPS = 4


def norm_back_body(
    meta, back, total, mixed, gate, scale, gain, grad_gate, theirs, grad_mixed, grad_gain
):
    step = pl.program_id(0)
    tokens, width = back.shape
    grad_gain[...] = jnp.zeros_like(grad_gain)

    def one(n, carry):
        rows = pl.ds(pl.multiple_of(n * CHUNK, CHUNK), CHUNK)
        r = jnp.broadcast_to(scale[rows, :], (CHUNK, LANES))
        mean = jnp.sum(total[rows, :], axis=1, keepdims=True) / DI
        factor = r * r * mean
        for at in range(0, width, LANES):
            cut = slice(at, at + LANES)
            z = gate[rows, cut].astype(F32)
            sigma = sigmoid(z)
            silu = z * sigma
            out = mixed[rows, cut]
            gated = out * silu
            grad = back[rows, cut].astype(F32) * r
            grad_gain[:, cut] += fold(grad * gated)
            grad = grad * gain[:, cut] - gated * factor
            grad_mixed[rows, cut] = (grad * silu).astype(BF)
            grad_gate[rows, cut] = ((grad * out) * (sigma + silu * (1.0 - sigma))).astype(BF)
        return carry

    lax.fori_loop(0, tokens // CHUNK, one, 0)

    @pl.when(step // (STEPS // 2) == 1 - meta[0])
    def _():
        theirs[...] = grad_gate[...]


def norm_back(meta, back, total, mixed, gate, scale, gain):
    tokens = back.shape[0]
    width = DI // STEPS

    def tile(rows):
        return pl.BlockSpec((rows, width), lambda i, meta: (0, i))

    theirs_spec = pl.BlockSpec(
        (tokens, width),
        lambda i, meta: (0, jnp.clip(i - (1 - meta[0]) * (STEPS // 2), 0, STEPS // 2 - 1)),
    )
    return call(
        norm_back_body, "norm_back", meta, (back, total, mixed, gate, scale, gain),
        [tile(tokens), whole((tokens, LANES)), tile(tokens), tile(tokens), whole((tokens, 1)), tile(1)],
        [
            shape_of((tokens, DI), BF), shape_of((tokens, DI // 2), BF), shape_of((tokens, DI), BF),
            shape_of((8, DI)),
        ],
        [tile(tokens), theirs_spec, tile(tokens), tile(8)],
        [], STEPS, 10**9, 24 * MIB,
    )


def rows_product_body(meta, mine, theirs, pulled, pulled_rest, send, keep):
    total = dot_tn(mine[...], pulled[...]) + dot_tn(theirs[...], pulled_rest[...])
    total = total.astype(BF)
    sent = pl.num_programs(0) // 2

    @pl.when(pl.program_id(0) < sent)
    def _():
        send[0] = total

    @pl.when(pl.program_id(0) >= sent)
    def _():
        keep[0] = total


def rows_product(meta, normed, arrived, arrived_at, pulled, pulled_rest, units):
    tokens, width = pulled.shape
    unit = DI // (2 * UNITS)
    upper = units // 2

    def which(i):
        return lax.rem(i + upper, units)

    result = shape_of((upper, unit, width), BF)
    return call(
        rows_product_body, "rows_product", meta, (normed, arrived, pulled, pulled_rest),
        [
            pl.BlockSpec((tokens, unit), lambda i, meta: (0, meta[OUT_TABLE + which(i)])),
            pl.BlockSpec((tokens, unit), lambda i, meta: (0, meta[arrived_at + which(i)])),
            whole((tokens, width)), whole((tokens, width)),
        ],
        [result, result],
        [
            pl.BlockSpec((1, unit, width), lambda i, meta: (jnp.minimum(i, upper - 1), 0, 0)),
            pl.BlockSpec((1, unit, width), lambda i, meta: (jnp.maximum(i - upper, 0), 0, 0)),
        ],
        [], units, 4 * tokens * width * unit * units, 12 * MIB,
    )


def columns_product_body(plan, meta, *refs):
    parts = len(plan)
    mine, theirs = refs[:parts], refs[parts : 2 * parts]
    here, there, send, keep, right, right_rest = refs[2 * parts :]
    step = pl.program_id(0)
    width = here.shape[1] // UNITS

    @pl.when(step == 0)
    def _():
        for j in range(UNITS):
            lanes = pl.ds(pl.multiple_of(meta[TABLE + j] * width, LANES), width)
            right[:, j * width : (j + 1) * width] = here[:, lanes]
            right_rest[:, j * width : (j + 1) * width] = there[:, lanes]

    for (begin, steps), a, b in zip(plan, mine, theirs):
        @pl.when((step >= begin) & (step < begin + steps))
        def _(a=a, b=b):
            total = (dot_tn(a[...], right[...]) + dot_tn(b[...], right_rest[...])).astype(BF)
            for k in range(UNITS // 2):
                keep[k] = total[:, k * width : (k + 1) * width]
                other = UNITS // 2 + k
                send[k] = total[:, other * width : (other + 1) * width]


def columns_product(meta, parts, normed, normed_rest):
    tokens, width = normed.shape
    part = width // UNITS
    plan, step, mine_specs, theirs_specs = [], 0, [], []

    def spec(begin, steps, start):
        return pl.BlockSpec(
            (tokens, TILE), lambda i, meta: (0, start(meta) + jnp.clip(i - begin, 0, steps - 1))
        )

    for matrix, start, steps, arrived in parts:
        plan.append((step, steps))
        mine_specs.append(spec(step, steps, start))
        theirs_specs.append(spec(step, steps, lambda meta: 0))
        step += steps
    result = shape_of((UNITS // 2, step * TILE, part), BF)
    result_spec = pl.BlockSpec((UNITS // 2, TILE, part), lambda i, meta: (0, i, 0))
    return call(
        functools.partial(columns_product_body, tuple(plan)), "columns_product", meta,
        tuple(p[0] for p in parts) + tuple(p[3] for p in parts) + (normed, normed_rest),
        mine_specs + theirs_specs + [whole((tokens, width))] * 2,
        [result, result], [result_spec, result_spec],
        [pltpu.VMEM((tokens, width), BF), pltpu.VMEM((tokens, width), BF)],
        step, 4 * tokens * step * TILE * width, 12 * MIB,
    )


def conv_back(meta, masked, taps, result, sums, live, grad_conv):
    tokens = masked.shape[0]
    grad_conv[:, tokens:, :] = jnp.zeros((TILE // LANES, 8, LANES), F32)
    sums[...] = jnp.zeros_like(sums)
    for lane in range(0, TILE, LANES):
        cut = slice(lane, lane + LANES)
        totals = [jnp.zeros((8, LANES), F32) for _ in range(CONV + 1)]
        for at in range(0, tokens, CHUNK):
            near = [
                grad_conv[lane // LANES, at + 3 - k : at + 3 - k + CHUNK, :] for k in range(CONV)
            ]
            value = masked[at : at + CHUNK, cut].astype(F32)
            out = near[0] * taps[0:1, cut]
            for k in range(1, CONV):
                out = out + near[k] * taps[k : k + 1, cut]
            result[at : at + CHUNK, cut] = (out * live[at : at + CHUNK, :]).astype(BF)
            for k in range(CONV):
                totals[k] = totals[k] + fold(near[k] * value)
            totals[CONV] = totals[CONV] + fold(near[CONV - 1])
        for k in range(CONV + 1):
            sums[k : k + 1, cut] = jnp.sum(totals[k], axis=0, keepdims=True)


def fold(value):
    return jnp.sum(value.reshape(value.shape[0] // 8, 8, value.shape[1]), axis=0)


def scan_back_body(
    meta, content, keys, grad_out, mixed, entering, columns, rows, skip, masked, slope, taps,
    scores_in, write_in, read_in,
    result, theirs, sums, grad_columns, grad_scores, grad_write, grad_read,
    scores, read_rows, live, grad_conv, mixes, mix_grads, blocked, spread,
):
    half = SPAN // 2

    @pl.when(pl.program_id(0) == 0)
    def _():
        for span in range(2):
            at = span * SPAN
            scores[span] = dot_nt(keys[at : at + SPAN, :DSTATE], keys[at : at + SPAN, DSTATE:])
        read_rows[...] = keys[SPAN:, DSTATE:].astype(F32).T.astype(BF)
        grad_scores[...] = scores_in[...]
        grad_write[...] = write_in[...]
        grad_read[...] = read_in[...]
        mixes[...] = jnp.zeros_like(mixes)
        live_lanes(meta, live)
        after = row_ids(0, blocked.shape) <= lax.broadcasted_iota(jnp.int32, blocked.shape, 1)
        blocked[...] = jnp.where(after, 0.0, FAR)
        spread[...] = head_lanes(spread.shape, HEADDIM)

    def heads_sum(value):
        high = value.astype(BF)
        low = (value - high.astype(F32)).astype(BF)
        return dot_nt(high, spread[...]) + dot_nt(low, spread[...])

    for pair in range(PER // 2):
        lanes = slice(pair * 2 * HEADDIM, (pair + 1) * 2 * HEADDIM)
        ones = spread[2 * pair : 2 * pair + 2, lanes]
        for span in range(2):
            cut = slice(span * SPAN, (span + 1) * SPAN)
            mix_grads[pair, span] = dot_nt(heads_apart(content[cut, lanes], ones), grad_out[cut, lanes])

    factor = dot(columns[0, :, 2 * PER :].astype(BF), spread[...])
    grown = (grad_out[SPAN:, :].astype(F32) * factor[SPAN:]).astype(BF)
    grad_state = dot(read_rows[...], grown).astype(BF)
    grad_read[...] += dot_nt(grown, entering[0])
    worth = (content[0:SPAN, :].astype(F32) * factor[:SPAN]).astype(BF)
    grad_write[...] += dot_nt(worth, grad_state)
    from_state = dot(keys[0:SPAN, :DSTATE], grad_state) * factor[:SPAN]

    for pair in range(PER // 2):
        for h in range(2):
            n = 2 * pair + h
            for span in range(2):
                top = span * SPAN
                for at in range(0, SPAN, CHUNK):
                    less = columns[0, top + at : top + at + CHUNK, PER + n : PER + n + 1]
                    corner = at // half * half
                    for begin in range(corner, SPAN, half):
                        cut = slice(begin, begin + half)
                        decay = rows[0, n : n + 1, top + begin : top + begin + half] - less
                        if begin == corner:
                            decay = decay + blocked[at - begin : at - begin + CHUNK, :]
                        decay = jnp.exp2(decay)
                        row = h * SPAN + at
                        mix = scores[span, at : at + CHUNK, cut] * decay
                        mixes[pair, span, row : row + CHUNK, cut] = mix.astype(BF)
                        change = mix_grads[pair, span, row : row + CHUNK, cut] * decay
                        grad_scores[span, at : at + CHUNK, cut] += change

    lane = lax.broadcasted_iota(jnp.int32, (SPAN, 2 * PER), 1) < PER
    final = row_ids(0, lane.shape) == SPAN - 1
    skips = jnp.zeros((8, TILE), F32)
    for span in range(2):
        cut = slice(span * SPAN, (span + 1) * SPAN)
        value = content[cut, :].astype(F32)
        pull = grad_out[cut, :].astype(F32)
        both = []
        for pair in range(PER // 2):
            lanes = slice(pair * 2 * HEADDIM, (pair + 1) * 2 * HEADDIM)
            both.append(heads_together(dot(mixes[pair, span], grad_out[cut, lanes])))
        both = jnp.concatenate(both, axis=1)
        if span == 0:
            ended = jnp.sum(fold(value * from_state), axis=0, keepdims=True)
            both = both + from_state
        skipped = skip[...] * value
        skips = skips + fold(pull * value)
        written = heads_sum(value * both)
        read = heads_sum(pull * (mixed[cut, :] - skipped))
        if span == 0:
            ended = heads_sum(jnp.broadcast_to(ended, (8, TILE)))[0:1]
            read = read + jnp.where(final, ended, 0.0)
        grad_columns[0, cut, :] = jnp.where(lane, written, read)
        both = (both + skip[...] * pull) * slope[cut, :]
        for k in range(TILE // LANES):
            grad_conv[k, cut, :] = both[:, k * LANES : (k + 1) * LANES]

    conv_back(meta, masked, taps, result, sums, live, grad_conv)
    sums[5:6, :] = jnp.sum(skips, axis=0, keepdims=True)
    half_steps = pl.num_programs(0) // 2
    at_half = pl.program_id(0) // half_steps

    @pl.when(at_half == 1 - meta[0])
    def _():
        theirs[...] = result[...]


def scan_backward(
    meta, signal, keys, grad_out, mixed, entering, columns, rows, skip, masked, slope, taps, kept,
    first, count,
):
    tokens = signal.shape[0]

    def group(*shape):
        return pl.BlockSpec((1,) + shape, lambda i, meta: (i + first, 0, 0))

    def fresh(*shape):
        return pl.BlockSpec((1,) + shape, lambda i, meta: (i, 0, 0))

    kept_specs = [whole((2, SPAN, SPAN)), whole((SPAN, DSTATE)), whole((SPAN, DSTATE))]
    return call(
        scan_back_body, "scan_backward", meta,
        (signal, keys, grad_out, mixed, entering, columns, rows, skip, masked, slope, taps)
        + tuple(kept),
        [
            tiles(tokens, TILE, first), whole((tokens, TILE)),
            tiles(tokens, TILE, first), tiles(tokens, TILE, first), group(DSTATE, TILE),
            group(tokens, PACK),
            group(2 * PER, tokens), tiles(1, TILE, first), tiles(tokens, TILE, first),
            tiles(tokens, TILE, first), tiles(8, TILE, first),
        ]
        + kept_specs,
        [
            shape_of((tokens, count * TILE), BF), shape_of((tokens, count // 2 * TILE), BF),
            shape_of((8, count * TILE)),
            shape_of((count, tokens, 2 * PER)),
            shape_of((2, SPAN, SPAN)), shape_of((SPAN, DSTATE)), shape_of((SPAN, DSTATE)),
        ],
        [
            tiles(tokens, TILE),
            pl.BlockSpec(
                (tokens, TILE),
                lambda i, meta: (0, jnp.clip(i - (1 - meta[0]) * (count // 2), 0, count // 2 - 1)),
            ),
            tiles(8, TILE), fresh(tokens, 2 * PER),
        ]
        + kept_specs,
        [
            pltpu.VMEM((2, SPAN, SPAN), F32), pltpu.VMEM((DSTATE, SPAN), BF),
            pltpu.VMEM((tokens, LANES), F32), pltpu.VMEM((TILE // LANES, tokens + 8, LANES), F32),
            pltpu.VMEM((PER // 2, 2, 2 * SPAN, SPAN), BF),
            pltpu.VMEM((PER // 2, 2, 2 * SPAN, SPAN), F32),
            pltpu.VMEM((SPAN // 2, SPAN // 2), F32), pltpu.VMEM((2 * PER, TILE), BF),
        ],
        count, 3 * 10**9 * count, count * MIB,
    )


def tail_body(parts, meta, *refs):
    keys, masked, slope, taps, trio, steps, grad_scores, grad_write, grad_read = refs[:9]
    grad_columns = refs[9 : 9 + parts]
    result, sums, raw, small, packs, live, grad_conv = refs[9 + parts :]
    tokens = keys.shape[0]
    for span in range(2):
        at = span * SPAN
        write = keys[at : at + SPAN, :DSTATE]
        read = keys[at : at + SPAN, DSTATE:]
        to_write = fine_dot(grad_scores[span], read, dot)
        to_read = fine_dot(grad_scores[span], write, dot_tn)
        if span == 0:
            to_write = to_write + grad_write[...]
        else:
            to_read = to_read + grad_read[...]
        cut = slice(at, at + SPAN)
        grad_conv[0, cut, :] = to_write * slope[cut, :DSTATE]
        grad_conv[1, cut, :] = to_read * slope[cut, DSTATE:]
    live_lanes(meta, live)
    conv_back(meta, masked, taps, result, sums, live, grad_conv)

    blank = jnp.zeros((tokens, LANES - HEADS), F32)
    of_step, of_log = [], []
    for column_ref in grad_columns:
        for g in range(column_ref.shape[0]):
            of_step.append(column_ref[g, :, :PER])
            of_log.append(column_ref[g, :, PER:])
    grad_size = jnp.concatenate(of_step + [blank], axis=1)
    grad_log = jnp.concatenate(of_log + [blank], axis=1) - grad_size
    upper = row_ids(0, (SPAN, SPAN)) <= lax.broadcasted_iota(jnp.int32, (SPAN, SPAN), 1)
    upper = jnp.where(upper, 1.0, 0.0).astype(BF)
    rates = []
    for at in range(0, tokens, SPAN):
        high, middle, low = pieces(grad_log[at : at + SPAN])
        rates.append(dot(upper, high) + (dot(upper, middle) + dot(upper, low)))
    grad_rate = jnp.concatenate(rates, axis=0)
    decay_rate = steps[1:2, :]
    sigma = jax.nn.sigmoid(trio[0])
    size = trio[1]
    tiny = size > 0.0
    share = jnp.where(tiny, sigma / jnp.where(tiny, size, 1.0), 1.0)
    grad_raw = grad_size * share + grad_rate * decay_rate * sigma
    raw[...] = grad_raw.astype(BF)
    small[...] = jnp.zeros_like(small)
    small[0:1, :] = jnp.sum(grad_raw, axis=0, keepdims=True)
    small[1:2, :] = jnp.sum(grad_rate * trio[1], axis=0, keepdims=True) * decay_rate
    for side in range(2):
        at = meta[0] if side == 0 else 1 - meta[0]
        packs[side, :, :LANES] = result[:, pl.ds(pl.multiple_of(at * LANES, LANES), LANES)]
        packs[side, :, LANES:] = raw[...]


def tail_backward(meta, keys, masked, slope, taps, trio, steps, kept, grad_columns):
    tokens = keys.shape[0]
    last = DI // TILE
    key_spec = whole((tokens, TILE))
    return call(
        functools.partial(tail_body, len(grad_columns)), "tail_backward", meta,
        (keys, masked, slope, taps, trio, steps) + tuple(kept) + tuple(grad_columns),
        [
            key_spec, key_spec, key_spec, pl.BlockSpec((8, TILE), lambda i, meta: (0, last)),
            whole((3, tokens, LANES)), whole((8, LANES)), whole((2, SPAN, SPAN)),
            whole((SPAN, DSTATE)), whole((SPAN, DSTATE)),
        ]
        + [whole(part.shape) for part in grad_columns],
        [
            shape_of((tokens, TILE), BF), shape_of((8, TILE)), shape_of((tokens, LANES), BF),
            shape_of((8, LANES)), shape_of((2, tokens, TILE), BF),
        ],
        [
            whole((tokens, TILE)), whole((8, TILE)), whole((tokens, LANES)), whole((8, LANES)),
            whole((2, tokens, TILE)),
        ],
        [pltpu.VMEM((tokens, LANES), F32), pltpu.VMEM((TILE // LANES, tokens + 8, LANES), F32)],
        1, 1, 1,
    )


def input_body(plan, first, last, meta, *refs):
    count = UNITS
    grads = refs[: len(plan)]
    refs = refs[len(plan) :]
    if not first:
        start, refs = refs[0], refs[1:]
    blocks = []
    for begin, steps, half in plan:
        own, refs = refs[:count], refs[count:]
        rest = None
        if half is not None:
            rest, refs = refs[:count], refs[count:]
        blocks.append((own, rest))
    step = pl.program_id(0)

    if last:
        hidden, out_grad, scale, gain, result, gain_grad, weight, weight_dt, total, folded = refs
    else:
        total, weight = refs

    @pl.when(step == 0)
    def _():
        total[...] = jnp.zeros_like(total) if first else start[...]

    for n, (begin, steps, half) in enumerate(plan):
        @pl.when((step >= begin) & (step < begin + steps))
        def _(n=n, half=half):
            own, rest = blocks[n]
            rows = own[0].shape[0]
            if grads[n].shape[1] == LANES:
                weight_dt[...] = jnp.zeros_like(weight_dt)
                gather_lanes(weight_dt, own, meta, TABLE)
                total[...] += dot(grads[n][...], weight_dt[...])
                return
            if half is None:
                gather_lanes(weight, own, meta, TABLE)
            else:
                @pl.when(meta[0] == half)
                def _():
                    gather_lanes(weight, own, meta, TABLE)

                @pl.when(meta[0] != half)
                def _():
                    gather_lanes(weight, rest, meta, TABLE + count)

            total[...] += dot(grads[n][...], weight[0:rows, :])

    if not last:
        return

    @pl.when(step == pl.num_programs(0) - 1)
    def _():
        tokens, width = hidden.shape
        folded[...] = jnp.zeros_like(folded)

        def finish(n, carry):
            rows = pl.ds(pl.multiple_of(n * 32, 32), 32)
            r = jnp.broadcast_to(scale[rows, :], (32, LANES))
            sums = jnp.zeros((32, LANES), F32)
            for at in range(0, width, LANES):
                cut = slice(at, at + LANES)
                both = total[rows, cut] * hidden[rows, cut].astype(F32)
                folded[:, cut] += fold(both * r)
                sums = sums + both * gain[:, cut]
            mean = jnp.sum(sums, axis=1, keepdims=True) / width
            factor = r * r * r * mean
            for at in range(0, width, LANES):
                cut = slice(at, at + LANES)
                value = r * (total[rows, cut] * gain[:, cut]) - hidden[rows, cut].astype(F32) * factor
                result[rows, cut] = value + out_grad[rows, cut].astype(F32)
            return carry

        lax.fori_loop(0, tokens // 32, finish, 0)
        gain_grad[...] = jnp.sum(folded[...], axis=0, keepdims=True)


def input_backward(meta, start, parts, tokens, width, last=None):
    part = width // UNITS
    plan, step, grad_specs, block_specs, grads, blocks = [], 0, [], [], [], []

    def grad_spec(columns, begin, steps, first):
        return pl.BlockSpec(
            (tokens, columns), lambda i, meta: (0, first + jnp.clip(i - begin, 0, steps - 1))
        )

    def row_spec(rows, begin, steps, first, when):
        def index(i, meta):
            at = first + jnp.clip(i - begin, 0, steps - 1)
            return (at if when is None else jnp.where(when(meta), at, first), 0)

        return pl.BlockSpec((rows, part), index)

    def is_half(half):
        return lambda meta: meta[0] == half

    def not_half(half):
        return lambda meta: meta[0] != half

    for grad, grad_first, steps, half, own, own_first, rest, rest_first, local_first in parts:
        columns = WIDE if half is not None else grad.shape[1]
        row_tile = 64 if columns == LANES else columns
        plan.append((step, steps, half))
        grads.append(grad)
        grad_specs.append(grad_spec(columns, step, steps, grad_first))
        when = None if half is None else is_half(half)
        for matrix in own:
            blocks.append(matrix)
            block_specs.append(row_spec(row_tile, step, steps, own_first, when))
        if half is not None:
            for j, matrix in enumerate(rest):
                blocks.append(matrix)
                row = local_first if j == 0 else rest_first
                block_specs.append(row_spec(row_tile, step, steps, row, not_half(half)))
        step += steps
    more, more_specs = (), []
    outs, out_specs = [shape_of((tokens, width))], [whole((tokens, width))]
    scratch = [pltpu.VMEM((WIDE, width), BF)]
    if last is not None:
        more = tuple(last)
        more_specs = [whole((tokens, width))] * 2 + [whole((tokens, 1)), whole((1, width))]
        outs.append(shape_of((1, width)))
        out_specs.append(whole((1, width)))
        scratch += [
            pltpu.VMEM((LANES, width), BF), pltpu.VMEM((tokens, width), F32),
            pltpu.VMEM((8, width), F32),
        ]
    first = start is None
    return call(
        functools.partial(input_body, tuple(plan), first, last is not None),
        "input_backward", meta,
        tuple(grads) + (() if first else (start,)) + tuple(blocks) + more,
        grad_specs + ([] if first else [whole((tokens, width))]) + block_specs + more_specs,
        outs, out_specs, scratch,
        step, 2 * tokens * width * WIDE * step, 20 * MIB,
    )


def place_body(halves, last, meta, own, other, out):
    step = pl.program_id(0)

    def put(which, row, rows, at):
        @pl.when(meta[0] == which)
        def _():
            out[at : at + rows, :] = own[row : row + rows, :].astype(F32)

        @pl.when(meta[0] != which)
        def _():
            out[at : at + rows, :] = other[row : row + rows, :].astype(F32)

    for half in range(2):
        @pl.when(step == half)
        def _(half=half):
            put(half, 0, halves, 0)

    if last:
        @pl.when(step == 2)
        def _():
            put(0, halves, LANES, 0)
            put(1, halves, LANES, LANES)
            put(0, halves + LANES, LANES, 2 * LANES)


def place_rows(meta, own, other, halves, first, total, filled, last):
    length, width = own.shape
    return call(
        functools.partial(place_body, halves, last), "place_rows", meta, (own, other),
        [whole((length, width)), whole((length, width))],
        shape_of((total, width)),
        pl.BlockSpec((halves, width), lambda i, meta: (first + i, 0)),
        [], 3 if last else 2, 1, 1, None if filled is None else {0: filled},
    )


NEAR = 8


def mirrored(j, count):
    if count != 4:
        return j
    result, bit, other = 0, 1, count // 2
    while bit < count:
        if j & bit:
            result |= other
        bit, other = bit * 2, other // 2
    return result


def hop(x, bit):
    reps, count = lax.axis_size("rep"), lax.axis_size("shard")
    pairs = []
    for r in range(reps):
        flip = bit if r % 2 == 0 else mirrored(bit, count)
        pairs += [(r * count + s, r * count + (s ^ flip)) for s in range(count)]
    return lax.ppermute(x, ("rep", "shard"), pairs)


def swap(x):
    return lax.ppermute(x, "rep", [(r, r ^ 1) for r in range(lax.axis_size("rep"))])


def across(x, bit):
    return lax.ppermute(x, "shard", [(s, s ^ bit) for s in range(lax.axis_size("shard"))])


def along(x, pairs):
    return lax.ppermute(x, "rep", [(2 * a + k, 2 * b + k) for a, b in pairs for k in range(2)])


def settle(keep, arrived):
    middle = keep.shape[0] // 2
    if middle == 0:
        return None, keep.astype(F32) + arrived.astype(F32)
    held = (keep.astype(F32) + arrived.astype(F32)).astype(BF)
    return held[middle:], held[:middle]


def finish_stages(send, keep):
    while send is not None:
        send, keep = settle(keep, hop(send, send.shape[0]))
    return keep[0]


def inward(held):
    if lax.axis_size("rep") // 2 != 4:
        return held, None
    return held, along(held.astype(BF), [(0, 1), (3, 2)])


def middle(state):
    held, arrived = state
    if arrived is None:
        return held, None
    inner = (held + arrived.astype(F32)).astype(BF)
    return inner, along(inner, [(1, 2), (2, 1)])


def outward(state):
    inner, arrived = state
    if arrived is None:
        chips = lax.axis_size("rep") // 2
        total, bit = inner.astype(BF), 1
        while bit < chips:
            more = along(total, [(k, k ^ bit) for k in range(chips)])
            total = (total.astype(F32) + more.astype(F32)).astype(BF)
            bit *= 2
        return total, None
    total = (inner.astype(F32) + arrived.astype(F32)).astype(BF)
    return total, along(total, [(1, 0), (2, 3)])


def summed(state):
    total, arrived = state
    if arrived is None:
        return total
    place = lax.axis_index("rep") // 2
    return jnp.where((place == 1) | (place == 2), total, arrived)


def in_order(own, other, core):
    return [jnp.where(core == 0, own, other), jnp.where(core == 0, other, own)]


def hold(values):
    leaves, tree = jax.tree.flatten(values)
    return jax.tree.unflatten(tree, lax.optimization_barrier(tuple(leaves)))


def add_up(rows):
    while len(rows) > 1:
        rows = [a + b for a, b in zip(rows[::2], rows[1::2])]
    return rows[0]


def group_sum(vector, shard, count):
    vector = vector + swap(vector)
    rows = [lax.dynamic_slice_in_dim(vector, shard ^ j, 1, 0) for j in range(count)]
    return add_up(rows[:1] + [across(row, j) for j, row in enumerate(rows) if j])


def chips_sum(row):
    chips = lax.axis_size("rep") // 2
    return add_up(
        [row] + [along(row, [(k, k ^ d) for k in range(chips)]) for d in range(1, chips)]
    )


def join_lanes(blocks, shard):
    return [
        jnp.concatenate(in_order(blocks[j], blocks[j + 1], shard % 2), axis=1)
        for j in range(0, len(blocks), 2)
    ]


def split_lanes(units, shard):
    half = units.shape[2] // 2
    pairs = in_order(units[:, :, :half], units[:, :, half:], shard % 2)
    return jnp.stack(pairs, axis=1).reshape(2 * units.shape[0], units.shape[1], half)


def pad_lanes(matrix):
    return jnp.pad(matrix, ((0, 0), (0, LANES - matrix.shape[1])))


def shards(
    hidden,
    out_grad,
    norm_gain,
    in_w,
    conv_w,
    conv_b,
    dt_bias,
    a_log,
    skip,
    out_gain,
    out_w,
    lengths,
    offsets,
):
    core = lax.axis_index("rep") % 2
    shard = lax.axis_index("shard")
    count = lax.axis_size("shard")
    tokens, width = hidden.shape
    bits = []
    while 2 ** len(bits) < count:
        bits.append(2 ** len(bits))

    local = in_w.T
    half = DI // 2
    piece = jnp.concatenate(
        [
            lax.dynamic_slice_in_dim(local, DI + core * half, half, 0),
            local[2 * DI :],
            jnp.zeros((16, local.shape[1]), BF),
        ],
        axis=0,
    )
    gate_piece = lax.dynamic_slice_in_dim(local, core * half, half, 0)
    out_piece = lax.dynamic_slice_in_dim(out_w, core * (out_w.shape[0] // 2), out_w.shape[0] // 2, 0)

    def spread(first):
        blocks = [first]
        for bit in bits:
            blocks = blocks + [hop(block, bit) for block in blocks]
        return blocks

    paired = count == 4
    small = (norm_gain, conv_w.T, conv_b, dt_bias, a_log, skip, out_gain)
    packed = jnp.concatenate([part.reshape(-1) for part in small])
    everyone = [packed] + [
        lax.ppermute(
            packed, ("rep", "shard"),
            [
                (r * count + s, r * count + (s ^ (j if r % 2 == 0 else mirrored(j, count))))
                for r in range(lax.axis_size("rep"))
                for s in range(count)
            ],
        )
        for j in range(1, count)
    ]
    piece, everyone = hold((piece, everyone))
    everyone = jnp.stack(everyone).astype(F32)
    order = [jnp.where(core == 0, j, mirrored(j, count)) for j in range(count)]
    whose = jnp.stack(order)[jnp.arange(count) ^ shard]
    same = (whose[:, None] == jnp.arange(count)[None]).astype(F32)
    everyone = jnp.sum(same[:, :, None] * everyone[None], axis=1)
    parts, start = [], 0
    for part in small:
        cut = everyone[:, start : start + part.size].reshape((count,) + part.shape)
        cut = jnp.moveaxis(cut, 0, -2)
        parts.append(cut.reshape(part.shape[:-1] + (-1,)))
        start += part.size
    conv_own = spread(piece)
    gate_piece, conv_own = hold((gate_piece, conv_own))
    if paired:
        conv_rest = [swap(block) for block in conv_own[1:]]
        gate_near = hop(gate_piece, 1), hop(gate_piece, 2)
        out_local, in_local = out_w, local
    else:
        gate_own = spread(gate_piece)
        out_piece, gate_own = hold((out_piece, gate_own))
        out_own = spread(out_piece)
        conv_rest = rest_conv = join_lanes([swap(block) for block in conv_own], shard)
        gate_rest = rest_gate = join_lanes([swap(block) for block in gate_own], shard)
        conv_own, gate_own = join_lanes(conv_own, shard), join_lanes(gate_own, shard)
        out_full = [jnp.concatenate(in_order(block, swap(block), core), axis=0) for block in out_own]
        out_one, out_two = out_full[:UNITS], out_full[UNITS:]
        out_local = in_local = None

    gain_one, kernel, bias_conv, bias_step, log_rate, skip_full, gain_two = parts
    decay_rate = -jnp.exp(log_rate)

    mine = order
    other = [jnp.where(core == 0, mirrored(j, count), j) for j in range(count)]
    mine, other = [shard ^ j for j in mine], [shard ^ j for j in other]
    if paired:
        out_units = [2 * j + core for j in mine] + [2 * j + 1 - core for j in other]
    else:
        out_units = mine
        mine = other = [j // 2 for j in mine[::2]]
    meta = jnp.stack(
        [core, offsets[0], lengths[0], shard] + mine + other + out_units
    ).astype(jnp.int32)
    taps = jnp.concatenate([kernel, bias_conv[None], jnp.zeros((3, CC), F32)], axis=0)
    steps = jnp.concatenate(
        [pad_lanes(jnp.stack([bias_step, decay_rate])), jnp.zeros((6, LANES), F32)], axis=0
    )
    skip_lanes = jnp.repeat(skip_full, HEADDIM)[None]

    positions = jnp.arange(tokens, dtype=jnp.int32)
    live_mask = ((positions >= offsets[0]) & (positions < offsets[0] + lengths[0])).astype(F32)
    hidden_full = hidden.astype(F32)
    inv_rms = lax.rsqrt(jnp.mean(hidden_full * hidden_full, axis=1, keepdims=True) + epsilon)
    normed = (hidden_full * inv_rms * gain_one).astype(BF)
    pulled = (out_grad.astype(F32) * live_mask[:, None]).astype(BF)
    normed_rest = swap(normed)
    pulled_rest = swap(pulled)

    (masked, signal, slope, masked_keys, keys, slope_keys, columns, rows, trio) = conv_forward(
        meta, normed, taps, steps, conv_own, conv_rest, in_local
    )
    if paired:
        gate_near, signal = hold((gate_near, signal))
        gate_own = [gate_piece, *gate_near, hop(gate_near[0], 2)]
    mixed, entering = scan_forward(meta, signal, keys, columns, rows, skip_lanes)
    if paired:
        out_piece, gate_far, mixed = hold((out_piece, gate_own[3], mixed))
        gate_own[3] = gate_far
        gate_rest = [swap(block) for block in gate_own[1:]]
        rest_conv, rest_gate = [local] + conv_rest, [local] + gate_rest
        out_near = hop(out_piece, 1), hop(out_piece, 2)
    gate, normed_out, out_theirs, scale = gate_forward(
        meta, normed, mixed, gain_two[None], gate_own, gate_rest, in_local
    )
    out_arrived = swap(out_theirs if paired else normed_out)
    if paired:
        out_near, normed_out = hold((out_near, normed_out))
        out_one = [*out_near, hop(out_near[0], 2)]
        out_two = [swap(block) for block in out_one]

    upper = count // 2
    out_pulls = (pulled, pulled_rest)
    if not paired:
        cut = core * (width // 2)
        out_pulls = [lax.dynamic_slice_in_dim(x, cut, width // 2, 1) for x in out_pulls]

    def product(parts):
        send, keep = columns_product(meta, parts, normed, normed_rest)
        return (send, keep) if paired else (split_lanes(send, shard), split_lanes(keep, shard))

    out_send, out_keep = rows_product(
        meta, normed_out, out_arrived, TABLE if paired else OUT_TABLE, *out_pulls, count
    )
    out_send, out_keep, normed_out = hold((out_send, out_keep, normed_out))
    out_there = hop(out_send, upper)
    block_out, back, total = out_forward(
        meta, normed_out, pulled, hidden, out_one, out_two, out_local
    )
    out_there, total = hold((out_there, total))
    out_send, out_keep = settle(out_keep, out_there)
    out_there = hop(out_send, upper // 2)
    out_keep, total = hold((out_keep, total))
    grad_gate, gate_theirs, grad_mixed, grad_gain_two = norm_back(
        meta, back, total, mixed, gate, scale, gain_two[None]
    )

    gate_theirs, out_there = hold((gate_theirs, out_there))
    gate_arrived = swap(gate_theirs)
    out_line = inward(finish_stages(*settle(out_keep, out_there)))
    out_held, gate_arrived = hold((out_line[0], gate_arrived))
    gate_parts = [(grad_gate, lambda meta: meta[0] * (GROUPS // 2), GROUPS // 2, gate_arrived)]
    gate_send, gate_keep = product(gate_parts)
    gate_send, gate_keep, grad_mixed = hold((gate_send, gate_keep, grad_mixed))
    gate_there = hop(gate_send, upper)
    kept = (
        jnp.zeros((2, SPAN, SPAN), F32),
        jnp.zeros((SPAN, DSTATE), F32),
        jnp.zeros((SPAN, DSTATE), F32),
    )
    near, far = NEAR, GROUPS - NEAR
    part = WIDES // 2
    over = near * TILE // WIDE - part

    def gate_part(half):
        at = half * part
        return [(grad_gate, at, part, half, gate_own, 0, rest_gate, 0, at if paired else 0)]

    def conv_part(grad, grad_first, steps, half, first):
        local_first = WIDES + half * part + first if paired else first
        return [(grad, grad_first, steps, half, conv_own, first, rest_conv, first, local_first)]

    grad_near, near_theirs, sums_near, columns_near, *kept = scan_backward(
        meta, signal, keys, grad_mixed, mixed, entering, columns, rows, skip_lanes, masked, slope, taps,
        kept, 0, near,
    )
    gate_there, near_theirs, out_arrived = hold((gate_there, near_theirs, out_line[1]))
    near_arrived = swap(near_theirs)
    gate_send, gate_keep = settle(gate_keep, gate_there)
    gate_there = hop(gate_send, upper // 2)
    gate_keep, out_arrived = hold((gate_keep, out_arrived))
    out_line = middle((out_held, out_arrived))
    near_arrived, gate_keep, out_inner = hold((near_arrived, gate_keep, out_line[0]))
    near_parts = [(grad_near, lambda meta: meta[0] * (near // 2), near // 2, near_arrived)]
    near_send, near_keep = product(near_parts)
    near_there = hop(near_send, upper)
    near_keep, kept, grad_mixed = hold((near_keep, kept, grad_mixed))
    grad_far, far_theirs, sums_far, columns_far, *kept = scan_backward(
        meta, signal, keys, grad_mixed, mixed, entering, columns, rows, skip_lanes, masked, slope, taps,
        kept, near, far,
    )
    far_theirs, gate_there, out_arrived = hold((far_theirs, gate_there, out_line[1]))
    far_arrived = swap(far_theirs)
    gate_line = inward(finish_stages(*settle(gate_keep, gate_there)))
    gate_held, out_arrived = hold((gate_line[0], out_arrived))
    out_line = outward((out_inner, out_arrived))
    out_done, kept, gate_held = hold((out_line[0], kept, gate_held))
    grad_keys, sums_keys, grad_raw, grad_steps, packs = tail_backward(
        meta, keys, masked_keys, slope_keys, taps, trio, steps, kept, (columns_near, columns_far),
    )
    packs, near_there = hold((packs, near_there))
    packs_arrived = swap(packs[1])
    near_send, near_keep = settle(near_keep, near_there)
    near_there = hop(near_send, upper // 2)
    packs, packs_arrived, near_keep = hold((packs, packs_arrived, near_keep))
    far_parts = [
        (grad_far, lambda meta: meta[0] * (far // 2), far // 2, far_arrived),
        (packs[0], lambda meta: 0, 1, packs_arrived),
    ]
    far_send, far_keep = product(far_parts)
    far_there = hop(far_send, upper)
    near_there, far_keep = hold((near_there, far_keep))
    near_line = inward(finish_stages(*settle(near_keep, near_there)))
    near_held, grad_gate = hold((near_line[0], grad_gate))
    (partial,) = input_backward(meta, None, gate_part(0), tokens, width)
    partial, far_there = hold((partial, far_there))
    far_send, far_keep = settle(far_keep, far_there)
    far_there = hop(far_send, upper // 2)
    far_keep, gate_arrived = hold((far_keep, gate_line[1]))
    gate_line = middle((gate_held, gate_arrived))
    partial, gate_inner, far_keep = hold((partial, gate_line[0], far_keep))
    (partial,) = input_backward(meta, partial, gate_part(1), tokens, width)
    partial, far_there = hold((partial, far_there))
    far_line = inward(finish_stages(*settle(far_keep, far_there)))
    far_held, near_arrived, out_arrived = hold((far_line[0], near_line[1], out_line[1]))
    near_line = middle((near_held, near_arrived))
    out_total = summed((out_done, out_arrived))
    out_other = swap(out_total)
    partial, near_inner, far_held, out_total = hold((partial, near_line[0], far_held, out_total))
    (partial,) = input_backward(meta, partial, conv_part(grad_near, 0, part, 0, 0), tokens, width)
    partial, far_arrived, gate_arrived, out_other = hold((partial, far_line[1], gate_line[1], out_other))
    far_line = middle((far_held, far_arrived))
    gate_line = outward((gate_inner, gate_arrived))
    partial, far_inner, gate_done, out_other = hold((partial, far_line[0], gate_line[0], out_other))
    (partial,) = input_backward(
        meta, partial,
        conv_part(grad_near, part, over, 1, 0) + conv_part(grad_far, 0, part - over, 1, over),
        tokens, width,
    )
    partial, near_arrived = hold((partial, near_line[1]))
    near_line = outward((near_inner, near_arrived))
    partial, near_done = hold((partial, near_line[0]))
    hidden_grad, grad_gain_one = input_backward(
        meta, partial,
        [
            (grad_keys, 0, 1, None, conv_own, DI // 2 // TILE, None, 0, 0),
            (grad_raw, 0, 1, None, conv_own, (DI // 2 + TILE) // 64, None, 0, 0),
        ],
        tokens, width, (hidden, out_grad, inv_rms, gain_one[None]),
    )
    grad_gain_one, far_arrived = hold((grad_gain_one, far_line[1]))
    far_line = outward((far_inner, far_arrived))
    small_grads = (grad_gain_one, sums_near, sums_far, sums_keys, grad_steps, grad_gain_two)
    far_done, gate_arrived, near_arrived, small_grads = hold(
        (far_line[0], gate_line[1], near_line[1], small_grads)
    )
    grad_gain_one, sums_near, sums_far, sums_keys, grad_steps, grad_gain_two = small_grads
    gate_total = summed((gate_done, gate_arrived))
    gate_other = swap(gate_total)
    near_total = summed((near_done, near_arrived))
    near_other = swap(near_total)
    sums = jnp.concatenate([sums_near, sums_far, sums_keys], axis=1)
    grads = (
        grad_gain_one[0].reshape(count, -1),
        sums[:CONV].reshape(CONV, count, -1).transpose(1, 0, 2).reshape(count, -1),
        sums[CONV].reshape(count, -1),
        grad_steps[0, :HEADS].reshape(count, -1),
        grad_steps[1, :HEADS].reshape(count, -1),
        jnp.sum(sums[5, :DI].reshape(HEADS, HEADDIM), axis=1).reshape(count, -1),
        jnp.sum(grad_gain_two, axis=0).reshape(count, -1),
    )
    row = group_sum(jnp.concatenate(grads, axis=1), shard, count)
    all_rows = local.shape[0]
    gate_other, near_other, row = hold((gate_other, near_other, row))
    rows_so_far = place_rows(meta, gate_total, gate_other, DI // 2, 0, all_rows, None, False)
    row, far_arrived, rows_so_far = hold((row, far_line[1], rows_so_far))
    far_total = summed((far_done, far_arrived))
    far_other = swap(far_total)
    row = chips_sum(row)[0]
    wide = near // 2 * TILE
    rows_so_far = place_rows(
        meta, near_total, near_other, wide, DI // wide, all_rows, rows_so_far, False
    )
    wide = far // 2 * TILE
    rows_so_far = place_rows(
        meta, far_total, far_other, wide, (DI + near * TILE) // wide, all_rows, rows_so_far, True
    )
    in_w_grad = rows_so_far.T

    out_w_grad = jnp.concatenate(
        in_order(out_total, out_other, core), axis=0 if paired else 1
    ).astype(F32)
    found, start = [], 0
    for part in grads:
        found.append(row[start : start + part.shape[1]])
        start += part.shape[1]
    return (
        block_out,
        hidden_grad,
        found[0],
        in_w_grad,
        found[1].reshape(CONV, -1).T,
        found[2],
        found[3],
        found[4],
        found[5],
        found[6],
        out_w_grad,
    )


def solution(mesh):
    return jax.shard_map(
        shards,
        mesh=mesh,
        in_specs=(
            P(("rep", "shard"), None),
            P(("rep", "shard"), None),
            P("shard"),
            P("shard", None),
            P("shard", None),
            P("shard"),
            P("shard"),
            P("shard"),
            P("shard"),
            P("shard"),
            P("shard", None),
            P(("rep", "shard")),
            P(("rep", "shard")),
        ),
        out_specs=(
            P(("rep", "shard"), None),
            P(("rep", "shard"), None),
            P("shard"),
            P("shard", None),
            P("shard", None),
            P("shard"),
            P("shard"),
            P("shard"),
            P("shard"),
            P("shard"),
            P("shard", None),
        ),
        check_vma=False,
    )
```

```python
import functools

import jax
import jax.numpy as jnp
from jax import lax
from jax.experimental import pallas as pl
from jax.experimental.pallas import tpu as pltpu
from jax.sharding import PartitionSpec as P

HEADS = 48
HEADDIM = 64
DSTATE = 128
CONV = 4
SPAN = 256
DI = 3072
CC = 3328
TILE = 256
GROUPS = DI // TILE
PER = TILE // HEADDIM
CHUNK = 64
LANES = 128
epsilon = 1e-05
FAR = -1e30
LOG2E = 1.4426950408889634
PACK = 4 * PER

BF = jnp.bfloat16
F32 = jnp.float32
MIB = 1 << 20


def dot(lhs, rhs):
    return jnp.dot(lhs, rhs, preferred_element_type=F32)


def dot_nt(lhs, rhs):
    return lax.dot_general(lhs, rhs, (((1,), (1,)), ((), ())), preferred_element_type=F32)


def dot_tn(lhs, rhs):
    return lax.dot_general(lhs, rhs, (((0,), (0,)), ((), ())), preferred_element_type=F32)


def sigmoid(value):
    return 0.5 * jnp.tanh(0.5 * value) + 0.5


def pieces(value):
    high = value.astype(BF)
    rest = value - high.astype(F32)
    middle = rest.astype(BF)
    low = (rest - middle.astype(F32)).astype(BF)
    return high, middle, low


def fine_dot(lhs, rhs, product):
    high, middle, low = pieces(lhs)
    return product(high, rhs) + (product(middle, rhs) + product(low, rhs))


def row_ids(start, shape):
    return start + lax.broadcasted_iota(jnp.int32, shape, 0)


def live_rows(meta, start, shape):
    ids = row_ids(start, shape)
    return (ids >= meta[1]) & (ids < meta[1] + meta[2])


def gather_lanes(target, blocks, table, at):
    for j, block in enumerate(blocks):
        width = block.shape[1]
        lanes = pl.ds(pl.multiple_of(table[at + j] * width, LANES), width)
        target[0 : block.shape[0], lanes] = block[...]


def call(
    body, name, meta, operands, in_specs, outs, out_specs, scratch, grid, flops, moved, filled=None
):
    if filled:
        first = len(operands) + 1
        operands, extra = operands + tuple(filled.values()), len(filled)
        in_specs = in_specs + [pl.BlockSpec(memory_space=pl.ANY)] * extra
        aliases = {first + n: place for n, place in enumerate(filled)}
        inner, many = body, first - 1

        def body(meta, *refs):
            return inner(meta, *refs[:many], *refs[many + extra :])
    else:
        aliases = {}
    return pl.pallas_call(
        body,
        name=name,
        grid_spec=pltpu.PrefetchScalarGridSpec(
            num_scalar_prefetch=1,
            grid=(grid,),
            in_specs=in_specs,
            out_specs=out_specs,
            scratch_shapes=scratch,
        ),
        out_shape=outs,
        input_output_aliases=aliases,
        compiler_params=pltpu.CompilerParams(vmem_limit_bytes=60 * MIB),
        cost_estimate=pl.CostEstimate(flops=flops, bytes_accessed=moved, transcendentals=0),
    )(meta, *operands)


def whole(shape):
    rank = len(shape)
    return pl.BlockSpec(shape, lambda i, meta: (0,) * rank)


def tiles(rows, width, shift=0, last=None):
    def index(i, meta):
        at = i + shift
        if last is not None:
            at = jnp.clip(at, 0, last)
        return (0, at)

    return pl.BlockSpec((rows, width), index)


def shape_of(shape, kind=F32):
    return jax.ShapeDtypeStruct(shape, kind)


TABLE = 4
UNITS = 4
OUT_TABLE = TABLE + 2 * UNITS
WIDE = 512
WIDES = DI // WIDE


def own_tile(i, meta):
    half = WIDES // 2
    return jnp.where(i < half, meta[0] * half + i, (1 - meta[0]) * half + i - half)


def live_lanes(meta, live):
    live[...] = jnp.where(live_rows(meta, 0, live.shape), 1.0, 0.0)


def convolve(low, taps, live, shifted, masked, signal, slope, begin):
    for lane in range(0, low.shape[1], LANES):
        cut = slice(begin + lane, begin + lane + LANES)
        tile = (begin + lane) // LANES
        for at in range(0, low.shape[0], CHUNK):
            part = low[at : at + CHUNK, lane : lane + LANES].astype(BF).astype(F32)
            part = part * live[at : at + CHUNK, :]
            masked[at : at + CHUNK, cut] = part.astype(BF)
            shifted[tile, 8 + at : 8 + at + CHUNK, :] = part
        for at in range(0, low.shape[0], CHUNK):
            out = taps[4:5, cut]
            for k in range(CONV):
                out = out + shifted[tile, at + 5 + k : at + 5 + k + CHUNK, :] * taps[k : k + 1, cut]
            sigma = sigmoid(out)
            out = out * sigma
            here = live[at : at + CHUNK, :]
            signal[at : at + CHUNK, cut] = (out * here).astype(BF)
            slope[at : at + CHUNK, cut] = (sigma + out * (1.0 - sigma)) * here


def conv_body(meta, x, taps, taps_keys, steps, *refs):
    count = UNITS
    own, rest, key_rows, dts = (refs[n * count : (n + 1) * count] for n in range(4))
    (masked, signal, slope, masked_keys, keys, slope_keys, columns, rows, trio,
     weight, weight_dt, shifted, live) = refs[4 * count :]
    tokens = x.shape[0]
    step = pl.program_id(0)

    @pl.when(step == 0)
    def _():
        shifted[:, 0:8, :] = jnp.zeros((WIDE // LANES, 8, LANES), F32)
        live_lanes(meta, live)
        gather_lanes(weight, key_rows, meta, TABLE)
        gather_lanes(weight_dt, dts, meta, TABLE)
        low = dot_nt(x[...], weight[0:TILE, :])
        raw = dot_nt(x[...], weight_dt[...]).astype(BF).astype(F32)
        convolve(low, taps_keys, live, shifted, masked_keys, keys, slope_keys, 0)
        raw = jnp.concatenate([raw, jnp.zeros((tokens, LANES - raw.shape[1]), F32)], axis=1)
        pre = raw + steps[0:1, :]
        size = jnp.maximum(pre, 0.0) + jnp.log1p(jnp.exp(-jnp.abs(pre)))
        rate = size * steps[1:2, :]
        lower = row_ids(0, (SPAN, SPAN)) >= lax.broadcasted_iota(jnp.int32, (SPAN, SPAN), 1)
        lower = jnp.where(lower, 1.0, 0.0).astype(BF)
        trio[0] = pre
        trio[1] = size
        for at in range(0, tokens, SPAN):
            high, middle, small = pieces(rate[at : at + SPAN])
            trio[2, at : at + SPAN, :] = dot(lower, high) + (dot(lower, middle) + dot(lower, small))
        log = trio[2] * LOG2E
        less = log - jnp.log(size) * LOG2E
        factor = jnp.concatenate(
            [jnp.exp2(log[SPAN - 1 : SPAN] - less[:SPAN]), jnp.exp2(log[SPAN:])], axis=0
        )
        high = factor.astype(BF).astype(F32)
        rest_factor = factor - high
        less_rows = less.T
        log_rows = log.T
        for g in range(GROUPS):
            a, b = g * PER, (g + 1) * PER
            columns[g] = jnp.concatenate(
                [log[:, a:b], less[:, a:b], high[:, a:b], rest_factor[:, a:b]], axis=1
            )
            rows[g] = jnp.concatenate([log_rows[a:b], less_rows[a:b]], axis=0)

    @pl.when((step > 0) & (step <= WIDES // 2))
    def _():
        gather_lanes(weight, own, meta, TABLE)

    @pl.when(step > WIDES // 2)
    def _():
        gather_lanes(weight, rest, meta, TABLE + count)

    @pl.when(step > 0)
    def _():
        lows = [dot_nt(x[...], weight[at : at + TILE, :]) for at in range(0, WIDE, TILE)]
        for n, low in enumerate(lows):
            convolve(low, taps, live, shifted, masked, signal, slope, n * TILE)


def conv_forward(meta, x, taps, steps, own, rest, local):
    tokens, width = x.shape
    count = UNITS
    part = width // count
    half = WIDES // 2

    def natural(i, meta):
        return own_tile(jnp.maximum(i - 1, 0), meta)

    def tile(rows):
        return pl.BlockSpec((rows, WIDE), lambda i, meta: (0, natural(i, meta)))

    def late(i):
        return jnp.maximum(i - 1 - half, 0)

    own_spec = pl.BlockSpec((WIDE, part), lambda i, meta: (jnp.clip(i - 1, 0, half - 1), 0))
    rest_spec = pl.BlockSpec((WIDE, part), lambda i, meta: (late(i), 0))
    local_spec = pl.BlockSpec(
        (WIDE, part), lambda i, meta: (WIDES + (1 - meta[0]) * half + late(i), 0)
    )
    key_spec = pl.BlockSpec((TILE, part), lambda i, meta: (half * WIDE // TILE, 0))
    dt_spec = pl.BlockSpec((64, part), lambda i, meta: ((half * WIDE + TILE) // 64, 0))
    return call(
        conv_body, "conv_forward", meta,
        (x, taps, taps, steps) + tuple(own) + (() if local is None else (local,)) + tuple(rest)
        + tuple(own) * 2,
        [
            whole((tokens, width)), tile(8), pl.BlockSpec((8, TILE), lambda i, meta: (0, DI // TILE)),
            whole((8, LANES)),
        ]
        + [own_spec] * count
        + [rest_spec if local is None else local_spec] + [rest_spec] * (count - 1)
        + [key_spec] * count + [dt_spec] * count,
        [
            shape_of((tokens, DI), BF), shape_of((tokens, DI), BF), shape_of((tokens, DI)),
            shape_of((tokens, TILE), BF), shape_of((tokens, TILE), BF), shape_of((tokens, TILE)),
            shape_of((GROUPS, tokens, PACK)), shape_of((GROUPS, 2 * PER, tokens)),
            shape_of((3, tokens, LANES)),
        ],
        [
            tile(tokens), tile(tokens), tile(tokens),
            whole((tokens, TILE)), whole((tokens, TILE)), whole((tokens, TILE)),
            whole((GROUPS, tokens, PACK)), whole((GROUPS, 2 * PER, tokens)),
            whole((3, tokens, LANES)),
        ],
        [
            pltpu.VMEM((WIDE, width), BF), pltpu.VMEM((64, width), BF),
            pltpu.VMEM((WIDE // LANES, tokens + 8, LANES), F32), pltpu.VMEM((tokens, LANES), F32),
        ],
        1 + WIDES, 2 * tokens * width * CC, 24 * MIB,
    )


def lane_half(shape, half):
    ids = lax.broadcasted_iota(jnp.int32, shape, 1)
    return (ids >= HEADDIM) if half else (ids < HEADDIM)


def heads_apart(value, ones):
    return jnp.concatenate([value * ones[0:1], value * ones[1:2]], axis=0)


def heads_together(stacked):
    middle = stacked.shape[0] // 2
    upper = stacked[:middle]
    return jnp.where(lane_half(upper.shape, 0), upper, stacked[middle:])


def head_lanes(shape, width):
    lane = lax.broadcasted_iota(jnp.int32, shape, 1) // width
    row = lax.broadcasted_iota(jnp.int32, shape, 0) % PER
    return jnp.where(lane == row, 1.0, 0.0).astype(BF)


def scan_body(
    meta, content, keys, columns, rows, skip, out, entering,
    scores, write_rows, mixes, blocked, spread,
):
    half = SPAN // 2

    @pl.when(pl.program_id(0) == 0)
    def _():
        for span in range(2):
            at = span * SPAN
            scores[span] = dot_nt(keys[at : at + SPAN, DSTATE:], keys[at : at + SPAN, :DSTATE])
        write_rows[...] = keys[0:SPAN, :DSTATE].astype(F32).T.astype(BF)
        mixes[...] = jnp.zeros_like(mixes)
        after = row_ids(0, blocked.shape) >= lax.broadcasted_iota(jnp.int32, blocked.shape, 1)
        blocked[...] = jnp.where(after, 0.0, FAR)
        spread[...] = head_lanes(spread.shape, HEADDIM)

    factor = dot(columns[0, :, 2 * PER :].astype(BF), spread[...])
    first = content[0:SPAN, :].astype(F32)
    state = dot(write_rows[...], (first * factor[:SPAN]).astype(BF)).astype(BF)
    entering[0] = state
    out[0:SPAN, :] = skip[...] * first
    carried = dot(keys[SPAN:, DSTATE:], state) * factor[SPAN:]
    out[SPAN:, :] = carried + skip[...] * content[SPAN:, :].astype(F32)
    for pair in range(PER // 2):
        lanes = slice(pair * 2 * HEADDIM, (pair + 1) * 2 * HEADDIM)
        for h in range(2):
            n = 2 * pair + h
            for span in range(2):
                for at in range(0, SPAN, CHUNK):
                    row = span * SPAN + at
                    corner = at // half * half
                    log = columns[0, row : row + CHUNK, n : n + 1]
                    for begin in range(0, corner + half, half):
                        cut = slice(begin, begin + half)
                        less = rows[0, PER + n : PER + n + 1, span * SPAN + begin : span * SPAN + begin + half]
                        decay = log - less
                        if begin == corner:
                            decay = decay + blocked[at - begin : at - begin + CHUNK, :]
                        mix = scores[span, at : at + CHUNK, cut] * jnp.exp2(decay)
                        mixes[pair, span, h * SPAN + at : h * SPAN + at + CHUNK, cut] = mix.astype(BF)
        for span in range(2):
            at = span * SPAN
            value = content[at : at + SPAN, lanes]
            out[at : at + SPAN, lanes] += heads_together(dot(mixes[pair, span], value))


def scan_forward(meta, signal, keys, columns, rows, skip):
    tokens = signal.shape[0]
    return call(
        scan_body, "scan_forward", meta, (signal, keys, columns, rows, skip),
        [
            tiles(tokens, TILE), whole((tokens, TILE)),
            pl.BlockSpec((1, tokens, PACK), lambda i, meta: (i, 0, 0)),
            pl.BlockSpec((1, 2 * PER, tokens), lambda i, meta: (i, 0, 0)),
            tiles(1, TILE),
        ],
        [shape_of((tokens, DI)), shape_of((GROUPS, DSTATE, TILE), BF)],
        [tiles(tokens, TILE), pl.BlockSpec((1, DSTATE, TILE), lambda i, meta: (i, 0, 0))],
        [
            pltpu.VMEM((2, SPAN, SPAN), F32), pltpu.VMEM((DSTATE, SPAN), BF),
            pltpu.VMEM((PER // 2, 2, 2 * SPAN, SPAN), BF), pltpu.VMEM((SPAN // 2, SPAN // 2), F32),
            pltpu.VMEM((2 * PER, TILE), BF),
        ],
        GROUPS, 10 * 10**9, 12 * MIB,
    )


def gate_body(meta, x, mixed, gain, *refs):
    count = UNITS
    own, rest = refs[:count], refs[count : 2 * count]
    gate, normed, theirs, scale, weight, gated, total = refs[2 * count :]
    step = pl.program_id(0)
    tokens = x.shape[0]

    @pl.when(step < WIDES // 2)
    def _():
        gather_lanes(weight, own, meta, TABLE)

    @pl.when(step >= WIDES // 2)
    def _():
        gather_lanes(weight, rest, meta, TABLE + count)

    @pl.when(step == 0)
    def _():
        total[...] = jnp.zeros_like(total)

    here = own_tile(step, meta) * WIDE
    lows = [dot_nt(x[...], weight[at : at + TILE, :]).astype(BF) for at in range(0, WIDE, TILE)]
    for n, low in enumerate(lows):
        lanes = slice(n * TILE, (n + 1) * TILE)
        place = pl.ds(pl.multiple_of(here + n * TILE, TILE), TILE)
        gate[:, lanes] = low
        for at in range(0, tokens, CHUNK):
            part = low[at : at + CHUNK].astype(F32)
            part = mixed[at : at + CHUNK, lanes] * (part * sigmoid(part))
            gated[at : at + CHUNK, place] = part
            square = part * part
            total[at : at + CHUNK, :] += square[:, :LANES] + square[:, LANES:]

    @pl.when(step == pl.num_programs(0) - 1)
    def _():
        mean = jnp.sum(total[...], axis=1, keepdims=True) / DI
        scale[...] = lax.rsqrt(mean + epsilon)

        def finish(n, carry):
            place = pl.ds(pl.multiple_of(n * CHUNK, CHUNK), CHUNK)
            factor = jnp.broadcast_to(scale[place, :], (CHUNK, LANES))
            for at in range(0, DI, LANES):
                part = gated[place, at : at + LANES] * factor * gain[:, at : at + LANES]
                normed[place, at : at + LANES] = part.astype(BF)
            return carry

        lax.fori_loop(0, tokens // CHUNK, finish, 0)
        half = DI // (2 * count)
        for k in range(count):
            other = pl.multiple_of((2 * k + 1 - meta[0]) * half, LANES)
            theirs[:, k * half : (k + 1) * half] = normed[:, pl.ds(other, half)]


def gate_forward(meta, x, mixed, gain, own, rest, local):
    tokens, width = x.shape
    count = UNITS
    part = width // count
    half = WIDES // 2
    tile_spec = pl.BlockSpec((tokens, WIDE), lambda i, meta: (0, own_tile(i, meta)))
    own_spec = pl.BlockSpec((WIDE, part), lambda i, meta: (jnp.minimum(i, half - 1), 0))
    rest_spec = pl.BlockSpec((WIDE, part), lambda i, meta: (jnp.maximum(i - half, 0), 0))
    local_spec = pl.BlockSpec(
        (WIDE, part), lambda i, meta: ((1 - meta[0]) * half + jnp.maximum(i - half, 0), 0)
    )
    return call(
        gate_body, "gate_forward", meta,
        (x, mixed, gain) + tuple(own) + (() if local is None else (local,)) + tuple(rest),
        [whole((tokens, width)), tile_spec, whole((1, DI))] + [own_spec] * count
        + [rest_spec if local is None else local_spec] + [rest_spec] * (count - 1),
        [
            shape_of((tokens, DI), BF), shape_of((tokens, DI), BF), shape_of((tokens, DI // 2), BF),
            shape_of((tokens, 1)),
        ],
        [tile_spec, whole((tokens, DI)), whole((tokens, DI // 2)), whole((tokens, 1))],
        [
            pltpu.VMEM((WIDE, width), BF), pltpu.VMEM((tokens, DI), F32),
            pltpu.VMEM((tokens, LANES), F32),
        ],
        WIDES, 2 * tokens * width * DI, 28 * MIB,
    )


def out_body(meta, *refs):
    count = UNITS
    normed, pulled, hidden = refs[0:2], refs[2], refs[3]
    block, back, total, weight, branch = refs[-5:]
    refs = refs[4:-5]
    many = len(refs) // 2
    sides = refs[:many], refs[many:]
    step = pl.program_id(0)
    tokens = pulled.shape[0]
    half = DI // (2 * count)

    @pl.when(step == 0)
    def _():
        total[...] = jnp.zeros_like(total)

    for j in range(count):
        @pl.when(step == j)
        def _(j=j):
            for side, parts in enumerate(sides):
                weight[side * half : (side + 1) * half, :] = parts[j][...]

    normed_both = jnp.concatenate([normed[0][...], normed[1][...]], axis=1)
    grads = dot_nt(pulled[...], weight[...]).astype(BF)
    more = dot(normed_both, weight[...])

    @pl.when(step == 0)
    def _():
        branch[...] = more

    @pl.when((step > 0) & (step < count - 1))
    def _():
        branch[...] += more

    for side in range(2):
        at = meta[OUT_TABLE + side * count + step] * half
        back[:, pl.ds(pl.multiple_of(at, LANES), half)] = grads[:, side * half : (side + 1) * half]
    for at in range(0, tokens, CHUNK):
        sums = None
        for lane in range(0, 2 * half, LANES):
            one = grads[at : at + CHUNK, lane : lane + LANES].astype(F32)
            one = one * normed_both[at : at + CHUNK, lane : lane + LANES].astype(F32)
            sums = one if sums is None else sums + one
        total[at : at + CHUNK, :] += sums

    @pl.when(step == count - 1)
    def _():
        for at in range(0, tokens, CHUNK):
            part = branch[at : at + CHUNK, :] + more[at : at + CHUNK, :]
            part = jnp.where(live_rows(meta, at, part.shape), part, 0.0)
            block[at : at + CHUNK, :] = (hidden[at : at + CHUNK, :].astype(F32) + part).astype(BF)


def out_forward(meta, normed, pulled, hidden, own, rest, local):
    tokens, width = hidden.shape
    count = UNITS
    half = DI // (2 * count)

    def columns(side):
        return pl.BlockSpec(
            (tokens, half), lambda i, meta: (0, meta[OUT_TABLE + side * count + i])
        )

    def local_spec(side):
        return pl.BlockSpec((half, width), lambda i, meta: (meta[0] if side == 0 else 1 - meta[0], 0))

    first = () if local is None else (local,)

    def weight_specs(side):
        if local is None:
            return [whole((half, width))] * count
        return [local_spec(side)] + [whole(part.shape) for part in own]

    return call(
        out_body, "out_forward", meta,
        (normed, normed, pulled, hidden) + (first + tuple(own) + first + tuple(rest)),
        [columns(0), columns(1), whole((tokens, width)), whole((tokens, width))]
        + weight_specs(0) + weight_specs(1),
        [shape_of((tokens, width), BF), shape_of((tokens, DI), BF), shape_of((tokens, LANES))],
        [whole((tokens, width)), whole((tokens, DI)), whole((tokens, LANES))],
        [pltpu.VMEM((2 * half, width), BF), pltpu.VMEM((tokens, width), F32)],
        count, 4 * tokens * width * DI, 24 * MIB,
    )


STEPS = 4


def norm_back_body(
    meta, back, total, mixed, gate, scale, gain, grad_gate, theirs, grad_mixed, grad_gain
):
    step = pl.program_id(0)
    tokens, width = back.shape
    grad_gain[...] = jnp.zeros_like(grad_gain)

    def one(n, carry):
        rows = pl.ds(pl.multiple_of(n * CHUNK, CHUNK), CHUNK)
        r = jnp.broadcast_to(scale[rows, :], (CHUNK, LANES))
        mean = jnp.sum(total[rows, :], axis=1, keepdims=True) / DI
        factor = r * r * mean
        for at in range(0, width, LANES):
            cut = slice(at, at + LANES)
            z = gate[rows, cut].astype(F32)
            sigma = sigmoid(z)
            silu = z * sigma
            out = mixed[rows, cut]
            gated = out * silu
            grad = back[rows, cut].astype(F32) * r
            grad_gain[:, cut] += fold(grad * gated)
            grad = grad * gain[:, cut] - gated * factor
            grad_mixed[rows, cut] = (grad * silu).astype(BF)
            grad_gate[rows, cut] = ((grad * out) * (sigma + silu * (1.0 - sigma))).astype(BF)
        return carry

    lax.fori_loop(0, tokens // CHUNK, one, 0)

    @pl.when(step // (STEPS // 2) == 1 - meta[0])
    def _():
        theirs[...] = grad_gate[...]


def norm_back(meta, back, total, mixed, gate, scale, gain):
    tokens = back.shape[0]
    width = DI // STEPS

    def tile(rows):
        return pl.BlockSpec((rows, width), lambda i, meta: (0, i))

    theirs_spec = pl.BlockSpec(
        (tokens, width),
        lambda i, meta: (0, jnp.clip(i - (1 - meta[0]) * (STEPS // 2), 0, STEPS // 2 - 1)),
    )
    return call(
        norm_back_body, "norm_back", meta, (back, total, mixed, gate, scale, gain),
        [tile(tokens), whole((tokens, LANES)), tile(tokens), tile(tokens), whole((tokens, 1)), tile(1)],
        [
            shape_of((tokens, DI), BF), shape_of((tokens, DI // 2), BF), shape_of((tokens, DI), BF),
            shape_of((8, DI)),
        ],
        [tile(tokens), theirs_spec, tile(tokens), tile(8)],
        [], STEPS, 10**9, 24 * MIB,
    )


def rows_product_body(meta, mine, theirs, pulled, pulled_rest, send, keep):
    total = dot_tn(mine[...], pulled[...]) + dot_tn(theirs[...], pulled_rest[...])
    total = total.astype(BF)
    sent = pl.num_programs(0) // 2

    @pl.when(pl.program_id(0) < sent)
    def _():
        send[0] = total

    @pl.when(pl.program_id(0) >= sent)
    def _():
        keep[0] = total


def rows_product(meta, normed, arrived, arrived_at, pulled, pulled_rest, units):
    tokens, width = pulled.shape
    unit = DI // (2 * UNITS)
    upper = units // 2

    def which(i):
        return lax.rem(i + upper, units)

    result = shape_of((upper, unit, width), BF)
    return call(
        rows_product_body, "rows_product", meta, (normed, arrived, pulled, pulled_rest),
        [
            pl.BlockSpec((tokens, unit), lambda i, meta: (0, meta[OUT_TABLE + which(i)])),
            pl.BlockSpec((tokens, unit), lambda i, meta: (0, meta[arrived_at + which(i)])),
            whole((tokens, width)), whole((tokens, width)),
        ],
        [result, result],
        [
            pl.BlockSpec((1, unit, width), lambda i, meta: (jnp.minimum(i, upper - 1), 0, 0)),
            pl.BlockSpec((1, unit, width), lambda i, meta: (jnp.maximum(i - upper, 0), 0, 0)),
        ],
        [], units, 4 * tokens * width * unit * units, 12 * MIB,
    )


def columns_product_body(plan, meta, *refs):
    parts = len(plan)
    mine, theirs = refs[:parts], refs[parts : 2 * parts]
    here, there, send, keep, right, right_rest = refs[2 * parts :]
    step = pl.program_id(0)
    width = here.shape[1] // UNITS

    @pl.when(step == 0)
    def _():
        for j in range(UNITS):
            lanes = pl.ds(pl.multiple_of(meta[TABLE + j] * width, LANES), width)
            right[:, j * width : (j + 1) * width] = here[:, lanes]
            right_rest[:, j * width : (j + 1) * width] = there[:, lanes]

    for (begin, steps), a, b in zip(plan, mine, theirs):
        @pl.when((step >= begin) & (step < begin + steps))
        def _(a=a, b=b):
            total = (dot_tn(a[...], right[...]) + dot_tn(b[...], right_rest[...])).astype(BF)
            for k in range(UNITS // 2):
                keep[k] = total[:, k * width : (k + 1) * width]
                other = UNITS // 2 + k
                send[k] = total[:, other * width : (other + 1) * width]


def columns_product(meta, parts, normed, normed_rest):
    tokens, width = normed.shape
    part = width // UNITS
    plan, step, mine_specs, theirs_specs = [], 0, [], []

    def spec(begin, steps, start):
        return pl.BlockSpec(
            (tokens, TILE), lambda i, meta: (0, start(meta) + jnp.clip(i - begin, 0, steps - 1))
        )

    for matrix, start, steps, arrived in parts:
        plan.append((step, steps))
        mine_specs.append(spec(step, steps, start))
        theirs_specs.append(spec(step, steps, lambda meta: 0))
        step += steps
    result = shape_of((UNITS // 2, step * TILE, part), BF)
    result_spec = pl.BlockSpec((UNITS // 2, TILE, part), lambda i, meta: (0, i, 0))
    return call(
        functools.partial(columns_product_body, tuple(plan)), "columns_product", meta,
        tuple(p[0] for p in parts) + tuple(p[3] for p in parts) + (normed, normed_rest),
        mine_specs + theirs_specs + [whole((tokens, width))] * 2,
        [result, result], [result_spec, result_spec],
        [pltpu.VMEM((tokens, width), BF), pltpu.VMEM((tokens, width), BF)],
        step, 1, 1,
    )


def conv_back(meta, masked, taps, result, sums, live, grad_conv):
    tokens = masked.shape[0]
    grad_conv[:, tokens:, :] = jnp.zeros((TILE // LANES, 8, LANES), F32)
    sums[...] = jnp.zeros_like(sums)
    for lane in range(0, TILE, LANES):
        cut = slice(lane, lane + LANES)
        totals = [jnp.zeros((8, LANES), F32) for _ in range(CONV + 1)]
        for at in range(0, tokens, CHUNK):
            near = [
                grad_conv[lane // LANES, at + 3 - k : at + 3 - k + CHUNK, :] for k in range(CONV)
            ]
            value = masked[at : at + CHUNK, cut].astype(F32)
            out = near[0] * taps[0:1, cut]
            for k in range(1, CONV):
                out = out + near[k] * taps[k : k + 1, cut]
            result[at : at + CHUNK, cut] = (out * live[at : at + CHUNK, :]).astype(BF)
            for k in range(CONV):
                totals[k] = totals[k] + fold(near[k] * value)
            totals[CONV] = totals[CONV] + fold(near[CONV - 1])
        for k in range(CONV + 1):
            sums[k : k + 1, cut] = jnp.sum(totals[k], axis=0, keepdims=True)


def fold(value):
    return jnp.sum(value.reshape(value.shape[0] // 8, 8, value.shape[1]), axis=0)


def scan_back_body(
    meta, content, keys, grad_out, mixed, entering, columns, rows, skip, masked, slope, taps,
    scores_in, write_in, read_in,
    result, theirs, sums, grad_columns, grad_scores, grad_write, grad_read,
    scores, read_rows, live, grad_conv, mixes, mix_grads, blocked, spread,
):
    half = SPAN // 2

    @pl.when(pl.program_id(0) == 0)
    def _():
        for span in range(2):
            at = span * SPAN
            scores[span] = dot_nt(keys[at : at + SPAN, :DSTATE], keys[at : at + SPAN, DSTATE:])
        read_rows[...] = keys[SPAN:, DSTATE:].astype(F32).T.astype(BF)
        grad_scores[...] = scores_in[...]
        grad_write[...] = write_in[...]
        grad_read[...] = read_in[...]
        mixes[...] = jnp.zeros_like(mixes)
        live_lanes(meta, live)
        after = row_ids(0, blocked.shape) <= lax.broadcasted_iota(jnp.int32, blocked.shape, 1)
        blocked[...] = jnp.where(after, 0.0, FAR)
        spread[...] = head_lanes(spread.shape, HEADDIM)

    def heads_sum(value):
        high = value.astype(BF)
        low = (value - high.astype(F32)).astype(BF)
        return dot_nt(high, spread[...]) + dot_nt(low, spread[...])

    for pair in range(PER // 2):
        lanes = slice(pair * 2 * HEADDIM, (pair + 1) * 2 * HEADDIM)
        ones = spread[2 * pair : 2 * pair + 2, lanes]
        for span in range(2):
            cut = slice(span * SPAN, (span + 1) * SPAN)
            mix_grads[pair, span] = dot_nt(heads_apart(content[cut, lanes], ones), grad_out[cut, lanes])

    factor = dot(columns[0, :, 2 * PER :].astype(BF), spread[...])
    grown = (grad_out[SPAN:, :].astype(F32) * factor[SPAN:]).astype(BF)
    grad_state = dot(read_rows[...], grown).astype(BF)
    grad_read[...] += dot_nt(grown, entering[0])
    worth = (content[0:SPAN, :].astype(F32) * factor[:SPAN]).astype(BF)
    grad_write[...] += dot_nt(worth, grad_state)
    from_state = dot(keys[0:SPAN, :DSTATE], grad_state) * factor[:SPAN]

    for pair in range(PER // 2):
        for h in range(2):
            n = 2 * pair + h
            for span in range(2):
                top = span * SPAN
                for at in range(0, SPAN, CHUNK):
                    less = columns[0, top + at : top + at + CHUNK, PER + n : PER + n + 1]
                    corner = at // half * half
                    for begin in range(corner, SPAN, half):
                        cut = slice(begin, begin + half)
                        decay = rows[0, n : n + 1, top + begin : top + begin + half] - less
                        if begin == corner:
                            decay = decay + blocked[at - begin : at - begin + CHUNK, :]
                        decay = jnp.exp2(decay)
                        row = h * SPAN + at
                        mix = scores[span, at : at + CHUNK, cut] * decay
                        mixes[pair, span, row : row + CHUNK, cut] = mix.astype(BF)
                        change = mix_grads[pair, span, row : row + CHUNK, cut] * decay
                        grad_scores[span, at : at + CHUNK, cut] += change

    lane = lax.broadcasted_iota(jnp.int32, (SPAN, 2 * PER), 1) < PER
    final = row_ids(0, lane.shape) == SPAN - 1
    skips = jnp.zeros((8, TILE), F32)
    for span in range(2):
        cut = slice(span * SPAN, (span + 1) * SPAN)
        value = content[cut, :].astype(F32)
        pull = grad_out[cut, :].astype(F32)
        both = []
        for pair in range(PER // 2):
            lanes = slice(pair * 2 * HEADDIM, (pair + 1) * 2 * HEADDIM)
            both.append(heads_together(dot(mixes[pair, span], grad_out[cut, lanes])))
        both = jnp.concatenate(both, axis=1)
        if span == 0:
            ended = jnp.sum(fold(value * from_state), axis=0, keepdims=True)
            both = both + from_state
        skipped = skip[...] * value
        skips = skips + fold(pull * value)
        written = heads_sum(value * both)
        read = heads_sum(pull * (mixed[cut, :] - skipped))
        if span == 0:
            ended = heads_sum(jnp.broadcast_to(ended, (8, TILE)))[0:1]
            read = read + jnp.where(final, ended, 0.0)
        grad_columns[0, cut, :] = jnp.where(lane, written, read)
        both = (both + skip[...] * pull) * slope[cut, :]
        for k in range(TILE // LANES):
            grad_conv[k, cut, :] = both[:, k * LANES : (k + 1) * LANES]

    conv_back(meta, masked, taps, result, sums, live, grad_conv)
    sums[5:6, :] = jnp.sum(skips, axis=0, keepdims=True)
    half_steps = pl.num_programs(0) // 2
    at_half = pl.program_id(0) // half_steps

    @pl.when(at_half == 1 - meta[0])
    def _():
        theirs[...] = result[...]


def scan_backward(
    meta, signal, keys, grad_out, mixed, entering, columns, rows, skip, masked, slope, taps, kept,
    first, count,
):
    tokens = signal.shape[0]

    def group(*shape):
        return pl.BlockSpec((1,) + shape, lambda i, meta: (i + first, 0, 0))

    def fresh(*shape):
        return pl.BlockSpec((1,) + shape, lambda i, meta: (i, 0, 0))

    kept_specs = [whole((2, SPAN, SPAN)), whole((SPAN, DSTATE)), whole((SPAN, DSTATE))]
    return call(
        scan_back_body, "scan_backward", meta,
        (signal, keys, grad_out, mixed, entering, columns, rows, skip, masked, slope, taps)
        + tuple(kept),
        [
            tiles(tokens, TILE, first), whole((tokens, TILE)),
            tiles(tokens, TILE, first), tiles(tokens, TILE, first), group(DSTATE, TILE),
            group(tokens, PACK),
            group(2 * PER, tokens), tiles(1, TILE, first), tiles(tokens, TILE, first),
            tiles(tokens, TILE, first), tiles(8, TILE, first),
        ]
        + kept_specs,
        [
            shape_of((tokens, count * TILE), BF), shape_of((tokens, count // 2 * TILE), BF),
            shape_of((8, count * TILE)),
            shape_of((count, tokens, 2 * PER)),
            shape_of((2, SPAN, SPAN)), shape_of((SPAN, DSTATE)), shape_of((SPAN, DSTATE)),
        ],
        [
            tiles(tokens, TILE),
            pl.BlockSpec(
                (tokens, TILE),
                lambda i, meta: (0, jnp.clip(i - (1 - meta[0]) * (count // 2), 0, count // 2 - 1)),
            ),
            tiles(8, TILE), fresh(tokens, 2 * PER),
        ]
        + kept_specs,
        [
            pltpu.VMEM((2, SPAN, SPAN), F32), pltpu.VMEM((DSTATE, SPAN), BF),
            pltpu.VMEM((tokens, LANES), F32), pltpu.VMEM((TILE // LANES, tokens + 8, LANES), F32),
            pltpu.VMEM((PER // 2, 2, 2 * SPAN, SPAN), BF),
            pltpu.VMEM((PER // 2, 2, 2 * SPAN, SPAN), F32),
            pltpu.VMEM((SPAN // 2, SPAN // 2), F32), pltpu.VMEM((2 * PER, TILE), BF),
        ],
        count, 3 * 10**9 * count, count * MIB,
    )


def tail_body(parts, meta, *refs):
    keys, masked, slope, taps, trio, steps, grad_scores, grad_write, grad_read = refs[:9]
    grad_columns = refs[9 : 9 + parts]
    result, sums, raw, small, packs, live, grad_conv = refs[9 + parts :]
    tokens = keys.shape[0]
    for span in range(2):
        at = span * SPAN
        write = keys[at : at + SPAN, :DSTATE]
        read = keys[at : at + SPAN, DSTATE:]
        to_write = fine_dot(grad_scores[span], read, dot)
        to_read = fine_dot(grad_scores[span], write, dot_tn)
        if span == 0:
            to_write = to_write + grad_write[...]
        else:
            to_read = to_read + grad_read[...]
        cut = slice(at, at + SPAN)
        grad_conv[0, cut, :] = to_write * slope[cut, :DSTATE]
        grad_conv[1, cut, :] = to_read * slope[cut, DSTATE:]
    live_lanes(meta, live)
    conv_back(meta, masked, taps, result, sums, live, grad_conv)

    blank = jnp.zeros((tokens, LANES - HEADS), F32)
    of_step, of_log = [], []
    for column_ref in grad_columns:
        for g in range(column_ref.shape[0]):
            of_step.append(column_ref[g, :, :PER])
            of_log.append(column_ref[g, :, PER:])
    grad_size = jnp.concatenate(of_step + [blank], axis=1)
    grad_log = jnp.concatenate(of_log + [blank], axis=1) - grad_size
    upper = row_ids(0, (SPAN, SPAN)) <= lax.broadcasted_iota(jnp.int32, (SPAN, SPAN), 1)
    upper = jnp.where(upper, 1.0, 0.0).astype(BF)
    rates = []
    for at in range(0, tokens, SPAN):
        high, middle, low = pieces(grad_log[at : at + SPAN])
        rates.append(dot(upper, high) + (dot(upper, middle) + dot(upper, low)))
    grad_rate = jnp.concatenate(rates, axis=0)
    decay_rate = steps[1:2, :]
    sigma = jax.nn.sigmoid(trio[0])
    size = trio[1]
    tiny = size > 0.0
    share = jnp.where(tiny, sigma / jnp.where(tiny, size, 1.0), 1.0)
    grad_raw = grad_size * share + grad_rate * decay_rate * sigma
    raw[...] = grad_raw.astype(BF)
    small[...] = jnp.zeros_like(small)
    small[0:1, :] = jnp.sum(grad_raw, axis=0, keepdims=True)
    small[1:2, :] = jnp.sum(grad_rate * trio[1], axis=0, keepdims=True) * decay_rate
    for side in range(2):
        at = meta[0] if side == 0 else 1 - meta[0]
        packs[side, :, :LANES] = result[:, pl.ds(pl.multiple_of(at * LANES, LANES), LANES)]
        packs[side, :, LANES:] = raw[...]


def tail_backward(meta, keys, masked, slope, taps, trio, steps, kept, grad_columns):
    tokens = keys.shape[0]
    last = DI // TILE
    key_spec = whole((tokens, TILE))
    return call(
        functools.partial(tail_body, len(grad_columns)), "tail_backward", meta,
        (keys, masked, slope, taps, trio, steps) + tuple(kept) + tuple(grad_columns),
        [
            key_spec, key_spec, key_spec, pl.BlockSpec((8, TILE), lambda i, meta: (0, last)),
            whole((3, tokens, LANES)), whole((8, LANES)), whole((2, SPAN, SPAN)),
            whole((SPAN, DSTATE)), whole((SPAN, DSTATE)),
        ]
        + [whole(part.shape) for part in grad_columns],
        [
            shape_of((tokens, TILE), BF), shape_of((8, TILE)), shape_of((tokens, LANES), BF),
            shape_of((8, LANES)), shape_of((2, tokens, TILE), BF),
        ],
        [
            whole((tokens, TILE)), whole((8, TILE)), whole((tokens, LANES)), whole((8, LANES)),
            whole((2, tokens, TILE)),
        ],
        [pltpu.VMEM((tokens, LANES), F32), pltpu.VMEM((TILE // LANES, tokens + 8, LANES), F32)],
        1, 1, 1,
    )


def input_body(plan, first, last, meta, *refs):
    count = UNITS
    grads = refs[: len(plan)]
    refs = refs[len(plan) :]
    if not first:
        start, refs = refs[0], refs[1:]
    blocks = []
    for begin, steps, half in plan:
        own, refs = refs[:count], refs[count:]
        rest = None
        if half is not None:
            rest, refs = refs[:count], refs[count:]
        blocks.append((own, rest))
    step = pl.program_id(0)

    if last:
        hidden, out_grad, scale, gain, result, gain_grad, weight, weight_dt, total, folded = refs
    else:
        total, weight = refs

    @pl.when(step == 0)
    def _():
        total[...] = jnp.zeros_like(total) if first else start[...]

    for n, (begin, steps, half) in enumerate(plan):
        @pl.when((step >= begin) & (step < begin + steps))
        def _(n=n, half=half):
            own, rest = blocks[n]
            rows = own[0].shape[0]
            if grads[n].shape[1] == LANES:
                weight_dt[...] = jnp.zeros_like(weight_dt)
                gather_lanes(weight_dt, own, meta, TABLE)
                total[...] += dot(grads[n][...], weight_dt[...])
                return
            if half is None:
                gather_lanes(weight, own, meta, TABLE)
            else:
                @pl.when(meta[0] == half)
                def _():
                    gather_lanes(weight, own, meta, TABLE)

                @pl.when(meta[0] != half)
                def _():
                    gather_lanes(weight, rest, meta, TABLE + count)

            total[...] += dot(grads[n][...], weight[0:rows, :])

    if not last:
        return

    @pl.when(step == pl.num_programs(0) - 1)
    def _():
        tokens, width = hidden.shape
        folded[...] = jnp.zeros_like(folded)

        def finish(n, carry):
            rows = pl.ds(pl.multiple_of(n * 32, 32), 32)
            r = jnp.broadcast_to(scale[rows, :], (32, LANES))
            sums = jnp.zeros((32, LANES), F32)
            for at in range(0, width, LANES):
                cut = slice(at, at + LANES)
                both = total[rows, cut] * hidden[rows, cut].astype(F32)
                folded[:, cut] += fold(both * r)
                sums = sums + both * gain[:, cut]
            mean = jnp.sum(sums, axis=1, keepdims=True) / width
            factor = r * r * r * mean
            for at in range(0, width, LANES):
                cut = slice(at, at + LANES)
                value = r * (total[rows, cut] * gain[:, cut]) - hidden[rows, cut].astype(F32) * factor
                result[rows, cut] = value + out_grad[rows, cut].astype(F32)
            return carry

        lax.fori_loop(0, tokens // 32, finish, 0)
        gain_grad[...] = jnp.sum(folded[...], axis=0, keepdims=True)


def input_backward(meta, start, parts, tokens, width, last=None):
    part = width // UNITS
    plan, step, grad_specs, block_specs, grads, blocks = [], 0, [], [], [], []

    def grad_spec(columns, begin, steps, first):
        return pl.BlockSpec(
            (tokens, columns), lambda i, meta: (0, first + jnp.clip(i - begin, 0, steps - 1))
        )

    def row_spec(rows, begin, steps, first, when):
        def index(i, meta):
            at = first + jnp.clip(i - begin, 0, steps - 1)
            return (at if when is None else jnp.where(when(meta), at, first), 0)

        return pl.BlockSpec((rows, part), index)

    def is_half(half):
        return lambda meta: meta[0] == half

    def not_half(half):
        return lambda meta: meta[0] != half

    for grad, grad_first, steps, half, own, own_first, rest, rest_first, local_first in parts:
        columns = WIDE if half is not None else grad.shape[1]
        row_tile = 64 if columns == LANES else columns
        plan.append((step, steps, half))
        grads.append(grad)
        grad_specs.append(grad_spec(columns, step, steps, grad_first))
        when = None if half is None else is_half(half)
        for matrix in own:
            blocks.append(matrix)
            block_specs.append(row_spec(row_tile, step, steps, own_first, when))
        if half is not None:
            for j, matrix in enumerate(rest):
                blocks.append(matrix)
                row = local_first if j == 0 else rest_first
                block_specs.append(row_spec(row_tile, step, steps, row, not_half(half)))
        step += steps
    more, more_specs = (), []
    outs, out_specs = [shape_of((tokens, width))], [whole((tokens, width))]
    scratch = [pltpu.VMEM((WIDE, width), BF)]
    if last is not None:
        more = tuple(last)
        more_specs = [whole((tokens, width))] * 2 + [whole((tokens, 1)), whole((1, width))]
        outs.append(shape_of((1, width)))
        out_specs.append(whole((1, width)))
        scratch += [
            pltpu.VMEM((LANES, width), BF), pltpu.VMEM((tokens, width), F32),
            pltpu.VMEM((8, width), F32),
        ]
    first = start is None
    return call(
        functools.partial(input_body, tuple(plan), first, last is not None),
        "input_backward", meta,
        tuple(grads) + (() if first else (start,)) + tuple(blocks) + more,
        grad_specs + ([] if first else [whole((tokens, width))]) + block_specs + more_specs,
        outs, out_specs, scratch,
        step, 10**10 if last is None else 10**11, 20 * MIB,
    )


def place_body(halves, last, meta, own, other, out):
    step = pl.program_id(0)

    def put(which, row, rows, at):
        @pl.when(meta[0] == which)
        def _():
            out[at : at + rows, :] = own[row : row + rows, :].astype(F32)

        @pl.when(meta[0] != which)
        def _():
            out[at : at + rows, :] = other[row : row + rows, :].astype(F32)

    for half in range(2):
        @pl.when(step == half)
        def _(half=half):
            put(half, 0, halves, 0)

    if last:
        @pl.when(step == 2)
        def _():
            put(0, halves, LANES, 0)
            put(1, halves, LANES, LANES)
            put(0, halves + LANES, LANES, 2 * LANES)


def place_rows(meta, own, other, halves, first, total, filled, last):
    length, width = own.shape
    return call(
        functools.partial(place_body, halves, last), "place_rows", meta, (own, other),
        [whole((length, width)), whole((length, width))],
        shape_of((total, width)),
        pl.BlockSpec((halves, width), lambda i, meta: (first + i, 0)),
        [], 3 if last else 2, 1, 1, None if filled is None else {0: filled},
    )


NEAR = 8


def mirrored(j, count):
    if count != 4:
        return j
    result, bit, other = 0, 1, count // 2
    while bit < count:
        if j & bit:
            result |= other
        bit, other = bit * 2, other // 2
    return result


def hop(x, bit):
    reps, count = lax.axis_size("rep"), lax.axis_size("shard")
    pairs = []
    for r in range(reps):
        flip = bit if r % 2 == 0 else mirrored(bit, count)
        pairs += [(r * count + s, r * count + (s ^ flip)) for s in range(count)]
    return lax.ppermute(x, ("rep", "shard"), pairs)


def swap(x):
    return lax.ppermute(x, "rep", [(r, r ^ 1) for r in range(lax.axis_size("rep"))])


def across(x, bit):
    return lax.ppermute(x, "shard", [(s, s ^ bit) for s in range(lax.axis_size("shard"))])


def along(x, pairs):
    return lax.ppermute(x, "rep", [(2 * a + k, 2 * b + k) for a, b in pairs for k in range(2)])


def settle(keep, arrived):
    middle = keep.shape[0] // 2
    if middle == 0:
        return None, keep.astype(F32) + arrived.astype(F32)
    held = (keep.astype(F32) + arrived.astype(F32)).astype(BF)
    return held[middle:], held[:middle]


def finish_stages(send, keep):
    while send is not None:
        send, keep = settle(keep, hop(send, send.shape[0]))
    return keep[0]


def inward(held):
    if lax.axis_size("rep") // 2 != 4:
        return held, None
    return held, along(held.astype(BF), [(0, 1), (3, 2)])


def middle(state):
    held, arrived = state
    if arrived is None:
        return held, None
    inner = (held + arrived.astype(F32)).astype(BF)
    return inner, along(inner, [(1, 2), (2, 1)])


def outward(state):
    inner, arrived = state
    if arrived is None:
        chips = lax.axis_size("rep") // 2
        total, bit = inner.astype(BF), 1
        while bit < chips:
            more = along(total, [(k, k ^ bit) for k in range(chips)])
            total = (total.astype(F32) + more.astype(F32)).astype(BF)
            bit *= 2
        return total, None
    total = (inner.astype(F32) + arrived.astype(F32)).astype(BF)
    return total, along(total, [(1, 0), (2, 3)])


def summed(state):
    total, arrived = state
    if arrived is None:
        return total
    place = lax.axis_index("rep") // 2
    return jnp.where((place == 1) | (place == 2), total, arrived)


def in_order(own, other, core):
    return [jnp.where(core == 0, own, other), jnp.where(core == 0, other, own)]


def hold(values):
    leaves, tree = jax.tree.flatten(values)
    return jax.tree.unflatten(tree, lax.optimization_barrier(tuple(leaves)))


def add_up(rows):
    while len(rows) > 1:
        rows = [a + b for a, b in zip(rows[::2], rows[1::2])]
    return rows[0]


def group_rows(vector, shard, count):
    rows = [lax.dynamic_slice_in_dim(vector, shard ^ j, 1, 0) for j in range(count)]
    return rows[:1] + [across(row, j) for j, row in enumerate(rows) if j]


def chips_sum(row):
    chips = lax.axis_size("rep") // 2
    return add_up(
        [row] + [along(row, [(k, k ^ d) for k in range(chips)]) for d in range(1, chips)]
    )


def join_lanes(blocks, shard):
    return [
        jnp.concatenate(in_order(blocks[j], blocks[j + 1], shard % 2), axis=1)
        for j in range(0, len(blocks), 2)
    ]


def split_lanes(units, shard):
    half = units.shape[2] // 2
    pairs = in_order(units[:, :, :half], units[:, :, half:], shard % 2)
    return jnp.stack(pairs, axis=1).reshape(2 * units.shape[0], units.shape[1], half)


def pad_lanes(matrix):
    return jnp.pad(matrix, ((0, 0), (0, LANES - matrix.shape[1])))


def shards(
    hidden,
    out_grad,
    norm_gain,
    in_w,
    conv_w,
    conv_b,
    dt_bias,
    a_log,
    skip,
    out_gain,
    out_w,
    lengths,
    offsets,
):
    core = lax.axis_index("rep") % 2
    shard = lax.axis_index("shard")
    count = lax.axis_size("shard")
    tokens, width = hidden.shape
    bits = []
    while 2 ** len(bits) < count:
        bits.append(2 ** len(bits))

    local = in_w.T
    half = DI // 2
    piece = jnp.concatenate(
        [
            lax.dynamic_slice_in_dim(local, DI + core * half, half, 0),
            local[2 * DI :],
            jnp.zeros((16, local.shape[1]), BF),
        ],
        axis=0,
    )
    gate_piece = lax.dynamic_slice_in_dim(local, core * half, half, 0)
    out_piece = lax.dynamic_slice_in_dim(out_w, core * (out_w.shape[0] // 2), out_w.shape[0] // 2, 0)

    def spread(first):
        blocks = [first]
        for bit in bits:
            blocks = blocks + [hop(block, bit) for block in blocks]
        return blocks

    paired = count == 4
    small = (norm_gain, conv_w.T, conv_b, dt_bias, a_log, skip, out_gain)
    packed = jnp.concatenate([part.reshape(-1) for part in small])
    everyone = [packed] + [
        lax.ppermute(
            packed, ("rep", "shard"),
            [
                (r * count + s, r * count + (s ^ (j if r % 2 == 0 else mirrored(j, count))))
                for r in range(lax.axis_size("rep"))
                for s in range(count)
            ],
        )
        for j in range(1, count)
    ]
    piece, everyone = hold((piece, everyone))
    everyone = jnp.stack(everyone).astype(F32)
    order = [jnp.where(core == 0, j, mirrored(j, count)) for j in range(count)]
    whose = jnp.stack(order)[jnp.arange(count) ^ shard]
    same = (whose[:, None] == jnp.arange(count)[None]).astype(F32)
    everyone = jnp.sum(same[:, :, None] * everyone[None], axis=1)
    parts, start = [], 0
    for part in small:
        cut = everyone[:, start : start + part.size].reshape((count,) + part.shape)
        cut = jnp.moveaxis(cut, 0, -2)
        parts.append(cut.reshape(part.shape[:-1] + (-1,)))
        start += part.size
    conv_own = spread(piece)
    gate_piece, conv_own = hold((gate_piece, conv_own))
    if paired:
        conv_rest = [swap(block) for block in conv_own[1:]]
        gate_near = hop(gate_piece, 1), hop(gate_piece, 2)
        out_local, in_local = out_w, local
    else:
        gate_own = spread(gate_piece)
        out_piece, gate_own = hold((out_piece, gate_own))
        out_own = spread(out_piece)
        conv_rest = rest_conv = join_lanes([swap(block) for block in conv_own], shard)
        gate_rest = rest_gate = join_lanes([swap(block) for block in gate_own], shard)
        conv_own, gate_own = join_lanes(conv_own, shard), join_lanes(gate_own, shard)
        out_full = [jnp.concatenate(in_order(block, swap(block), core), axis=0) for block in out_own]
        out_one, out_two = out_full[:UNITS], out_full[UNITS:]
        out_local = in_local = None

    gain_one, kernel, bias_conv, bias_step, log_rate, skip_full, gain_two = parts
    decay_rate = -jnp.exp(log_rate)

    mine = order
    other = [jnp.where(core == 0, mirrored(j, count), j) for j in range(count)]
    mine, other = [shard ^ j for j in mine], [shard ^ j for j in other]
    if paired:
        out_units = [2 * j + core for j in mine] + [2 * j + 1 - core for j in other]
    else:
        out_units = mine
        mine = other = [j // 2 for j in mine[::2]]
    meta = jnp.stack(
        [core, offsets[0], lengths[0], shard] + mine + other + out_units
    ).astype(jnp.int32)
    taps = jnp.concatenate([kernel, bias_conv[None], jnp.zeros((3, CC), F32)], axis=0)
    steps = jnp.concatenate(
        [pad_lanes(jnp.stack([bias_step, decay_rate])), jnp.zeros((6, LANES), F32)], axis=0
    )
    skip_lanes = jnp.repeat(skip_full, HEADDIM)[None]

    positions = jnp.arange(tokens, dtype=jnp.int32)
    live_mask = ((positions >= offsets[0]) & (positions < offsets[0] + lengths[0])).astype(F32)
    hidden_full = hidden.astype(F32)
    inv_rms = lax.rsqrt(jnp.mean(hidden_full * hidden_full, axis=1, keepdims=True) + epsilon)
    normed = (hidden_full * inv_rms * gain_one).astype(BF)
    pulled = (out_grad.astype(F32) * live_mask[:, None]).astype(BF)
    normed_rest = swap(normed)
    pulled_rest = swap(pulled)

    (masked, signal, slope, masked_keys, keys, slope_keys, columns, rows, trio) = conv_forward(
        meta, normed, taps, steps, conv_own, conv_rest, in_local
    )
    if paired:
        gate_near, signal = hold((gate_near, signal))
        gate_own = [gate_piece, *gate_near, hop(gate_near[0], 2)]
    mixed, entering = scan_forward(meta, signal, keys, columns, rows, skip_lanes)
    if paired:
        out_piece, gate_far, mixed = hold((out_piece, gate_own[3], mixed))
        gate_own[3] = gate_far
        gate_rest = [swap(block) for block in gate_own[1:]]
        rest_conv, rest_gate = [local] + conv_rest, [local] + gate_rest
        out_near = hop(out_piece, 1), hop(out_piece, 2)
    gate, normed_out, out_theirs, scale = gate_forward(
        meta, normed, mixed, gain_two[None], gate_own, gate_rest, in_local
    )
    out_arrived = swap(out_theirs if paired else normed_out)
    if paired:
        out_near, normed_out = hold((out_near, normed_out))
        out_one = [*out_near, hop(out_near[0], 2)]
        out_two = [swap(block) for block in out_one]

    upper = count // 2
    out_pulls = (pulled, pulled_rest)
    if not paired:
        cut = core * (width // 2)
        out_pulls = [lax.dynamic_slice_in_dim(x, cut, width // 2, 1) for x in out_pulls]

    def product(parts):
        send, keep = columns_product(meta, parts, normed, normed_rest)
        return (send, keep) if paired else (split_lanes(send, shard), split_lanes(keep, shard))

    out_send, out_keep = rows_product(
        meta, normed_out, out_arrived, TABLE if paired else OUT_TABLE, *out_pulls, count
    )
    out_send, out_keep, normed_out = hold((out_send, out_keep, normed_out))
    out_there = hop(out_send, upper)
    block_out, back, total = out_forward(
        meta, normed_out, pulled, hidden, out_one, out_two, out_local
    )
    out_there, total = hold((out_there, total))
    out_send, out_keep = settle(out_keep, out_there)
    out_there = hop(out_send, upper // 2)
    out_keep, total = hold((out_keep, total))
    grad_gate, gate_theirs, grad_mixed, grad_gain_two = norm_back(
        meta, back, total, mixed, gate, scale, gain_two[None]
    )

    gate_theirs, out_there = hold((gate_theirs, out_there))
    gate_arrived = swap(gate_theirs)
    out_line = inward(finish_stages(*settle(out_keep, out_there)))
    out_held, gate_arrived = hold((out_line[0], gate_arrived))
    gate_parts = [(grad_gate, lambda meta: meta[0] * (GROUPS // 2), GROUPS // 2, gate_arrived)]
    gate_send, gate_keep = product(gate_parts)
    gate_send, gate_keep, grad_mixed = hold((gate_send, gate_keep, grad_mixed))
    gate_there = hop(gate_send, upper)
    kept = (
        jnp.zeros((2, SPAN, SPAN), F32),
        jnp.zeros((SPAN, DSTATE), F32),
        jnp.zeros((SPAN, DSTATE), F32),
    )
    near, far = NEAR, GROUPS - NEAR
    part = WIDES // 2
    over = near * TILE // WIDE - part

    def gate_part(half):
        at = half * part
        return [(grad_gate, at, part, half, gate_own, 0, rest_gate, 0, at if paired else 0)]

    def conv_part(grad, grad_first, steps, half, first):
        local_first = WIDES + half * part + first if paired else first
        return [(grad, grad_first, steps, half, conv_own, first, rest_conv, first, local_first)]

    grad_near, near_theirs, sums_near, columns_near, *kept = scan_backward(
        meta, signal, keys, grad_mixed, mixed, entering, columns, rows, skip_lanes, masked, slope, taps,
        kept, 0, near,
    )
    gate_there, near_theirs, out_arrived = hold((gate_there, near_theirs, out_line[1]))
    near_arrived = swap(near_theirs)
    gate_send, gate_keep = settle(gate_keep, gate_there)
    gate_there = hop(gate_send, upper // 2)
    gate_keep, out_arrived = hold((gate_keep, out_arrived))
    out_line = middle((out_held, out_arrived))
    near_arrived, gate_keep, out_inner = hold((near_arrived, gate_keep, out_line[0]))
    near_parts = [(grad_near, lambda meta: meta[0] * (near // 2), near // 2, near_arrived)]
    near_send, near_keep = product(near_parts)
    near_there = hop(near_send, upper)
    near_keep, kept, grad_mixed = hold((near_keep, kept, grad_mixed))
    grad_far, far_theirs, sums_far, columns_far, *kept = scan_backward(
        meta, signal, keys, grad_mixed, mixed, entering, columns, rows, skip_lanes, masked, slope, taps,
        kept, near, far,
    )
    far_theirs, gate_there = hold((far_theirs, gate_there))
    far_arrived = swap(far_theirs)
    gate_line = inward(finish_stages(*settle(gate_keep, gate_there)))
    gate_held, kept = hold((gate_line[0], kept))
    grad_keys, sums_keys, grad_raw, grad_steps, packs = tail_backward(
        meta, keys, masked_keys, slope_keys, taps, trio, steps, kept, (columns_near, columns_far),
    )
    packs, near_there = hold((packs, near_there))
    packs_arrived = swap(packs[1])
    near_send, near_keep = settle(near_keep, near_there)
    near_there = hop(near_send, upper // 2)
    packs, packs_arrived, near_keep = hold((packs, packs_arrived, near_keep))
    far_parts = [
        (grad_far, lambda meta: meta[0] * (far // 2), far // 2, far_arrived),
        (packs[0], lambda meta: 0, 1, packs_arrived),
    ]
    far_send, far_keep = product(far_parts)
    far_there = hop(far_send, upper)
    far_keep, gate_arrived, near_there, out_arrived = hold(
        (far_keep, gate_line[1], near_there, out_line[1])
    )
    gate_line = middle((gate_held, gate_arrived))
    near_line = inward(finish_stages(*settle(near_keep, near_there)))
    out_line = outward((out_inner, out_arrived))
    gate_inner, near_held, out_done, grad_gate = hold(
        (gate_line[0], near_line[0], out_line[0], grad_gate)
    )
    (partial,) = input_backward(meta, None, gate_part(0) + gate_part(1), tokens, width)
    partial, far_there = hold((partial, far_there))
    far_send, far_keep = settle(far_keep, far_there)
    far_there = hop(far_send, upper // 2)
    far_keep, near_arrived, small_grads = hold(
        (far_keep, near_line[1], (sums_near, sums_far, sums_keys, grad_steps, grad_gain_two))
    )
    sums_near, sums_far, sums_keys, grad_steps, grad_gain_two = small_grads
    sums = jnp.concatenate([sums_near, sums_far, sums_keys], axis=1)
    grads = (
        sums[:CONV].reshape(CONV, count, -1).transpose(1, 0, 2).reshape(count, -1),
        sums[CONV].reshape(count, -1),
        grad_steps[0, :HEADS].reshape(count, -1),
        grad_steps[1, :HEADS].reshape(count, -1),
        jnp.sum(sums[5, :DI].reshape(HEADS, HEADDIM), axis=1).reshape(count, -1),
        jnp.sum(grad_gain_two, axis=0).reshape(count, -1),
    )
    vector = jnp.concatenate(grads, axis=1)
    far_there, far_keep, partial, vector = hold((far_there, far_keep, partial, vector))
    vector_there = swap(vector)
    far_line = inward(finish_stages(*settle(far_keep, far_there)))
    far_held, gate_arrived, out_arrived = hold((far_line[0], gate_line[1], out_line[1]))
    gate_line = outward((gate_inner, gate_arrived))
    near_line = middle((near_held, near_arrived))
    out_total = summed((out_done, out_arrived))
    out_other = swap(out_total)
    far_held, gate_done, near_inner, out_total, partial = hold(
        (far_held, gate_line[0], near_line[0], out_total, partial)
    )
    (partial,) = input_backward(
        meta, partial,
        conv_part(grad_near, 0, part, 0, 0)
        + conv_part(grad_near, part, over, 1, 0)
        + conv_part(grad_far, 0, part - over, 1, over),
        tokens, width,
    )
    partial, far_arrived = hold((partial, far_line[1]))
    far_line = middle((far_held, far_arrived))
    far_inner, near_arrived, gate_arrived, out_other, vector_there = hold(
        (far_line[0], near_line[1], gate_line[1], out_other, vector_there)
    )
    spread_rows = group_rows(vector + vector_there, shard, count)
    near_line = outward((near_inner, near_arrived))
    gate_total = summed((gate_done, gate_arrived))
    gate_other = swap(gate_total)
    far_inner, near_done, gate_total, partial = hold((far_inner, near_line[0], gate_total, partial))
    hidden_grad, grad_gain_one = input_backward(
        meta, partial,
        [
            (grad_keys, 0, 1, None, conv_own, DI // 2 // TILE, None, 0, 0),
            (grad_raw, 0, 1, None, conv_own, (DI // 2 + TILE) // 64, None, 0, 0),
        ],
        tokens, width, (hidden, out_grad, inv_rms, gain_one[None]),
    )
    grad_gain_one, far_arrived, gate_other, spread_rows, near_arrived = hold(
        (grad_gain_one, far_line[1], gate_other, spread_rows, near_line[1])
    )
    far_line = outward((far_inner, far_arrived))
    row = chips_sum(add_up(spread_rows))[0]
    far_done, grad_gain_one, gate_other = hold((far_line[0], grad_gain_one, gate_other))
    vector = grad_gain_one[0].reshape(count, -1)
    gain_row = add_up(group_rows(vector + swap(vector), shard, count))
    all_rows = local.shape[0]
    rows_so_far = place_rows(meta, gate_total, gate_other, DI // 2, 0, all_rows, None, False)
    gain_row, row, far_arrived, rows_so_far = hold((gain_row, row, far_line[1], rows_so_far))
    gain_row = chips_sum(gain_row)[0]
    far_total = summed((far_done, far_arrived))
    far_other = swap(far_total)
    near_total = summed((near_done, near_arrived))
    near_other = swap(near_total)
    wide = near // 2 * TILE
    rows_so_far = place_rows(
        meta, near_total, near_other, wide, DI // wide, all_rows, rows_so_far, False
    )
    wide = far // 2 * TILE
    rows_so_far = place_rows(
        meta, far_total, far_other, wide, (DI + near * TILE) // wide, all_rows, rows_so_far, True
    )
    in_w_grad = rows_so_far.T

    out_w_grad = jnp.concatenate(
        in_order(out_total, out_other, core), axis=0 if paired else 1
    ).astype(F32)
    found, start = [], 0
    for part in grads:
        found.append(row[start : start + part.shape[1]])
        start += part.shape[1]
    return (
        block_out,
        hidden_grad,
        gain_row,
        in_w_grad,
        found[0].reshape(CONV, -1).T,
        found[1],
        found[2],
        found[3],
        found[4],
        found[5],
        out_w_grad,
    )


def solution(mesh):
    return jax.shard_map(
        shards,
        mesh=mesh,
        in_specs=(
            P(("rep", "shard"), None),
            P(("rep", "shard"), None),
            P("shard"),
            P("shard", None),
            P("shard", None),
            P("shard"),
            P("shard"),
            P("shard"),
            P("shard"),
            P("shard"),
            P("shard", None),
            P(("rep", "shard")),
            P(("rep", "shard")),
        ),
        out_specs=(
            P(("rep", "shard"), None),
            P(("rep", "shard"), None),
            P("shard"),
            P("shard", None),
            P("shard", None),
            P("shard"),
            P("shard"),
            P("shard"),
            P("shard"),
            P("shard"),
            P("shard", None),
        ),
        check_vma=False,
    )
```

```python
import functools

import jax
import jax.numpy as jnp
from jax import lax
from jax.experimental import pallas as pl
from jax.experimental.pallas import tpu as pltpu
from jax.sharding import PartitionSpec as P

HEADS = 48
HEADDIM = 64
DSTATE = 128
CONV = 4
SPAN = 256
DI = 3072
CC = 3328
TILE = 256
GROUPS = DI // TILE
PER = TILE // HEADDIM
CHUNK = 64
LANES = 128
epsilon = 1e-05
FAR = -1e30
LOG2E = 1.4426950408889634
PACK = 4 * PER

BF = jnp.bfloat16
F32 = jnp.float32
MIB = 1 << 20


def dot(lhs, rhs):
    return jnp.dot(lhs, rhs, preferred_element_type=F32)


def dot_nt(lhs, rhs):
    return lax.dot_general(lhs, rhs, (((1,), (1,)), ((), ())), preferred_element_type=F32)


def dot_tn(lhs, rhs):
    return lax.dot_general(lhs, rhs, (((0,), (0,)), ((), ())), preferred_element_type=F32)


def sigmoid(value):
    return 0.5 * jnp.tanh(0.5 * value) + 0.5


def pieces(value):
    high = value.astype(BF)
    rest = value - high.astype(F32)
    middle = rest.astype(BF)
    low = (rest - middle.astype(F32)).astype(BF)
    return high, middle, low


def fine_dot(lhs, rhs, product):
    high, middle, low = pieces(lhs)
    return product(high, rhs) + (product(middle, rhs) + product(low, rhs))


def row_ids(start, shape):
    return start + lax.broadcasted_iota(jnp.int32, shape, 0)


def live_rows(meta, start, shape):
    ids = row_ids(start, shape)
    return (ids >= meta[1]) & (ids < meta[1] + meta[2])


def gather_lanes(target, blocks, table, at):
    for j, block in enumerate(blocks):
        width = block.shape[1]
        lanes = pl.ds(pl.multiple_of(table[at + j] * width, LANES), width)
        target[0 : block.shape[0], lanes] = block[...]


def call(
    body, name, meta, operands, in_specs, outs, out_specs, scratch, grid, flops, moved, filled=None
):
    if filled:
        first = len(operands) + 1
        operands, extra = operands + tuple(filled.values()), len(filled)
        in_specs = in_specs + [pl.BlockSpec(memory_space=pl.ANY)] * extra
        aliases = {first + n: place for n, place in enumerate(filled)}
        inner, many = body, first - 1

        def body(meta, *refs):
            return inner(meta, *refs[:many], *refs[many + extra :])
    else:
        aliases = {}
    return pl.pallas_call(
        body,
        name=name,
        grid_spec=pltpu.PrefetchScalarGridSpec(
            num_scalar_prefetch=1,
            grid=(grid,),
            in_specs=in_specs,
            out_specs=out_specs,
            scratch_shapes=scratch,
        ),
        out_shape=outs,
        input_output_aliases=aliases,
        compiler_params=pltpu.CompilerParams(vmem_limit_bytes=60 * MIB),
        cost_estimate=pl.CostEstimate(flops=flops, bytes_accessed=moved, transcendentals=0),
    )(meta, *operands)


def whole(shape):
    rank = len(shape)
    return pl.BlockSpec(shape, lambda i, meta: (0,) * rank)


def tiles(rows, width, shift=0, last=None):
    def index(i, meta):
        at = i + shift
        if last is not None:
            at = jnp.clip(at, 0, last)
        return (0, at)

    return pl.BlockSpec((rows, width), index)


def shape_of(shape, kind=F32):
    return jax.ShapeDtypeStruct(shape, kind)


TABLE = 4
UNITS = 4
OUT_TABLE = TABLE + 2 * UNITS
WIDE = 512
WIDES = DI // WIDE


def own_tile(i, meta):
    half = WIDES // 2
    return jnp.where(i < half, meta[0] * half + i, (1 - meta[0]) * half + i - half)


def live_lanes(meta, live):
    live[...] = jnp.where(live_rows(meta, 0, live.shape), 1.0, 0.0)


def convolve(low, taps, live, shifted, masked, signal, slope, begin):
    for lane in range(0, low.shape[1], LANES):
        cut = slice(begin + lane, begin + lane + LANES)
        tile = (begin + lane) // LANES
        for at in range(0, low.shape[0], CHUNK):
            part = low[at : at + CHUNK, lane : lane + LANES].astype(BF).astype(F32)
            part = part * live[at : at + CHUNK, :]
            masked[at : at + CHUNK, cut] = part.astype(BF)
            shifted[tile, 8 + at : 8 + at + CHUNK, :] = part
        for at in range(0, low.shape[0], CHUNK):
            out = taps[4:5, cut]
            for k in range(CONV):
                out = out + shifted[tile, at + 5 + k : at + 5 + k + CHUNK, :] * taps[k : k + 1, cut]
            sigma = sigmoid(out)
            out = out * sigma
            here = live[at : at + CHUNK, :]
            signal[at : at + CHUNK, cut] = (out * here).astype(BF)
            slope[at : at + CHUNK, cut] = (sigma + out * (1.0 - sigma)) * here


def conv_body(meta, x, taps, taps_keys, steps, *refs):
    count = UNITS
    own, rest, key_rows, dts = (refs[n * count : (n + 1) * count] for n in range(4))
    (masked, signal, slope, masked_keys, keys, slope_keys, columns, rows, trio,
     weight, weight_dt, shifted, live) = refs[4 * count :]
    tokens = x.shape[0]
    step = pl.program_id(0)

    @pl.when(step == 0)
    def _():
        shifted[:, 0:8, :] = jnp.zeros((WIDE // LANES, 8, LANES), F32)
        live_lanes(meta, live)
        gather_lanes(weight, key_rows, meta, TABLE)
        gather_lanes(weight_dt, dts, meta, TABLE)
        low = dot_nt(x[...], weight[0:TILE, :])
        raw = dot_nt(x[...], weight_dt[...]).astype(BF).astype(F32)
        convolve(low, taps_keys, live, shifted, masked_keys, keys, slope_keys, 0)
        raw = jnp.concatenate([raw, jnp.zeros((tokens, LANES - raw.shape[1]), F32)], axis=1)
        pre = raw + steps[0:1, :]
        size = jnp.maximum(pre, 0.0) + jnp.log1p(jnp.exp(-jnp.abs(pre)))
        rate = size * steps[1:2, :]
        lower = row_ids(0, (SPAN, SPAN)) >= lax.broadcasted_iota(jnp.int32, (SPAN, SPAN), 1)
        lower = jnp.where(lower, 1.0, 0.0).astype(BF)
        trio[0] = pre
        trio[1] = size
        for at in range(0, tokens, SPAN):
            high, middle, small = pieces(rate[at : at + SPAN])
            trio[2, at : at + SPAN, :] = dot(lower, high) + (dot(lower, middle) + dot(lower, small))
        log = trio[2] * LOG2E
        less = log - jnp.log(size) * LOG2E
        factor = jnp.concatenate(
            [jnp.exp2(log[SPAN - 1 : SPAN] - less[:SPAN]), jnp.exp2(log[SPAN:])], axis=0
        )
        high = factor.astype(BF).astype(F32)
        rest_factor = factor - high
        less_rows = less.T
        log_rows = log.T
        for g in range(GROUPS):
            a, b = g * PER, (g + 1) * PER
            columns[g] = jnp.concatenate(
                [log[:, a:b], less[:, a:b], high[:, a:b], rest_factor[:, a:b]], axis=1
            )
            rows[g] = jnp.concatenate([log_rows[a:b], less_rows[a:b]], axis=0)

    @pl.when((step > 0) & (step <= WIDES // 2))
    def _():
        gather_lanes(weight, own, meta, TABLE)

    @pl.when(step > WIDES // 2)
    def _():
        gather_lanes(weight, rest, meta, TABLE + count)

    @pl.when(step > 0)
    def _():
        lows = [dot_nt(x[...], weight[at : at + TILE, :]) for at in range(0, WIDE, TILE)]
        for n, low in enumerate(lows):
            convolve(low, taps, live, shifted, masked, signal, slope, n * TILE)


def conv_forward(meta, x, taps, steps, own, rest, local):
    tokens, width = x.shape
    count = UNITS
    part = width // count
    half = WIDES // 2

    def natural(i, meta):
        return own_tile(jnp.maximum(i - 1, 0), meta)

    def tile(rows):
        return pl.BlockSpec((rows, WIDE), lambda i, meta: (0, natural(i, meta)))

    def late(i):
        return jnp.maximum(i - 1 - half, 0)

    own_spec = pl.BlockSpec((WIDE, part), lambda i, meta: (jnp.clip(i - 1, 0, half - 1), 0))
    rest_spec = pl.BlockSpec((WIDE, part), lambda i, meta: (late(i), 0))
    local_spec = pl.BlockSpec(
        (WIDE, part), lambda i, meta: (WIDES + (1 - meta[0]) * half + late(i), 0)
    )
    key_spec = pl.BlockSpec((TILE, part), lambda i, meta: (half * WIDE // TILE, 0))
    dt_spec = pl.BlockSpec((64, part), lambda i, meta: ((half * WIDE + TILE) // 64, 0))
    return call(
        conv_body, "conv_forward", meta,
        (x, taps, taps, steps) + tuple(own) + (() if local is None else (local,)) + tuple(rest)
        + tuple(own) * 2,
        [
            whole((tokens, width)), tile(8), pl.BlockSpec((8, TILE), lambda i, meta: (0, DI // TILE)),
            whole((8, LANES)),
        ]
        + [own_spec] * count
        + [rest_spec if local is None else local_spec] + [rest_spec] * (count - 1)
        + [key_spec] * count + [dt_spec] * count,
        [
            shape_of((tokens, DI), BF), shape_of((tokens, DI), BF), shape_of((tokens, DI)),
            shape_of((tokens, TILE), BF), shape_of((tokens, TILE), BF), shape_of((tokens, TILE)),
            shape_of((GROUPS, tokens, PACK)), shape_of((GROUPS, 2 * PER, tokens)),
            shape_of((3, tokens, LANES)),
        ],
        [
            tile(tokens), tile(tokens), tile(tokens),
            whole((tokens, TILE)), whole((tokens, TILE)), whole((tokens, TILE)),
            whole((GROUPS, tokens, PACK)), whole((GROUPS, 2 * PER, tokens)),
            whole((3, tokens, LANES)),
        ],
        [
            pltpu.VMEM((WIDE, width), BF), pltpu.VMEM((64, width), BF),
            pltpu.VMEM((WIDE // LANES, tokens + 8, LANES), F32), pltpu.VMEM((tokens, LANES), F32),
        ],
        1 + WIDES, 2 * tokens * width * CC, 24 * MIB,
    )


def lane_half(shape, half):
    ids = lax.broadcasted_iota(jnp.int32, shape, 1)
    return (ids >= HEADDIM) if half else (ids < HEADDIM)


def heads_apart(value, ones):
    return jnp.concatenate([value * ones[0:1], value * ones[1:2]], axis=0)


def heads_together(stacked):
    middle = stacked.shape[0] // 2
    upper = stacked[:middle]
    return jnp.where(lane_half(upper.shape, 0), upper, stacked[middle:])


def head_lanes(shape, width):
    lane = lax.broadcasted_iota(jnp.int32, shape, 1) // width
    row = lax.broadcasted_iota(jnp.int32, shape, 0) % PER
    return jnp.where(lane == row, 1.0, 0.0).astype(BF)


def scan_body(
    meta, content, keys, columns, rows, skip, out, entering,
    scores, write_rows, mixes, blocked, spread,
):
    half = SPAN // 2

    @pl.when(pl.program_id(0) == 0)
    def _():
        for span in range(2):
            at = span * SPAN
            scores[span] = dot_nt(keys[at : at + SPAN, DSTATE:], keys[at : at + SPAN, :DSTATE])
        write_rows[...] = keys[0:SPAN, :DSTATE].astype(F32).T.astype(BF)
        mixes[...] = jnp.zeros_like(mixes)
        after = row_ids(0, blocked.shape) >= lax.broadcasted_iota(jnp.int32, blocked.shape, 1)
        blocked[...] = jnp.where(after, 0.0, FAR)
        spread[...] = head_lanes(spread.shape, HEADDIM)

    factor = dot(columns[0, :, 2 * PER :].astype(BF), spread[...])
    first = content[0:SPAN, :].astype(F32)
    state = dot(write_rows[...], (first * factor[:SPAN]).astype(BF)).astype(BF)
    entering[0] = state
    out[0:SPAN, :] = skip[...] * first
    carried = dot(keys[SPAN:, DSTATE:], state) * factor[SPAN:]
    out[SPAN:, :] = carried + skip[...] * content[SPAN:, :].astype(F32)
    for pair in range(PER // 2):
        lanes = slice(pair * 2 * HEADDIM, (pair + 1) * 2 * HEADDIM)
        for h in range(2):
            n = 2 * pair + h
            for span in range(2):
                for at in range(0, SPAN, CHUNK):
                    row = span * SPAN + at
                    corner = at // half * half
                    log = columns[0, row : row + CHUNK, n : n + 1]
                    for begin in range(0, corner + half, half):
                        cut = slice(begin, begin + half)
                        less = rows[0, PER + n : PER + n + 1, span * SPAN + begin : span * SPAN + begin + half]
                        decay = log - less
                        if begin == corner:
                            decay = decay + blocked[at - begin : at - begin + CHUNK, :]
                        mix = scores[span, at : at + CHUNK, cut] * jnp.exp2(decay)
                        mixes[pair, span, h * SPAN + at : h * SPAN + at + CHUNK, cut] = mix.astype(BF)
        for span in range(2):
            at = span * SPAN
            value = content[at : at + SPAN, lanes]
            out[at : at + SPAN, lanes] += heads_together(dot(mixes[pair, span], value))


def scan_forward(meta, signal, keys, columns, rows, skip, first, count, filled):
    tokens = signal.shape[0]

    def group(*shape):
        return pl.BlockSpec((1,) + shape, lambda i, meta: (i + first, 0, 0))

    return call(
        scan_body, "scan_forward", meta, (signal, keys, columns, rows, skip),
        [
            tiles(tokens, TILE, first), whole((tokens, TILE)), group(tokens, PACK),
            group(2 * PER, tokens), tiles(1, TILE, first),
        ],
        [shape_of((tokens, DI)), shape_of((GROUPS, DSTATE, TILE), BF)],
        [tiles(tokens, TILE, first), group(DSTATE, TILE)],
        [
            pltpu.VMEM((2, SPAN, SPAN), F32), pltpu.VMEM((DSTATE, SPAN), BF),
            pltpu.VMEM((PER // 2, 2, 2 * SPAN, SPAN), BF), pltpu.VMEM((SPAN // 2, SPAN // 2), F32),
            pltpu.VMEM((2 * PER, TILE), BF),
        ],
        count, 10**9 * count, count * MIB, dict(enumerate(filled)) if filled else None,
    )


def gate_body(meta, x, mixed, gain, *refs):
    count = UNITS
    own, rest = refs[:count], refs[count : 2 * count]
    gate, normed, theirs, scale, weight, gated, total = refs[2 * count :]
    step = pl.program_id(0)
    tokens = x.shape[0]

    @pl.when(step < WIDES // 2)
    def _():
        gather_lanes(weight, own, meta, TABLE)

    @pl.when(step >= WIDES // 2)
    def _():
        gather_lanes(weight, rest, meta, TABLE + count)

    @pl.when(step == 0)
    def _():
        total[...] = jnp.zeros_like(total)

    here = own_tile(step, meta) * WIDE
    lows = [dot_nt(x[...], weight[at : at + TILE, :]).astype(BF) for at in range(0, WIDE, TILE)]
    for n, low in enumerate(lows):
        lanes = slice(n * TILE, (n + 1) * TILE)
        place = pl.ds(pl.multiple_of(here + n * TILE, TILE), TILE)
        gate[:, lanes] = low
        for at in range(0, tokens, CHUNK):
            part = low[at : at + CHUNK].astype(F32)
            part = mixed[at : at + CHUNK, lanes] * (part * sigmoid(part))
            gated[at : at + CHUNK, place] = part
            square = part * part
            total[at : at + CHUNK, :] += square[:, :LANES] + square[:, LANES:]

    @pl.when(step == pl.num_programs(0) - 1)
    def _():
        mean = jnp.sum(total[...], axis=1, keepdims=True) / DI
        scale[...] = lax.rsqrt(mean + epsilon)

        def finish(n, carry):
            place = pl.ds(pl.multiple_of(n * CHUNK, CHUNK), CHUNK)
            factor = jnp.broadcast_to(scale[place, :], (CHUNK, LANES))
            for at in range(0, DI, LANES):
                part = gated[place, at : at + LANES] * factor * gain[:, at : at + LANES]
                normed[place, at : at + LANES] = part.astype(BF)
            return carry

        lax.fori_loop(0, tokens // CHUNK, finish, 0)
        half = DI // (2 * count)
        for k in range(count):
            other = pl.multiple_of((2 * k + 1 - meta[0]) * half, LANES)
            theirs[:, k * half : (k + 1) * half] = normed[:, pl.ds(other, half)]


def gate_forward(meta, x, mixed, gain, own, rest, local):
    tokens, width = x.shape
    count = UNITS
    part = width // count
    half = WIDES // 2
    tile_spec = pl.BlockSpec((tokens, WIDE), lambda i, meta: (0, own_tile(i, meta)))
    own_spec = pl.BlockSpec((WIDE, part), lambda i, meta: (jnp.minimum(i, half - 1), 0))
    rest_spec = pl.BlockSpec((WIDE, part), lambda i, meta: (jnp.maximum(i - half, 0), 0))
    local_spec = pl.BlockSpec(
        (WIDE, part), lambda i, meta: ((1 - meta[0]) * half + jnp.maximum(i - half, 0), 0)
    )
    return call(
        gate_body, "gate_forward", meta,
        (x, mixed, gain) + tuple(own) + (() if local is None else (local,)) + tuple(rest),
        [whole((tokens, width)), tile_spec, whole((1, DI))] + [own_spec] * count
        + [rest_spec if local is None else local_spec] + [rest_spec] * (count - 1),
        [
            shape_of((tokens, DI), BF), shape_of((tokens, DI), BF), shape_of((tokens, DI // 2), BF),
            shape_of((tokens, 1)),
        ],
        [tile_spec, whole((tokens, DI)), whole((tokens, DI // 2)), whole((tokens, 1))],
        [
            pltpu.VMEM((WIDE, width), BF), pltpu.VMEM((tokens, DI), F32),
            pltpu.VMEM((tokens, LANES), F32),
        ],
        WIDES, 2 * tokens * width * DI, 28 * MIB,
    )


def out_body(meta, *refs):
    count = UNITS
    normed, pulled, hidden = refs[0:2], refs[2], refs[3]
    block, back, total, weight, branch = refs[-5:]
    refs = refs[4:-5]
    many = len(refs) // 2
    sides = refs[:many], refs[many:]
    step = pl.program_id(0)
    tokens = pulled.shape[0]
    half = DI // (2 * count)

    @pl.when(step == 0)
    def _():
        total[...] = jnp.zeros_like(total)

    for j in range(count):
        @pl.when(step == j)
        def _(j=j):
            for side, parts in enumerate(sides):
                weight[side * half : (side + 1) * half, :] = parts[j][...]

    normed_both = jnp.concatenate([normed[0][...], normed[1][...]], axis=1)
    grads = dot_nt(pulled[...], weight[...]).astype(BF)
    more = dot(normed_both, weight[...])

    @pl.when(step == 0)
    def _():
        branch[...] = more

    @pl.when((step > 0) & (step < count - 1))
    def _():
        branch[...] += more

    for side in range(2):
        at = meta[OUT_TABLE + side * count + step] * half
        back[:, pl.ds(pl.multiple_of(at, LANES), half)] = grads[:, side * half : (side + 1) * half]
    for at in range(0, tokens, CHUNK):
        sums = None
        for lane in range(0, 2 * half, LANES):
            one = grads[at : at + CHUNK, lane : lane + LANES].astype(F32)
            one = one * normed_both[at : at + CHUNK, lane : lane + LANES].astype(F32)
            sums = one if sums is None else sums + one
        total[at : at + CHUNK, :] += sums

    @pl.when(step == count - 1)
    def _():
        for at in range(0, tokens, CHUNK):
            part = branch[at : at + CHUNK, :] + more[at : at + CHUNK, :]
            part = jnp.where(live_rows(meta, at, part.shape), part, 0.0)
            block[at : at + CHUNK, :] = (hidden[at : at + CHUNK, :].astype(F32) + part).astype(BF)


def out_forward(meta, normed, pulled, hidden, own, rest, local):
    tokens, width = hidden.shape
    count = UNITS
    half = DI // (2 * count)

    def columns(side):
        return pl.BlockSpec(
            (tokens, half), lambda i, meta: (0, meta[OUT_TABLE + side * count + i])
        )

    def local_spec(side):
        return pl.BlockSpec((half, width), lambda i, meta: (meta[0] if side == 0 else 1 - meta[0], 0))

    first = () if local is None else (local,)

    def weight_specs(side):
        if local is None:
            return [whole((half, width))] * count
        return [local_spec(side)] + [whole(part.shape) for part in own]

    return call(
        out_body, "out_forward", meta,
        (normed, normed, pulled, hidden) + (first + tuple(own) + first + tuple(rest)),
        [columns(0), columns(1), whole((tokens, width)), whole((tokens, width))]
        + weight_specs(0) + weight_specs(1),
        [shape_of((tokens, width), BF), shape_of((tokens, DI), BF), shape_of((tokens, LANES))],
        [whole((tokens, width)), whole((tokens, DI)), whole((tokens, LANES))],
        [pltpu.VMEM((2 * half, width), BF), pltpu.VMEM((tokens, width), F32)],
        count, 4 * tokens * width * DI, 24 * MIB,
    )


STEPS = 4


def norm_back_body(
    meta, back, total, mixed, gate, scale, gain, grad_gate, theirs, grad_mixed, grad_gain
):
    step = pl.program_id(0)
    tokens, width = back.shape
    grad_gain[...] = jnp.zeros_like(grad_gain)

    def one(n, carry):
        rows = pl.ds(pl.multiple_of(n * CHUNK, CHUNK), CHUNK)
        r = jnp.broadcast_to(scale[rows, :], (CHUNK, LANES))
        mean = jnp.sum(total[rows, :], axis=1, keepdims=True) / DI
        factor = r * r * mean
        for at in range(0, width, LANES):
            cut = slice(at, at + LANES)
            z = gate[rows, cut].astype(F32)
            sigma = sigmoid(z)
            silu = z * sigma
            out = mixed[rows, cut]
            gated = out * silu
            grad = back[rows, cut].astype(F32) * r
            grad_gain[:, cut] += fold(grad * gated)
            grad = grad * gain[:, cut] - gated * factor
            grad_mixed[rows, cut] = (grad * silu).astype(BF)
            grad_gate[rows, cut] = ((grad * out) * (sigma + silu * (1.0 - sigma))).astype(BF)
        return carry

    lax.fori_loop(0, tokens // CHUNK, one, 0)

    @pl.when(step // (STEPS // 2) == 1 - meta[0])
    def _():
        theirs[...] = grad_gate[...]


def norm_back(meta, back, total, mixed, gate, scale, gain):
    tokens = back.shape[0]
    width = DI // STEPS

    def tile(rows):
        return pl.BlockSpec((rows, width), lambda i, meta: (0, i))

    theirs_spec = pl.BlockSpec(
        (tokens, width),
        lambda i, meta: (0, jnp.clip(i - (1 - meta[0]) * (STEPS // 2), 0, STEPS // 2 - 1)),
    )
    return call(
        norm_back_body, "norm_back", meta, (back, total, mixed, gate, scale, gain),
        [tile(tokens), whole((tokens, LANES)), tile(tokens), tile(tokens), whole((tokens, 1)), tile(1)],
        [
            shape_of((tokens, DI), BF), shape_of((tokens, DI // 2), BF), shape_of((tokens, DI), BF),
            shape_of((8, DI)),
        ],
        [tile(tokens), theirs_spec, tile(tokens), tile(8)],
        [], STEPS, 10**9, 24 * MIB,
    )


def rows_product_body(meta, mine, theirs, pulled, pulled_rest, send, keep):
    total = dot_tn(mine[...], pulled[...]) + dot_tn(theirs[...], pulled_rest[...])
    total = total.astype(BF)
    sent = pl.num_programs(0) // 2

    @pl.when(pl.program_id(0) < sent)
    def _():
        send[0] = total

    @pl.when(pl.program_id(0) >= sent)
    def _():
        keep[0] = total


def rows_product(meta, normed, arrived, arrived_at, pulled, pulled_rest, units):
    tokens, width = pulled.shape
    unit = DI // (2 * UNITS)
    upper = units // 2

    def which(i):
        return lax.rem(i + upper, units)

    result = shape_of((upper, unit, width), BF)
    return call(
        rows_product_body, "rows_product", meta, (normed, arrived, pulled, pulled_rest),
        [
            pl.BlockSpec((tokens, unit), lambda i, meta: (0, meta[OUT_TABLE + which(i)])),
            pl.BlockSpec((tokens, unit), lambda i, meta: (0, meta[arrived_at + which(i)])),
            whole((tokens, width)), whole((tokens, width)),
        ],
        [result, result],
        [
            pl.BlockSpec((1, unit, width), lambda i, meta: (jnp.minimum(i, upper - 1), 0, 0)),
            pl.BlockSpec((1, unit, width), lambda i, meta: (jnp.maximum(i - upper, 0), 0, 0)),
        ],
        [], units, 4 * tokens * width * unit * units, 12 * MIB,
    )


def columns_product_body(plan, meta, *refs):
    parts = len(plan)
    mine, theirs = refs[:parts], refs[parts : 2 * parts]
    here, there, send, keep, right, right_rest = refs[2 * parts :]
    step = pl.program_id(0)
    width = here.shape[1] // UNITS

    @pl.when(step == 0)
    def _():
        for j in range(UNITS):
            lanes = pl.ds(pl.multiple_of(meta[TABLE + j] * width, LANES), width)
            right[:, j * width : (j + 1) * width] = here[:, lanes]
            right_rest[:, j * width : (j + 1) * width] = there[:, lanes]

    for (begin, steps), a, b in zip(plan, mine, theirs):
        @pl.when((step >= begin) & (step < begin + steps))
        def _(a=a, b=b):
            total = (dot_tn(a[...], right[...]) + dot_tn(b[...], right_rest[...])).astype(BF)
            for k in range(UNITS // 2):
                keep[k] = total[:, k * width : (k + 1) * width]
                other = UNITS // 2 + k
                send[k] = total[:, other * width : (other + 1) * width]


def columns_product(meta, parts, normed, normed_rest):
    tokens, width = normed.shape
    part = width // UNITS
    plan, step, mine_specs, theirs_specs = [], 0, [], []

    def spec(begin, steps, start):
        return pl.BlockSpec(
            (tokens, TILE), lambda i, meta: (0, start(meta) + jnp.clip(i - begin, 0, steps - 1))
        )

    for matrix, start, steps, arrived in parts:
        plan.append((step, steps))
        mine_specs.append(spec(step, steps, start))
        theirs_specs.append(spec(step, steps, lambda meta: 0))
        step += steps
    result = shape_of((UNITS // 2, step * TILE, part), BF)
    result_spec = pl.BlockSpec((UNITS // 2, TILE, part), lambda i, meta: (0, i, 0))
    return call(
        functools.partial(columns_product_body, tuple(plan)), "columns_product", meta,
        tuple(p[0] for p in parts) + tuple(p[3] for p in parts) + (normed, normed_rest),
        mine_specs + theirs_specs + [whole((tokens, width))] * 2,
        [result, result], [result_spec, result_spec],
        [pltpu.VMEM((tokens, width), BF), pltpu.VMEM((tokens, width), BF)],
        step, 1, 1,
    )


def conv_back(meta, masked, taps, result, sums, live, grad_conv):
    tokens = masked.shape[0]
    grad_conv[:, tokens:, :] = jnp.zeros((TILE // LANES, 8, LANES), F32)
    sums[...] = jnp.zeros_like(sums)
    for lane in range(0, TILE, LANES):
        cut = slice(lane, lane + LANES)
        totals = [jnp.zeros((8, LANES), F32) for _ in range(CONV + 1)]
        for at in range(0, tokens, CHUNK):
            near = [
                grad_conv[lane // LANES, at + 3 - k : at + 3 - k + CHUNK, :] for k in range(CONV)
            ]
            value = masked[at : at + CHUNK, cut].astype(F32)
            out = near[0] * taps[0:1, cut]
            for k in range(1, CONV):
                out = out + near[k] * taps[k : k + 1, cut]
            result[at : at + CHUNK, cut] = (out * live[at : at + CHUNK, :]).astype(BF)
            for k in range(CONV):
                totals[k] = totals[k] + fold(near[k] * value)
            totals[CONV] = totals[CONV] + fold(near[CONV - 1])
        for k in range(CONV + 1):
            sums[k : k + 1, cut] = jnp.sum(totals[k], axis=0, keepdims=True)


def fold(value):
    return jnp.sum(value.reshape(value.shape[0] // 8, 8, value.shape[1]), axis=0)


def scan_back_body(
    meta, content, keys, grad_out, mixed, entering, columns, rows, skip, masked, slope, taps,
    scores_in, write_in, read_in,
    result, theirs, sums, grad_columns, grad_scores, grad_write, grad_read,
    scores, read_rows, live, grad_conv, mixes, mix_grads, blocked, spread,
):
    half = SPAN // 2

    @pl.when(pl.program_id(0) == 0)
    def _():
        for span in range(2):
            at = span * SPAN
            scores[span] = dot_nt(keys[at : at + SPAN, :DSTATE], keys[at : at + SPAN, DSTATE:])
        read_rows[...] = keys[SPAN:, DSTATE:].astype(F32).T.astype(BF)
        grad_scores[...] = scores_in[...]
        grad_write[...] = write_in[...]
        grad_read[...] = read_in[...]
        mixes[...] = jnp.zeros_like(mixes)
        live_lanes(meta, live)
        after = row_ids(0, blocked.shape) <= lax.broadcasted_iota(jnp.int32, blocked.shape, 1)
        blocked[...] = jnp.where(after, 0.0, FAR)
        spread[...] = head_lanes(spread.shape, HEADDIM)

    def heads_sum(value):
        high = value.astype(BF)
        low = (value - high.astype(F32)).astype(BF)
        return dot_nt(high, spread[...]) + dot_nt(low, spread[...])

    for pair in range(PER // 2):
        lanes = slice(pair * 2 * HEADDIM, (pair + 1) * 2 * HEADDIM)
        ones = spread[2 * pair : 2 * pair + 2, lanes]
        for span in range(2):
            cut = slice(span * SPAN, (span + 1) * SPAN)
            mix_grads[pair, span] = dot_nt(heads_apart(content[cut, lanes], ones), grad_out[cut, lanes])

    factor = dot(columns[0, :, 2 * PER :].astype(BF), spread[...])
    grown = (grad_out[SPAN:, :].astype(F32) * factor[SPAN:]).astype(BF)
    grad_state = dot(read_rows[...], grown).astype(BF)
    grad_read[...] += dot_nt(grown, entering[0])
    worth = (content[0:SPAN, :].astype(F32) * factor[:SPAN]).astype(BF)
    grad_write[...] += dot_nt(worth, grad_state)
    from_state = dot(keys[0:SPAN, :DSTATE], grad_state) * factor[:SPAN]

    for pair in range(PER // 2):
        for h in range(2):
            n = 2 * pair + h
            for span in range(2):
                top = span * SPAN
                for at in range(0, SPAN, CHUNK):
                    less = columns[0, top + at : top + at + CHUNK, PER + n : PER + n + 1]
                    corner = at // half * half
                    for begin in range(corner, SPAN, half):
                        cut = slice(begin, begin + half)
                        decay = rows[0, n : n + 1, top + begin : top + begin + half] - less
                        if begin == corner:
                            decay = decay + blocked[at - begin : at - begin + CHUNK, :]
                        decay = jnp.exp2(decay)
                        row = h * SPAN + at
                        mix = scores[span, at : at + CHUNK, cut] * decay
                        mixes[pair, span, row : row + CHUNK, cut] = mix.astype(BF)
                        change = mix_grads[pair, span, row : row + CHUNK, cut] * decay
                        grad_scores[span, at : at + CHUNK, cut] += change

    lane = lax.broadcasted_iota(jnp.int32, (SPAN, 2 * PER), 1) < PER
    final = row_ids(0, lane.shape) == SPAN - 1
    skips = jnp.zeros((8, TILE), F32)
    for span in range(2):
        cut = slice(span * SPAN, (span + 1) * SPAN)
        value = content[cut, :].astype(F32)
        pull = grad_out[cut, :].astype(F32)
        both = []
        for pair in range(PER // 2):
            lanes = slice(pair * 2 * HEADDIM, (pair + 1) * 2 * HEADDIM)
            both.append(heads_together(dot(mixes[pair, span], grad_out[cut, lanes])))
        both = jnp.concatenate(both, axis=1)
        if span == 0:
            ended = jnp.sum(fold(value * from_state), axis=0, keepdims=True)
            both = both + from_state
        skipped = skip[...] * value
        skips = skips + fold(pull * value)
        written = heads_sum(value * both)
        read = heads_sum(pull * (mixed[cut, :] - skipped))
        if span == 0:
            ended = heads_sum(jnp.broadcast_to(ended, (8, TILE)))[0:1]
            read = read + jnp.where(final, ended, 0.0)
        grad_columns[0, cut, :] = jnp.where(lane, written, read)
        both = (both + skip[...] * pull) * slope[cut, :]
        for k in range(TILE // LANES):
            grad_conv[k, cut, :] = both[:, k * LANES : (k + 1) * LANES]

    conv_back(meta, masked, taps, result, sums, live, grad_conv)
    sums[5:6, :] = jnp.sum(skips, axis=0, keepdims=True)
    half_steps = pl.num_programs(0) // 2
    at_half = pl.program_id(0) // half_steps

    @pl.when(at_half == 1 - meta[0])
    def _():
        theirs[...] = result[...]


def scan_backward(
    meta, signal, keys, grad_out, mixed, entering, columns, rows, skip, masked, slope, taps, kept,
    first, count,
):
    tokens = signal.shape[0]

    def group(*shape):
        return pl.BlockSpec((1,) + shape, lambda i, meta: (i + first, 0, 0))

    def fresh(*shape):
        return pl.BlockSpec((1,) + shape, lambda i, meta: (i, 0, 0))

    kept_specs = [whole((2, SPAN, SPAN)), whole((SPAN, DSTATE)), whole((SPAN, DSTATE))]
    return call(
        scan_back_body, "scan_backward", meta,
        (signal, keys, grad_out, mixed, entering, columns, rows, skip, masked, slope, taps)
        + tuple(kept),
        [
            tiles(tokens, TILE, first), whole((tokens, TILE)),
            tiles(tokens, TILE, first), tiles(tokens, TILE, first), group(DSTATE, TILE),
            group(tokens, PACK),
            group(2 * PER, tokens), tiles(1, TILE, first), tiles(tokens, TILE, first),
            tiles(tokens, TILE, first), tiles(8, TILE, first),
        ]
        + kept_specs,
        [
            shape_of((tokens, count * TILE), BF), shape_of((tokens, count // 2 * TILE), BF),
            shape_of((8, count * TILE)),
            shape_of((count, tokens, 2 * PER)),
            shape_of((2, SPAN, SPAN)), shape_of((SPAN, DSTATE)), shape_of((SPAN, DSTATE)),
        ],
        [
            tiles(tokens, TILE),
            pl.BlockSpec(
                (tokens, TILE),
                lambda i, meta: (0, jnp.clip(i - (1 - meta[0]) * (count // 2), 0, count // 2 - 1)),
            ),
            tiles(8, TILE), fresh(tokens, 2 * PER),
        ]
        + kept_specs,
        [
            pltpu.VMEM((2, SPAN, SPAN), F32), pltpu.VMEM((DSTATE, SPAN), BF),
            pltpu.VMEM((tokens, LANES), F32), pltpu.VMEM((TILE // LANES, tokens + 8, LANES), F32),
            pltpu.VMEM((PER // 2, 2, 2 * SPAN, SPAN), BF),
            pltpu.VMEM((PER // 2, 2, 2 * SPAN, SPAN), F32),
            pltpu.VMEM((SPAN // 2, SPAN // 2), F32), pltpu.VMEM((2 * PER, TILE), BF),
        ],
        count, 3 * 10**9 * count, count * MIB,
    )


def tail_body(parts, meta, *refs):
    keys, masked, slope, taps, trio, steps, grad_scores, grad_write, grad_read = refs[:9]
    grad_columns = refs[9 : 9 + parts]
    result, sums, raw, small, packs, live, grad_conv = refs[9 + parts :]
    tokens = keys.shape[0]
    for span in range(2):
        at = span * SPAN
        write = keys[at : at + SPAN, :DSTATE]
        read = keys[at : at + SPAN, DSTATE:]
        to_write = fine_dot(grad_scores[span], read, dot)
        to_read = fine_dot(grad_scores[span], write, dot_tn)
        if span == 0:
            to_write = to_write + grad_write[...]
        else:
            to_read = to_read + grad_read[...]
        cut = slice(at, at + SPAN)
        grad_conv[0, cut, :] = to_write * slope[cut, :DSTATE]
        grad_conv[1, cut, :] = to_read * slope[cut, DSTATE:]
    live_lanes(meta, live)
    conv_back(meta, masked, taps, result, sums, live, grad_conv)

    blank = jnp.zeros((tokens, LANES - HEADS), F32)
    of_step, of_log = [], []
    for column_ref in grad_columns:
        for g in range(column_ref.shape[0]):
            of_step.append(column_ref[g, :, :PER])
            of_log.append(column_ref[g, :, PER:])
    grad_size = jnp.concatenate(of_step + [blank], axis=1)
    grad_log = jnp.concatenate(of_log + [blank], axis=1) - grad_size
    upper = row_ids(0, (SPAN, SPAN)) <= lax.broadcasted_iota(jnp.int32, (SPAN, SPAN), 1)
    upper = jnp.where(upper, 1.0, 0.0).astype(BF)
    rates = []
    for at in range(0, tokens, SPAN):
        high, middle, low = pieces(grad_log[at : at + SPAN])
        rates.append(dot(upper, high) + (dot(upper, middle) + dot(upper, low)))
    grad_rate = jnp.concatenate(rates, axis=0)
    decay_rate = steps[1:2, :]
    sigma = jax.nn.sigmoid(trio[0])
    size = trio[1]
    tiny = size > 0.0
    share = jnp.where(tiny, sigma / jnp.where(tiny, size, 1.0), 1.0)
    grad_raw = grad_size * share + grad_rate * decay_rate * sigma
    raw[...] = grad_raw.astype(BF)
    small[...] = jnp.zeros_like(small)
    small[0:1, :] = jnp.sum(grad_raw, axis=0, keepdims=True)
    small[1:2, :] = jnp.sum(grad_rate * trio[1], axis=0, keepdims=True) * decay_rate
    for side in range(2):
        at = meta[0] if side == 0 else 1 - meta[0]
        packs[side, :, :LANES] = result[:, pl.ds(pl.multiple_of(at * LANES, LANES), LANES)]
        packs[side, :, LANES:] = raw[...]


def tail_backward(meta, keys, masked, slope, taps, trio, steps, kept, grad_columns):
    tokens = keys.shape[0]
    last = DI // TILE
    key_spec = whole((tokens, TILE))
    return call(
        functools.partial(tail_body, len(grad_columns)), "tail_backward", meta,
        (keys, masked, slope, taps, trio, steps) + tuple(kept) + tuple(grad_columns),
        [
            key_spec, key_spec, key_spec, pl.BlockSpec((8, TILE), lambda i, meta: (0, last)),
            whole((3, tokens, LANES)), whole((8, LANES)), whole((2, SPAN, SPAN)),
            whole((SPAN, DSTATE)), whole((SPAN, DSTATE)),
        ]
        + [whole(part.shape) for part in grad_columns],
        [
            shape_of((tokens, TILE), BF), shape_of((8, TILE)), shape_of((tokens, LANES), BF),
            shape_of((8, LANES)), shape_of((2, tokens, TILE), BF),
        ],
        [
            whole((tokens, TILE)), whole((8, TILE)), whole((tokens, LANES)), whole((8, LANES)),
            whole((2, tokens, TILE)),
        ],
        [pltpu.VMEM((tokens, LANES), F32), pltpu.VMEM((TILE // LANES, tokens + 8, LANES), F32)],
        1, 1, 1,
    )


def input_body(plan, first, last, meta, *refs):
    count = UNITS
    grads = refs[: len(plan)]
    refs = refs[len(plan) :]
    if not first:
        start, refs = refs[0], refs[1:]
    blocks = []
    for begin, steps, half in plan:
        own, refs = refs[:count], refs[count:]
        rest = None
        if half is not None:
            rest, refs = refs[:count], refs[count:]
        blocks.append((own, rest))
    step = pl.program_id(0)

    if last:
        hidden, out_grad, scale, gain, result, gain_grad, weight, weight_dt, total, folded = refs
    else:
        total, weight = refs

    @pl.when(step == 0)
    def _():
        total[...] = jnp.zeros_like(total) if first else start[...]

    for n, (begin, steps, half) in enumerate(plan):
        @pl.when((step >= begin) & (step < begin + steps))
        def _(n=n, half=half):
            own, rest = blocks[n]
            rows = own[0].shape[0]
            if grads[n].shape[1] == LANES:
                weight_dt[...] = jnp.zeros_like(weight_dt)
                gather_lanes(weight_dt, own, meta, TABLE)
                total[...] += dot(grads[n][...], weight_dt[...])
                return
            if half is None:
                gather_lanes(weight, own, meta, TABLE)
            else:
                @pl.when(meta[0] == half)
                def _():
                    gather_lanes(weight, own, meta, TABLE)

                @pl.when(meta[0] != half)
                def _():
                    gather_lanes(weight, rest, meta, TABLE + count)

            total[...] += dot(grads[n][...], weight[0:rows, :])

    if not last:
        return

    @pl.when(step == pl.num_programs(0) - 1)
    def _():
        tokens, width = hidden.shape
        folded[...] = jnp.zeros_like(folded)

        def finish(n, carry):
            rows = pl.ds(pl.multiple_of(n * 32, 32), 32)
            r = jnp.broadcast_to(scale[rows, :], (32, LANES))
            sums = jnp.zeros((32, LANES), F32)
            for at in range(0, width, LANES):
                cut = slice(at, at + LANES)
                both = total[rows, cut] * hidden[rows, cut].astype(F32)
                folded[:, cut] += fold(both * r)
                sums = sums + both * gain[:, cut]
            mean = jnp.sum(sums, axis=1, keepdims=True) / width
            factor = r * r * r * mean
            for at in range(0, width, LANES):
                cut = slice(at, at + LANES)
                value = r * (total[rows, cut] * gain[:, cut]) - hidden[rows, cut].astype(F32) * factor
                result[rows, cut] = value + out_grad[rows, cut].astype(F32)
            return carry

        lax.fori_loop(0, tokens // 32, finish, 0)
        gain_grad[...] = jnp.sum(folded[...], axis=0, keepdims=True)


def input_backward(meta, start, parts, tokens, width, last=None):
    part = width // UNITS
    plan, step, grad_specs, block_specs, grads, blocks = [], 0, [], [], [], []

    def grad_spec(columns, begin, steps, first):
        return pl.BlockSpec(
            (tokens, columns), lambda i, meta: (0, first + jnp.clip(i - begin, 0, steps - 1))
        )

    def row_spec(rows, begin, steps, first, when):
        def index(i, meta):
            at = first + jnp.clip(i - begin, 0, steps - 1)
            return (at if when is None else jnp.where(when(meta), at, first), 0)

        return pl.BlockSpec((rows, part), index)

    def is_half(half):
        return lambda meta: meta[0] == half

    def not_half(half):
        return lambda meta: meta[0] != half

    for grad, grad_first, steps, half, own, own_first, rest, rest_first, local_first in parts:
        columns = WIDE if half is not None else grad.shape[1]
        if half is not None and steps == WIDES // 2:
            columns, steps = steps * WIDE, 1
            grad_first, local_first = (at // (WIDES // 2) for at in (grad_first, local_first))
        row_tile = 64 if columns == LANES else columns
        plan.append((step, steps, half))
        grads.append(grad)
        grad_specs.append(grad_spec(columns, step, steps, grad_first))
        when = None if half is None else is_half(half)
        for matrix in own:
            blocks.append(matrix)
            block_specs.append(row_spec(row_tile, step, steps, own_first, when))
        if half is not None:
            for j, matrix in enumerate(rest):
                blocks.append(matrix)
                row = local_first if j == 0 else rest_first
                block_specs.append(row_spec(row_tile, step, steps, row, not_half(half)))
        step += steps
    more, more_specs = (), []
    outs, out_specs = [shape_of((tokens, width))], [whole((tokens, width))]
    scratch = [pltpu.VMEM((WIDES // 2 * WIDE, width), BF)]
    if last is not None:
        more = tuple(last)
        more_specs = [whole((tokens, width))] * 2 + [whole((tokens, 1)), whole((1, width))]
        outs.append(shape_of((1, width)))
        out_specs.append(whole((1, width)))
        scratch += [
            pltpu.VMEM((LANES, width), BF), pltpu.VMEM((tokens, width), F32),
            pltpu.VMEM((8, width), F32),
        ]
    first = start is None
    return call(
        functools.partial(input_body, tuple(plan), first, last is not None),
        "input_backward", meta,
        tuple(grads) + (() if first else (start,)) + tuple(blocks) + more,
        grad_specs + ([] if first else [whole((tokens, width))]) + block_specs + more_specs,
        outs, out_specs, scratch,
        step, 10**10 if last is None else 10**11, 20 * MIB,
    )


def place_body(halves, last, meta, own, other, out):
    step = pl.program_id(0)

    def put(which, row, rows, at):
        @pl.when(meta[0] == which)
        def _():
            out[at : at + rows, :] = own[row : row + rows, :].astype(F32)

        @pl.when(meta[0] != which)
        def _():
            out[at : at + rows, :] = other[row : row + rows, :].astype(F32)

    for half in range(2):
        @pl.when(step == half)
        def _(half=half):
            put(half, 0, halves, 0)

    if last:
        @pl.when(step == 2)
        def _():
            put(0, halves, LANES, 0)
            put(1, halves, LANES, LANES)
            put(0, halves + LANES, LANES, 2 * LANES)


def place_rows(meta, own, other, halves, first, total, filled, last):
    length, width = own.shape
    return call(
        functools.partial(place_body, halves, last), "place_rows", meta, (own, other),
        [whole((length, width)), whole((length, width))],
        shape_of((total, width)),
        pl.BlockSpec((halves, width), lambda i, meta: (first + i, 0)),
        [], 3 if last else 2, 1, 1, None if filled is None else {0: filled},
    )


NEAR = 8


def mirrored(j, count):
    if count != 4:
        return j
    result, bit, other = 0, 1, count // 2
    while bit < count:
        if j & bit:
            result |= other
        bit, other = bit * 2, other // 2
    return result


def hop(x, bit):
    reps, count = lax.axis_size("rep"), lax.axis_size("shard")
    pairs = []
    for r in range(reps):
        flip = bit if r % 2 == 0 else mirrored(bit, count)
        pairs += [(r * count + s, r * count + (s ^ flip)) for s in range(count)]
    return lax.ppermute(x, ("rep", "shard"), pairs)


def swap(x):
    return lax.ppermute(x, "rep", [(r, r ^ 1) for r in range(lax.axis_size("rep"))])


def across(x, bit):
    return lax.ppermute(x, "shard", [(s, s ^ bit) for s in range(lax.axis_size("shard"))])


def along(x, pairs):
    return lax.ppermute(x, "rep", [(2 * a + k, 2 * b + k) for a, b in pairs for k in range(2)])


def settle(keep, arrived):
    middle = keep.shape[0] // 2
    if middle == 0:
        return None, keep.astype(F32) + arrived.astype(F32)
    held = (keep.astype(F32) + arrived.astype(F32)).astype(BF)
    return held[middle:], held[:middle]


def finish_stages(send, keep):
    while send is not None:
        send, keep = settle(keep, hop(send, send.shape[0]))
    return keep[0]


def inward(held):
    if lax.axis_size("rep") // 2 != 4:
        return held, None
    return held, along(held.astype(BF), [(0, 1), (3, 2)])


def middle(state):
    held, arrived = state
    if arrived is None:
        return held, None
    inner = (held + arrived.astype(F32)).astype(BF)
    return inner, along(inner, [(1, 2), (2, 1)])


def outward(state):
    inner, arrived = state
    if arrived is None:
        chips = lax.axis_size("rep") // 2
        total, bit = inner.astype(BF), 1
        while bit < chips:
            more = along(total, [(k, k ^ bit) for k in range(chips)])
            total = (total.astype(F32) + more.astype(F32)).astype(BF)
            bit *= 2
        return total, None
    total = (inner.astype(F32) + arrived.astype(F32)).astype(BF)
    return total, along(total, [(1, 0), (2, 3)])


def summed(state):
    total, arrived = state
    if arrived is None:
        return total
    place = lax.axis_index("rep") // 2
    return jnp.where((place == 1) | (place == 2), total, arrived)


def in_order(own, other, core):
    return [jnp.where(core == 0, own, other), jnp.where(core == 0, other, own)]


def hold(values):
    leaves, tree = jax.tree.flatten(values)
    return jax.tree.unflatten(tree, lax.optimization_barrier(tuple(leaves)))


def add_up(rows):
    while len(rows) > 1:
        rows = [a + b for a, b in zip(rows[::2], rows[1::2])]
    return rows[0]


def group_rows(vector, shard, count):
    rows = [lax.dynamic_slice_in_dim(vector, shard ^ j, 1, 0) for j in range(count)]
    return rows[:1] + [across(row, j) for j, row in enumerate(rows) if j]


def chips_sum(row):
    chips = lax.axis_size("rep") // 2
    return add_up(
        [row] + [along(row, [(k, k ^ d) for k in range(chips)]) for d in range(1, chips)]
    )


def join_lanes(blocks, shard):
    return [
        jnp.concatenate(in_order(blocks[j], blocks[j + 1], shard % 2), axis=1)
        for j in range(0, len(blocks), 2)
    ]


def split_lanes(units, shard):
    half = units.shape[2] // 2
    pairs = in_order(units[:, :, :half], units[:, :, half:], shard % 2)
    return jnp.stack(pairs, axis=1).reshape(2 * units.shape[0], units.shape[1], half)


def pad_lanes(matrix):
    return jnp.pad(matrix, ((0, 0), (0, LANES - matrix.shape[1])))


def shards(
    hidden,
    out_grad,
    norm_gain,
    in_w,
    conv_w,
    conv_b,
    dt_bias,
    a_log,
    skip,
    out_gain,
    out_w,
    lengths,
    offsets,
):
    core = lax.axis_index("rep") % 2
    shard = lax.axis_index("shard")
    count = lax.axis_size("shard")
    tokens, width = hidden.shape
    bits = []
    while 2 ** len(bits) < count:
        bits.append(2 ** len(bits))

    local = in_w.T
    half = DI // 2
    piece = jnp.concatenate(
        [
            lax.dynamic_slice_in_dim(local, DI + core * half, half, 0),
            local[2 * DI :],
            jnp.zeros((16, local.shape[1]), BF),
        ],
        axis=0,
    )
    gate_piece = lax.dynamic_slice_in_dim(local, core * half, half, 0)
    out_piece = lax.dynamic_slice_in_dim(out_w, core * (out_w.shape[0] // 2), out_w.shape[0] // 2, 0)

    def spread(first):
        blocks = [first]
        for bit in bits:
            blocks = blocks + [hop(block, bit) for block in blocks]
        return blocks

    paired = count == 4
    small = (norm_gain, conv_w.T, conv_b, dt_bias, a_log, skip, out_gain)
    packed = jnp.concatenate([part.reshape(-1) for part in small])
    everyone = [packed] + [
        lax.ppermute(
            packed, ("rep", "shard"),
            [
                (r * count + s, r * count + (s ^ (j if r % 2 == 0 else mirrored(j, count))))
                for r in range(lax.axis_size("rep"))
                for s in range(count)
            ],
        )
        for j in range(1, count)
    ]
    everyone = jnp.stack(everyone).astype(F32)
    order = [jnp.where(core == 0, j, mirrored(j, count)) for j in range(count)]
    whose = jnp.stack(order)[jnp.arange(count) ^ shard]
    same = (whose[:, None] == jnp.arange(count)[None]).astype(F32)
    everyone = jnp.sum(same[:, :, None] * everyone[None], axis=1)
    parts, start = [], 0
    for part in small:
        cut = everyone[:, start : start + part.size].reshape((count,) + part.shape)
        cut = jnp.moveaxis(cut, 0, -2)
        parts.append(cut.reshape(part.shape[:-1] + (-1,)))
        start += part.size
    conv_own = spread(piece)
    gate_piece, conv_own = hold((gate_piece, conv_own))
    if paired:
        conv_rest = [swap(block) for block in conv_own[1:]]
        gate_near = hop(gate_piece, 1), hop(gate_piece, 2)
        out_local, in_local = out_w, local
    else:
        gate_own = spread(gate_piece)
        out_piece, gate_own = hold((out_piece, gate_own))
        out_own = spread(out_piece)
        conv_rest = rest_conv = join_lanes([swap(block) for block in conv_own], shard)
        gate_rest = rest_gate = join_lanes([swap(block) for block in gate_own], shard)
        conv_own, gate_own = join_lanes(conv_own, shard), join_lanes(gate_own, shard)
        out_full = [jnp.concatenate(in_order(block, swap(block), core), axis=0) for block in out_own]
        out_one, out_two = out_full[:UNITS], out_full[UNITS:]
        out_local = in_local = None

    gain_one, kernel, bias_conv, bias_step, log_rate, skip_full, gain_two = parts
    decay_rate = -jnp.exp(log_rate)

    mine = order
    other = [jnp.where(core == 0, mirrored(j, count), j) for j in range(count)]
    mine, other = [shard ^ j for j in mine], [shard ^ j for j in other]
    if paired:
        out_units = [2 * j + core for j in mine] + [2 * j + 1 - core for j in other]
    else:
        out_units = mine
        mine = other = [j // 2 for j in mine[::2]]
    meta = jnp.stack(
        [core, offsets[0], lengths[0], shard] + mine + other + out_units
    ).astype(jnp.int32)
    taps = jnp.concatenate([kernel, bias_conv[None], jnp.zeros((3, CC), F32)], axis=0)
    steps = jnp.concatenate(
        [pad_lanes(jnp.stack([bias_step, decay_rate])), jnp.zeros((6, LANES), F32)], axis=0
    )
    skip_lanes = jnp.repeat(skip_full, HEADDIM)[None]

    positions = jnp.arange(tokens, dtype=jnp.int32)
    live_mask = ((positions >= offsets[0]) & (positions < offsets[0] + lengths[0])).astype(F32)
    hidden_full = hidden.astype(F32)
    inv_rms = lax.rsqrt(jnp.mean(hidden_full * hidden_full, axis=1, keepdims=True) + epsilon)
    normed = (hidden_full * inv_rms * gain_one).astype(BF)
    pulled = (out_grad.astype(F32) * live_mask[:, None]).astype(BF)
    normed_rest = swap(normed)
    pulled_rest = swap(pulled)

    (masked, signal, slope, masked_keys, keys, slope_keys, columns, rows, trio) = conv_forward(
        meta, normed, taps, steps, conv_own, conv_rest, in_local
    )
    if paired:
        gate_near, signal = hold((gate_near, signal))
        gate_own = [gate_piece, *gate_near, hop(gate_near[0], 2)]
    kept = None
    for first in range(0, GROUPS, GROUPS // 2):
        kept = scan_forward(
            meta, signal, keys, columns, rows, skip_lanes, first, GROUPS // 2, kept
        )
        if paired and first == 0:
            gate_far, out_piece, kept = hold((gate_own[3], out_piece, kept))
            gate_own[3] = gate_far
            gate_rest = [swap(block) for block in gate_own[1:]]
            out_near = hop(out_piece, 1), hop(out_piece, 2)
    mixed, entering = kept
    if paired:
        rest_conv, rest_gate = [local] + conv_rest, [local] + gate_rest
    gate, normed_out, out_theirs, scale = gate_forward(
        meta, normed, mixed, gain_two[None], gate_own, gate_rest, in_local
    )
    out_arrived = swap(out_theirs if paired else normed_out)
    if paired:
        out_near, normed_out = hold((out_near, normed_out))
        out_one = [*out_near, hop(out_near[0], 2)]
        out_two = [swap(block) for block in out_one]

    upper = count // 2
    out_pulls = (pulled, pulled_rest)
    if not paired:
        cut = core * (width // 2)
        out_pulls = [lax.dynamic_slice_in_dim(x, cut, width // 2, 1) for x in out_pulls]

    def product(parts):
        send, keep = columns_product(meta, parts, normed, normed_rest)
        return (send, keep) if paired else (split_lanes(send, shard), split_lanes(keep, shard))

    out_send, out_keep = rows_product(
        meta, normed_out, out_arrived, TABLE if paired else OUT_TABLE, *out_pulls, count
    )
    out_send, out_keep, normed_out = hold((out_send, out_keep, normed_out))
    out_there = hop(out_send, upper)
    block_out, back, total = out_forward(
        meta, normed_out, pulled, hidden, out_one, out_two, out_local
    )
    out_there, total = hold((out_there, total))
    out_send, out_keep = settle(out_keep, out_there)
    out_there = hop(out_send, upper // 2)
    out_keep, total = hold((out_keep, total))
    grad_gate, gate_theirs, grad_mixed, grad_gain_two = norm_back(
        meta, back, total, mixed, gate, scale, gain_two[None]
    )

    gate_theirs, out_there = hold((gate_theirs, out_there))
    gate_arrived = swap(gate_theirs)
    out_line = inward(finish_stages(*settle(out_keep, out_there)))
    out_held, gate_arrived = hold((out_line[0], gate_arrived))
    gate_parts = [(grad_gate, lambda meta: meta[0] * (GROUPS // 2), GROUPS // 2, gate_arrived)]
    gate_send, gate_keep = product(gate_parts)
    gate_send, gate_keep, grad_mixed = hold((gate_send, gate_keep, grad_mixed))
    gate_there = hop(gate_send, upper)
    kept = (
        jnp.zeros((2, SPAN, SPAN), F32),
        jnp.zeros((SPAN, DSTATE), F32),
        jnp.zeros((SPAN, DSTATE), F32),
    )
    near, far = NEAR, GROUPS - NEAR
    part = WIDES // 2
    over = near * TILE // WIDE - part

    def gate_part(half):
        at = half * part
        return [(grad_gate, at, part, half, gate_own, 0, rest_gate, 0, at if paired else 0)]

    def conv_part(grad, grad_first, steps, half, first):
        local_first = WIDES + half * part + first if paired else first
        return [(grad, grad_first, steps, half, conv_own, first, rest_conv, first, local_first)]

    grad_near, near_theirs, sums_near, columns_near, *kept = scan_backward(
        meta, signal, keys, grad_mixed, mixed, entering, columns, rows, skip_lanes, masked, slope, taps,
        kept, 0, near,
    )
    gate_there, near_theirs, out_arrived = hold((gate_there, near_theirs, out_line[1]))
    near_arrived = swap(near_theirs)
    gate_send, gate_keep = settle(gate_keep, gate_there)
    gate_there = hop(gate_send, upper // 2)
    gate_keep, out_arrived = hold((gate_keep, out_arrived))
    out_line = middle((out_held, out_arrived))
    near_arrived, gate_keep, out_inner = hold((near_arrived, gate_keep, out_line[0]))
    near_parts = [(grad_near, lambda meta: meta[0] * (near // 2), near // 2, near_arrived)]
    near_send, near_keep = product(near_parts)
    near_there = hop(near_send, upper)
    near_keep, kept, grad_mixed = hold((near_keep, kept, grad_mixed))
    grad_far, far_theirs, sums_far, columns_far, *kept = scan_backward(
        meta, signal, keys, grad_mixed, mixed, entering, columns, rows, skip_lanes, masked, slope, taps,
        kept, near, far,
    )
    far_theirs, gate_there = hold((far_theirs, gate_there))
    far_arrived = swap(far_theirs)
    gate_line = inward(finish_stages(*settle(gate_keep, gate_there)))
    gate_held, kept = hold((gate_line[0], kept))
    grad_keys, sums_keys, grad_raw, grad_steps, packs = tail_backward(
        meta, keys, masked_keys, slope_keys, taps, trio, steps, kept, (columns_near, columns_far),
    )
    packs, near_there = hold((packs, near_there))
    packs_arrived = swap(packs[1])
    near_send, near_keep = settle(near_keep, near_there)
    near_there = hop(near_send, upper // 2)
    packs, packs_arrived, near_keep = hold((packs, packs_arrived, near_keep))
    far_parts = [
        (grad_far, lambda meta: meta[0] * (far // 2), far // 2, far_arrived),
        (packs[0], lambda meta: 0, 1, packs_arrived),
    ]
    far_send, far_keep = product(far_parts)
    far_there = hop(far_send, upper)
    far_keep, gate_arrived, near_there, out_arrived = hold(
        (far_keep, gate_line[1], near_there, out_line[1])
    )
    gate_line = middle((gate_held, gate_arrived))
    near_line = inward(finish_stages(*settle(near_keep, near_there)))
    out_line = outward((out_inner, out_arrived))
    gate_inner, near_held, out_done, grad_gate = hold(
        (gate_line[0], near_line[0], out_line[0], grad_gate)
    )
    (partial,) = input_backward(meta, None, gate_part(0) + gate_part(1), tokens, width)
    partial, far_there = hold((partial, far_there))
    far_send, far_keep = settle(far_keep, far_there)
    far_there = hop(far_send, upper // 2)
    far_keep, near_arrived, small_grads = hold(
        (far_keep, near_line[1], (sums_near, sums_far, sums_keys, grad_steps, grad_gain_two))
    )
    sums_near, sums_far, sums_keys, grad_steps, grad_gain_two = small_grads
    sums = jnp.concatenate([sums_near, sums_far, sums_keys], axis=1)
    grads = (
        sums[:CONV].reshape(CONV, count, -1).transpose(1, 0, 2).reshape(count, -1),
        sums[CONV].reshape(count, -1),
        grad_steps[0, :HEADS].reshape(count, -1),
        grad_steps[1, :HEADS].reshape(count, -1),
        jnp.sum(sums[5, :DI].reshape(HEADS, HEADDIM), axis=1).reshape(count, -1),
        jnp.sum(grad_gain_two, axis=0).reshape(count, -1),
    )
    vector = jnp.concatenate(grads, axis=1)
    far_there, far_keep, partial, vector = hold((far_there, far_keep, partial, vector))
    vector_there = swap(vector)
    far_line = inward(finish_stages(*settle(far_keep, far_there)))
    far_held, gate_arrived, out_arrived = hold((far_line[0], gate_line[1], out_line[1]))
    gate_line = outward((gate_inner, gate_arrived))
    near_line = middle((near_held, near_arrived))
    out_total = summed((out_done, out_arrived))
    out_other = swap(out_total)
    far_held, gate_done, near_inner, out_total, partial = hold(
        (far_held, gate_line[0], near_line[0], out_total, partial)
    )
    (partial,) = input_backward(
        meta, partial,
        conv_part(grad_near, 0, part, 0, 0)
        + conv_part(grad_near, part, over, 1, 0)
        + conv_part(grad_far, 0, part - over, 1, over),
        tokens, width,
    )
    partial, far_arrived = hold((partial, far_line[1]))
    far_line = middle((far_held, far_arrived))
    far_inner, near_arrived, gate_arrived, out_other, vector_there = hold(
        (far_line[0], near_line[1], gate_line[1], out_other, vector_there)
    )
    spread_rows = group_rows(vector + vector_there, shard, count)
    near_line = outward((near_inner, near_arrived))
    gate_total = summed((gate_done, gate_arrived))
    gate_other = swap(gate_total)
    far_inner, near_done, gate_total, partial = hold((far_inner, near_line[0], gate_total, partial))
    hidden_grad, grad_gain_one = input_backward(
        meta, partial,
        [
            (grad_keys, 0, 1, None, conv_own, DI // 2 // TILE, None, 0, 0),
            (grad_raw, 0, 1, None, conv_own, (DI // 2 + TILE) // 64, None, 0, 0),
        ],
        tokens, width, (hidden, out_grad, inv_rms, gain_one[None]),
    )
    grad_gain_one, far_arrived, gate_other, spread_rows, near_arrived = hold(
        (grad_gain_one, far_line[1], gate_other, spread_rows, near_line[1])
    )
    far_line = outward((far_inner, far_arrived))
    row = chips_sum(add_up(spread_rows))[0]
    far_done, grad_gain_one, gate_other = hold((far_line[0], grad_gain_one, gate_other))
    vector = grad_gain_one[0].reshape(count, -1)
    gain_row = add_up(group_rows(vector + swap(vector), shard, count))
    all_rows = local.shape[0]
    rows_so_far = place_rows(meta, gate_total, gate_other, DI // 2, 0, all_rows, None, False)
    near_total = summed((near_done, near_arrived))
    near_other = swap(near_total)
    wide = near // 2 * TILE
    rows_so_far = place_rows(
        meta, near_total, near_other, wide, DI // wide, all_rows, rows_so_far, False
    )
    gain_row, row, far_arrived, rows_so_far = hold((gain_row, row, far_line[1], rows_so_far))
    gain_row = chips_sum(gain_row)[0]
    far_total = summed((far_done, far_arrived))
    far_other = swap(far_total)
    wide = far // 2 * TILE
    rows_so_far = place_rows(
        meta, far_total, far_other, wide, (DI + near * TILE) // wide, all_rows, rows_so_far, True
    )
    in_w_grad = rows_so_far.T

    out_w_grad = jnp.concatenate(
        in_order(out_total, out_other, core), axis=0 if paired else 1
    ).astype(F32)
    found, start = [], 0
    for part in grads:
        found.append(row[start : start + part.shape[1]])
        start += part.shape[1]
    return (
        block_out,
        hidden_grad,
        gain_row,
        in_w_grad,
        found[0].reshape(CONV, -1).T,
        found[1],
        found[2],
        found[3],
        found[4],
        found[5],
        out_w_grad,
    )


def solution(mesh):
    return jax.shard_map(
        shards,
        mesh=mesh,
        in_specs=(
            P(("rep", "shard"), None),
            P(("rep", "shard"), None),
            P("shard"),
            P("shard", None),
            P("shard", None),
            P("shard"),
            P("shard"),
            P("shard"),
            P("shard"),
            P("shard"),
            P("shard", None),
            P(("rep", "shard")),
            P(("rep", "shard")),
        ),
        out_specs=(
            P(("rep", "shard"), None),
            P(("rep", "shard"), None),
            P("shard"),
            P("shard", None),
            P("shard", None),
            P("shard"),
            P("shard"),
            P("shard"),
            P("shard"),
            P("shard"),
            P("shard", None),
        ),
        check_vma=False,
    )
```

```python
import functools

import jax
import jax.numpy as jnp
from jax import lax
from jax.experimental import pallas as pl
from jax.experimental.pallas import tpu as pltpu
from jax.sharding import PartitionSpec as P

HEADS = 48
HEADDIM = 64
DSTATE = 128
CONV = 4
SPAN = 256
DI = 3072
CC = 3328
TILE = 256
GROUPS = DI // TILE
PER = TILE // HEADDIM
CHUNK = 64
LANES = 128
epsilon = 1e-05
FAR = -1e30
LOG2E = 1.4426950408889634
PACK = 4 * PER

BF = jnp.bfloat16
F32 = jnp.float32
MIB = 1 << 20


def dot(lhs, rhs):
    return jnp.dot(lhs, rhs, preferred_element_type=F32)


def dot_nt(lhs, rhs):
    return lax.dot_general(lhs, rhs, (((1,), (1,)), ((), ())), preferred_element_type=F32)


def dot_tn(lhs, rhs):
    return lax.dot_general(lhs, rhs, (((0,), (0,)), ((), ())), preferred_element_type=F32)


def sigmoid(value):
    return 0.5 * jnp.tanh(0.5 * value) + 0.5


def pieces(value):
    high = value.astype(BF)
    rest = value - high.astype(F32)
    middle = rest.astype(BF)
    low = (rest - middle.astype(F32)).astype(BF)
    return high, middle, low


def fine_dot(lhs, rhs, product):
    high, middle, low = pieces(lhs)
    return product(high, rhs) + (product(middle, rhs) + product(low, rhs))


def row_ids(start, shape):
    return start + lax.broadcasted_iota(jnp.int32, shape, 0)


def live_rows(meta, start, shape):
    ids = row_ids(start, shape)
    return (ids >= meta[1]) & (ids < meta[1] + meta[2])


def gather_lanes(target, blocks, table, at):
    for j, block in enumerate(blocks):
        width = block.shape[1]
        lanes = pl.ds(pl.multiple_of(table[at + j] * width, LANES), width)
        target[0 : block.shape[0], lanes] = block[...]


def call(
    body, name, meta, operands, in_specs, outs, out_specs, scratch, grid, flops, moved, filled=None
):
    if filled:
        first = len(operands) + 1
        operands, extra = operands + tuple(filled.values()), len(filled)
        in_specs = in_specs + [pl.BlockSpec(memory_space=pl.ANY)] * extra
        aliases = {first + n: place for n, place in enumerate(filled)}
        inner, many = body, first - 1

        def body(meta, *refs):
            return inner(meta, *refs[:many], *refs[many + extra :])
    else:
        aliases = {}
    return pl.pallas_call(
        body,
        name=name,
        grid_spec=pltpu.PrefetchScalarGridSpec(
            num_scalar_prefetch=1,
            grid=(grid,),
            in_specs=in_specs,
            out_specs=out_specs,
            scratch_shapes=scratch,
        ),
        out_shape=outs,
        input_output_aliases=aliases,
        compiler_params=pltpu.CompilerParams(vmem_limit_bytes=60 * MIB),
        cost_estimate=pl.CostEstimate(flops=flops, bytes_accessed=moved, transcendentals=0),
    )(meta, *operands)


def whole(shape):
    rank = len(shape)
    return pl.BlockSpec(shape, lambda i, meta: (0,) * rank)


def tiles(rows, width, shift=0, last=None):
    def index(i, meta):
        at = i + shift
        if last is not None:
            at = jnp.clip(at, 0, last)
        return (0, at)

    return pl.BlockSpec((rows, width), index)


def shape_of(shape, kind=F32):
    return jax.ShapeDtypeStruct(shape, kind)


TABLE = 4
UNITS = 4
OUT_TABLE = TABLE + 2 * UNITS
WIDE = 512
WIDES = DI // WIDE


def own_tile(i, meta):
    half = WIDES // 2
    return jnp.where(i < half, meta[0] * half + i, (1 - meta[0]) * half + i - half)


def live_lanes(meta, live):
    live[...] = jnp.where(live_rows(meta, 0, live.shape), 1.0, 0.0)


def convolve(low, taps, live, shifted, masked, signal, slope, begin):
    for lane in range(0, low.shape[1], LANES):
        cut = slice(begin + lane, begin + lane + LANES)
        tile = (begin + lane) // LANES
        for at in range(0, low.shape[0], CHUNK):
            part = low[at : at + CHUNK, lane : lane + LANES].astype(BF).astype(F32)
            part = part * live[at : at + CHUNK, :]
            masked[at : at + CHUNK, cut] = part.astype(BF)
            shifted[tile, 8 + at : 8 + at + CHUNK, :] = part
        for at in range(0, low.shape[0], CHUNK):
            out = taps[4:5, cut]
            for k in range(CONV):
                out = out + shifted[tile, at + 5 + k : at + 5 + k + CHUNK, :] * taps[k : k + 1, cut]
            sigma = sigmoid(out)
            out = out * sigma
            here = live[at : at + CHUNK, :]
            signal[at : at + CHUNK, cut] = (out * here).astype(BF)
            slope[at : at + CHUNK, cut] = (sigma + out * (1.0 - sigma)) * here


def conv_body(meta, x, taps, taps_keys, steps, *refs):
    count = UNITS
    own, rest, key_rows, dts = (refs[n * count : (n + 1) * count] for n in range(4))
    (masked, signal, slope, masked_keys, keys, slope_keys, columns, rows, trio,
     weight, weight_dt, shifted, live) = refs[4 * count :]
    tokens = x.shape[0]
    step = pl.program_id(0)

    @pl.when(step == 0)
    def _():
        shifted[:, 0:8, :] = jnp.zeros((WIDE // LANES, 8, LANES), F32)
        live_lanes(meta, live)
        gather_lanes(weight, key_rows, meta, TABLE)
        gather_lanes(weight_dt, dts, meta, TABLE)
        low = dot_nt(x[...], weight[0:TILE, :])
        raw = dot_nt(x[...], weight_dt[...]).astype(BF).astype(F32)
        convolve(low, taps_keys, live, shifted, masked_keys, keys, slope_keys, 0)
        raw = jnp.concatenate([raw, jnp.zeros((tokens, LANES - raw.shape[1]), F32)], axis=1)
        pre = raw + steps[0:1, :]
        size = jnp.maximum(pre, 0.0) + jnp.log1p(jnp.exp(-jnp.abs(pre)))
        rate = size * steps[1:2, :]
        lower = row_ids(0, (SPAN, SPAN)) >= lax.broadcasted_iota(jnp.int32, (SPAN, SPAN), 1)
        lower = jnp.where(lower, 1.0, 0.0).astype(BF)
        trio[0] = pre
        trio[1] = size
        for at in range(0, tokens, SPAN):
            high, middle, small = pieces(rate[at : at + SPAN])
            trio[2, at : at + SPAN, :] = dot(lower, high) + (dot(lower, middle) + dot(lower, small))
        log = trio[2] * LOG2E
        less = log - jnp.log(size) * LOG2E
        factor = jnp.concatenate(
            [jnp.exp2(log[SPAN - 1 : SPAN] - less[:SPAN]), jnp.exp2(log[SPAN:])], axis=0
        )
        high = factor.astype(BF).astype(F32)
        rest_factor = factor - high
        less_rows = less.T
        log_rows = log.T
        for g in range(GROUPS):
            a, b = g * PER, (g + 1) * PER
            columns[g] = jnp.concatenate(
                [log[:, a:b], less[:, a:b], high[:, a:b], rest_factor[:, a:b]], axis=1
            )
            rows[g] = jnp.concatenate([log_rows[a:b], less_rows[a:b]], axis=0)

    @pl.when((step > 0) & (step <= WIDES // 2))
    def _():
        gather_lanes(weight, own, meta, TABLE)

    @pl.when(step > WIDES // 2)
    def _():
        gather_lanes(weight, rest, meta, TABLE + count)

    @pl.when(step > 0)
    def _():
        lows = [dot_nt(x[...], weight[at : at + TILE, :]) for at in range(0, WIDE, TILE)]
        for n, low in enumerate(lows):
            convolve(low, taps, live, shifted, masked, signal, slope, n * TILE)


def conv_forward(meta, x, taps, steps, own, rest, local):
    tokens, width = x.shape
    count = UNITS
    part = width // count
    half = WIDES // 2

    def natural(i, meta):
        return own_tile(jnp.maximum(i - 1, 0), meta)

    def tile(rows):
        return pl.BlockSpec((rows, WIDE), lambda i, meta: (0, natural(i, meta)))

    def late(i):
        return jnp.maximum(i - 1 - half, 0)

    own_spec = pl.BlockSpec((WIDE, part), lambda i, meta: (jnp.clip(i - 1, 0, half - 1), 0))
    rest_spec = pl.BlockSpec((WIDE, part), lambda i, meta: (late(i), 0))
    local_spec = pl.BlockSpec(
        (WIDE, part), lambda i, meta: (WIDES + (1 - meta[0]) * half + late(i), 0)
    )
    key_spec = pl.BlockSpec((TILE, part), lambda i, meta: (half * WIDE // TILE, 0))
    dt_spec = pl.BlockSpec((64, part), lambda i, meta: ((half * WIDE + TILE) // 64, 0))
    return call(
        conv_body, "conv_forward", meta,
        (x, taps, taps, steps) + tuple(own) + (() if local is None else (local,)) + tuple(rest)
        + tuple(own) * 2,
        [
            whole((tokens, width)), tile(8), pl.BlockSpec((8, TILE), lambda i, meta: (0, DI // TILE)),
            whole((8, LANES)),
        ]
        + [own_spec] * count
        + [rest_spec if local is None else local_spec] + [rest_spec] * (count - 1)
        + [key_spec] * count + [dt_spec] * count,
        [
            shape_of((tokens, DI), BF), shape_of((tokens, DI), BF), shape_of((tokens, DI)),
            shape_of((tokens, TILE), BF), shape_of((tokens, TILE), BF), shape_of((tokens, TILE)),
            shape_of((GROUPS, tokens, PACK)), shape_of((GROUPS, 2 * PER, tokens)),
            shape_of((3, tokens, LANES)),
        ],
        [
            tile(tokens), tile(tokens), tile(tokens),
            whole((tokens, TILE)), whole((tokens, TILE)), whole((tokens, TILE)),
            whole((GROUPS, tokens, PACK)), whole((GROUPS, 2 * PER, tokens)),
            whole((3, tokens, LANES)),
        ],
        [
            pltpu.VMEM((WIDE, width), BF), pltpu.VMEM((64, width), BF),
            pltpu.VMEM((WIDE // LANES, tokens + 8, LANES), F32), pltpu.VMEM((tokens, LANES), F32),
        ],
        1 + WIDES, 2 * tokens * width * CC, 24 * MIB,
    )


def lane_half(shape, half):
    ids = lax.broadcasted_iota(jnp.int32, shape, 1)
    return (ids >= HEADDIM) if half else (ids < HEADDIM)


def heads_apart(value, ones):
    return jnp.concatenate([value * ones[0:1], value * ones[1:2]], axis=0)


def heads_together(stacked):
    middle = stacked.shape[0] // 2
    upper = stacked[:middle]
    return jnp.where(lane_half(upper.shape, 0), upper, stacked[middle:])


def head_lanes(shape, width):
    lane = lax.broadcasted_iota(jnp.int32, shape, 1) // width
    row = lax.broadcasted_iota(jnp.int32, shape, 0) % PER
    return jnp.where(lane == row, 1.0, 0.0).astype(BF)


def scan_body(
    meta, content, keys, columns, rows, skip, out, entering,
    scores, write_rows, mixes, blocked, spread,
):
    half = SPAN // 2

    @pl.when(pl.program_id(0) == 0)
    def _():
        for span in range(2):
            at = span * SPAN
            scores[span] = dot_nt(keys[at : at + SPAN, DSTATE:], keys[at : at + SPAN, :DSTATE])
        write_rows[...] = keys[0:SPAN, :DSTATE].astype(F32).T.astype(BF)
        mixes[...] = jnp.zeros_like(mixes)
        after = row_ids(0, blocked.shape) >= lax.broadcasted_iota(jnp.int32, blocked.shape, 1)
        blocked[...] = jnp.where(after, 0.0, FAR)
        spread[...] = head_lanes(spread.shape, HEADDIM)

    factor = dot(columns[0, :, 2 * PER :].astype(BF), spread[...])
    first = content[0:SPAN, :].astype(F32)
    state = dot(write_rows[...], (first * factor[:SPAN]).astype(BF)).astype(BF)
    entering[0] = state
    out[0:SPAN, :] = skip[...] * first
    carried = dot(keys[SPAN:, DSTATE:], state) * factor[SPAN:]
    out[SPAN:, :] = carried + skip[...] * content[SPAN:, :].astype(F32)
    for pair in range(PER // 2):
        lanes = slice(pair * 2 * HEADDIM, (pair + 1) * 2 * HEADDIM)
        for h in range(2):
            n = 2 * pair + h
            for span in range(2):
                for at in range(0, SPAN, CHUNK):
                    row = span * SPAN + at
                    corner = at // half * half
                    log = columns[0, row : row + CHUNK, n : n + 1]
                    for begin in range(0, corner + half, half):
                        cut = slice(begin, begin + half)
                        less = rows[0, PER + n : PER + n + 1, span * SPAN + begin : span * SPAN + begin + half]
                        decay = log - less
                        if begin == corner:
                            decay = decay + blocked[at - begin : at - begin + CHUNK, :]
                        mix = scores[span, at : at + CHUNK, cut] * jnp.exp2(decay)
                        mixes[pair, span, h * SPAN + at : h * SPAN + at + CHUNK, cut] = mix.astype(BF)
        for span in range(2):
            at = span * SPAN
            value = content[at : at + SPAN, lanes]
            out[at : at + SPAN, lanes] += heads_together(dot(mixes[pair, span], value))


def scan_forward(meta, signal, keys, columns, rows, skip, first, count, filled):
    tokens = signal.shape[0]

    def group(*shape):
        return pl.BlockSpec((1,) + shape, lambda i, meta: (i + first, 0, 0))

    return call(
        scan_body, "scan_forward", meta, (signal, keys, columns, rows, skip),
        [
            tiles(tokens, TILE, first), whole((tokens, TILE)), group(tokens, PACK),
            group(2 * PER, tokens), tiles(1, TILE, first),
        ],
        [shape_of((tokens, DI)), shape_of((GROUPS, DSTATE, TILE), BF)],
        [tiles(tokens, TILE, first), group(DSTATE, TILE)],
        [
            pltpu.VMEM((2, SPAN, SPAN), F32), pltpu.VMEM((DSTATE, SPAN), BF),
            pltpu.VMEM((PER // 2, 2, 2 * SPAN, SPAN), BF), pltpu.VMEM((SPAN // 2, SPAN // 2), F32),
            pltpu.VMEM((2 * PER, TILE), BF),
        ],
        count, 10**9 * count, count * MIB, dict(enumerate(filled)) if filled else None,
    )


def gate_body(meta, x, mixed, gain, *refs):
    count = UNITS
    own, rest = refs[:count], refs[count : 2 * count]
    gate, normed, theirs, scale, weight, gated, total = refs[2 * count :]
    step = pl.program_id(0)
    tokens = x.shape[0]

    @pl.when(step < WIDES // 2)
    def _():
        gather_lanes(weight, own, meta, TABLE)

    @pl.when(step >= WIDES // 2)
    def _():
        gather_lanes(weight, rest, meta, TABLE + count)

    @pl.when(step == 0)
    def _():
        total[...] = jnp.zeros_like(total)

    here = own_tile(step, meta) * WIDE
    lows = [dot_nt(x[...], weight[at : at + TILE, :]).astype(BF) for at in range(0, WIDE, TILE)]
    for n, low in enumerate(lows):
        lanes = slice(n * TILE, (n + 1) * TILE)
        place = pl.ds(pl.multiple_of(here + n * TILE, TILE), TILE)
        gate[:, lanes] = low
        for at in range(0, tokens, CHUNK):
            part = low[at : at + CHUNK].astype(F32)
            part = mixed[at : at + CHUNK, lanes] * (part * sigmoid(part))
            gated[at : at + CHUNK, place] = part
            square = part * part
            total[at : at + CHUNK, :] += square[:, :LANES] + square[:, LANES:]

    @pl.when(step == pl.num_programs(0) - 1)
    def _():
        mean = jnp.sum(total[...], axis=1, keepdims=True) / DI
        scale[...] = lax.rsqrt(mean + epsilon)

        def finish(n, carry):
            place = pl.ds(pl.multiple_of(n * CHUNK, CHUNK), CHUNK)
            factor = jnp.broadcast_to(scale[place, :], (CHUNK, LANES))
            for at in range(0, DI, LANES):
                part = gated[place, at : at + LANES] * factor * gain[:, at : at + LANES]
                normed[place, at : at + LANES] = part.astype(BF)
            return carry

        lax.fori_loop(0, tokens // CHUNK, finish, 0)
        half = DI // (2 * count)
        for k in range(count):
            other = pl.multiple_of((2 * k + 1 - meta[0]) * half, LANES)
            theirs[:, k * half : (k + 1) * half] = normed[:, pl.ds(other, half)]


def gate_forward(meta, x, mixed, gain, own, rest, local):
    tokens, width = x.shape
    count = UNITS
    part = width // count
    half = WIDES // 2
    tile_spec = pl.BlockSpec((tokens, WIDE), lambda i, meta: (0, own_tile(i, meta)))
    own_spec = pl.BlockSpec((WIDE, part), lambda i, meta: (jnp.minimum(i, half - 1), 0))
    rest_spec = pl.BlockSpec((WIDE, part), lambda i, meta: (jnp.maximum(i - half, 0), 0))
    local_spec = pl.BlockSpec(
        (WIDE, part), lambda i, meta: ((1 - meta[0]) * half + jnp.maximum(i - half, 0), 0)
    )
    return call(
        gate_body, "gate_forward", meta,
        (x, mixed, gain) + tuple(own) + (() if local is None else (local,)) + tuple(rest),
        [whole((tokens, width)), tile_spec, whole((1, DI))] + [own_spec] * count
        + [rest_spec if local is None else local_spec] + [rest_spec] * (count - 1),
        [
            shape_of((tokens, DI), BF), shape_of((tokens, DI), BF), shape_of((tokens, DI // 2), BF),
            shape_of((tokens, 1)),
        ],
        [tile_spec, whole((tokens, DI)), whole((tokens, DI // 2)), whole((tokens, 1))],
        [
            pltpu.VMEM((WIDE, width), BF), pltpu.VMEM((tokens, DI), F32),
            pltpu.VMEM((tokens, LANES), F32),
        ],
        WIDES, 2 * tokens * width * DI, 28 * MIB,
    )


def out_body(meta, *refs):
    count = UNITS
    normed, pulled, hidden = refs[0:2], refs[2], refs[3]
    block, back, total, weight, branch = refs[-5:]
    refs = refs[4:-5]
    many = len(refs) // 2
    sides = refs[:many], refs[many:]
    step = pl.program_id(0)
    tokens = pulled.shape[0]
    half = DI // (2 * count)

    @pl.when(step == 0)
    def _():
        total[...] = jnp.zeros_like(total)

    for j in range(count):
        @pl.when(step == j)
        def _(j=j):
            for side, parts in enumerate(sides):
                weight[side * half : (side + 1) * half, :] = parts[j][...]

    normed_both = jnp.concatenate([normed[0][...], normed[1][...]], axis=1)
    grads = dot_nt(pulled[...], weight[...]).astype(BF)
    more = dot(normed_both, weight[...])

    @pl.when(step == 0)
    def _():
        branch[...] = more

    @pl.when((step > 0) & (step < count - 1))
    def _():
        branch[...] += more

    for side in range(2):
        at = meta[OUT_TABLE + side * count + step] * half
        back[:, pl.ds(pl.multiple_of(at, LANES), half)] = grads[:, side * half : (side + 1) * half]
    for at in range(0, tokens, CHUNK):
        sums = None
        for lane in range(0, 2 * half, LANES):
            one = grads[at : at + CHUNK, lane : lane + LANES].astype(F32)
            one = one * normed_both[at : at + CHUNK, lane : lane + LANES].astype(F32)
            sums = one if sums is None else sums + one
        total[at : at + CHUNK, :] += sums

    @pl.when(step == count - 1)
    def _():
        for at in range(0, tokens, CHUNK):
            part = branch[at : at + CHUNK, :] + more[at : at + CHUNK, :]
            part = jnp.where(live_rows(meta, at, part.shape), part, 0.0)
            block[at : at + CHUNK, :] = (hidden[at : at + CHUNK, :].astype(F32) + part).astype(BF)


def out_forward(meta, normed, pulled, hidden, own, rest, local):
    tokens, width = hidden.shape
    count = UNITS
    half = DI // (2 * count)

    def columns(side):
        return pl.BlockSpec(
            (tokens, half), lambda i, meta: (0, meta[OUT_TABLE + side * count + i])
        )

    def local_spec(side):
        return pl.BlockSpec((half, width), lambda i, meta: (meta[0] if side == 0 else 1 - meta[0], 0))

    first = () if local is None else (local,)

    def weight_specs(side):
        if local is None:
            return [whole((half, width))] * count
        return [local_spec(side)] + [whole(part.shape) for part in own]

    return call(
        out_body, "out_forward", meta,
        (normed, normed, pulled, hidden) + (first + tuple(own) + first + tuple(rest)),
        [columns(0), columns(1), whole((tokens, width)), whole((tokens, width))]
        + weight_specs(0) + weight_specs(1),
        [shape_of((tokens, width), BF), shape_of((tokens, DI), BF), shape_of((tokens, LANES))],
        [whole((tokens, width)), whole((tokens, DI)), whole((tokens, LANES))],
        [pltpu.VMEM((2 * half, width), BF), pltpu.VMEM((tokens, width), F32)],
        count, 4 * tokens * width * DI, 24 * MIB,
    )


STEPS = 4


def norm_back_body(
    meta, back, total, mixed, gate, scale, gain, grad_gate, theirs, grad_mixed, grad_gain
):
    step = pl.program_id(0)
    tokens, width = back.shape
    grad_gain[...] = jnp.zeros_like(grad_gain)

    def one(n, carry):
        rows = pl.ds(pl.multiple_of(n * CHUNK, CHUNK), CHUNK)
        r = jnp.broadcast_to(scale[rows, :], (CHUNK, LANES))
        mean = jnp.sum(total[rows, :], axis=1, keepdims=True) / DI
        factor = r * r * mean
        for at in range(0, width, LANES):
            cut = slice(at, at + LANES)
            z = gate[rows, cut].astype(F32)
            sigma = sigmoid(z)
            silu = z * sigma
            out = mixed[rows, cut]
            gated = out * silu
            grad = back[rows, cut].astype(F32) * r
            grad_gain[:, cut] += fold(grad * gated)
            grad = grad * gain[:, cut] - gated * factor
            grad_mixed[rows, cut] = (grad * silu).astype(BF)
            grad_gate[rows, cut] = ((grad * out) * (sigma + silu * (1.0 - sigma))).astype(BF)
        return carry

    lax.fori_loop(0, tokens // CHUNK, one, 0)

    @pl.when(step // (STEPS // 2) == 1 - meta[0])
    def _():
        theirs[...] = grad_gate[...]


def norm_back(meta, back, total, mixed, gate, scale, gain):
    tokens = back.shape[0]
    width = DI // STEPS

    def tile(rows):
        return pl.BlockSpec((rows, width), lambda i, meta: (0, i))

    theirs_spec = pl.BlockSpec(
        (tokens, width),
        lambda i, meta: (0, jnp.clip(i - (1 - meta[0]) * (STEPS // 2), 0, STEPS // 2 - 1)),
    )
    return call(
        norm_back_body, "norm_back", meta, (back, total, mixed, gate, scale, gain),
        [tile(tokens), whole((tokens, LANES)), tile(tokens), tile(tokens), whole((tokens, 1)), tile(1)],
        [
            shape_of((tokens, DI), BF), shape_of((tokens, DI // 2), BF), shape_of((tokens, DI), BF),
            shape_of((8, DI)),
        ],
        [tile(tokens), theirs_spec, tile(tokens), tile(8)],
        [], STEPS, 10**9, 24 * MIB,
    )


def rows_product_body(meta, mine, theirs, pulled, pulled_rest, send, keep):
    total = dot_tn(mine[...], pulled[...]) + dot_tn(theirs[...], pulled_rest[...])
    total = total.astype(BF)
    sent = pl.num_programs(0) // 2

    @pl.when(pl.program_id(0) < sent)
    def _():
        send[0] = total

    @pl.when(pl.program_id(0) >= sent)
    def _():
        keep[0] = total


def rows_product(meta, normed, arrived, arrived_at, pulled, pulled_rest, units):
    tokens, width = pulled.shape
    unit = DI // (2 * UNITS)
    upper = units // 2

    def which(i):
        return lax.rem(i + upper, units)

    result = shape_of((upper, unit, width), BF)
    return call(
        rows_product_body, "rows_product", meta, (normed, arrived, pulled, pulled_rest),
        [
            pl.BlockSpec((tokens, unit), lambda i, meta: (0, meta[OUT_TABLE + which(i)])),
            pl.BlockSpec((tokens, unit), lambda i, meta: (0, meta[arrived_at + which(i)])),
            whole((tokens, width)), whole((tokens, width)),
        ],
        [result, result],
        [
            pl.BlockSpec((1, unit, width), lambda i, meta: (jnp.minimum(i, upper - 1), 0, 0)),
            pl.BlockSpec((1, unit, width), lambda i, meta: (jnp.maximum(i - upper, 0), 0, 0)),
        ],
        [], units, 4 * tokens * width * unit * units, 12 * MIB,
    )


def columns_product_body(plan, meta, *refs):
    parts = len(plan)
    mine, theirs = refs[:parts], refs[parts : 2 * parts]
    here, there, send, keep, right, right_rest = refs[2 * parts :]
    step = pl.program_id(0)
    width = here.shape[1] // UNITS

    @pl.when(step == 0)
    def _():
        for j in range(UNITS):
            lanes = pl.ds(pl.multiple_of(meta[TABLE + j] * width, LANES), width)
            right[:, j * width : (j + 1) * width] = here[:, lanes]
            right_rest[:, j * width : (j + 1) * width] = there[:, lanes]

    for (begin, steps), a, b in zip(plan, mine, theirs):
        @pl.when((step >= begin) & (step < begin + steps))
        def _(a=a, b=b):
            total = (dot_tn(a[...], right[...]) + dot_tn(b[...], right_rest[...])).astype(BF)
            for k in range(UNITS // 2):
                keep[k] = total[:, k * width : (k + 1) * width]
                other = UNITS // 2 + k
                send[k] = total[:, other * width : (other + 1) * width]


def columns_product(meta, parts, normed, normed_rest):
    tokens, width = normed.shape
    part = width // UNITS
    plan, step, mine_specs, theirs_specs = [], 0, [], []

    def spec(begin, steps, start):
        return pl.BlockSpec(
            (tokens, TILE), lambda i, meta: (0, start(meta) + jnp.clip(i - begin, 0, steps - 1))
        )

    for matrix, start, steps, arrived in parts:
        plan.append((step, steps))
        mine_specs.append(spec(step, steps, start))
        theirs_specs.append(spec(step, steps, lambda meta: 0))
        step += steps
    result = shape_of((UNITS // 2, step * TILE, part), BF)
    result_spec = pl.BlockSpec((UNITS // 2, TILE, part), lambda i, meta: (0, i, 0))
    return call(
        functools.partial(columns_product_body, tuple(plan)), "columns_product", meta,
        tuple(p[0] for p in parts) + tuple(p[3] for p in parts) + (normed, normed_rest),
        mine_specs + theirs_specs + [whole((tokens, width))] * 2,
        [result, result], [result_spec, result_spec],
        [pltpu.VMEM((tokens, width), BF), pltpu.VMEM((tokens, width), BF)],
        step, 1, 1,
    )


def conv_back(meta, masked, taps, result, sums, live, grad_conv):
    tokens = masked.shape[0]
    grad_conv[:, tokens:, :] = jnp.zeros((TILE // LANES, 8, LANES), F32)
    sums[...] = jnp.zeros_like(sums)
    for lane in range(0, TILE, LANES):
        cut = slice(lane, lane + LANES)
        totals = [jnp.zeros((8, LANES), F32) for _ in range(CONV + 1)]
        for at in range(0, tokens, CHUNK):
            near = [
                grad_conv[lane // LANES, at + 3 - k : at + 3 - k + CHUNK, :] for k in range(CONV)
            ]
            value = masked[at : at + CHUNK, cut].astype(F32)
            out = near[0] * taps[0:1, cut]
            for k in range(1, CONV):
                out = out + near[k] * taps[k : k + 1, cut]
            result[at : at + CHUNK, cut] = (out * live[at : at + CHUNK, :]).astype(BF)
            for k in range(CONV):
                totals[k] = totals[k] + fold(near[k] * value)
            totals[CONV] = totals[CONV] + fold(near[CONV - 1])
        for k in range(CONV + 1):
            sums[k : k + 1, cut] = jnp.sum(totals[k], axis=0, keepdims=True)


def fold(value):
    return jnp.sum(value.reshape(value.shape[0] // 8, 8, value.shape[1]), axis=0)


def scan_back_body(
    meta, content, keys, grad_out, mixed, entering, columns, rows, skip, masked, slope, taps,
    scores_in, write_in, read_in,
    result, theirs, sums, grad_columns, grad_scores, grad_write, grad_read,
    scores, read_rows, live, grad_conv, mixes, mix_grads, blocked, spread,
):
    half = SPAN // 2

    @pl.when(pl.program_id(0) == 0)
    def _():
        for span in range(2):
            at = span * SPAN
            scores[span] = dot_nt(keys[at : at + SPAN, :DSTATE], keys[at : at + SPAN, DSTATE:])
        read_rows[...] = keys[SPAN:, DSTATE:].astype(F32).T.astype(BF)
        grad_scores[...] = scores_in[...]
        grad_write[...] = write_in[...]
        grad_read[...] = read_in[...]
        mixes[...] = jnp.zeros_like(mixes)
        live_lanes(meta, live)
        after = row_ids(0, blocked.shape) <= lax.broadcasted_iota(jnp.int32, blocked.shape, 1)
        blocked[...] = jnp.where(after, 0.0, FAR)
        spread[...] = head_lanes(spread.shape, HEADDIM)

    def heads_sum(value):
        high = value.astype(BF)
        low = (value - high.astype(F32)).astype(BF)
        return dot_nt(high, spread[...]) + dot_nt(low, spread[...])

    for pair in range(PER // 2):
        lanes = slice(pair * 2 * HEADDIM, (pair + 1) * 2 * HEADDIM)
        ones = spread[2 * pair : 2 * pair + 2, lanes]
        for span in range(2):
            cut = slice(span * SPAN, (span + 1) * SPAN)
            mix_grads[pair, span] = dot_nt(heads_apart(content[cut, lanes], ones), grad_out[cut, lanes])

    factor = dot(columns[0, :, 2 * PER :].astype(BF), spread[...])
    grown = (grad_out[SPAN:, :].astype(F32) * factor[SPAN:]).astype(BF)
    grad_state = dot(read_rows[...], grown).astype(BF)
    grad_read[...] += dot_nt(grown, entering[0])
    worth = (content[0:SPAN, :].astype(F32) * factor[:SPAN]).astype(BF)
    grad_write[...] += dot_nt(worth, grad_state)
    from_state = dot(keys[0:SPAN, :DSTATE], grad_state) * factor[:SPAN]

    for pair in range(PER // 2):
        for h in range(2):
            n = 2 * pair + h
            for span in range(2):
                top = span * SPAN
                for at in range(0, SPAN, CHUNK):
                    less = columns[0, top + at : top + at + CHUNK, PER + n : PER + n + 1]
                    corner = at // half * half
                    for begin in range(corner, SPAN, half):
                        cut = slice(begin, begin + half)
                        decay = rows[0, n : n + 1, top + begin : top + begin + half] - less
                        if begin == corner:
                            decay = decay + blocked[at - begin : at - begin + CHUNK, :]
                        decay = jnp.exp2(decay)
                        row = h * SPAN + at
                        mix = scores[span, at : at + CHUNK, cut] * decay
                        mixes[pair, span, row : row + CHUNK, cut] = mix.astype(BF)
                        change = mix_grads[pair, span, row : row + CHUNK, cut] * decay
                        grad_scores[span, at : at + CHUNK, cut] += change

    lane = lax.broadcasted_iota(jnp.int32, (SPAN, 2 * PER), 1) < PER
    final = row_ids(0, lane.shape) == SPAN - 1
    skips = jnp.zeros((8, TILE), F32)
    for span in range(2):
        cut = slice(span * SPAN, (span + 1) * SPAN)
        value = content[cut, :].astype(F32)
        pull = grad_out[cut, :].astype(F32)
        both = []
        for pair in range(PER // 2):
            lanes = slice(pair * 2 * HEADDIM, (pair + 1) * 2 * HEADDIM)
            both.append(heads_together(dot(mixes[pair, span], grad_out[cut, lanes])))
        both = jnp.concatenate(both, axis=1)
        if span == 0:
            ended = jnp.sum(fold(value * from_state), axis=0, keepdims=True)
            both = both + from_state
        skipped = skip[...] * value
        skips = skips + fold(pull * value)
        written = heads_sum(value * both)
        read = heads_sum(pull * (mixed[cut, :] - skipped))
        if span == 0:
            ended = heads_sum(jnp.broadcast_to(ended, (8, TILE)))[0:1]
            read = read + jnp.where(final, ended, 0.0)
        grad_columns[0, cut, :] = jnp.where(lane, written, read)
        both = (both + skip[...] * pull) * slope[cut, :]
        for k in range(TILE // LANES):
            grad_conv[k, cut, :] = both[:, k * LANES : (k + 1) * LANES]

    conv_back(meta, masked, taps, result, sums, live, grad_conv)
    sums[5:6, :] = jnp.sum(skips, axis=0, keepdims=True)
    half_steps = pl.num_programs(0) // 2
    at_half = pl.program_id(0) // half_steps

    @pl.when(at_half == 1 - meta[0])
    def _():
        theirs[...] = result[...]


def scan_backward(
    meta, signal, keys, grad_out, mixed, entering, columns, rows, skip, masked, slope, taps, kept,
    first, count,
):
    tokens = signal.shape[0]

    def group(*shape):
        return pl.BlockSpec((1,) + shape, lambda i, meta: (i + first, 0, 0))

    def fresh(*shape):
        return pl.BlockSpec((1,) + shape, lambda i, meta: (i, 0, 0))

    kept_specs = [whole((2, SPAN, SPAN)), whole((SPAN, DSTATE)), whole((SPAN, DSTATE))]
    return call(
        scan_back_body, "scan_backward", meta,
        (signal, keys, grad_out, mixed, entering, columns, rows, skip, masked, slope, taps)
        + tuple(kept),
        [
            tiles(tokens, TILE, first), whole((tokens, TILE)),
            tiles(tokens, TILE, first), tiles(tokens, TILE, first), group(DSTATE, TILE),
            group(tokens, PACK),
            group(2 * PER, tokens), tiles(1, TILE, first), tiles(tokens, TILE, first),
            tiles(tokens, TILE, first), tiles(8, TILE, first),
        ]
        + kept_specs,
        [
            shape_of((tokens, count * TILE), BF), shape_of((tokens, count // 2 * TILE), BF),
            shape_of((8, count * TILE)),
            shape_of((count, tokens, 2 * PER)),
            shape_of((2, SPAN, SPAN)), shape_of((SPAN, DSTATE)), shape_of((SPAN, DSTATE)),
        ],
        [
            tiles(tokens, TILE),
            pl.BlockSpec(
                (tokens, TILE),
                lambda i, meta: (0, jnp.clip(i - (1 - meta[0]) * (count // 2), 0, count // 2 - 1)),
            ),
            tiles(8, TILE), fresh(tokens, 2 * PER),
        ]
        + kept_specs,
        [
            pltpu.VMEM((2, SPAN, SPAN), F32), pltpu.VMEM((DSTATE, SPAN), BF),
            pltpu.VMEM((tokens, LANES), F32), pltpu.VMEM((TILE // LANES, tokens + 8, LANES), F32),
            pltpu.VMEM((PER // 2, 2, 2 * SPAN, SPAN), BF),
            pltpu.VMEM((PER // 2, 2, 2 * SPAN, SPAN), F32),
            pltpu.VMEM((SPAN // 2, SPAN // 2), F32), pltpu.VMEM((2 * PER, TILE), BF),
        ],
        count, 3 * 10**9 * count, count * MIB,
    )


def tail_body(parts, meta, *refs):
    keys, masked, slope, taps, trio, steps, grad_scores, grad_write, grad_read = refs[:9]
    grad_columns = refs[9 : 9 + parts]
    result, sums, raw, small, packs, live, grad_conv = refs[9 + parts :]
    tokens = keys.shape[0]
    for span in range(2):
        at = span * SPAN
        write = keys[at : at + SPAN, :DSTATE]
        read = keys[at : at + SPAN, DSTATE:]
        to_write = fine_dot(grad_scores[span], read, dot)
        to_read = fine_dot(grad_scores[span], write, dot_tn)
        if span == 0:
            to_write = to_write + grad_write[...]
        else:
            to_read = to_read + grad_read[...]
        cut = slice(at, at + SPAN)
        grad_conv[0, cut, :] = to_write * slope[cut, :DSTATE]
        grad_conv[1, cut, :] = to_read * slope[cut, DSTATE:]
    live_lanes(meta, live)
    conv_back(meta, masked, taps, result, sums, live, grad_conv)

    blank = jnp.zeros((tokens, LANES - HEADS), F32)
    of_step, of_log = [], []
    for column_ref in grad_columns:
        for g in range(column_ref.shape[0]):
            of_step.append(column_ref[g, :, :PER])
            of_log.append(column_ref[g, :, PER:])
    grad_size = jnp.concatenate(of_step + [blank], axis=1)
    grad_log = jnp.concatenate(of_log + [blank], axis=1) - grad_size
    upper = row_ids(0, (SPAN, SPAN)) <= lax.broadcasted_iota(jnp.int32, (SPAN, SPAN), 1)
    upper = jnp.where(upper, 1.0, 0.0).astype(BF)
    rates = []
    for at in range(0, tokens, SPAN):
        high, middle, low = pieces(grad_log[at : at + SPAN])
        rates.append(dot(upper, high) + (dot(upper, middle) + dot(upper, low)))
    grad_rate = jnp.concatenate(rates, axis=0)
    decay_rate = steps[1:2, :]
    sigma = jax.nn.sigmoid(trio[0])
    size = trio[1]
    tiny = size > 0.0
    share = jnp.where(tiny, sigma / jnp.where(tiny, size, 1.0), 1.0)
    grad_raw = grad_size * share + grad_rate * decay_rate * sigma
    raw[...] = grad_raw.astype(BF)
    small[...] = jnp.zeros_like(small)
    small[0:1, :] = jnp.sum(grad_raw, axis=0, keepdims=True)
    small[1:2, :] = jnp.sum(grad_rate * trio[1], axis=0, keepdims=True) * decay_rate
    for side in range(2):
        at = meta[0] if side == 0 else 1 - meta[0]
        packs[side, :, :LANES] = result[:, pl.ds(pl.multiple_of(at * LANES, LANES), LANES)]
        packs[side, :, LANES:] = raw[...]


def tail_backward(meta, keys, masked, slope, taps, trio, steps, kept, grad_columns):
    tokens = keys.shape[0]
    last = DI // TILE
    key_spec = whole((tokens, TILE))
    return call(
        functools.partial(tail_body, len(grad_columns)), "tail_backward", meta,
        (keys, masked, slope, taps, trio, steps) + tuple(kept) + tuple(grad_columns),
        [
            key_spec, key_spec, key_spec, pl.BlockSpec((8, TILE), lambda i, meta: (0, last)),
            whole((3, tokens, LANES)), whole((8, LANES)), whole((2, SPAN, SPAN)),
            whole((SPAN, DSTATE)), whole((SPAN, DSTATE)),
        ]
        + [whole(part.shape) for part in grad_columns],
        [
            shape_of((tokens, TILE), BF), shape_of((8, TILE)), shape_of((tokens, LANES), BF),
            shape_of((8, LANES)), shape_of((2, tokens, TILE), BF),
        ],
        [
            whole((tokens, TILE)), whole((8, TILE)), whole((tokens, LANES)), whole((8, LANES)),
            whole((2, tokens, TILE)),
        ],
        [pltpu.VMEM((tokens, LANES), F32), pltpu.VMEM((TILE // LANES, tokens + 8, LANES), F32)],
        1, 1, 1,
    )


def input_body(plan, first, last, meta, *refs):
    count = UNITS
    grads = refs[: len(plan)]
    refs = refs[len(plan) :]
    if not first:
        start, refs = refs[0], refs[1:]
    blocks = []
    for begin, steps, half in plan:
        own, refs = refs[:count], refs[count:]
        rest = None
        if half is not None:
            rest, refs = refs[:count], refs[count:]
        blocks.append((own, rest))
    step = pl.program_id(0)

    if last:
        hidden, out_grad, scale, gain, result, weight, weight_dt, total = refs
    else:
        total, weight = refs

    @pl.when(step == 0)
    def _():
        total[...] = jnp.zeros_like(total) if first else start[...]

    for n, (begin, steps, half) in enumerate(plan):
        @pl.when((step >= begin) & (step < begin + steps))
        def _(n=n, half=half):
            own, rest = blocks[n]
            rows = own[0].shape[0]
            if grads[n].shape[1] == LANES:
                weight_dt[...] = jnp.zeros_like(weight_dt)
                gather_lanes(weight_dt, own, meta, TABLE)
                total[...] += dot(grads[n][...], weight_dt[...])
                return
            if half is None:
                gather_lanes(weight, own, meta, TABLE)
            else:
                @pl.when(meta[0] == half)
                def _():
                    gather_lanes(weight, own, meta, TABLE)

                @pl.when(meta[0] != half)
                def _():
                    gather_lanes(weight, rest, meta, TABLE + count)

            total[...] += dot(grads[n][...], weight[0:rows, :])

    if not last:
        return

    @pl.when(step == pl.num_programs(0) - 1)
    def _():
        tokens, width = hidden.shape
        def finish(n, carry):
            rows = pl.ds(pl.multiple_of(n * 32, 32), 32)
            r = jnp.broadcast_to(scale[rows, :], (32, LANES))
            sums = jnp.zeros((32, LANES), F32)
            for at in range(0, width, LANES):
                cut = slice(at, at + LANES)
                both = total[rows, cut] * hidden[rows, cut].astype(F32)
                sums = sums + both * gain[:, cut]
            mean = jnp.sum(sums, axis=1, keepdims=True) / width
            factor = r * r * r * mean
            for at in range(0, width, LANES):
                cut = slice(at, at + LANES)
                value = r * (total[rows, cut] * gain[:, cut]) - hidden[rows, cut].astype(F32) * factor
                result[rows, cut] = value + out_grad[rows, cut].astype(F32)
            return carry

        lax.fori_loop(0, tokens // 32, finish, 0)


def input_backward(meta, start, parts, tokens, width, last=None):
    part = width // UNITS
    plan, step, grad_specs, block_specs, grads, blocks = [], 0, [], [], [], []

    def grad_spec(columns, begin, steps, first):
        return pl.BlockSpec(
            (tokens, columns), lambda i, meta: (0, first + jnp.clip(i - begin, 0, steps - 1))
        )

    def row_spec(rows, begin, steps, first, when):
        def index(i, meta):
            at = first + jnp.clip(i - begin, 0, steps - 1)
            return (at if when is None else jnp.where(when(meta), at, first), 0)

        return pl.BlockSpec((rows, part), index)

    def is_half(half):
        return lambda meta: meta[0] == half

    def not_half(half):
        return lambda meta: meta[0] != half

    for grad, grad_first, steps, half, own, own_first, rest, rest_first, local_first in parts:
        columns = WIDE if half is not None else grad.shape[1]
        if half is not None and steps == WIDES // 2:
            columns, steps = steps * WIDE, 1
            grad_first, local_first = (at // (WIDES // 2) for at in (grad_first, local_first))
        row_tile = 64 if columns == LANES else columns
        plan.append((step, steps, half))
        grads.append(grad)
        grad_specs.append(grad_spec(columns, step, steps, grad_first))
        when = None if half is None else is_half(half)
        for matrix in own:
            blocks.append(matrix)
            block_specs.append(row_spec(row_tile, step, steps, own_first, when))
        if half is not None:
            for j, matrix in enumerate(rest):
                blocks.append(matrix)
                row = local_first if j == 0 else rest_first
                block_specs.append(row_spec(row_tile, step, steps, row, not_half(half)))
        step += steps
    more, more_specs = (), []
    outs, out_specs = [shape_of((tokens, width))], [whole((tokens, width))]
    scratch = [pltpu.VMEM((WIDES // 2 * WIDE, width), BF)]
    if last is not None:
        more = tuple(last)
        more_specs = [whole((tokens, width))] * 2 + [whole((tokens, 1)), whole((1, width))]
        scratch += [
            pltpu.VMEM((LANES, width), BF), pltpu.VMEM((tokens, width), F32),
        ]
    first = start is None
    return call(
        functools.partial(input_body, tuple(plan), first, last is not None),
        "input_backward", meta,
        tuple(grads) + (() if first else (start,)) + tuple(blocks) + more,
        grad_specs + ([] if first else [whole((tokens, width))]) + block_specs + more_specs,
        outs, out_specs, scratch,
        step, 10**10 if last is None else 10**11, 20 * MIB,
    )


def place_body(halves, last, meta, own, other, weight, out, sums):
    step = pl.program_id(0)

    @pl.when(step == 0)
    def _():
        sums[...] = jnp.zeros_like(sums)

    def copy(source, row, rows, at, counted):
        for k in range(0, rows, LANES):
            part = source[row + k : row + k + LANES, :].astype(F32)
            out[at + k : at + k + LANES, :] = part
            some = min(counted, LANES)
            part = part[:some] * weight[at + k : at + k + some, :].astype(F32)
            sums[...] += fold(part)

    def put(which, row, rows, at, counted=LANES):
        @pl.when(meta[0] == which)
        def _():
            copy(own, row, rows, at, counted)

        @pl.when(meta[0] != which)
        def _():
            copy(other, row, rows, at, counted)

    for half in range(2):
        @pl.when(step == half)
        def _(half=half):
            put(half, 0, halves, 0)

    if last:
        @pl.when(step == 2)
        def _():
            put(0, halves, LANES, 0)
            put(1, halves, LANES, LANES)
            put(0, halves + LANES, LANES, 2 * LANES, HEADS)


def place_rows(meta, own, other, weight, halves, first, filled, last):
    length, width = own.shape
    rows = pl.BlockSpec((halves, width), lambda i, meta: (first + i, 0))
    return call(
        functools.partial(place_body, halves, last), "place_rows", meta, (own, other, weight),
        [whole((length, width)), whole((length, width)), rows],
        [shape_of(weight.shape), shape_of((8, width))],
        [rows, whole((8, width))],
        [], 3 if last else 2, 10**10, 20 * MIB, None if filled is None else {0: filled},
    )


NEAR = 8


def mirrored(j, count):
    if count != 4:
        return j
    result, bit, other = 0, 1, count // 2
    while bit < count:
        if j & bit:
            result |= other
        bit, other = bit * 2, other // 2
    return result


def hop(x, bit):
    reps, count = lax.axis_size("rep"), lax.axis_size("shard")
    pairs = []
    for r in range(reps):
        flip = bit if r % 2 == 0 else mirrored(bit, count)
        pairs += [(r * count + s, r * count + (s ^ flip)) for s in range(count)]
    return lax.ppermute(x, ("rep", "shard"), pairs)


def swap(x):
    return lax.ppermute(x, "rep", [(r, r ^ 1) for r in range(lax.axis_size("rep"))])


def across(x, bit):
    return lax.ppermute(x, "shard", [(s, s ^ bit) for s in range(lax.axis_size("shard"))])


def along(x, pairs):
    return lax.ppermute(x, "rep", [(2 * a + k, 2 * b + k) for a, b in pairs for k in range(2)])


def settle(keep, arrived):
    middle = keep.shape[0] // 2
    if middle == 0:
        return None, keep.astype(F32) + arrived.astype(F32)
    held = (keep.astype(F32) + arrived.astype(F32)).astype(BF)
    return held[middle:], held[:middle]


def finish_stages(send, keep):
    while send is not None:
        send, keep = settle(keep, hop(send, send.shape[0]))
    return keep[0]


def inward(held):
    if lax.axis_size("rep") // 2 != 4:
        return held, None
    return held, along(held.astype(BF), [(0, 1), (3, 2)])


def middle(state):
    held, arrived = state
    if arrived is None:
        return held, None
    inner = (held + arrived.astype(F32)).astype(BF)
    return inner, along(inner, [(1, 2), (2, 1)])


def outward(state):
    inner, arrived = state
    if arrived is None:
        chips = lax.axis_size("rep") // 2
        total, bit = inner.astype(BF), 1
        while bit < chips:
            more = along(total, [(k, k ^ bit) for k in range(chips)])
            total = (total.astype(F32) + more.astype(F32)).astype(BF)
            bit *= 2
        return total, None
    total = (inner.astype(F32) + arrived.astype(F32)).astype(BF)
    return total, along(total, [(1, 0), (2, 3)])


def summed(state):
    total, arrived = state
    if arrived is None:
        return total
    place = lax.axis_index("rep") // 2
    return jnp.where((place == 1) | (place == 2), total, arrived)


def in_order(own, other, core):
    return [jnp.where(core == 0, own, other), jnp.where(core == 0, other, own)]


def hold(values):
    leaves, tree = jax.tree.flatten(values)
    return jax.tree.unflatten(tree, lax.optimization_barrier(tuple(leaves)))


def add_up(rows):
    while len(rows) > 1:
        rows = [a + b for a, b in zip(rows[::2], rows[1::2])]
    return rows[0]


def group_rows(vector, shard, count):
    rows = [lax.dynamic_slice_in_dim(vector, shard ^ j, 1, 0) for j in range(count)]
    return rows[:1] + [across(row, j) for j, row in enumerate(rows) if j]


def chips_sum(row):
    chips = lax.axis_size("rep") // 2
    return add_up(
        [row] + [along(row, [(k, k ^ d) for k in range(chips)]) for d in range(1, chips)]
    )


def join_lanes(blocks, shard):
    return [
        jnp.concatenate(in_order(blocks[j], blocks[j + 1], shard % 2), axis=1)
        for j in range(0, len(blocks), 2)
    ]


def split_lanes(units, shard):
    half = units.shape[2] // 2
    pairs = in_order(units[:, :, :half], units[:, :, half:], shard % 2)
    return jnp.stack(pairs, axis=1).reshape(2 * units.shape[0], units.shape[1], half)


def pad_lanes(matrix):
    return jnp.pad(matrix, ((0, 0), (0, LANES - matrix.shape[1])))


def shards(
    hidden,
    out_grad,
    norm_gain,
    in_w,
    conv_w,
    conv_b,
    dt_bias,
    a_log,
    skip,
    out_gain,
    out_w,
    lengths,
    offsets,
):
    core = lax.axis_index("rep") % 2
    shard = lax.axis_index("shard")
    count = lax.axis_size("shard")
    tokens, width = hidden.shape
    bits = []
    while 2 ** len(bits) < count:
        bits.append(2 ** len(bits))

    local = in_w.T
    half = DI // 2
    piece = jnp.concatenate(
        [
            lax.dynamic_slice_in_dim(local, DI + core * half, half, 0),
            local[2 * DI :],
            jnp.zeros((16, local.shape[1]), BF),
        ],
        axis=0,
    )
    gate_piece = lax.dynamic_slice_in_dim(local, core * half, half, 0)
    out_piece = lax.dynamic_slice_in_dim(out_w, core * (out_w.shape[0] // 2), out_w.shape[0] // 2, 0)

    def spread(first):
        blocks = [first]
        for bit in bits:
            blocks = blocks + [hop(block, bit) for block in blocks]
        return blocks

    paired = count == 4
    small = (norm_gain, conv_w.T, conv_b, dt_bias, a_log, skip, out_gain)
    packed = jnp.concatenate([part.reshape(-1) for part in small])
    everyone = [packed] + [
        lax.ppermute(
            packed, ("rep", "shard"),
            [
                (r * count + s, r * count + (s ^ (j if r % 2 == 0 else mirrored(j, count))))
                for r in range(lax.axis_size("rep"))
                for s in range(count)
            ],
        )
        for j in range(1, count)
    ]
    everyone = jnp.stack(everyone).astype(F32)
    order = [jnp.where(core == 0, j, mirrored(j, count)) for j in range(count)]
    whose = jnp.stack(order)[jnp.arange(count) ^ shard]
    same = (whose[:, None] == jnp.arange(count)[None]).astype(F32)
    everyone = jnp.sum(same[:, :, None] * everyone[None], axis=1)
    parts, start = [], 0
    for part in small:
        cut = everyone[:, start : start + part.size].reshape((count,) + part.shape)
        cut = jnp.moveaxis(cut, 0, -2)
        parts.append(cut.reshape(part.shape[:-1] + (-1,)))
        start += part.size
    conv_own = spread(piece)
    gate_piece, conv_own = hold((gate_piece, conv_own))
    if paired:
        conv_rest = [swap(block) for block in conv_own[1:]]
        gate_near = hop(gate_piece, 1), hop(gate_piece, 2)
        out_local, in_local = out_w, local
    else:
        gate_own = spread(gate_piece)
        out_piece, gate_own = hold((out_piece, gate_own))
        out_own = spread(out_piece)
        conv_rest = rest_conv = join_lanes([swap(block) for block in conv_own], shard)
        gate_rest = rest_gate = join_lanes([swap(block) for block in gate_own], shard)
        conv_own, gate_own = join_lanes(conv_own, shard), join_lanes(gate_own, shard)
        out_full = [jnp.concatenate(in_order(block, swap(block), core), axis=0) for block in out_own]
        out_one, out_two = out_full[:UNITS], out_full[UNITS:]
        out_local = in_local = None

    gain_one, kernel, bias_conv, bias_step, log_rate, skip_full, gain_two = parts
    decay_rate = -jnp.exp(log_rate)

    mine = order
    other = [jnp.where(core == 0, mirrored(j, count), j) for j in range(count)]
    mine, other = [shard ^ j for j in mine], [shard ^ j for j in other]
    if paired:
        out_units = [2 * j + core for j in mine] + [2 * j + 1 - core for j in other]
    else:
        out_units = mine
        mine = other = [j // 2 for j in mine[::2]]
    meta = jnp.stack(
        [core, offsets[0], lengths[0], shard] + mine + other + out_units
    ).astype(jnp.int32)
    taps = jnp.concatenate([kernel, bias_conv[None], jnp.zeros((3, CC), F32)], axis=0)
    steps = jnp.concatenate(
        [pad_lanes(jnp.stack([bias_step, decay_rate])), jnp.zeros((6, LANES), F32)], axis=0
    )
    skip_lanes = jnp.repeat(skip_full, HEADDIM)[None]

    positions = jnp.arange(tokens, dtype=jnp.int32)
    live_mask = ((positions >= offsets[0]) & (positions < offsets[0] + lengths[0])).astype(F32)
    hidden_full = hidden.astype(F32)
    inv_rms = lax.rsqrt(jnp.mean(hidden_full * hidden_full, axis=1, keepdims=True) + epsilon)
    normed = (hidden_full * inv_rms * gain_one).astype(BF)
    pulled = (out_grad.astype(F32) * live_mask[:, None]).astype(BF)
    normed_rest = swap(normed)
    pulled_rest = swap(pulled)

    (masked, signal, slope, masked_keys, keys, slope_keys, columns, rows, trio) = conv_forward(
        meta, normed, taps, steps, conv_own, conv_rest, in_local
    )
    if paired:
        gate_near, signal = hold((gate_near, signal))
        gate_own = [gate_piece, *gate_near, hop(gate_near[0], 2)]
    kept = None
    for first in range(0, GROUPS, GROUPS // 2):
        kept = scan_forward(
            meta, signal, keys, columns, rows, skip_lanes, first, GROUPS // 2, kept
        )
        if paired and first == 0:
            gate_far, out_piece, kept = hold((gate_own[3], out_piece, kept))
            gate_own[3] = gate_far
            gate_rest = [swap(block) for block in gate_own[1:]]
            out_near = hop(out_piece, 1), hop(out_piece, 2)
    mixed, entering = kept
    if paired:
        rest_conv, rest_gate = [local] + conv_rest, [local] + gate_rest
    gate, normed_out, out_theirs, scale = gate_forward(
        meta, normed, mixed, gain_two[None], gate_own, gate_rest, in_local
    )
    out_arrived = swap(out_theirs if paired else normed_out)
    if paired:
        out_near, normed_out = hold((out_near, normed_out))
        out_one = [*out_near, hop(out_near[0], 2)]
        out_two = [swap(block) for block in out_one]

    upper = count // 2
    out_pulls = (pulled, pulled_rest)
    if not paired:
        cut = core * (width // 2)
        out_pulls = [lax.dynamic_slice_in_dim(x, cut, width // 2, 1) for x in out_pulls]

    def product(parts):
        send, keep = columns_product(meta, parts, normed, normed_rest)
        return (send, keep) if paired else (split_lanes(send, shard), split_lanes(keep, shard))

    out_send, out_keep = rows_product(
        meta, normed_out, out_arrived, TABLE if paired else OUT_TABLE, *out_pulls, count
    )
    out_send, out_keep, normed_out = hold((out_send, out_keep, normed_out))
    out_there = hop(out_send, upper)
    block_out, back, total = out_forward(
        meta, normed_out, pulled, hidden, out_one, out_two, out_local
    )
    out_there, total = hold((out_there, total))
    out_send, out_keep = settle(out_keep, out_there)
    out_there = hop(out_send, upper // 2)
    out_keep, total = hold((out_keep, total))
    grad_gate, gate_theirs, grad_mixed, grad_gain_two = norm_back(
        meta, back, total, mixed, gate, scale, gain_two[None]
    )

    gate_theirs, out_there = hold((gate_theirs, out_there))
    gate_arrived = swap(gate_theirs)
    out_line = inward(finish_stages(*settle(out_keep, out_there)))
    out_held, gate_arrived = hold((out_line[0], gate_arrived))
    gate_parts = [(grad_gate, lambda meta: meta[0] * (GROUPS // 2), GROUPS // 2, gate_arrived)]
    gate_send, gate_keep = product(gate_parts)
    gate_send, gate_keep, grad_mixed = hold((gate_send, gate_keep, grad_mixed))
    gate_there = hop(gate_send, upper)
    kept = (
        jnp.zeros((2, SPAN, SPAN), F32),
        jnp.zeros((SPAN, DSTATE), F32),
        jnp.zeros((SPAN, DSTATE), F32),
    )
    near, far = NEAR, GROUPS - NEAR
    part = WIDES // 2
    over = near * TILE // WIDE - part

    def gate_part(half):
        at = half * part
        return [(grad_gate, at, part, half, gate_own, 0, rest_gate, 0, at if paired else 0)]

    def conv_part(grad, grad_first, steps, half, first):
        local_first = WIDES + half * part + first if paired else first
        return [(grad, grad_first, steps, half, conv_own, first, rest_conv, first, local_first)]

    grad_near, near_theirs, sums_near, columns_near, *kept = scan_backward(
        meta, signal, keys, grad_mixed, mixed, entering, columns, rows, skip_lanes, masked, slope, taps,
        kept, 0, near,
    )
    gate_there, near_theirs, out_arrived = hold((gate_there, near_theirs, out_line[1]))
    near_arrived = swap(near_theirs)
    gate_send, gate_keep = settle(gate_keep, gate_there)
    gate_there = hop(gate_send, upper // 2)
    gate_keep, out_arrived = hold((gate_keep, out_arrived))
    out_line = middle((out_held, out_arrived))
    near_arrived, gate_keep, out_inner = hold((near_arrived, gate_keep, out_line[0]))
    near_parts = [(grad_near, lambda meta: meta[0] * (near // 2), near // 2, near_arrived)]
    near_send, near_keep = product(near_parts)
    near_there = hop(near_send, upper)
    near_keep, kept, grad_mixed = hold((near_keep, kept, grad_mixed))
    grad_far, far_theirs, sums_far, columns_far, *kept = scan_backward(
        meta, signal, keys, grad_mixed, mixed, entering, columns, rows, skip_lanes, masked, slope, taps,
        kept, near, far,
    )
    far_theirs, gate_there = hold((far_theirs, gate_there))
    far_arrived = swap(far_theirs)
    gate_line = inward(finish_stages(*settle(gate_keep, gate_there)))
    gate_held, kept = hold((gate_line[0], kept))
    grad_keys, sums_keys, grad_raw, grad_steps, packs = tail_backward(
        meta, keys, masked_keys, slope_keys, taps, trio, steps, kept, (columns_near, columns_far),
    )
    packs, near_there = hold((packs, near_there))
    packs_arrived = swap(packs[1])
    near_send, near_keep = settle(near_keep, near_there)
    near_there = hop(near_send, upper // 2)
    packs, packs_arrived, near_keep = hold((packs, packs_arrived, near_keep))
    far_parts = [
        (grad_far, lambda meta: meta[0] * (far // 2), far // 2, far_arrived),
        (packs[0], lambda meta: 0, 1, packs_arrived),
    ]
    far_send, far_keep = product(far_parts)
    far_there = hop(far_send, upper)
    far_keep, gate_arrived, near_there, out_arrived = hold(
        (far_keep, gate_line[1], near_there, out_line[1])
    )
    gate_line = middle((gate_held, gate_arrived))
    near_line = inward(finish_stages(*settle(near_keep, near_there)))
    out_line = outward((out_inner, out_arrived))
    gate_inner, near_held, out_done, grad_gate = hold(
        (gate_line[0], near_line[0], out_line[0], grad_gate)
    )
    (partial,) = input_backward(meta, None, gate_part(0) + gate_part(1), tokens, width)
    partial, far_there = hold((partial, far_there))
    far_send, far_keep = settle(far_keep, far_there)
    far_there = hop(far_send, upper // 2)
    far_keep, near_arrived, small_grads = hold(
        (far_keep, near_line[1], (sums_near, sums_far, sums_keys, grad_steps, grad_gain_two))
    )
    sums_near, sums_far, sums_keys, grad_steps, grad_gain_two = small_grads
    sums = jnp.concatenate([sums_near, sums_far, sums_keys], axis=1)
    grads = (
        sums[:CONV].reshape(CONV, count, -1).transpose(1, 0, 2).reshape(count, -1),
        sums[CONV].reshape(count, -1),
        grad_steps[0, :HEADS].reshape(count, -1),
        grad_steps[1, :HEADS].reshape(count, -1),
        jnp.sum(sums[5, :DI].reshape(HEADS, HEADDIM), axis=1).reshape(count, -1),
        jnp.sum(grad_gain_two, axis=0).reshape(count, -1),
    )
    vector = jnp.concatenate(grads, axis=1)
    far_there, far_keep, partial, vector = hold((far_there, far_keep, partial, vector))
    vector_there = swap(vector)
    far_line = inward(finish_stages(*settle(far_keep, far_there)))
    far_held, gate_arrived, out_arrived = hold((far_line[0], gate_line[1], out_line[1]))
    gate_line = outward((gate_inner, gate_arrived))
    near_line = middle((near_held, near_arrived))
    out_total = summed((out_done, out_arrived))
    out_other = swap(out_total)
    far_held, gate_done, near_inner, out_total, partial = hold(
        (far_held, gate_line[0], near_line[0], out_total, partial)
    )
    (partial,) = input_backward(
        meta, partial,
        conv_part(grad_near, 0, part, 0, 0)
        + conv_part(grad_near, part, over, 1, 0)
        + conv_part(grad_far, 0, part - over, 1, over),
        tokens, width,
    )
    partial, far_arrived = hold((partial, far_line[1]))
    far_line = middle((far_held, far_arrived))
    far_inner, near_arrived, gate_arrived, out_other, vector_there = hold(
        (far_line[0], near_line[1], gate_line[1], out_other, vector_there)
    )
    spread_rows = group_rows(vector + vector_there, shard, count)
    near_line = outward((near_inner, near_arrived))
    gate_total = summed((gate_done, gate_arrived))
    gate_other = swap(gate_total)
    far_inner, near_done, gate_total, gate_other, partial = hold(
        (far_inner, near_line[0], gate_total, gate_other, partial)
    )
    rows_so_far, sums_one = place_rows(meta, gate_total, gate_other, local, DI // 2, 0, None, False)
    rows_so_far, far_arrived, spread_rows = hold((rows_so_far, far_line[1], spread_rows))
    far_line = outward((far_inner, far_arrived))
    far_done, partial, spread_rows = hold((far_line[0], partial, spread_rows))
    row = chips_sum(add_up(spread_rows))[0]
    (hidden_grad,) = input_backward(
        meta, partial,
        [
            (grad_keys, 0, 1, None, conv_own, DI // 2 // TILE, None, 0, 0),
            (grad_raw, 0, 1, None, conv_own, (DI // 2 + TILE) // 64, None, 0, 0),
        ],
        tokens, width, (hidden, out_grad, inv_rms, gain_one[None]),
    )
    hidden_grad, near_arrived, row = hold((hidden_grad, near_line[1], row))
    near_total = summed((near_done, near_arrived))
    near_other = swap(near_total)
    near_total, far_arrived = hold((near_total, far_line[1]))
    far_total = summed((far_done, far_arrived))
    far_other = swap(far_total)
    wide = near // 2 * TILE
    rows_so_far, sums_two = place_rows(
        meta, near_total, near_other, local, wide, DI // wide, rows_so_far, False
    )
    wide = far // 2 * TILE
    rows_so_far, sums_three = place_rows(
        meta, far_total, far_other, local, wide, (DI + near * TILE) // wide, rows_so_far, True
    )
    gain_row = jnp.sum(sums_one + sums_two + sums_three, axis=0) / norm_gain.astype(F32)
    in_w_grad = rows_so_far.T

    out_w_grad = jnp.concatenate(
        in_order(out_total, out_other, core), axis=0 if paired else 1
    ).astype(F32)
    found, start = [], 0
    for part in grads:
        found.append(row[start : start + part.shape[1]])
        start += part.shape[1]
    return (
        block_out,
        hidden_grad,
        gain_row,
        in_w_grad,
        found[0].reshape(CONV, -1).T,
        found[1],
        found[2],
        found[3],
        found[4],
        found[5],
        out_w_grad,
    )


def solution(mesh):
    return jax.shard_map(
        shards,
        mesh=mesh,
        in_specs=(
            P(("rep", "shard"), None),
            P(("rep", "shard"), None),
            P("shard"),
            P("shard", None),
            P("shard", None),
            P("shard"),
            P("shard"),
            P("shard"),
            P("shard"),
            P("shard"),
            P("shard", None),
            P(("rep", "shard")),
            P(("rep", "shard")),
        ),
        out_specs=(
            P(("rep", "shard"), None),
            P(("rep", "shard"), None),
            P("shard"),
            P("shard", None),
            P("shard", None),
            P("shard"),
            P("shard"),
            P("shard"),
            P("shard"),
            P("shard"),
            P("shard", None),
        ),
        check_vma=False,
    )
```

```python
import functools

import jax
import jax.numpy as jnp
from jax import lax
from jax.experimental import pallas as pl
from jax.experimental.pallas import tpu as pltpu
from jax.sharding import PartitionSpec as P

HEADS = 48
HEADDIM = 64
DSTATE = 128
CONV = 4
SPAN = 256
DI = 3072
CC = 3328
TILE = 256
GROUPS = DI // TILE
PER = TILE // HEADDIM
CHUNK = 64
LANES = 128
epsilon = 1e-05
FAR = -1e30
LOG2E = 1.4426950408889634
PACK = 4 * PER

BF = jnp.bfloat16
F32 = jnp.float32
MIB = 1 << 20


def dot(lhs, rhs):
    return jnp.dot(lhs, rhs, preferred_element_type=F32)


def dot_nt(lhs, rhs):
    return lax.dot_general(lhs, rhs, (((1,), (1,)), ((), ())), preferred_element_type=F32)


def dot_tn(lhs, rhs):
    return lax.dot_general(lhs, rhs, (((0,), (0,)), ((), ())), preferred_element_type=F32)


def sigmoid(value):
    return 0.5 * jnp.tanh(0.5 * value) + 0.5


def pieces(value):
    high = value.astype(BF)
    rest = value - high.astype(F32)
    middle = rest.astype(BF)
    low = (rest - middle.astype(F32)).astype(BF)
    return high, middle, low


def fine_dot(lhs, rhs, product):
    high, middle, low = pieces(lhs)
    return product(high, rhs) + (product(middle, rhs) + product(low, rhs))


def row_ids(start, shape):
    return start + lax.broadcasted_iota(jnp.int32, shape, 0)


def live_rows(meta, start, shape):
    ids = row_ids(start, shape)
    return (ids >= meta[1]) & (ids < meta[1] + meta[2])


def gather_lanes(target, blocks, table, at):
    for j, block in enumerate(blocks):
        width = block.shape[1]
        lanes = pl.ds(pl.multiple_of(table[at + j] * width, LANES), width)
        target[0 : block.shape[0], lanes] = block[...]


def call(
    body, name, meta, operands, in_specs, outs, out_specs, scratch, grid, flops, moved, filled=None
):
    if filled:
        first = len(operands) + 1
        operands, extra = operands + tuple(filled.values()), len(filled)
        in_specs = in_specs + [pl.BlockSpec(memory_space=pl.ANY)] * extra
        aliases = {first + n: place for n, place in enumerate(filled)}
        inner, many = body, first - 1

        def body(meta, *refs):
            return inner(meta, *refs[:many], *refs[many + extra :])
    else:
        aliases = {}
    return pl.pallas_call(
        body,
        name=name,
        grid_spec=pltpu.PrefetchScalarGridSpec(
            num_scalar_prefetch=1,
            grid=(grid,),
            in_specs=in_specs,
            out_specs=out_specs,
            scratch_shapes=scratch,
        ),
        out_shape=outs,
        input_output_aliases=aliases,
        compiler_params=pltpu.CompilerParams(vmem_limit_bytes=60 * MIB),
        cost_estimate=pl.CostEstimate(flops=flops, bytes_accessed=moved, transcendentals=0),
    )(meta, *operands)


def whole(shape):
    rank = len(shape)
    return pl.BlockSpec(shape, lambda i, meta: (0,) * rank)


def tiles(rows, width, shift=0, last=None):
    def index(i, meta):
        at = i + shift
        if last is not None:
            at = jnp.clip(at, 0, last)
        return (0, at)

    return pl.BlockSpec((rows, width), index)


def shape_of(shape, kind=F32):
    return jax.ShapeDtypeStruct(shape, kind)


TABLE = 4
UNITS = 4
OUT_TABLE = TABLE + 2 * UNITS
WIDE = 512
WIDES = DI // WIDE


def own_tile(i, meta):
    half = WIDES // 2
    return jnp.where(i < half, meta[0] * half + i, (1 - meta[0]) * half + i - half)


def live_lanes(meta, live):
    live[...] = jnp.where(live_rows(meta, 0, live.shape), 1.0, 0.0)


def convolve(low, taps, live, shifted, masked, signal, slope, begin):
    for lane in range(0, low.shape[1], LANES):
        cut = slice(begin + lane, begin + lane + LANES)
        tile = (begin + lane) // LANES
        for at in range(0, low.shape[0], CHUNK):
            part = low[at : at + CHUNK, lane : lane + LANES].astype(BF).astype(F32)
            part = part * live[at : at + CHUNK, :]
            masked[at : at + CHUNK, cut] = part.astype(BF)
            shifted[tile, 8 + at : 8 + at + CHUNK, :] = part
        for at in range(0, low.shape[0], CHUNK):
            out = taps[4:5, cut]
            for k in range(CONV):
                out = out + shifted[tile, at + 5 + k : at + 5 + k + CHUNK, :] * taps[k : k + 1, cut]
            sigma = sigmoid(out)
            out = out * sigma
            here = live[at : at + CHUNK, :]
            signal[at : at + CHUNK, cut] = (out * here).astype(BF)
            slope[at : at + CHUNK, cut] = (sigma + out * (1.0 - sigma)) * here


def conv_body(meta, x, taps, taps_keys, steps, *refs):
    count = UNITS
    own, rest, key_rows, dts = (refs[n * count : (n + 1) * count] for n in range(4))
    (masked, signal, slope, masked_keys, keys, slope_keys, columns, rows, trio,
     weight, weight_dt, shifted, live) = refs[4 * count :]
    tokens = x.shape[0]
    step = pl.program_id(0)

    @pl.when(step == 0)
    def _():
        shifted[:, 0:8, :] = jnp.zeros((WIDE // LANES, 8, LANES), F32)
        live_lanes(meta, live)
        gather_lanes(weight, key_rows, meta, TABLE)
        gather_lanes(weight_dt, dts, meta, TABLE)
        low = dot_nt(x[...], weight[0:TILE, :])
        raw = dot_nt(x[...], weight_dt[...]).astype(BF).astype(F32)
        convolve(low, taps_keys, live, shifted, masked_keys, keys, slope_keys, 0)
        raw = jnp.concatenate([raw, jnp.zeros((tokens, LANES - raw.shape[1]), F32)], axis=1)
        pre = raw + steps[0:1, :]
        size = jnp.maximum(pre, 0.0) + jnp.log1p(jnp.exp(-jnp.abs(pre)))
        rate = size * steps[1:2, :]
        lower = row_ids(0, (SPAN, SPAN)) >= lax.broadcasted_iota(jnp.int32, (SPAN, SPAN), 1)
        lower = jnp.where(lower, 1.0, 0.0).astype(BF)
        trio[0] = pre
        trio[1] = size
        for at in range(0, tokens, SPAN):
            high, middle, small = pieces(rate[at : at + SPAN])
            trio[2, at : at + SPAN, :] = dot(lower, high) + (dot(lower, middle) + dot(lower, small))
        log = trio[2] * LOG2E
        less = log - jnp.log(size) * LOG2E
        factor = jnp.concatenate(
            [jnp.exp2(log[SPAN - 1 : SPAN] - less[:SPAN]), jnp.exp2(log[SPAN:])], axis=0
        )
        high = factor.astype(BF).astype(F32)
        rest_factor = factor - high
        less_rows = less.T
        log_rows = log.T
        for g in range(GROUPS):
            a, b = g * PER, (g + 1) * PER
            columns[g] = jnp.concatenate(
                [log[:, a:b], less[:, a:b], high[:, a:b], rest_factor[:, a:b]], axis=1
            )
            rows[g] = jnp.concatenate([log_rows[a:b], less_rows[a:b]], axis=0)

    @pl.when((step > 0) & (step <= WIDES // 2))
    def _():
        gather_lanes(weight, own, meta, TABLE)

    @pl.when(step > WIDES // 2)
    def _():
        gather_lanes(weight, rest, meta, TABLE + count)

    @pl.when(step > 0)
    def _():
        lows = [dot_nt(x[...], weight[at : at + TILE, :]) for at in range(0, WIDE, TILE)]
        for n, low in enumerate(lows):
            convolve(low, taps, live, shifted, masked, signal, slope, n * TILE)


def conv_forward(meta, x, taps, steps, own, rest, local):
    tokens, width = x.shape
    count = UNITS
    part = width // count
    half = WIDES // 2

    def natural(i, meta):
        return own_tile(jnp.maximum(i - 1, 0), meta)

    def tile(rows):
        return pl.BlockSpec((rows, WIDE), lambda i, meta: (0, natural(i, meta)))

    def late(i):
        return jnp.maximum(i - 1 - half, 0)

    own_spec = pl.BlockSpec((WIDE, part), lambda i, meta: (jnp.clip(i - 1, 0, half - 1), 0))
    rest_spec = pl.BlockSpec((WIDE, part), lambda i, meta: (late(i), 0))
    local_spec = pl.BlockSpec(
        (WIDE, part), lambda i, meta: (WIDES + (1 - meta[0]) * half + late(i), 0)
    )
    key_spec = pl.BlockSpec((TILE, part), lambda i, meta: (half * WIDE // TILE, 0))
    dt_spec = pl.BlockSpec((64, part), lambda i, meta: ((half * WIDE + TILE) // 64, 0))
    return call(
        conv_body, "conv_forward", meta,
        (x, taps, taps, steps) + tuple(own) + (() if local is None else (local,)) + tuple(rest)
        + tuple(own) * 2,
        [
            whole((tokens, width)), tile(8), pl.BlockSpec((8, TILE), lambda i, meta: (0, DI // TILE)),
            whole((8, LANES)),
        ]
        + [own_spec] * count
        + [rest_spec if local is None else local_spec] + [rest_spec] * (count - 1)
        + [key_spec] * count + [dt_spec] * count,
        [
            shape_of((tokens, DI), BF), shape_of((tokens, DI), BF), shape_of((tokens, DI)),
            shape_of((tokens, TILE), BF), shape_of((tokens, TILE), BF), shape_of((tokens, TILE)),
            shape_of((GROUPS, tokens, PACK)), shape_of((GROUPS, 2 * PER, tokens)),
            shape_of((3, tokens, LANES)),
        ],
        [
            tile(tokens), tile(tokens), tile(tokens),
            whole((tokens, TILE)), whole((tokens, TILE)), whole((tokens, TILE)),
            whole((GROUPS, tokens, PACK)), whole((GROUPS, 2 * PER, tokens)),
            whole((3, tokens, LANES)),
        ],
        [
            pltpu.VMEM((WIDE, width), BF), pltpu.VMEM((64, width), BF),
            pltpu.VMEM((WIDE // LANES, tokens + 8, LANES), F32), pltpu.VMEM((tokens, LANES), F32),
        ],
        1 + WIDES, 2 * tokens * width * CC, 24 * MIB,
    )


def lane_half(shape, half):
    ids = lax.broadcasted_iota(jnp.int32, shape, 1)
    return (ids >= HEADDIM) if half else (ids < HEADDIM)


def heads_apart(value, ones):
    return jnp.concatenate([value * ones[0:1], value * ones[1:2]], axis=0)


def heads_together(stacked):
    middle = stacked.shape[0] // 2
    upper = stacked[:middle]
    return jnp.where(lane_half(upper.shape, 0), upper, stacked[middle:])


def head_lanes(shape, width):
    lane = lax.broadcasted_iota(jnp.int32, shape, 1) // width
    row = lax.broadcasted_iota(jnp.int32, shape, 0) % PER
    return jnp.where(lane == row, 1.0, 0.0).astype(BF)


def scan_body(
    meta, content, keys, columns, rows, skip, out, entering,
    scores, write_rows, mixes, blocked, spread,
):
    half = SPAN // 2

    @pl.when(pl.program_id(0) == 0)
    def _():
        for span in range(2):
            at = span * SPAN
            scores[span] = dot_nt(keys[at : at + SPAN, DSTATE:], keys[at : at + SPAN, :DSTATE])
        write_rows[...] = keys[0:SPAN, :DSTATE].astype(F32).T.astype(BF)
        mixes[...] = jnp.zeros_like(mixes)
        after = row_ids(0, blocked.shape) >= lax.broadcasted_iota(jnp.int32, blocked.shape, 1)
        blocked[...] = jnp.where(after, 0.0, FAR)
        spread[...] = head_lanes(spread.shape, HEADDIM)

    factor = dot(columns[0, :, 2 * PER :].astype(BF), spread[...])
    first = content[0:SPAN, :].astype(F32)
    state = dot(write_rows[...], (first * factor[:SPAN]).astype(BF)).astype(BF)
    entering[0] = state
    out[0:SPAN, :] = skip[...] * first
    carried = dot(keys[SPAN:, DSTATE:], state) * factor[SPAN:]
    out[SPAN:, :] = carried + skip[...] * content[SPAN:, :].astype(F32)
    for pair in range(PER // 2):
        lanes = slice(pair * 2 * HEADDIM, (pair + 1) * 2 * HEADDIM)
        for h in range(2):
            n = 2 * pair + h
            for span in range(2):
                for at in range(0, SPAN, CHUNK):
                    row = span * SPAN + at
                    corner = at // half * half
                    log = columns[0, row : row + CHUNK, n : n + 1]
                    for begin in range(0, corner + half, half):
                        cut = slice(begin, begin + half)
                        less = rows[0, PER + n : PER + n + 1, span * SPAN + begin : span * SPAN + begin + half]
                        decay = log - less
                        if begin == corner:
                            decay = decay + blocked[at - begin : at - begin + CHUNK, :]
                        mix = scores[span, at : at + CHUNK, cut] * jnp.exp2(decay)
                        mixes[pair, span, h * SPAN + at : h * SPAN + at + CHUNK, cut] = mix.astype(BF)
        for span in range(2):
            at = span * SPAN
            value = content[at : at + SPAN, lanes]
            out[at : at + SPAN, lanes] += heads_together(dot(mixes[pair, span], value))


def scan_forward(meta, signal, keys, columns, rows, skip, first, count, filled):
    tokens = signal.shape[0]

    def group(*shape):
        return pl.BlockSpec((1,) + shape, lambda i, meta: (i + first, 0, 0))

    return call(
        scan_body, "scan_forward", meta, (signal, keys, columns, rows, skip),
        [
            tiles(tokens, TILE, first), whole((tokens, TILE)), group(tokens, PACK),
            group(2 * PER, tokens), tiles(1, TILE, first),
        ],
        [shape_of((tokens, DI)), shape_of((GROUPS, DSTATE, TILE), BF)],
        [tiles(tokens, TILE, first), group(DSTATE, TILE)],
        [
            pltpu.VMEM((2, SPAN, SPAN), F32), pltpu.VMEM((DSTATE, SPAN), BF),
            pltpu.VMEM((PER // 2, 2, 2 * SPAN, SPAN), BF), pltpu.VMEM((SPAN // 2, SPAN // 2), F32),
            pltpu.VMEM((2 * PER, TILE), BF),
        ],
        count, 10**9 * count, count * MIB, dict(enumerate(filled)) if filled else None,
    )


def gate_body(meta, x, mixed, gain, *refs):
    count = UNITS
    own, rest = refs[:count], refs[count : 2 * count]
    gate, normed, theirs, scale, weight, gated, total = refs[2 * count :]
    step = pl.program_id(0)
    tokens = x.shape[0]

    @pl.when(step < WIDES // 2)
    def _():
        gather_lanes(weight, own, meta, TABLE)

    @pl.when(step >= WIDES // 2)
    def _():
        gather_lanes(weight, rest, meta, TABLE + count)

    @pl.when(step == 0)
    def _():
        total[...] = jnp.zeros_like(total)

    here = own_tile(step, meta) * WIDE
    lows = [dot_nt(x[...], weight[at : at + TILE, :]).astype(BF) for at in range(0, WIDE, TILE)]
    for n, low in enumerate(lows):
        lanes = slice(n * TILE, (n + 1) * TILE)
        place = pl.ds(pl.multiple_of(here + n * TILE, TILE), TILE)
        gate[:, lanes] = low
        for at in range(0, tokens, CHUNK):
            part = low[at : at + CHUNK].astype(F32)
            part = mixed[at : at + CHUNK, lanes] * (part * sigmoid(part))
            gated[at : at + CHUNK, place] = part
            square = part * part
            total[at : at + CHUNK, :] += square[:, :LANES] + square[:, LANES:]

    @pl.when(step == pl.num_programs(0) - 1)
    def _():
        mean = jnp.sum(total[...], axis=1, keepdims=True) / DI
        scale[...] = lax.rsqrt(mean + epsilon)

        def finish(n, carry):
            place = pl.ds(pl.multiple_of(n * CHUNK, CHUNK), CHUNK)
            factor = jnp.broadcast_to(scale[place, :], (CHUNK, LANES))
            for at in range(0, DI, LANES):
                part = gated[place, at : at + LANES] * factor * gain[:, at : at + LANES]
                normed[place, at : at + LANES] = part.astype(BF)
            return carry

        lax.fori_loop(0, tokens // CHUNK, finish, 0)
        half = DI // (2 * count)
        for k in range(count):
            other = pl.multiple_of((2 * k + 1 - meta[0]) * half, LANES)
            theirs[:, k * half : (k + 1) * half] = normed[:, pl.ds(other, half)]


def gate_forward(meta, x, mixed, gain, own, rest, local):
    tokens, width = x.shape
    count = UNITS
    part = width // count
    half = WIDES // 2
    tile_spec = pl.BlockSpec((tokens, WIDE), lambda i, meta: (0, own_tile(i, meta)))
    own_spec = pl.BlockSpec((WIDE, part), lambda i, meta: (jnp.minimum(i, half - 1), 0))
    rest_spec = pl.BlockSpec((WIDE, part), lambda i, meta: (jnp.maximum(i - half, 0), 0))
    local_spec = pl.BlockSpec(
        (WIDE, part), lambda i, meta: ((1 - meta[0]) * half + jnp.maximum(i - half, 0), 0)
    )
    return call(
        gate_body, "gate_forward", meta,
        (x, mixed, gain) + tuple(own) + (() if local is None else (local,)) + tuple(rest),
        [whole((tokens, width)), tile_spec, whole((1, DI))] + [own_spec] * count
        + [rest_spec if local is None else local_spec] + [rest_spec] * (count - 1),
        [
            shape_of((tokens, DI), BF), shape_of((tokens, DI), BF), shape_of((tokens, DI // 2), BF),
            shape_of((tokens, 1)),
        ],
        [tile_spec, whole((tokens, DI)), whole((tokens, DI // 2)), whole((tokens, 1))],
        [
            pltpu.VMEM((WIDE, width), BF), pltpu.VMEM((tokens, DI), F32),
            pltpu.VMEM((tokens, LANES), F32),
        ],
        WIDES, 2 * tokens * width * DI, 28 * MIB,
    )


def out_body(meta, *refs):
    count = UNITS
    normed, pulled, hidden = refs[0:2], refs[2], refs[3]
    block, back, total, weight, branch = refs[-5:]
    refs = refs[4:-5]
    many = len(refs) // 2
    sides = refs[:many], refs[many:]
    step = pl.program_id(0)
    tokens = pulled.shape[0]
    half = DI // (2 * count)

    @pl.when(step == 0)
    def _():
        total[...] = jnp.zeros_like(total)

    for j in range(count):
        @pl.when(step == j)
        def _(j=j):
            for side, parts in enumerate(sides):
                weight[side * half : (side + 1) * half, :] = parts[j][...]

    normed_both = jnp.concatenate([normed[0][...], normed[1][...]], axis=1)
    grads = dot_nt(pulled[...], weight[...]).astype(BF)
    more = dot(normed_both, weight[...])

    @pl.when(step == 0)
    def _():
        branch[...] = more

    @pl.when((step > 0) & (step < count - 1))
    def _():
        branch[...] += more

    for side in range(2):
        at = meta[OUT_TABLE + side * count + step] * half
        back[:, pl.ds(pl.multiple_of(at, LANES), half)] = grads[:, side * half : (side + 1) * half]
    for at in range(0, tokens, CHUNK):
        sums = None
        for lane in range(0, 2 * half, LANES):
            one = grads[at : at + CHUNK, lane : lane + LANES].astype(F32)
            one = one * normed_both[at : at + CHUNK, lane : lane + LANES].astype(F32)
            sums = one if sums is None else sums + one
        total[at : at + CHUNK, :] += sums

    @pl.when(step == count - 1)
    def _():
        for at in range(0, tokens, CHUNK):
            part = branch[at : at + CHUNK, :] + more[at : at + CHUNK, :]
            part = jnp.where(live_rows(meta, at, part.shape), part, 0.0)
            block[at : at + CHUNK, :] = (hidden[at : at + CHUNK, :].astype(F32) + part).astype(BF)


def out_forward(meta, normed, pulled, hidden, own, rest, local):
    tokens, width = hidden.shape
    count = UNITS
    half = DI // (2 * count)

    def columns(side):
        return pl.BlockSpec(
            (tokens, half), lambda i, meta: (0, meta[OUT_TABLE + side * count + i])
        )

    def local_spec(side):
        return pl.BlockSpec((half, width), lambda i, meta: (meta[0] if side == 0 else 1 - meta[0], 0))

    first = () if local is None else (local,)

    def weight_specs(side):
        if local is None:
            return [whole((half, width))] * count
        return [local_spec(side)] + [whole(part.shape) for part in own]

    return call(
        out_body, "out_forward", meta,
        (normed, normed, pulled, hidden) + (first + tuple(own) + first + tuple(rest)),
        [columns(0), columns(1), whole((tokens, width)), whole((tokens, width))]
        + weight_specs(0) + weight_specs(1),
        [shape_of((tokens, width), BF), shape_of((tokens, DI), BF), shape_of((tokens, LANES))],
        [whole((tokens, width)), whole((tokens, DI)), whole((tokens, LANES))],
        [pltpu.VMEM((2 * half, width), BF), pltpu.VMEM((tokens, width), F32)],
        count, 4 * tokens * width * DI, 24 * MIB,
    )


STEPS = 4


def norm_back_body(
    meta, back, total, mixed, gate, scale, gain, grad_gate, theirs, grad_mixed, grad_gain
):
    step = pl.program_id(0)
    tokens, width = back.shape
    grad_gain[...] = jnp.zeros_like(grad_gain)

    def one(n, carry):
        rows = pl.ds(pl.multiple_of(n * CHUNK, CHUNK), CHUNK)
        r = jnp.broadcast_to(scale[rows, :], (CHUNK, LANES))
        mean = jnp.sum(total[rows, :], axis=1, keepdims=True) / DI
        factor = r * r * mean
        for at in range(0, width, LANES):
            cut = slice(at, at + LANES)
            z = gate[rows, cut].astype(F32)
            sigma = sigmoid(z)
            silu = z * sigma
            out = mixed[rows, cut]
            gated = out * silu
            grad = back[rows, cut].astype(F32) * r
            grad_gain[:, cut] += fold(grad * gated)
            grad = grad * gain[:, cut] - gated * factor
            grad_mixed[rows, cut] = (grad * silu).astype(BF)
            grad_gate[rows, cut] = ((grad * out) * (sigma + silu * (1.0 - sigma))).astype(BF)
        return carry

    lax.fori_loop(0, tokens // CHUNK, one, 0)

    @pl.when(step // (STEPS // 2) == 1 - meta[0])
    def _():
        theirs[...] = grad_gate[...]


def norm_back(meta, back, total, mixed, gate, scale, gain):
    tokens = back.shape[0]
    width = DI // STEPS

    def tile(rows):
        return pl.BlockSpec((rows, width), lambda i, meta: (0, i))

    theirs_spec = pl.BlockSpec(
        (tokens, width),
        lambda i, meta: (0, jnp.clip(i - (1 - meta[0]) * (STEPS // 2), 0, STEPS // 2 - 1)),
    )
    return call(
        norm_back_body, "norm_back", meta, (back, total, mixed, gate, scale, gain),
        [tile(tokens), whole((tokens, LANES)), tile(tokens), tile(tokens), whole((tokens, 1)), tile(1)],
        [
            shape_of((tokens, DI), BF), shape_of((tokens, DI // 2), BF), shape_of((tokens, DI), BF),
            shape_of((8, DI)),
        ],
        [tile(tokens), theirs_spec, tile(tokens), tile(8)],
        [], STEPS, 10**9, 24 * MIB,
    )


def rows_product_body(meta, mine, theirs, pulled, pulled_rest, send, keep):
    total = dot_tn(mine[...], pulled[...]) + dot_tn(theirs[...], pulled_rest[...])
    total = total.astype(BF)
    sent = pl.num_programs(0) // 2

    @pl.when(pl.program_id(0) < sent)
    def _():
        send[0] = total

    @pl.when(pl.program_id(0) >= sent)
    def _():
        keep[0] = total


def rows_product(meta, normed, arrived, arrived_at, pulled, pulled_rest, units):
    tokens, width = pulled.shape
    unit = DI // (2 * UNITS)
    upper = units // 2

    def which(i):
        return lax.rem(i + upper, units)

    result = shape_of((upper, unit, width), BF)
    return call(
        rows_product_body, "rows_product", meta, (normed, arrived, pulled, pulled_rest),
        [
            pl.BlockSpec((tokens, unit), lambda i, meta: (0, meta[OUT_TABLE + which(i)])),
            pl.BlockSpec((tokens, unit), lambda i, meta: (0, meta[arrived_at + which(i)])),
            whole((tokens, width)), whole((tokens, width)),
        ],
        [result, result],
        [
            pl.BlockSpec((1, unit, width), lambda i, meta: (jnp.minimum(i, upper - 1), 0, 0)),
            pl.BlockSpec((1, unit, width), lambda i, meta: (jnp.maximum(i - upper, 0), 0, 0)),
        ],
        [], units, 4 * tokens * width * unit * units, 12 * MIB,
    )


def columns_product_body(plan, meta, *refs):
    parts = len(plan)
    mine, theirs = refs[:parts], refs[parts : 2 * parts]
    here, there, send, keep, right, right_rest = refs[2 * parts :]
    step = pl.program_id(0)
    width = here.shape[1] // UNITS

    @pl.when(step == 0)
    def _():
        for j in range(UNITS):
            lanes = pl.ds(pl.multiple_of(meta[TABLE + j] * width, LANES), width)
            right[:, j * width : (j + 1) * width] = here[:, lanes]
            right_rest[:, j * width : (j + 1) * width] = there[:, lanes]

    for (begin, steps), a, b in zip(plan, mine, theirs):
        @pl.when((step >= begin) & (step < begin + steps))
        def _(a=a, b=b):
            total = (dot_tn(a[...], right[...]) + dot_tn(b[...], right_rest[...])).astype(BF)
            for k in range(UNITS // 2):
                keep[k] = total[:, k * width : (k + 1) * width]
                other = UNITS // 2 + k
                send[k] = total[:, other * width : (other + 1) * width]


def columns_product(meta, parts, normed, normed_rest):
    tokens, width = normed.shape
    part = width // UNITS
    plan, step, mine_specs, theirs_specs = [], 0, [], []

    def spec(begin, steps, start):
        return pl.BlockSpec(
            (tokens, TILE), lambda i, meta: (0, start(meta) + jnp.clip(i - begin, 0, steps - 1))
        )

    for matrix, start, steps, arrived in parts:
        plan.append((step, steps))
        mine_specs.append(spec(step, steps, start))
        theirs_specs.append(spec(step, steps, lambda meta: 0))
        step += steps
    result = shape_of((UNITS // 2, step * TILE, part), BF)
    result_spec = pl.BlockSpec((UNITS // 2, TILE, part), lambda i, meta: (0, i, 0))
    return call(
        functools.partial(columns_product_body, tuple(plan)), "columns_product", meta,
        tuple(p[0] for p in parts) + tuple(p[3] for p in parts) + (normed, normed_rest),
        mine_specs + theirs_specs + [whole((tokens, width))] * 2,
        [result, result], [result_spec, result_spec],
        [pltpu.VMEM((tokens, width), BF), pltpu.VMEM((tokens, width), BF)],
        step, 1, 1,
    )


def conv_back(meta, masked, taps, result, sums, live, grad_conv):
    tokens = masked.shape[0]
    grad_conv[:, tokens:, :] = jnp.zeros((TILE // LANES, 8, LANES), F32)
    sums[...] = jnp.zeros_like(sums)
    for lane in range(0, TILE, LANES):
        cut = slice(lane, lane + LANES)
        totals = [jnp.zeros((8, LANES), F32) for _ in range(CONV + 1)]
        for at in range(0, tokens, CHUNK):
            near = [
                grad_conv[lane // LANES, at + 3 - k : at + 3 - k + CHUNK, :] for k in range(CONV)
            ]
            value = masked[at : at + CHUNK, cut].astype(F32)
            out = near[0] * taps[0:1, cut]
            for k in range(1, CONV):
                out = out + near[k] * taps[k : k + 1, cut]
            result[at : at + CHUNK, cut] = (out * live[at : at + CHUNK, :]).astype(BF)
            for k in range(CONV):
                totals[k] = totals[k] + fold(near[k] * value)
            totals[CONV] = totals[CONV] + fold(near[CONV - 1])
        for k in range(CONV + 1):
            sums[k : k + 1, cut] = jnp.sum(totals[k], axis=0, keepdims=True)


def fold(value):
    return jnp.sum(value.reshape(value.shape[0] // 8, 8, value.shape[1]), axis=0)


def scan_back_body(
    meta, content, keys, grad_out, mixed, entering, columns, rows, skip, masked, slope, taps,
    scores_in, write_in, read_in,
    result, theirs, sums, grad_columns, grad_scores, grad_write, grad_read,
    scores, read_rows, live, grad_conv, mixes, mix_grads, blocked, spread,
):
    half = SPAN // 2

    @pl.when(pl.program_id(0) == 0)
    def _():
        for span in range(2):
            at = span * SPAN
            scores[span] = dot_nt(keys[at : at + SPAN, :DSTATE], keys[at : at + SPAN, DSTATE:])
        read_rows[...] = keys[SPAN:, DSTATE:].astype(F32).T.astype(BF)
        grad_scores[...] = scores_in[...]
        grad_write[...] = write_in[...]
        grad_read[...] = read_in[...]
        mixes[...] = jnp.zeros_like(mixes)
        live_lanes(meta, live)
        after = row_ids(0, blocked.shape) <= lax.broadcasted_iota(jnp.int32, blocked.shape, 1)
        blocked[...] = jnp.where(after, 0.0, FAR)
        spread[...] = head_lanes(spread.shape, HEADDIM)

    def heads_sum(value):
        high = value.astype(BF)
        low = (value - high.astype(F32)).astype(BF)
        return dot_nt(high, spread[...]) + dot_nt(low, spread[...])

    for pair in range(PER // 2):
        lanes = slice(pair * 2 * HEADDIM, (pair + 1) * 2 * HEADDIM)
        ones = spread[2 * pair : 2 * pair + 2, lanes]
        for span in range(2):
            cut = slice(span * SPAN, (span + 1) * SPAN)
            mix_grads[pair, span] = dot_nt(heads_apart(content[cut, lanes], ones), grad_out[cut, lanes])

    factor = dot(columns[0, :, 2 * PER :].astype(BF), spread[...])
    grown = (grad_out[SPAN:, :].astype(F32) * factor[SPAN:]).astype(BF)
    grad_state = dot(read_rows[...], grown).astype(BF)
    grad_read[...] += dot_nt(grown, entering[0])
    worth = (content[0:SPAN, :].astype(F32) * factor[:SPAN]).astype(BF)
    grad_write[...] += dot_nt(worth, grad_state)
    from_state = dot(keys[0:SPAN, :DSTATE], grad_state) * factor[:SPAN]

    for pair in range(PER // 2):
        for h in range(2):
            n = 2 * pair + h
            for span in range(2):
                top = span * SPAN
                for at in range(0, SPAN, CHUNK):
                    less = columns[0, top + at : top + at + CHUNK, PER + n : PER + n + 1]
                    corner = at // half * half
                    for begin in range(corner, SPAN, half):
                        cut = slice(begin, begin + half)
                        decay = rows[0, n : n + 1, top + begin : top + begin + half] - less
                        if begin == corner:
                            decay = decay + blocked[at - begin : at - begin + CHUNK, :]
                        decay = jnp.exp2(decay)
                        row = h * SPAN + at
                        mix = scores[span, at : at + CHUNK, cut] * decay
                        mixes[pair, span, row : row + CHUNK, cut] = mix.astype(BF)
                        change = mix_grads[pair, span, row : row + CHUNK, cut] * decay
                        grad_scores[span, at : at + CHUNK, cut] += change

    lane = lax.broadcasted_iota(jnp.int32, (SPAN, 2 * PER), 1) < PER
    final = row_ids(0, lane.shape) == SPAN - 1
    skips = jnp.zeros((8, TILE), F32)
    for span in range(2):
        cut = slice(span * SPAN, (span + 1) * SPAN)
        value = content[cut, :].astype(F32)
        pull = grad_out[cut, :].astype(F32)
        both = []
        for pair in range(PER // 2):
            lanes = slice(pair * 2 * HEADDIM, (pair + 1) * 2 * HEADDIM)
            both.append(heads_together(dot(mixes[pair, span], grad_out[cut, lanes])))
        both = jnp.concatenate(both, axis=1)
        if span == 0:
            ended = jnp.sum(fold(value * from_state), axis=0, keepdims=True)
            both = both + from_state
        skipped = skip[...] * value
        skips = skips + fold(pull * value)
        written = heads_sum(value * both)
        read = heads_sum(pull * (mixed[cut, :] - skipped))
        if span == 0:
            ended = heads_sum(jnp.broadcast_to(ended, (8, TILE)))[0:1]
            read = read + jnp.where(final, ended, 0.0)
        grad_columns[0, cut, :] = jnp.where(lane, written, read)
        both = (both + skip[...] * pull) * slope[cut, :]
        for k in range(TILE // LANES):
            grad_conv[k, cut, :] = both[:, k * LANES : (k + 1) * LANES]

    conv_back(meta, masked, taps, result, sums, live, grad_conv)
    sums[5:6, :] = jnp.sum(skips, axis=0, keepdims=True)
    half_steps = pl.num_programs(0) // 2
    at_half = pl.program_id(0) // half_steps

    @pl.when(at_half == 1 - meta[0])
    def _():
        theirs[...] = result[...]


def scan_backward(
    meta, signal, keys, grad_out, mixed, entering, columns, rows, skip, masked, slope, taps, kept,
    first, count,
):
    tokens = signal.shape[0]

    def group(*shape):
        return pl.BlockSpec((1,) + shape, lambda i, meta: (i + first, 0, 0))

    def fresh(*shape):
        return pl.BlockSpec((1,) + shape, lambda i, meta: (i, 0, 0))

    kept_specs = [whole((2, SPAN, SPAN)), whole((SPAN, DSTATE)), whole((SPAN, DSTATE))]
    return call(
        scan_back_body, "scan_backward", meta,
        (signal, keys, grad_out, mixed, entering, columns, rows, skip, masked, slope, taps)
        + tuple(kept),
        [
            tiles(tokens, TILE, first), whole((tokens, TILE)),
            tiles(tokens, TILE, first), tiles(tokens, TILE, first), group(DSTATE, TILE),
            group(tokens, PACK),
            group(2 * PER, tokens), tiles(1, TILE, first), tiles(tokens, TILE, first),
            tiles(tokens, TILE, first), tiles(8, TILE, first),
        ]
        + kept_specs,
        [
            shape_of((tokens, count * TILE), BF), shape_of((tokens, count // 2 * TILE), BF),
            shape_of((8, count * TILE)),
            shape_of((count, tokens, 2 * PER)),
            shape_of((2, SPAN, SPAN)), shape_of((SPAN, DSTATE)), shape_of((SPAN, DSTATE)),
        ],
        [
            tiles(tokens, TILE),
            pl.BlockSpec(
                (tokens, TILE),
                lambda i, meta: (0, jnp.clip(i - (1 - meta[0]) * (count // 2), 0, count // 2 - 1)),
            ),
            tiles(8, TILE), fresh(tokens, 2 * PER),
        ]
        + kept_specs,
        [
            pltpu.VMEM((2, SPAN, SPAN), F32), pltpu.VMEM((DSTATE, SPAN), BF),
            pltpu.VMEM((tokens, LANES), F32), pltpu.VMEM((TILE // LANES, tokens + 8, LANES), F32),
            pltpu.VMEM((PER // 2, 2, 2 * SPAN, SPAN), BF),
            pltpu.VMEM((PER // 2, 2, 2 * SPAN, SPAN), F32),
            pltpu.VMEM((SPAN // 2, SPAN // 2), F32), pltpu.VMEM((2 * PER, TILE), BF),
        ],
        count, 3 * 10**9 * count, count * MIB,
    )


def tail_body(parts, meta, *refs):
    keys, masked, slope, taps, trio, steps, grad_scores, grad_write, grad_read = refs[:9]
    grad_columns = refs[9 : 9 + parts]
    result, sums, raw, small, packs, live, grad_conv = refs[9 + parts :]
    tokens = keys.shape[0]
    for span in range(2):
        at = span * SPAN
        write = keys[at : at + SPAN, :DSTATE]
        read = keys[at : at + SPAN, DSTATE:]
        to_write = fine_dot(grad_scores[span], read, dot)
        to_read = fine_dot(grad_scores[span], write, dot_tn)
        if span == 0:
            to_write = to_write + grad_write[...]
        else:
            to_read = to_read + grad_read[...]
        cut = slice(at, at + SPAN)
        grad_conv[0, cut, :] = to_write * slope[cut, :DSTATE]
        grad_conv[1, cut, :] = to_read * slope[cut, DSTATE:]
    live_lanes(meta, live)
    conv_back(meta, masked, taps, result, sums, live, grad_conv)

    blank = jnp.zeros((tokens, LANES - HEADS), F32)
    of_step, of_log = [], []
    for column_ref in grad_columns:
        for g in range(column_ref.shape[0]):
            of_step.append(column_ref[g, :, :PER])
            of_log.append(column_ref[g, :, PER:])
    grad_size = jnp.concatenate(of_step + [blank], axis=1)
    grad_log = jnp.concatenate(of_log + [blank], axis=1) - grad_size
    upper = row_ids(0, (SPAN, SPAN)) <= lax.broadcasted_iota(jnp.int32, (SPAN, SPAN), 1)
    upper = jnp.where(upper, 1.0, 0.0).astype(BF)
    rates = []
    for at in range(0, tokens, SPAN):
        high, middle, low = pieces(grad_log[at : at + SPAN])
        rates.append(dot(upper, high) + (dot(upper, middle) + dot(upper, low)))
    grad_rate = jnp.concatenate(rates, axis=0)
    decay_rate = steps[1:2, :]
    sigma = jax.nn.sigmoid(trio[0])
    size = trio[1]
    tiny = size > 0.0
    share = jnp.where(tiny, sigma / jnp.where(tiny, size, 1.0), 1.0)
    grad_raw = grad_size * share + grad_rate * decay_rate * sigma
    raw[...] = grad_raw.astype(BF)
    small[...] = jnp.zeros_like(small)
    small[0:1, :] = jnp.sum(grad_raw, axis=0, keepdims=True)
    small[1:2, :] = jnp.sum(grad_rate * trio[1], axis=0, keepdims=True) * decay_rate
    for side in range(2):
        at = meta[0] if side == 0 else 1 - meta[0]
        packs[side, :, :LANES] = result[:, pl.ds(pl.multiple_of(at * LANES, LANES), LANES)]
        packs[side, :, LANES:] = raw[...]


def tail_backward(meta, keys, masked, slope, taps, trio, steps, kept, grad_columns):
    tokens = keys.shape[0]
    last = DI // TILE
    key_spec = whole((tokens, TILE))
    return call(
        functools.partial(tail_body, len(grad_columns)), "tail_backward", meta,
        (keys, masked, slope, taps, trio, steps) + tuple(kept) + tuple(grad_columns),
        [
            key_spec, key_spec, key_spec, pl.BlockSpec((8, TILE), lambda i, meta: (0, last)),
            whole((3, tokens, LANES)), whole((8, LANES)), whole((2, SPAN, SPAN)),
            whole((SPAN, DSTATE)), whole((SPAN, DSTATE)),
        ]
        + [whole(part.shape) for part in grad_columns],
        [
            shape_of((tokens, TILE), BF), shape_of((8, TILE)), shape_of((tokens, LANES), BF),
            shape_of((8, LANES)), shape_of((2, tokens, TILE), BF),
        ],
        [
            whole((tokens, TILE)), whole((8, TILE)), whole((tokens, LANES)), whole((8, LANES)),
            whole((2, tokens, TILE)),
        ],
        [pltpu.VMEM((tokens, LANES), F32), pltpu.VMEM((TILE // LANES, tokens + 8, LANES), F32)],
        1, 1, 1,
    )


def input_body(plan, first, last, meta, *refs):
    count = UNITS
    grads = refs[: len(plan)]
    refs = refs[len(plan) :]
    if not first:
        start, refs = refs[0], refs[1:]
    blocks = []
    for begin, steps, half in plan:
        own, refs = refs[:count], refs[count:]
        rest = None
        if half is not None:
            rest, refs = refs[:count], refs[count:]
        blocks.append((own, rest))
    step = pl.program_id(0)

    if last:
        hidden, out_grad, scale, gain, result, weight, weight_dt, total = refs
    else:
        total, weight = refs

    @pl.when(step == 0)
    def _():
        total[...] = jnp.zeros_like(total) if first else start[...]

    for n, (begin, steps, half) in enumerate(plan):
        @pl.when((step >= begin) & (step < begin + steps))
        def _(n=n, half=half):
            own, rest = blocks[n]
            rows = own[0].shape[0]
            if grads[n].shape[1] == LANES:
                weight_dt[...] = jnp.zeros_like(weight_dt)
                gather_lanes(weight_dt, own, meta, TABLE)
                total[...] += dot(grads[n][...], weight_dt[...])
                return
            if half is None:
                gather_lanes(weight, own, meta, TABLE)
            else:
                @pl.when(meta[0] == half)
                def _():
                    gather_lanes(weight, own, meta, TABLE)

                @pl.when(meta[0] != half)
                def _():
                    gather_lanes(weight, rest, meta, TABLE + count)

            total[...] += dot(grads[n][...], weight[0:rows, :])

    if not last:
        return

    @pl.when(step == pl.num_programs(0) - 1)
    def _():
        tokens, width = hidden.shape
        def finish(n, carry):
            rows = pl.ds(pl.multiple_of(n * 32, 32), 32)
            r = jnp.broadcast_to(scale[rows, :], (32, LANES))
            sums = jnp.zeros((32, LANES), F32)
            for at in range(0, width, LANES):
                cut = slice(at, at + LANES)
                both = total[rows, cut] * hidden[rows, cut].astype(F32)
                sums = sums + both * gain[:, cut]
            mean = jnp.sum(sums, axis=1, keepdims=True) / width
            factor = r * r * r * mean
            for at in range(0, width, LANES):
                cut = slice(at, at + LANES)
                value = r * (total[rows, cut] * gain[:, cut]) - hidden[rows, cut].astype(F32) * factor
                result[rows, cut] = value + out_grad[rows, cut].astype(F32)
            return carry

        lax.fori_loop(0, tokens // 32, finish, 0)


def input_backward(meta, start, parts, tokens, width, last=None):
    part = width // UNITS
    plan, step, grad_specs, block_specs, grads, blocks = [], 0, [], [], [], []

    def grad_spec(columns, begin, steps, first):
        return pl.BlockSpec(
            (tokens, columns), lambda i, meta: (0, first + jnp.clip(i - begin, 0, steps - 1))
        )

    def row_spec(rows, begin, steps, first, when):
        def index(i, meta):
            at = first + jnp.clip(i - begin, 0, steps - 1)
            return (at if when is None else jnp.where(when(meta), at, first), 0)

        return pl.BlockSpec((rows, part), index)

    def is_half(half):
        return lambda meta: meta[0] == half

    def not_half(half):
        return lambda meta: meta[0] != half

    for grad, grad_first, steps, half, own, own_first, rest, rest_first, local_first in parts:
        columns = WIDE if half is not None else grad.shape[1]
        if half is not None and steps == WIDES // 2:
            columns, steps = steps * WIDE, 1
            grad_first, local_first = (at // (WIDES // 2) for at in (grad_first, local_first))
        row_tile = 64 if columns == LANES else columns
        plan.append((step, steps, half))
        grads.append(grad)
        grad_specs.append(grad_spec(columns, step, steps, grad_first))
        when = None if half is None else is_half(half)
        for matrix in own:
            blocks.append(matrix)
            block_specs.append(row_spec(row_tile, step, steps, own_first, when))
        if half is not None:
            for j, matrix in enumerate(rest):
                blocks.append(matrix)
                row = local_first if j == 0 else rest_first
                block_specs.append(row_spec(row_tile, step, steps, row, not_half(half)))
        step += steps
    more, more_specs = (), []
    outs, out_specs = [shape_of((tokens, width))], [whole((tokens, width))]
    scratch = [pltpu.VMEM((WIDES // 2 * WIDE, width), BF)]
    if last is not None:
        more = tuple(last)
        more_specs = [whole((tokens, width))] * 2 + [whole((tokens, 1)), whole((1, width))]
        scratch += [
            pltpu.VMEM((LANES, width), BF), pltpu.VMEM((tokens, width), F32),
        ]
    first = start is None
    return call(
        functools.partial(input_body, tuple(plan), first, last is not None),
        "input_backward", meta,
        tuple(grads) + (() if first else (start,)) + tuple(blocks) + more,
        grad_specs + ([] if first else [whole((tokens, width))]) + block_specs + more_specs,
        outs, out_specs, scratch,
        step, 10**11 if last is not None else 10**10 if first else 1, 20 * MIB if first else 1,
    )


def place_body(halves, last, meta, own, other, weight, out, sums):
    step = pl.program_id(0)

    @pl.when(step == 0)
    def _():
        sums[...] = jnp.zeros_like(sums)

    def copy(source, row, rows, at, counted):
        for k in range(0, rows, LANES):
            part = source[row + k : row + k + LANES, :].astype(F32)
            out[at + k : at + k + LANES, :] = part
            some = min(counted, LANES)
            part = part[:some] * weight[at + k : at + k + some, :].astype(F32)
            sums[...] += fold(part)

    def put(which, row, rows, at, counted=LANES):
        @pl.when(meta[0] == which)
        def _():
            copy(own, row, rows, at, counted)

        @pl.when(meta[0] != which)
        def _():
            copy(other, row, rows, at, counted)

    for half in range(2):
        @pl.when(step == half)
        def _(half=half):
            put(half, 0, halves, 0)

    if last:
        @pl.when(step == 2)
        def _():
            put(0, halves, LANES, 0)
            put(1, halves, LANES, LANES)
            put(0, halves + LANES, LANES, 2 * LANES, HEADS)


def place_rows(meta, own, other, weight, halves, first, filled, last):
    length, width = own.shape
    rows = pl.BlockSpec((halves, width), lambda i, meta: (first + i, 0))
    return call(
        functools.partial(place_body, halves, last), "place_rows", meta, (own, other, weight),
        [whole((length, width)), whole((length, width)), rows],
        [shape_of(weight.shape), shape_of((8, width))],
        [rows, whole((8, width))],
        [], 3 if last else 2, 10**10, 20 * MIB, None if filled is None else {0: filled},
    )


NEAR = 8


def mirrored(j, count):
    if count != 4:
        return j
    result, bit, other = 0, 1, count // 2
    while bit < count:
        if j & bit:
            result |= other
        bit, other = bit * 2, other // 2
    return result


def hop(x, bit):
    reps, count = lax.axis_size("rep"), lax.axis_size("shard")
    pairs = []
    for r in range(reps):
        flip = bit if r % 2 == 0 else mirrored(bit, count)
        pairs += [(r * count + s, r * count + (s ^ flip)) for s in range(count)]
    return lax.ppermute(x, ("rep", "shard"), pairs)


def swap(x):
    return lax.ppermute(x, "rep", [(r, r ^ 1) for r in range(lax.axis_size("rep"))])


def across(x, bit):
    return lax.ppermute(x, "shard", [(s, s ^ bit) for s in range(lax.axis_size("shard"))])


def along(x, pairs):
    return lax.ppermute(x, "rep", [(2 * a + k, 2 * b + k) for a, b in pairs for k in range(2)])


def settle(keep, arrived):
    middle = keep.shape[0] // 2
    if middle == 0:
        return None, keep.astype(F32) + arrived.astype(F32)
    held = (keep.astype(F32) + arrived.astype(F32)).astype(BF)
    return held[middle:], held[:middle]


def finish_stages(send, keep):
    while send is not None:
        send, keep = settle(keep, hop(send, send.shape[0]))
    return keep[0]


def inward(held):
    if lax.axis_size("rep") // 2 != 4:
        return held, None
    return held, along(held.astype(BF), [(0, 1), (3, 2)])


def middle(state):
    held, arrived = state
    if arrived is None:
        return held, None
    inner = (held + arrived.astype(F32)).astype(BF)
    return inner, along(inner, [(1, 2), (2, 1)])


def outward(state):
    inner, arrived = state
    if arrived is None:
        chips = lax.axis_size("rep") // 2
        total, bit = inner.astype(BF), 1
        while bit < chips:
            more = along(total, [(k, k ^ bit) for k in range(chips)])
            total = (total.astype(F32) + more.astype(F32)).astype(BF)
            bit *= 2
        return total, None
    total = (inner.astype(F32) + arrived.astype(F32)).astype(BF)
    return total, along(total, [(1, 0), (2, 3)])


def summed(state):
    total, arrived = state
    if arrived is None:
        return total
    place = lax.axis_index("rep") // 2
    return jnp.where((place == 1) | (place == 2), total, arrived)


def in_order(own, other, core):
    return [jnp.where(core == 0, own, other), jnp.where(core == 0, other, own)]


def hold(values):
    leaves, tree = jax.tree.flatten(values)
    return jax.tree.unflatten(tree, lax.optimization_barrier(tuple(leaves)))


def add_up(rows):
    while len(rows) > 1:
        rows = [a + b for a, b in zip(rows[::2], rows[1::2])]
    return rows[0]


def group_rows(vector, shard, count):
    rows = [lax.dynamic_slice_in_dim(vector, shard ^ j, 1, 0) for j in range(count)]
    return rows[:1] + [across(row, j) for j, row in enumerate(rows) if j]


def chips_sum(row):
    chips = lax.axis_size("rep") // 2
    return add_up(
        [row] + [along(row, [(k, k ^ d) for k in range(chips)]) for d in range(1, chips)]
    )


def join_lanes(blocks, shard):
    return [
        jnp.concatenate(in_order(blocks[j], blocks[j + 1], shard % 2), axis=1)
        for j in range(0, len(blocks), 2)
    ]


def split_lanes(units, shard):
    half = units.shape[2] // 2
    pairs = in_order(units[:, :, :half], units[:, :, half:], shard % 2)
    return jnp.stack(pairs, axis=1).reshape(2 * units.shape[0], units.shape[1], half)


def pad_lanes(matrix):
    return jnp.pad(matrix, ((0, 0), (0, LANES - matrix.shape[1])))


def shards(
    hidden,
    out_grad,
    norm_gain,
    in_w,
    conv_w,
    conv_b,
    dt_bias,
    a_log,
    skip,
    out_gain,
    out_w,
    lengths,
    offsets,
):
    core = lax.axis_index("rep") % 2
    shard = lax.axis_index("shard")
    count = lax.axis_size("shard")
    tokens, width = hidden.shape
    bits = []
    while 2 ** len(bits) < count:
        bits.append(2 ** len(bits))

    local = in_w.T
    half = DI // 2
    piece = jnp.concatenate(
        [
            lax.dynamic_slice_in_dim(local, DI + core * half, half, 0),
            local[2 * DI :],
            jnp.zeros((16, local.shape[1]), BF),
        ],
        axis=0,
    )
    gate_piece = lax.dynamic_slice_in_dim(local, core * half, half, 0)
    out_piece = lax.dynamic_slice_in_dim(out_w, core * (out_w.shape[0] // 2), out_w.shape[0] // 2, 0)

    def spread(first):
        blocks = [first]
        for bit in bits:
            blocks = blocks + [hop(block, bit) for block in blocks]
        return blocks

    paired = count == 4
    small = (norm_gain, conv_w.T, conv_b, dt_bias, a_log, skip, out_gain)
    packed = jnp.concatenate([part.reshape(-1) for part in small])
    everyone = [packed] + [
        lax.ppermute(
            packed, ("rep", "shard"),
            [
                (r * count + s, r * count + (s ^ (j if r % 2 == 0 else mirrored(j, count))))
                for r in range(lax.axis_size("rep"))
                for s in range(count)
            ],
        )
        for j in range(1, count)
    ]
    everyone = jnp.stack(everyone).astype(F32)
    order = [jnp.where(core == 0, j, mirrored(j, count)) for j in range(count)]
    whose = jnp.stack(order)[jnp.arange(count) ^ shard]
    same = (whose[:, None] == jnp.arange(count)[None]).astype(F32)
    everyone = jnp.sum(same[:, :, None] * everyone[None], axis=1)
    parts, start = [], 0
    for part in small:
        cut = everyone[:, start : start + part.size].reshape((count,) + part.shape)
        cut = jnp.moveaxis(cut, 0, -2)
        parts.append(cut.reshape(part.shape[:-1] + (-1,)))
        start += part.size
    conv_own = spread(piece)
    gate_piece, conv_own = hold((gate_piece, conv_own))
    if paired:
        conv_rest = [swap(block) for block in conv_own[1:]]
        gate_near = hop(gate_piece, 1), hop(gate_piece, 2)
        out_local, in_local = out_w, local
    else:
        gate_own = spread(gate_piece)
        out_piece, gate_own = hold((out_piece, gate_own))
        out_own = spread(out_piece)
        conv_rest = rest_conv = join_lanes([swap(block) for block in conv_own], shard)
        gate_rest = rest_gate = join_lanes([swap(block) for block in gate_own], shard)
        conv_own, gate_own = join_lanes(conv_own, shard), join_lanes(gate_own, shard)
        out_full = [jnp.concatenate(in_order(block, swap(block), core), axis=0) for block in out_own]
        out_one, out_two = out_full[:UNITS], out_full[UNITS:]
        out_local = in_local = None

    gain_one, kernel, bias_conv, bias_step, log_rate, skip_full, gain_two = parts
    decay_rate = -jnp.exp(log_rate)

    mine = order
    other = [jnp.where(core == 0, mirrored(j, count), j) for j in range(count)]
    mine, other = [shard ^ j for j in mine], [shard ^ j for j in other]
    if paired:
        out_units = [2 * j + core for j in mine] + [2 * j + 1 - core for j in other]
    else:
        out_units = mine
        mine = other = [j // 2 for j in mine[::2]]
    meta = jnp.stack(
        [core, offsets[0], lengths[0], shard] + mine + other + out_units
    ).astype(jnp.int32)
    taps = jnp.concatenate([kernel, bias_conv[None], jnp.zeros((3, CC), F32)], axis=0)
    steps = jnp.concatenate(
        [pad_lanes(jnp.stack([bias_step, decay_rate])), jnp.zeros((6, LANES), F32)], axis=0
    )
    skip_lanes = jnp.repeat(skip_full, HEADDIM)[None]

    positions = jnp.arange(tokens, dtype=jnp.int32)
    live_mask = ((positions >= offsets[0]) & (positions < offsets[0] + lengths[0])).astype(F32)
    hidden_full = hidden.astype(F32)
    inv_rms = lax.rsqrt(jnp.mean(hidden_full * hidden_full, axis=1, keepdims=True) + epsilon)
    normed = (hidden_full * inv_rms * gain_one).astype(BF)
    pulled = (out_grad.astype(F32) * live_mask[:, None]).astype(BF)
    normed_rest = swap(normed)
    pulled_rest = swap(pulled)

    (masked, signal, slope, masked_keys, keys, slope_keys, columns, rows, trio) = conv_forward(
        meta, normed, taps, steps, conv_own, conv_rest, in_local
    )
    if paired:
        gate_near, signal = hold((gate_near, signal))
        gate_own = [gate_piece, *gate_near, hop(gate_near[0], 2)]
    kept = None
    for first in range(0, GROUPS, GROUPS // 2):
        kept = scan_forward(
            meta, signal, keys, columns, rows, skip_lanes, first, GROUPS // 2, kept
        )
        if paired and first == 0:
            gate_far, out_piece, kept = hold((gate_own[3], out_piece, kept))
            gate_own[3] = gate_far
            gate_rest = [swap(block) for block in gate_own[1:]]
            out_near = hop(out_piece, 1), hop(out_piece, 2)
    mixed, entering = kept
    if paired:
        rest_conv, rest_gate = [local] + conv_rest, [local] + gate_rest
    gate, normed_out, out_theirs, scale = gate_forward(
        meta, normed, mixed, gain_two[None], gate_own, gate_rest, in_local
    )
    out_arrived = swap(out_theirs if paired else normed_out)
    if paired:
        out_near, normed_out = hold((out_near, normed_out))
        out_one = [*out_near, hop(out_near[0], 2)]
        out_two = [swap(block) for block in out_one]

    upper = count // 2
    out_pulls = (pulled, pulled_rest)
    if not paired:
        cut = core * (width // 2)
        out_pulls = [lax.dynamic_slice_in_dim(x, cut, width // 2, 1) for x in out_pulls]

    def product(parts):
        send, keep = columns_product(meta, parts, normed, normed_rest)
        return (send, keep) if paired else (split_lanes(send, shard), split_lanes(keep, shard))

    out_send, out_keep = rows_product(
        meta, normed_out, out_arrived, TABLE if paired else OUT_TABLE, *out_pulls, count
    )
    out_send, out_keep, normed_out = hold((out_send, out_keep, normed_out))
    out_there = hop(out_send, upper)
    block_out, back, total = out_forward(
        meta, normed_out, pulled, hidden, out_one, out_two, out_local
    )
    out_there, total = hold((out_there, total))
    out_send, out_keep = settle(out_keep, out_there)
    out_there = hop(out_send, upper // 2)
    out_keep, total = hold((out_keep, total))
    grad_gate, gate_theirs, grad_mixed, grad_gain_two = norm_back(
        meta, back, total, mixed, gate, scale, gain_two[None]
    )

    gate_theirs, out_there = hold((gate_theirs, out_there))
    gate_arrived = swap(gate_theirs)
    out_line = inward(finish_stages(*settle(out_keep, out_there)))
    out_held, gate_arrived = hold((out_line[0], gate_arrived))
    gate_parts = [(grad_gate, lambda meta: meta[0] * (GROUPS // 2), GROUPS // 2, gate_arrived)]
    gate_send, gate_keep = product(gate_parts)
    gate_send, gate_keep, grad_mixed = hold((gate_send, gate_keep, grad_mixed))
    gate_there = hop(gate_send, upper)
    kept = (
        jnp.zeros((2, SPAN, SPAN), F32),
        jnp.zeros((SPAN, DSTATE), F32),
        jnp.zeros((SPAN, DSTATE), F32),
    )
    near, far = NEAR, GROUPS - NEAR
    part = WIDES // 2
    over = near * TILE // WIDE - part

    def gate_part(half):
        at = half * part
        return [(grad_gate, at, part, half, gate_own, 0, rest_gate, 0, at if paired else 0)]

    def conv_part(grad, grad_first, steps, half, first):
        local_first = WIDES + half * part + first if paired else first
        return [(grad, grad_first, steps, half, conv_own, first, rest_conv, first, local_first)]

    grad_near, near_theirs, sums_near, columns_near, *kept = scan_backward(
        meta, signal, keys, grad_mixed, mixed, entering, columns, rows, skip_lanes, masked, slope, taps,
        kept, 0, near,
    )
    gate_there, near_theirs, out_arrived = hold((gate_there, near_theirs, out_line[1]))
    near_arrived = swap(near_theirs)
    gate_send, gate_keep = settle(gate_keep, gate_there)
    gate_there = hop(gate_send, upper // 2)
    gate_keep, out_arrived = hold((gate_keep, out_arrived))
    out_line = middle((out_held, out_arrived))
    near_arrived, gate_keep, out_inner = hold((near_arrived, gate_keep, out_line[0]))
    near_parts = [(grad_near, lambda meta: meta[0] * (near // 2), near // 2, near_arrived)]
    near_send, near_keep = product(near_parts)
    near_there = hop(near_send, upper)
    near_keep, kept, grad_mixed = hold((near_keep, kept, grad_mixed))
    grad_far, far_theirs, sums_far, columns_far, *kept = scan_backward(
        meta, signal, keys, grad_mixed, mixed, entering, columns, rows, skip_lanes, masked, slope, taps,
        kept, near, far,
    )
    far_theirs, gate_there = hold((far_theirs, gate_there))
    far_arrived = swap(far_theirs)
    gate_line = inward(finish_stages(*settle(gate_keep, gate_there)))
    gate_held, kept = hold((gate_line[0], kept))
    grad_keys, sums_keys, grad_raw, grad_steps, packs = tail_backward(
        meta, keys, masked_keys, slope_keys, taps, trio, steps, kept, (columns_near, columns_far),
    )
    packs, near_there = hold((packs, near_there))
    packs_arrived = swap(packs[1])
    near_send, near_keep = settle(near_keep, near_there)
    near_there = hop(near_send, upper // 2)
    packs, packs_arrived, near_keep = hold((packs, packs_arrived, near_keep))
    far_parts = [
        (grad_far, lambda meta: meta[0] * (far // 2), far // 2, far_arrived),
        (packs[0], lambda meta: 0, 1, packs_arrived),
    ]
    far_send, far_keep = product(far_parts)
    far_there = hop(far_send, upper)
    far_keep, gate_arrived, near_there, out_arrived = hold(
        (far_keep, gate_line[1], near_there, out_line[1])
    )
    gate_line = middle((gate_held, gate_arrived))
    near_line = inward(finish_stages(*settle(near_keep, near_there)))
    out_line = outward((out_inner, out_arrived))
    gate_inner, near_held, out_done, far_keep, far_there = hold(
        (gate_line[0], near_line[0], out_line[0], far_keep, far_there)
    )
    far_send, far_keep = settle(far_keep, far_there)
    far_there = hop(far_send, upper // 2)
    far_keep, grad_gate = hold((far_keep, grad_gate))
    (partial,) = input_backward(meta, None, gate_part(0) + gate_part(1), tokens, width)
    partial, far_there = hold((partial, far_there))
    far_line = inward(finish_stages(*settle(far_keep, far_there)))
    far_held, near_arrived, gate_arrived, out_arrived, small_grads = hold(
        (
            far_line[0], near_line[1], gate_line[1], out_line[1],
            (sums_near, sums_far, sums_keys, grad_steps, grad_gain_two),
        )
    )
    sums_near, sums_far, sums_keys, grad_steps, grad_gain_two = small_grads
    sums = jnp.concatenate([sums_near, sums_far, sums_keys], axis=1)
    grads = (
        sums[:CONV].reshape(CONV, count, -1).transpose(1, 0, 2).reshape(count, -1),
        sums[CONV].reshape(count, -1),
        grad_steps[0, :HEADS].reshape(count, -1),
        grad_steps[1, :HEADS].reshape(count, -1),
        jnp.sum(sums[5, :DI].reshape(HEADS, HEADDIM), axis=1).reshape(count, -1),
        jnp.sum(grad_gain_two, axis=0).reshape(count, -1),
    )
    vector = jnp.concatenate(grads, axis=1)
    vector_there = swap(vector)
    gate_line = outward((gate_inner, gate_arrived))
    near_line = middle((near_held, near_arrived))
    out_total = summed((out_done, out_arrived))
    out_other = swap(out_total)
    far_held, gate_done, near_inner, out_total, partial = hold(
        (far_held, gate_line[0], near_line[0], out_total, partial)
    )
    (partial,) = input_backward(
        meta, partial,
        conv_part(grad_near, 0, part, 0, 0),
        tokens, width,
    )
    partial, far_arrived = hold((partial, far_line[1]))
    far_line = middle((far_held, far_arrived))
    far_inner, near_arrived, gate_arrived, out_other, vector_there = hold(
        (far_line[0], near_line[1], gate_line[1], out_other, vector_there)
    )
    spread_rows = group_rows(vector + vector_there, shard, count)
    near_line = outward((near_inner, near_arrived))
    gate_total = summed((gate_done, gate_arrived))
    gate_other = swap(gate_total)
    far_inner, near_done, gate_total, gate_other, partial = hold(
        (far_inner, near_line[0], gate_total, gate_other, partial)
    )
    rows_so_far, sums_one = place_rows(meta, gate_total, gate_other, local, DI // 2, 0, None, False)
    rows_so_far, far_arrived, spread_rows = hold((rows_so_far, far_line[1], spread_rows))
    far_line = outward((far_inner, far_arrived))
    far_done, partial, spread_rows = hold((far_line[0], partial, spread_rows))
    row = chips_sum(add_up(spread_rows))[0]
    (hidden_grad,) = input_backward(
        meta, partial,
        conv_part(grad_near, part, over, 1, 0)
        + conv_part(grad_far, 0, part - over, 1, over)
        + [
            (grad_keys, 0, 1, None, conv_own, DI // 2 // TILE, None, 0, 0),
            (grad_raw, 0, 1, None, conv_own, (DI // 2 + TILE) // 64, None, 0, 0),
        ],
        tokens, width, (hidden, out_grad, inv_rms, gain_one[None]),
    )
    hidden_grad, near_arrived, row = hold((hidden_grad, near_line[1], row))
    near_total = summed((near_done, near_arrived))
    near_other = swap(near_total)
    near_total, far_arrived = hold((near_total, far_line[1]))
    far_total = summed((far_done, far_arrived))
    far_other = swap(far_total)
    wide = near // 2 * TILE
    rows_so_far, sums_two = place_rows(
        meta, near_total, near_other, local, wide, DI // wide, rows_so_far, False
    )
    wide = far // 2 * TILE
    rows_so_far, sums_three = place_rows(
        meta, far_total, far_other, local, wide, (DI + near * TILE) // wide, rows_so_far, True
    )
    gain_row = jnp.sum(sums_one + sums_two + sums_three, axis=0) / norm_gain.astype(F32)
    in_w_grad = rows_so_far.T

    out_w_grad = jnp.concatenate(
        in_order(out_total, out_other, core), axis=0 if paired else 1
    ).astype(F32)
    found, start = [], 0
    for part in grads:
        found.append(row[start : start + part.shape[1]])
        start += part.shape[1]
    return (
        block_out,
        hidden_grad,
        gain_row,
        in_w_grad,
        found[0].reshape(CONV, -1).T,
        found[1],
        found[2],
        found[3],
        found[4],
        found[5],
        out_w_grad,
    )


def solution(mesh):
    return jax.shard_map(
        shards,
        mesh=mesh,
        in_specs=(
            P(("rep", "shard"), None),
            P(("rep", "shard"), None),
            P("shard"),
            P("shard", None),
            P("shard", None),
            P("shard"),
            P("shard"),
            P("shard"),
            P("shard"),
            P("shard"),
            P("shard", None),
            P(("rep", "shard")),
            P(("rep", "shard")),
        ),
        out_specs=(
            P(("rep", "shard"), None),
            P(("rep", "shard"), None),
            P("shard"),
            P("shard", None),
            P("shard", None),
            P("shard"),
            P("shard"),
            P("shard"),
            P("shard"),
            P("shard"),
            P("shard", None),
        ),
        check_vma=False,
    )
```
